128 devices in a mesh: seq: 4 (over z), fsdp: 32 (over x, y, core).
Axes of the slice: x: 4, y: 4, z: 4, core: 2. Of those that a mesh axis runs over, the one named last changes fastest.
Arguments:
- activations: bfloat16 [32, 512, 1536], P('fsdp', 'seq'), may hold values from -6 to 6
- cotangent: bfloat16 [32, 512, 1536], P('fsdp', 'seq'), may hold values from -6 to 6
- seq_lengths: int32 [32, 3], P('fsdp'), may hold values from 1 to 448, 512 in all within a row
- deal_order: int32 [32, 512], P('fsdp'), may hold values from 0 to 511, each once within a row
- routes: int32 [32, 512, 8], P('fsdp', 'seq'), may hold values from 0 to 39, all different within a row; in each aligned block of 128 rows (0 to 127, 128 to 255, ..., all dimensions but the last counted through in order) at most 29 rows name the same one
- entry_weight: float32 [1536, 2560], P(('seq', 'fsdp')), may hold values from -0.15625 to 0.15625
- entry_mean: float32 [1536, 2560], P(('seq', 'fsdp'))
- entry_square: float32 [1536, 2560], P(('seq', 'fsdp')), as said below
- exit_weight: float32 [1536, 1536], P(('seq', 'fsdp')), may hold values from -2.5 to 2.5
- exit_mean: float32 [1536, 1536], P(('seq', 'fsdp'))
- exit_square: float32 [1536, 1536], P(('seq', 'fsdp')), as said below
- router_weight: float32 [1536, 40], P(('seq', 'fsdp')), may hold values from -0.078125 to 0.078125
- router_mean: float32 [1536, 40], P(('seq', 'fsdp'))
- router_square: float32 [1536, 40], P(('seq', 'fsdp')), as said below
- expand_weight: float32 [40, 1536, 1024], P('seq', 'fsdp'), may hold values from -0.15625 to 0.15625
- expand_mean: float32 [40, 1536, 1024], P('seq', 'fsdp')
- expand_square: float32 [40, 1536, 1024], P('seq', 'fsdp'), as said below
- shrink_weight: float32 [40, 512, 1536], P('seq', 'fsdp'), may hold values from -1 to 1
- shrink_mean: float32 [40, 512, 1536], P('seq', 'fsdp')
- shrink_square: float32 [40, 512, 1536], P('seq', 'fsdp'), as said below
- norm_gains: float32 [2, 1536], P(None, ('seq', 'fsdp')), may hold values from 0.5 to 1.5
- gains_mean: float32 [2, 1536], P(None, ('seq', 'fsdp'))
- gains_square: float32 [2, 1536], P(None, ('seq', 'fsdp')), as said below
Outputs:
- block_output: bfloat16 [32, 512, 1536], P('fsdp', 'seq')
- input_grad: bfloat16 [32, 512, 1536], P('fsdp', 'seq')
- entry_drift: float32 [1536, 2560], P(('seq', 'fsdp'))
- entry_spread: float32 [1536, 2560], P(('seq', 'fsdp'))
- entry_master: float32 [1536, 2560], P(('seq', 'fsdp'))
- exit_drift: float32 [1536, 1536], P(('seq', 'fsdp'))
- exit_spread: float32 [1536, 1536], P(('seq', 'fsdp'))
- exit_master: float32 [1536, 1536], P(('seq', 'fsdp'))
- router_drift: float32 [1536, 40], P(('seq', 'fsdp'))
- router_spread: float32 [1536, 40], P(('seq', 'fsdp'))
- router_master: float32 [1536, 40], P(('seq', 'fsdp'))
- expand_drift: float32 [40, 1536, 1024], P('seq', 'fsdp')
- expand_spread: float32 [40, 1536, 1024], P('seq', 'fsdp')
- expand_master: float32 [40, 1536, 1024], P('seq', 'fsdp')
- shrink_drift: float32 [40, 512, 1536], P('seq', 'fsdp')
- shrink_spread: float32 [40, 512, 1536], P('seq', 'fsdp')
- shrink_master: float32 [40, 512, 1536], P('seq', 'fsdp')
- gains_drift: float32 [2, 1536], P(None, ('seq', 'fsdp'))
- gains_spread: float32 [2, 1536], P(None, ('seq', 'fsdp'))
- gains_master: float32 [2, 1536], P(None, ('seq', 'fsdp'))
The draws below stay inside these ranges and needn't reach their ends.
Inputs may be any that keep to these rules, and one draw needn't show every extreme that they name: `seq_lengths`: each row sums to 512 and its longest entry is 448. `deal_order`: each row names every slot's token once. `routes`: each slot names 8 different experts; among the 128 slots of one device no expert is named more than 29 times. `entry_square`: positive. `exit_square`: positive. `router_square`: positive. `expand_square`: positive. `shrink_square`: positive. `gains_square`: positive.
All inputs are finite; a program needn't handle non-finite values.
Results may differ from the reference program's by a relative error of at most 0.025.
Values may be sent and summed in bfloat16 or wider, within the bound.
A program may use at most 320 MiB of HBM per device.

```python
import math
import jax
import jax.numpy as jnp
import numpy as np
from jax import lax

D = 1536
QH = 24
KVH = 8
HD = 64
FF = 512
EXPERTS = 40
TOP = 8
TOK_DEV = 128
SEQS = 3
STEP = 10
GROUPS = 32
GROUP_TOK = 512
MOST = 448
TOKENS = 16384
CAP = 29
N_SEQ = 4
N_FSDP = 32


def grad_rms(weight_kind):
    attn_rms = 1.5 / (2.0 * TOK_DEV) ** 0.5
    exit_std = max(1, QH * HD // (2 * TOK_DEV)) ** (-0.5)
    routed = TOKENS * TOP / EXPERTS
    if weight_kind == 0:
        return 1.3 * exit_std * D ** 0.5 * attn_rms * TOKENS ** 0.5
    if weight_kind == 1:
        return 1.3 * attn_rms * TOKENS ** 0.5
    if weight_kind == 2:
        return 2.4 * D ** 0.5 / TOP * routed ** 0.5
    if weight_kind == 3:
        return 2.4 / TOP * routed ** 0.5
    if weight_kind == 4:
        return 0.6 / TOP * routed ** 0.5
    return TOKENS ** 0.5


def shape_of(weight_kind):
    if weight_kind == 0:
        return (D, (QH + 2 * KVH) * HD)
    if weight_kind == 1:
        return (QH * HD, D)
    if weight_kind == 2:
        return (D, EXPERTS)
    if weight_kind == 3:
        return (EXPERTS, D, 2 * FF)
    if weight_kind == 4:
        return (EXPERTS, FF, D)
    return (2, D)


def first_moment(key, weight_kind):
    scale_now = grad_rms(weight_kind) / 9.0
    return scale_now * jax.random.truncated_normal(key, -3.0, 3.0, shape_of(weight_kind), jnp.float32)


def second_moment(key, weight_kind):
    scale_now = grad_rms(weight_kind) ** 2 / 19.0
    factor = jnp.exp(jax.random.uniform(key, shape_of(weight_kind), jnp.float32, 0.0, 1.3862944))
    return scale_now * factor


def draw_entry_mean(key, part):
    key = jax.random.fold_in(key, 11)
    return first_moment(key, 0)


def draw_entry_square(key, part):
    key = jax.random.fold_in(key, 12)
    return second_moment(key, 0)


def draw_exit_mean(key, part):
    key = jax.random.fold_in(key, 21)
    return first_moment(key, 1)


def draw_exit_square(key, part):
    key = jax.random.fold_in(key, 22)
    return second_moment(key, 1)


def draw_router_mean(key, part):
    key = jax.random.fold_in(key, 31)
    return first_moment(key, 2)


def draw_router_square(key, part):
    key = jax.random.fold_in(key, 32)
    return second_moment(key, 2)


def draw_expand_mean(key, part):
    key = jax.random.fold_in(key, 41)
    return first_moment(key, 3)


def draw_expand_square(key, part):
    key = jax.random.fold_in(key, 42)
    return second_moment(key, 3)


def draw_shrink_mean(key, part):
    key = jax.random.fold_in(key, 51)
    return first_moment(key, 4)


def draw_shrink_square(key, part):
    key = jax.random.fold_in(key, 52)
    return second_moment(key, 4)


def draw_gains_mean(key, part):
    key = jax.random.fold_in(key, 61)
    return first_moment(key, 5)


def draw_gains_square(key, part):
    key = jax.random.fold_in(key, 62)
    return second_moment(key, 5)


def levels(rng, extent, shards, least, largest):
    def one(axis_at, shards_of):
        draws = jax.random.uniform(jax.random.fold_in(jax.random.fold_in(rng, 6), axis_at), (shards_of,), jnp.float32, least / len(shards), largest / len(shards))
        return jnp.repeat(jnp.exp(draws), extent[axis_at] // shards_of).reshape((-1,) + (1,) * (len(extent) - axis_at - 1))

    loudness = one(*shards[0])
    for cut in shards[1:]:
        loudness = loudness * one(*cut)
    return loudness


def split_up(number_of, total, limit, skew):
    weights = [(1 << 20) // math.isqrt(rank ** skew) + 1 for rank in range(2, number_of + 1)]
    spare, given = total - limit - (number_of - 1), [1] * (number_of - 1)
    while spare > 0:
        free = [i for i in range(number_of - 1) if given[i] < limit]
        mass, budget = sum([weights[i] for i in free]), spare
        for i in free:
            addition = min(limit - given[i], max(1, budget * weights[i] // mass), spare)
            given[i] = given[i] + addition
            spare = spare - addition
    return np.array([limit] + given)


def uneven(own_key, count, total, reach, lean):
    if count == 2:
        one = jax.random.randint(own_key, (), max(1, total - reach), min(reach, total - 1) + 1)
        return jnp.stack([one, total - one])
    sizes = jnp.asarray(split_up(count, total, reach, lean), jnp.int32)
    pairs = (count - 1) // 2
    source_of, taker = sizes[1:1 + 2 * pairs:2], sizes[2:2 + 2 * pairs:2]
    slack = jnp.minimum(source_of - 1, reach - taker)
    moved = jax.random.randint(jax.random.fold_in(own_key, 1), (pairs,), 0, 1 << 20) % (slack + 1)
    sizes = sizes.at[1:1 + 2 * pairs:2].set(source_of - moved).at[2:2 + 2 * pairs:2].set(taker + moved)
    return sizes[jax.random.permutation(jax.random.fold_in(own_key, 2), count)]


def routed_block(key, own, number, rows, count, top, limit, lean):
    ranking = jax.random.permutation(key, count)
    crowded, common = load_shares(count, rows * top, limit, lean, True), load_shares(count, rows * top, limit, lean, False)
    places = jnp.arange(count)

    def named(lengths, offset_by):
        used = int((lengths > 0).sum())
        fixed = max(1, used // 4)
        shifted = fixed + (places - fixed + offset_by * (used - fixed)) % max(1, count - fixed)
        return jnp.zeros((count,), jnp.int32).at[ranking[jnp.where(places < fixed, places, shifted)]].set(jnp.asarray(lengths, jnp.int32))

    lengths = jnp.where(number % 4 == 0, named(crowded, number // 4), named(common, number - number // 4 - 1))
    mixed = jax.random.permutation(jax.random.fold_in(own, 3), count)
    donor, taker = mixed[0:count // 2 * 2:2], mixed[1:count // 2 * 2:2]
    margin = jnp.minimum(lengths[donor] - 1, limit - lengths[taker]) // 2
    margin = jnp.where((donor == ranking[0]) | (taker == ranking[0]) | (lengths[taker] == 0), 0, jnp.maximum(margin, 0))
    shifted = jax.random.randint(jax.random.fold_in(own, 4), (count // 2,), 0, 1 << 20) % (margin + 1)
    lengths = lengths.at[donor].add(-shifted).at[taker].add(shifted)
    members = jnp.searchsorted(jnp.cumsum(lengths), jnp.arange(rows * top), side="right").astype(jnp.int32)
    listing = members.reshape(top, rows).T
    listing = listing[jax.random.permutation(jax.random.fold_in(own, 1), rows)]
    offset_by = jax.random.randint(jax.random.fold_in(own, 2), (rows, 1), 0, top)
    return jnp.take_along_axis(listing, (jnp.arange(top)[None, :] + offset_by) % top, axis=1)


def load_shares(count, total, bound, slope, full):
    portions = [(1 << 20) // math.isqrt(standing ** slope) + 1 for standing in range(1, count + 1)]
    largest = bound if full else min(bound, max(-(-total // count), total * portions[0] // sum(portions)))
    least = 1 if total - largest >= count - 1 else 0
    counts, rest = [largest] + [least] * (count - 1), total - largest - least * (count - 1)
    while rest > 0:
        free = [i for i in range(1, count) if counts[i] < largest] or [i for i in range(1, count) if counts[i] < bound]
        whole, left = sum([portions[i] for i in free]), rest
        for i in free:
            more = min(bound - counts[i], max(1, left * portions[i] // whole), rest)
            counts[i] = counts[i] + more
            rest = rest - more
    return np.array(counts)


def noise(key, shape, scale, limit, split=(), held_as=jnp.bfloat16):
    result = jax.random.normal(key, shape, jnp.float32) * scale
    if len(split) > 0:
        result = levels(key, shape, split, -0.22, 0.18) * result
    return jnp.clip(result, min=-limit, max=limit).astype(held_as)


def setup_inputs(seed: int = 0) -> dict:
    key_list = jax.random.split(jax.random.key(seed), 24)
    activations = noise(key_list[0], (GROUPS, GROUP_TOK, D), 1.0, 6.0, ((0, 32), (1, 4)))
    cotangent = noise(key_list[1], (GROUPS, GROUP_TOK, D), 1.0, 6.0, ((0, 32), (1, 4)))
    seq_lengths = jax.vmap(lambda own: uneven(own, SEQS, GROUP_TOK, MOST, 2))(jax.random.split(key_list[2], GROUPS)).reshape((GROUPS, SEQS)).astype(jnp.int32)
    deal_order = jax.vmap(lambda own: jax.random.permutation(own, GROUP_TOK))(jax.random.split(key_list[3], GROUPS)).reshape((GROUPS, GROUP_TOK)).astype(jnp.int32)
    routes_keys = jax.random.split(jax.random.fold_in(key_list[4], 1), GROUPS * GROUP_TOK // TOK_DEV)
    routes_turns = jax.random.permutation(jax.random.fold_in(key_list[4], 3), GROUPS * GROUP_TOK // TOK_DEV)
    routes = jax.vmap(lambda own, number: routed_block(jax.random.fold_in(key_list[4], 2), own, number, TOK_DEV, EXPERTS, TOP, CAP, 2))(routes_keys, routes_turns).reshape((GROUPS, GROUP_TOK, TOP))
    entry_weight = noise(key_list[5], (D, (QH + 2 * KVH) * HD), D ** -0.5, 0.15625, ((0, 128),), jnp.float32)
    entry_mean = draw_entry_mean(jax.random.fold_in(key_list[23], 71), 0)
    entry_square = draw_entry_square(jax.random.fold_in(key_list[23], 71), 0)
    exit_weight = noise(key_list[8], (QH * HD, D), (max(1, QH * HD // (2 * TOK_DEV))) ** -0.5, 2.5, ((0, 128),), jnp.float32)
    exit_mean = draw_exit_mean(jax.random.fold_in(key_list[23], 71), 0)
    exit_square = draw_exit_square(jax.random.fold_in(key_list[23], 71), 0)
    router_weight = noise(key_list[11], (D, EXPERTS), (4 * D) ** -0.5, 0.078125, ((0, 128),), jnp.float32)
    router_mean = draw_router_mean(jax.random.fold_in(key_list[23], 71), 0)
    router_square = draw_router_square(jax.random.fold_in(key_list[23], 71), 0)
    expand_weight = noise(key_list[14], (EXPERTS, D, 2 * FF), D ** -0.5, 0.15625, ((0, 4), (1, 32)), jnp.float32)
    expand_mean = draw_expand_mean(jax.random.fold_in(key_list[23], 71), 0)
    expand_square = draw_expand_square(jax.random.fold_in(key_list[23], 71), 0)
    shrink_weight = noise(key_list[17], (EXPERTS, FF, D), (max(1, FF // 16)) ** -0.5, 1.0, ((0, 4), (1, 32)), jnp.float32)
    shrink_mean = draw_shrink_mean(jax.random.fold_in(key_list[23], 71), 0)
    shrink_square = draw_shrink_square(jax.random.fold_in(key_list[23], 71), 0)
    norm_gains = jnp.clip(1.0 + 0.1 * jax.random.normal(key_list[20], (2, D), jnp.float32), 0.5, 1.5)
    gains_mean = draw_gains_mean(jax.random.fold_in(key_list[23], 71), 0)
    gains_square = draw_gains_square(jax.random.fold_in(key_list[23], 71), 0)
    return dict(activations=activations, cotangent=cotangent, seq_lengths=seq_lengths, deal_order=deal_order, routes=routes, entry_weight=entry_weight, entry_mean=entry_mean, entry_square=entry_square, exit_weight=exit_weight, exit_mean=exit_mean, exit_square=exit_square, router_weight=router_weight, router_mean=router_mean, router_square=router_square, expand_weight=expand_weight, expand_mean=expand_mean, expand_square=expand_square, shrink_weight=shrink_weight, shrink_mean=shrink_mean, shrink_square=shrink_square, norm_gains=norm_gains, gains_mean=gains_mean, gains_square=gains_square)


@jax.custom_vjp
def low(v):
    return lax.optimization_barrier(v.astype(jnp.bfloat16)).astype(jnp.float32)

@jax.custom_vjp
def low_back(v):
    return v

def low_keep(v):
    return (low(v), None)

def low_pass(kept, grad):
    return (grad,)

def back_keep(v):
    return (v, None)

def back_low(kept, grad):
    return (low(grad),)
low.defvjp(low_keep, low_pass)
low_back.defvjp(back_keep, back_low)
norm_eps = 1e-06
rope_base = 10000.0
beta_first = 0.9
beta_second = 0.95
adam_eps = 1e-08
weight_decay = 0.1
highest = lax.Precision.HIGHEST

def rms_norm(vector, gain_vec):
    return vector * lax.rsqrt(lax.optimization_barrier(jnp.mean(vector * vector, axis=-1, keepdims=True)) + norm_eps) * gain_vec

def seq_layout(lengths_row, order_row):
    seq_ends = jnp.cumsum(lengths_row).astype(jnp.int32)
    starts = (seq_ends - lengths_row).astype(jnp.int32)
    seq_ids = lax.optimization_barrier(jnp.sum((order_row[:, None] >= seq_ends[None, :]).astype(jnp.int32), axis=1)).astype(jnp.int32)
    seq_match = seq_ids[:, None] == jnp.arange(lengths_row.shape[0], dtype=jnp.int32)[None, :]
    positions = (order_row - lax.optimization_barrier(jnp.sum(jnp.where(seq_match, starts[None, :], 0), axis=1))).astype(jnp.int32)
    return (seq_ids, positions)

def rotate(vector, positions):
    width = vector.shape[-1]
    half_width = width // 2
    frequency = rope_base ** (-jnp.arange(half_width, dtype=jnp.float32) * 2.0 / width)
    phase_angle = positions.astype(jnp.float32)[:, None] * frequency[None, :]
    cosine = jnp.cos(phase_angle)[:, None, :]
    sine_part = jnp.sin(phase_angle)[:, None, :]
    first_half = vector[..., :half_width]
    second_half = vector[..., half_width:]
    return jnp.concatenate([first_half * cosine - second_half * sine_part, second_half * cosine + first_half * sine_part], axis=-1)

def attend_group(queries, key_heads, values, seq_ids, positions):
    group_tok = queries.shape[0]
    grouped = queries.reshape(group_tok, KVH, QH // KVH, HD)
    raw_scores = jnp.einsum('qhgd,khd->hgqk', grouped, key_heads, precision=highest, preferred_element_type=jnp.float32)
    scores = low_back(raw_scores) * HD ** (-0.5)
    allowed = (seq_ids[:, None] == seq_ids[None, :]) & (positions[None, :] <= positions[:, None])
    scores = jnp.where(allowed[None, None], scores, -1e+30)
    row_peak = lax.optimization_barrier(jnp.max(scores, axis=-1, keepdims=True))
    row_expo = jnp.exp(scores - row_peak)
    prob_rows = low(row_expo / lax.optimization_barrier(jnp.sum(row_expo, axis=-1, keepdims=True)))
    mixed_heads = jnp.einsum('hgqk,khd->qhgd', prob_rows, values, precision=highest, preferred_element_type=jnp.float32)
    return mixed_heads.reshape(group_tok, QH * HD)

def expert_tables(flat_routes):
    total_rows = flat_routes.shape[0]
    most_rows = N_SEQ * N_FSDP * CAP

    def one_expert(expert):
        route_hit = (flat_routes == expert).astype(jnp.int32)
        chosen = lax.optimization_barrier(jnp.sum(route_hit, axis=1))
        route_pick = lax.optimization_barrier(jnp.sum(route_hit * jnp.arange(TOP, dtype=jnp.int32)[None, :], axis=1)).astype(jnp.int32)
        slot_rank = (jnp.cumsum(chosen) - 1).astype(jnp.int32)
        target = jnp.where(chosen > 0, slot_rank, most_rows).astype(jnp.int32)
        tokens_at = jnp.zeros((most_rows,), jnp.int32).at[target].set(jnp.arange(total_rows, dtype=jnp.int32), mode='drop')
        slot_at = jnp.zeros((most_rows,), jnp.int32).at[target].set(route_pick, mode='drop')
        row_count = jnp.sum(chosen)
        return (tokens_at, slot_at, jnp.arange(most_rows, dtype=jnp.int32) < row_count)
    return lax.map(one_expert, jnp.arange(EXPERTS, dtype=jnp.int32))

def adamw_step(weight, gradient, mean_old, square_old, rate, decay):
    drift = beta_first * mean_old + (1.0 - beta_first) * gradient
    spread = beta_second * square_old + (1.0 - beta_second) * gradient * gradient
    mean_hat = drift / (1.0 - beta_first ** STEP)
    square_hat = spread / (1.0 - beta_second ** STEP)
    master = weight - rate * (mean_hat / (jnp.sqrt(square_hat) + adam_eps) + decay * weight)
    return (drift, spread, master)

def take_rows(table, order_row):
    return jnp.take(table, order_row, axis=0)

def put_rows(rows_in, order_row):
    return jnp.zeros_like(rows_in).at[order_row].set(rows_in)

def reference(activations, cotangent, seq_lengths, deal_order, routes, entry_weight, entry_mean, entry_square, exit_weight, exit_mean, exit_square, router_weight, router_mean, router_square, expand_weight, expand_mean, expand_square, shrink_weight, shrink_mean, shrink_square, norm_gains, gains_mean, gains_square):
    dealt_rows = jax.vmap(take_rows)(activations, deal_order).astype(jnp.float32)
    dealt_cot = jax.vmap(take_rows)(cotangent, deal_order).astype(jnp.float32)
    seq_ids, positions = jax.vmap(seq_layout)(seq_lengths, deal_order)
    groups, group_tok = (dealt_rows.shape[0], dealt_rows.shape[1])
    flat_routes = routes.reshape(groups * group_tok, TOP)
    tokens_at, slot_at, row_valid = expert_tables(flat_routes)
    row_keep = row_valid.astype(jnp.float32)

    def forward(weights, inputs):
        entry_w, exit_w, router_w, expand_w, shrink_w, gains_w = [low(weight) for weight in weights]
        normed = low(rms_norm(inputs, gains_w[0]))
        mixed_proj = low_back(jnp.einsum('gtd,dc->gtc', normed, entry_w, precision=highest, preferred_element_type=jnp.float32))
        query_raw = mixed_proj[..., :QH * HD].reshape(groups, group_tok, QH, HD)
        pair_proj = mixed_proj[..., QH * HD:].reshape(groups, group_tok, KVH, 2, HD)
        queries = low(jax.vmap(rotate)(query_raw, positions))
        key_heads = low(jax.vmap(rotate)(pair_proj[..., 0, :], positions))
        values = low(pair_proj[..., 1, :])

        def group_attend(packed):
            return attend_group(packed[0], packed[1], packed[2], packed[3], packed[4])
        attended = lax.map(jax.checkpoint(group_attend), (queries, key_heads, values, seq_ids, positions))
        attended = low(low_back(attended))
        branch = low_back(jnp.einsum('gtc,cd->gtd', attended, exit_w, precision=highest, preferred_element_type=jnp.float32))
        middle = inputs + branch
        normed_two = low(rms_norm(middle, gains_w[1]))
        logits = low_back(jnp.einsum('gtd,de->gte', normed_two, router_w, precision=highest, preferred_element_type=jnp.float32))
        picked = jnp.take_along_axis(logits, routes, axis=-1)
        gate_peak = lax.optimization_barrier(jnp.max(picked, axis=-1, keepdims=True))
        gate_expo = jnp.exp(picked - gate_peak)
        gate_probs = gate_expo / lax.optimization_barrier(jnp.sum(gate_expo, axis=-1, keepdims=True))
        flat_normed = normed_two.reshape(groups * group_tok, D)

        def expert_one(packed):
            expand_mat, shrink_mat, row_index, row_mask = packed
            rows_in = low_back(jnp.take(flat_normed, row_index, axis=0)) * row_mask[:, None]
            gate_up = low_back(jnp.dot(rows_in, expand_mat, precision=highest, preferred_element_type=jnp.float32))
            hidden = low(jax.nn.silu(gate_up[:, :FF]) * gate_up[:, FF:])
            return low(low_back(jnp.dot(hidden, shrink_mat, precision=highest, preferred_element_type=jnp.float32)))
        expert_outs = lax.map(jax.checkpoint(expert_one), (expand_w, shrink_w, tokens_at, row_keep))
        flat_gates = gate_probs.reshape(groups * group_tok, TOP)
        row_gates = flat_gates[tokens_at, slot_at] * row_keep
        summed = jnp.zeros_like(flat_normed).at[tokens_at.reshape(-1)].add((row_gates[..., None] * expert_outs).reshape(-1, D))
        return middle + summed.reshape(groups, group_tok, D)
    masters = (entry_weight, exit_weight, router_weight, expand_weight, shrink_weight, norm_gains)
    outputs, pullback = jax.vjp(forward, masters, dealt_rows)
    weight_grads, dealt_grad = pullback(dealt_cot)
    block_output = jax.vmap(put_rows)(outputs, deal_order).astype(jnp.bfloat16)
    input_grad = jax.vmap(put_rows)(dealt_grad, deal_order).astype(jnp.bfloat16)
    entry_drift, entry_spread, entry_master = adamw_step(entry_weight, weight_grads[0], entry_mean, entry_square, 0.02, weight_decay)
    exit_drift, exit_spread, exit_master = adamw_step(exit_weight, weight_grads[1], exit_mean, exit_square, 0.15, weight_decay)
    router_drift, router_spread, router_master = adamw_step(router_weight, weight_grads[2], router_mean, router_square, 0.01, weight_decay)
    expand_drift, expand_spread, expand_master = adamw_step(expand_weight, weight_grads[3], expand_mean, expand_square, 0.02, weight_decay)
    shrink_drift, shrink_spread, shrink_master = adamw_step(shrink_weight, weight_grads[4], shrink_mean, shrink_square, 0.12, weight_decay)
    gains_drift, gains_spread, gains_master = adamw_step(norm_gains, weight_grads[5], gains_mean, gains_square, 0.5, 0.0)
    return (block_output, input_grad, entry_drift, entry_spread, entry_master, exit_drift, exit_spread, exit_master, router_drift, router_spread, router_master, expand_drift, expand_spread, expand_master, shrink_drift, shrink_spread, shrink_master, gains_drift, gains_spread, gains_master)
```

```python
import jax
import jax.numpy as jnp
from jax import lax
from jax.experimental import pallas as pl
from jax.experimental.pallas import tpu as pltpu
from jax.sharding import Mesh, PartitionSpec as P

D = 1536
QH = 24
KVH = 8
HD = 64
FF = 512
EXPERTS = 40
TOP = 8
STEP = 10
CAP = 29

N_SEQ = 4
TOK_DEV = 128
GROUP = 512
PAIR_TOK = 2 * GROUP
LOCAL_E = EXPERTS // (2 * N_SEQ)
SLOTS = 240
Q_OWN = QH * HD // N_SEQ
KV_OWN = 2 * KVH * HD // N_SEQ
MIX_OWN = Q_OWN + KV_OWN
HEADS_OWN = QH // N_SEQ
KV_HEADS_OWN = KVH // N_SEQ
PER_KV = QH // KVH
ROWS = 12

norm_eps = 1e-06
rope_base = 10000.0
beta_first = 0.9
beta_second = 0.95
adam_eps = 1e-08
weight_decay = 0.1

FSDP = ("x", "y", "core")
PLANE = ("x", "y")
f32 = jnp.float32
bf16 = jnp.bfloat16


def dot(a, b, dims):
    return lax.dot_general(a, b, (dims, ((), ())), preferred_element_type=f32)


def z_exchange(call_id, gathered=(), scattered=()):
    arrays = list(gathered) + list(scattered)
    n_gather = len(gathered)
    count = len(arrays)

    def kernel(*refs):
        ins, outs = refs[:count], refs[count : 2 * count]
        send_sem, recv_sem, copy_sem = refs[2 * count :]
        me = lax.axis_index("seq")
        peers = [lax.rem(me + k, N_SEQ) for k in range(1, N_SEQ)]
        barrier = pltpu.get_barrier_semaphore()
        for peer in peers:
            pl.semaphore_signal(
                barrier, inc=1, device_id={"seq": peer}, device_id_type=pl.DeviceIdType.MESH
            )
        pl.semaphore_wait(barrier, N_SEQ - 1)
        copies = []
        for i in range(count):
            for k in (0, 2, 1):
                peer = peers[k]
                source = ins[i] if i < n_gather else ins[i].at[peer]
                copy = pltpu.make_async_remote_copy(
                    src_ref=source,
                    dst_ref=outs[i].at[me],
                    send_sem=send_sem.at[i, k],
                    recv_sem=recv_sem.at[i, k],
                    device_id={"seq": peer},
                    device_id_type=pl.DeviceIdType.MESH,
                )
                copy.start()
                copies.append(copy)
        for i in range(count):
            source = ins[i] if i < n_gather else ins[i].at[me]
            copy = pltpu.make_async_copy(source, outs[i].at[me], copy_sem.at[i])
            copy.start()
            copies.append(copy)
        for copy in copies:
            copy.wait()

    shapes = [
        jax.ShapeDtypeStruct((N_SEQ,) + a.shape if i < n_gather else a.shape, a.dtype)
        for i, a in enumerate(arrays)
    ]
    return pl.pallas_call(
        kernel,
        out_shape=shapes,
        in_specs=[pl.BlockSpec(memory_space=pl.ANY)] * count,
        out_specs=[pl.BlockSpec(memory_space=pl.ANY)] * count,
        scratch_shapes=[
            pltpu.SemaphoreType.DMA((count, N_SEQ - 1)),
            pltpu.SemaphoreType.DMA((count, N_SEQ - 1)),
            pltpu.SemaphoreType.DMA((count,)),
        ],
        compiler_params=pltpu.CompilerParams(collective_id=call_id, has_side_effects=True),
    )(*arrays)


def core_swap(value):
    return lax.ppermute(value, "core", [(0, 1), (1, 0)])


def core_order(core, mine, other, axis):
    return jnp.concatenate(
        [jnp.where(core == 0, mine, other), jnp.where(core == 0, other, mine)], axis=axis
    )


def flat_rows(parts, rows):
    flat = jnp.concatenate([p.reshape(-1) for p in parts])
    return jnp.pad(flat, (0, rows * 128 - flat.shape[0])).reshape(rows, 128)


def norm_back(vector, gain, grad):
    scale = lax.rsqrt(jnp.mean(vector * vector, axis=-1, keepdims=True) + norm_eps)
    unit = vector * scale
    pulled = grad * gain
    back = scale * (pulled - unit * jnp.mean(pulled * unit, axis=-1, keepdims=True))
    return back, jnp.sum(unit * grad, axis=0)


def norm_apply(vector, gain):
    scale = lax.rsqrt(jnp.mean(vector * vector, axis=-1, keepdims=True) + norm_eps)
    return vector * scale * gain


def adamw_step(weight, gradient, mean_old, square_old, rate, decay):
    drift = beta_first * mean_old + (1.0 - beta_first) * gradient
    spread = beta_second * square_old + (1.0 - beta_second) * gradient * gradient
    mean_hat = drift / (1.0 - beta_first**STEP)
    square_hat = spread / (1.0 - beta_second**STEP)
    master = weight - rate * (mean_hat / (jnp.sqrt(square_hat) + adam_eps) + decay * weight)
    return (drift, spread, master)


def rotate(vector, cosine, sine):
    first, second = vector[..., : HD // 2], vector[..., HD // 2 :]
    return jnp.concatenate(
        [first * cosine - second * sine, second * cosine + first * sine], axis=-1
    )


def on_device(
    activations,
    cotangent,
    seq_lengths,
    deal_order,
    routes,
    entry_weight,
    entry_mean,
    entry_square,
    exit_weight,
    exit_mean,
    exit_square,
    router_weight,
    router_mean,
    router_square,
    expand_weight,
    expand_mean,
    expand_square,
    shrink_weight,
    shrink_mean,
    shrink_square,
    norm_gains,
    gains_mean,
    gains_square,
):
    seq = lax.axis_index("seq")
    core = lax.axis_index("core")

    def to_core(weight):
        weight = weight.astype(bf16)
        mine = lax.dynamic_slice_in_dim(weight, core * LOCAL_E, LOCAL_E, 0)
        other = lax.dynamic_slice_in_dim(weight, (1 - core) * LOCAL_E, LOCAL_E, 0)
        return core_order(core, mine, core_swap(other), 1)

    expand_part, shrink_part = to_core(expand_weight), to_core(shrink_weight)

    entry_b = entry_weight.astype(bf16)
    entry_cols = jnp.concatenate(
        [
            entry_b[:, : QH * HD].reshape(ROWS, N_SEQ, Q_OWN),
            entry_b[:, QH * HD :].reshape(ROWS, N_SEQ, KV_OWN),
        ],
        axis=2,
    ).transpose(1, 0, 2)
    expert_ids = jnp.arange(EXPERTS, dtype=jnp.int32)
    hit_slots = jnp.any(routes[0][:, :, None] == expert_ids[None, None, :], axis=1).astype(bf16)
    shared = jnp.concatenate(
        [
            router_weight.astype(bf16).reshape(-1),
            norm_gains.astype(bf16).reshape(-1),
            hit_slots.reshape(-1),
        ]
    )
    payload = jnp.concatenate(
        [
            entry_cols.reshape(N_SEQ, -1),
            jnp.broadcast_to(shared[None], (N_SEQ,) + shared.shape),
        ],
        axis=1,
    )
    payload = jnp.pad(payload, ((0, 0), (0, 112 * 128 - payload.shape[1])))
    in_all, cot_all, small = z_exchange(
        1, gathered=(activations[0], cotangent[0]), scattered=(payload.reshape(N_SEQ, 112, 128),)
    )
    in_all = in_all.reshape(GROUP, D)
    cot_all = cot_all.reshape(GROUP, D)
    small = small.reshape(N_SEQ, 112 * 128)
    n_entry, n_router, n_gain = ROWS * MIX_OWN, ROWS * EXPERTS, 2 * ROWS
    hit_base = n_entry + n_router + n_gain
    hit_slot_all = small[:, hit_base : hit_base + TOK_DEV * EXPERTS].reshape(GROUP, EXPERTS)
    packed = flat_rows([small[:, :hit_base], exit_weight.astype(bf16)], 400)
    full = lax.all_gather(packed, FSDP, axis=0, tiled=False).reshape(32, 400 * 128)
    n_small = N_SEQ * hit_base
    from_z = full[:, :n_small].reshape(32, N_SEQ, hit_base).transpose(1, 0, 2)
    entry_own = from_z[:, :, :n_entry].reshape(D, MIX_OWN)
    router_full = from_z[:, :, n_entry : n_entry + n_router].reshape(D, EXPERTS)
    gains_full = (
        from_z[:, :, n_entry + n_router :]
        .reshape(N_SEQ, 32, 2, ROWS)
        .transpose(2, 0, 1, 3)
        .reshape(2, D)
        .astype(f32)
    )
    exit_own = full[:, n_small : n_small + ROWS * D].reshape(Q_OWN, D)

    expand_full = lax.all_gather(expand_part, PLANE, axis=1, tiled=True)
    shrink_full = lax.all_gather(shrink_part, PLANE, axis=1, tiled=True)

    order_row = deal_order[0]
    token = jnp.arange(GROUP, dtype=jnp.int32)
    back_hot = (order_row[None, :] == token[:, None]).astype(bf16)
    hit = dot(back_hot, hit_slot_all, ((1,), (0,)))
    seq_ends = jnp.cumsum(seq_lengths[0])
    starts = seq_ends - seq_lengths[0]
    seq_ids = jnp.sum((token[:, None] >= seq_ends[None, :]).astype(jnp.int32), axis=1)
    seq_match = seq_ids[:, None] == jnp.arange(seq_ends.shape[0], dtype=jnp.int32)[None, :]
    positions = token - jnp.sum(jnp.where(seq_match, starts[None, :], 0), axis=1)
    frequency = rope_base ** (-jnp.arange(HD // 2, dtype=f32) * 2.0 / HD)
    phase = positions.astype(f32)[:, None] * frequency[None, :]
    cosine, sine = jnp.cos(phase)[:, None, :], jnp.sin(phase)[:, None, :]
    allowed = (seq_ids[:, None] == seq_ids[None, :]) & (token[None, :] <= token[:, None])

    normed = norm_apply(in_all.astype(f32), gains_full[0]).astype(bf16)
    mixed = dot(normed, entry_own, ((1,), (0,)))
    queries = rotate(mixed[:, :Q_OWN].reshape(GROUP, HEADS_OWN, HD), cosine, sine)
    pairs = mixed[:, Q_OWN:].reshape(GROUP, KV_HEADS_OWN, 2, HD)
    keys = rotate(pairs[:, :, 0], cosine, sine)
    queries = queries.astype(bf16).reshape(GROUP, KV_HEADS_OWN, PER_KV, HD)
    keys, values = keys.astype(bf16), pairs[:, :, 1].astype(bf16)
    scores = jnp.einsum("qhgd,khd->hgqk", queries, keys, preferred_element_type=f32) * HD**-0.5
    scores = jnp.where(allowed[None, None], scores, -1e30)
    peak = jnp.max(scores, axis=-1, keepdims=True)
    expo = jnp.exp(scores - peak)
    probs = expo / jnp.sum(expo, axis=-1, keepdims=True)
    probs_b = probs.astype(bf16)
    attended = (
        jnp.einsum("hgqk,khd->qhgd", probs_b, values, preferred_element_type=f32)
        .reshape(GROUP, Q_OWN)
        .astype(bf16)
    )
    branch_part = dot(attended, exit_own, ((1,), (0,))).astype(bf16)
    (branch,) = z_exchange(2, scattered=(branch_part.reshape(N_SEQ, TOK_DEV, D),))
    middle = activations[0].astype(f32) + jnp.sum(branch.astype(f32), axis=0)
    normed_two = norm_apply(middle, gains_full[1]).astype(bf16)
    (two_all,) = z_exchange(3, gathered=(normed_two,))
    two_all = two_all.reshape(GROUP, D)

    tokens = core_order(core, two_all, core_swap(two_all), 0)
    cots = core_order(core, cot_all, core_swap(cot_all), 0)
    hits = core_order(core, hit, core_swap(hit), 0)

    logits = dot(tokens, router_full, ((1,), (0,)))
    masked = jnp.where(hits > 0, logits, -jnp.inf)
    gate_expo = jnp.exp(masked - jnp.max(masked, axis=1, keepdims=True))
    gates = gate_expo / jnp.sum(gate_expo, axis=1, keepdims=True)
    first = (seq * 2 + core) * LOCAL_E
    own_hits = lax.dynamic_slice_in_dim(hits, first, LOCAL_E, 1)
    own_gates = lax.dynamic_slice_in_dim(gates, first, LOCAL_E, 1).T
    rank = jnp.cumsum(own_hits.astype(jnp.int32), axis=0) - 1
    rank = jnp.where(own_hits > 0, rank, -1).T
    pick = rank[:, None, :] == jnp.arange(SLOTS, dtype=jnp.int32)[None, :, None]
    row_gates = jnp.sum(jnp.where(pick, own_gates[:, None, :], 0.0), axis=2, keepdims=True)
    pick = pick.astype(bf16)

    rows = jnp.einsum("est,td->esd", pick, tokens, preferred_element_type=bf16)
    cot_rows = jnp.einsum("est,td->esd", pick, cots, preferred_element_type=f32)
    grad_rows = (row_gates * cot_rows).astype(bf16)
    gate_up = jnp.einsum("esd,edf->esf", rows, expand_full, preferred_element_type=f32)
    gate_pre, up_part = gate_up[..., :FF], gate_up[..., FF:]
    gate_sig = jax.nn.sigmoid(gate_pre)
    hidden = (gate_pre * gate_sig * up_part).astype(bf16)
    shrink_grad = jnp.einsum("esf,esd->efd", hidden, grad_rows, preferred_element_type=f32)
    shrink_sum = lax.psum_scatter(shrink_grad.astype(bf16), PLANE, scatter_dimension=1, tiled=True)
    hidden_grad = jnp.einsum("esd,efd->esf", grad_rows, shrink_full, preferred_element_type=f32)
    up_grad = jnp.concatenate(
        [
            hidden_grad * up_part * gate_sig * (1.0 + gate_pre * (1.0 - gate_sig)),
            hidden_grad * gate_pre * gate_sig,
        ],
        axis=-1,
    ).astype(bf16)
    expand_grad = jnp.einsum("esd,esf->edf", rows, up_grad, preferred_element_type=f32)
    expand_sum = lax.psum_scatter(expand_grad.astype(bf16), PLANE, scatter_dimension=1, tiled=True)
    row_grad = jnp.einsum("esf,edf->esd", up_grad, expand_full, preferred_element_type=f32)
    back_part = jnp.einsum(
        "est,esd->td", pick, row_grad.astype(bf16), preferred_element_type=f32
    )
    expert_out = jnp.einsum(
        "esf,efd->esd", hidden, shrink_full, preferred_element_type=f32
    ).astype(bf16).astype(f32)
    row_gate_grad = jnp.sum(expert_out * cot_rows, axis=2)
    gate_grad_part = jnp.einsum("est,es->te", pick.astype(f32), row_gate_grad, precision="highest")
    out_part = jnp.einsum(
        "est,esd->td", pick, (row_gates * expert_out).astype(bf16), preferred_element_type=f32
    )

    def core_sum(part):
        mine = lax.dynamic_slice_in_dim(part, core * GROUP, GROUP, 0)
        other = lax.dynamic_slice_in_dim(part, (1 - core) * GROUP, GROUP, 0)
        return mine + core_swap(other.astype(bf16)).astype(f32)

    back_send = core_sum(back_part).astype(bf16).reshape(N_SEQ, TOK_DEV, D)
    out_send = core_sum(out_part).astype(bf16).reshape(N_SEQ, TOK_DEV, D)
    gg_mine = lax.dynamic_slice_in_dim(gate_grad_part, core * GROUP, GROUP, 0)
    gg_other = core_swap(lax.dynamic_slice_in_dim(gate_grad_part, (1 - core) * GROUP, GROUP, 0))
    gg_send = core_order(core, gg_mine, gg_other, 1)
    gg_send = jnp.pad(gg_send, ((0, 0), (0, 128 - 2 * LOCAL_E))).reshape(N_SEQ, TOK_DEV, 128)
    back_got, gg_got = z_exchange(4, scattered=(back_send, gg_send))
    normed_two_grad = jnp.sum(back_got.astype(f32), axis=0)
    gate_grad = gg_got[:, :, : 2 * LOCAL_E].transpose(1, 0, 2).reshape(TOK_DEV, EXPERTS)
    my_gates = lax.dynamic_slice_in_dim(gates, core * GROUP + seq * TOK_DEV, TOK_DEV, 0)
    mean_term = jnp.sum(my_gates * gate_grad, axis=1, keepdims=True)
    logit_grad = (my_gates * (gate_grad - mean_term)).astype(bf16)
    router_grad = dot(normed_two, logit_grad, ((0,), (0,)))
    normed_two_grad = normed_two_grad + dot(logit_grad, router_full, ((1,), (1,)))
    middle_back, gain_two_grad = norm_back(middle, gains_full[1], normed_two_grad)
    middle_grad = cotangent[0].astype(f32) + middle_back
    (branch_grad,) = z_exchange(5, gathered=(middle_grad.astype(bf16),))
    branch_grad = branch_grad.reshape(GROUP, D)
    exit_grad = dot(attended, branch_grad, ((0,), (0,)))
    attended_grad = dot(branch_grad, exit_own, ((1,), (1,))).astype(bf16)
    attended_grad = attended_grad.reshape(GROUP, KV_HEADS_OWN, PER_KV, HD)
    prob_grad = jnp.einsum("qhgd,khd->hgqk", attended_grad, values, preferred_element_type=f32)
    delta = jnp.sum(probs * prob_grad, axis=-1, keepdims=True)
    score_grad = (probs * (prob_grad - delta) * HD**-0.5).astype(bf16)
    query_grad = jnp.einsum("hgqk,khd->qhgd", score_grad, keys, preferred_element_type=f32)
    key_grad = jnp.einsum("hgqk,qhgd->khd", score_grad, queries, preferred_element_type=f32)
    value_grad = jnp.einsum("hgqk,qhgd->khd", probs_b, attended_grad, preferred_element_type=f32)
    query_grad = rotate(query_grad.reshape(GROUP, HEADS_OWN, HD), cosine, -sine)
    key_grad = rotate(key_grad, cosine, -sine)
    mixed_grad = jnp.concatenate(
        [
            query_grad.reshape(GROUP, Q_OWN),
            jnp.stack([key_grad, value_grad], axis=2).reshape(GROUP, KV_OWN),
        ],
        axis=1,
    ).astype(bf16)
    entry_grad = dot(normed, mixed_grad, ((0,), (0,))).astype(bf16)
    normed_part = dot(mixed_grad, entry_own, ((1,), (1,))).astype(bf16)
    (normed_got,) = z_exchange(6, scattered=(normed_part.reshape(N_SEQ, TOK_DEV, D),))
    (out_got,) = z_exchange(7, scattered=(out_send,))
    block_output = (middle + jnp.sum(out_got.astype(f32), axis=0)).astype(bf16)
    normed_grad = jnp.sum(normed_got.astype(f32), axis=0)
    dealt_back, gain_one_grad = norm_back(activations[0].astype(f32), gains_full[0], normed_grad)
    input_grad = (middle_grad + dealt_back).astype(bf16)

    gains_grad = jnp.stack([gain_one_grad, gain_two_grad])
    z_small = jnp.concatenate(
        [
            router_grad.reshape(N_SEQ, -1),
            gains_grad.reshape(2, N_SEQ, -1).transpose(1, 0, 2).reshape(N_SEQ, -1),
        ],
        axis=1,
    )
    z_small = jnp.pad(z_small, ((0, 0), (0, 128 * 128 - z_small.shape[1])))
    (z_small,) = z_exchange(8, scattered=(z_small.reshape(N_SEQ, 128, 128),))
    z_small = jnp.sum(z_small, axis=0).reshape(-1)
    router_part = z_small[: Q_OWN * EXPERTS].reshape(32, -1)
    gains_part = (
        z_small[Q_OWN * EXPERTS : Q_OWN * (EXPERTS + 2)]
        .reshape(2, 32, ROWS)
        .transpose(1, 0, 2)
        .reshape(32, -1)
    )
    owed = jnp.concatenate(
        [
            entry_grad.reshape(N_SEQ, 32, ROWS * MIX_OWN).transpose(1, 0, 2).reshape(32, -1),
            exit_grad.astype(bf16).reshape(32, -1),
            router_part.astype(bf16),
            gains_part.astype(bf16),
        ],
        axis=1,
    )
    owed = jnp.pad(owed, ((0, 0), (0, 400 * 128 - owed.shape[1])))
    summed = lax.psum_scatter(
        owed.reshape(32 * 400, 128), FSDP, scatter_dimension=0, tiled=True
    ).reshape(-1)
    entry_cols = summed[: N_SEQ * n_entry].reshape(N_SEQ, ROWS * MIX_OWN // 128, 128)
    entry_cols = jnp.pad(entry_cols, ((0, 0), (0, 4), (0, 0)))
    (entry_cols,) = z_exchange(9, scattered=(entry_cols,))
    entry_cols = entry_cols[:, :60].reshape(N_SEQ, ROWS, MIX_OWN).transpose(1, 0, 2).astype(f32)
    entry_sum = jnp.concatenate(
        [
            entry_cols[:, :, :Q_OWN].reshape(ROWS, QH * HD),
            entry_cols[:, :, Q_OWN:].reshape(ROWS, 2 * KVH * HD),
        ],
        axis=1,
    )
    base = N_SEQ * n_entry
    exit_sum = summed[base : base + ROWS * D].reshape(ROWS, D).astype(f32)
    base += ROWS * D
    router_sum = summed[base : base + n_router].reshape(ROWS, EXPERTS).astype(f32)
    base += n_router
    gains_sum = summed[base : base + n_gain].reshape(2, ROWS).astype(f32)

    def to_owner(summed, rows):
        mine = lax.dynamic_slice_in_dim(summed, core * rows, rows, 1)
        other = lax.dynamic_slice_in_dim(summed, (1 - core) * rows, rows, 1)
        return core_order(core, mine, core_swap(other), 0).astype(f32)

    expand_sum = to_owner(expand_sum, 48)
    shrink_sum = to_owner(shrink_sum, 16)
    entry_new = adamw_step(entry_weight, entry_sum, entry_mean, entry_square, 0.02, weight_decay)
    exit_new = adamw_step(exit_weight, exit_sum, exit_mean, exit_square, 0.15, weight_decay)
    router_new = adamw_step(
        router_weight, router_sum, router_mean, router_square, 0.01, weight_decay
    )
    expand_new = adamw_step(
        expand_weight, expand_sum, expand_mean, expand_square, 0.02, weight_decay
    )
    shrink_new = adamw_step(
        shrink_weight, shrink_sum, shrink_mean, shrink_square, 0.12, weight_decay
    )
    gains_new = adamw_step(norm_gains, gains_sum, gains_mean, gains_square, 0.5, 0.0)
    return (
        block_output[None],
        input_grad[None],
        *entry_new,
        *exit_new,
        *router_new,
        *expand_new,
        *shrink_new,
        *gains_new,
    )


def solution(mesh):
    fine = Mesh(mesh.devices.reshape(4, 4, 4, 2), ("seq", "x", "y", "core"))
    rows = P(FSDP, "seq", None)
    lists = P(FSDP, None)
    owned = P(("seq",) + FSDP, None)
    experts = P("seq", FSDP, None)
    gains = P(None, ("seq",) + FSDP)
    return jax.shard_map(
        on_device,
        mesh=fine,
        in_specs=(rows, rows, lists, lists, rows)
        + (owned,) * 9
        + (experts,) * 6
        + (gains,) * 3,
        out_specs=(rows, rows) + (owned,) * 9 + (experts,) * 6 + (gains,) * 3,
        check_vma=False,
    )
```

```python
import jax
import jax.numpy as jnp
from jax import lax
from jax.experimental import pallas as pl
from jax.experimental.pallas import tpu as pltpu
from jax.sharding import Mesh, PartitionSpec as P

D = 1536
QH = 24
KVH = 8
HD = 64
FF = 512
EXPERTS = 40
TOP = 8
STEP = 10
CAP = 29

N_SEQ = 4
TOK_DEV = 128
GROUP = 512
PAIR_TOK = 2 * GROUP
LOCAL_E = EXPERTS // (2 * N_SEQ)
SLOTS = 256
Q_OWN = QH * HD // N_SEQ
KV_OWN = 2 * KVH * HD // N_SEQ
MIX_OWN = Q_OWN + KV_OWN
HEADS_OWN = QH // N_SEQ
KV_HEADS_OWN = KVH // N_SEQ
PER_KV = QH // KVH
ROWS = 12

norm_eps = 1e-06
rope_base = 10000.0
beta_first = 0.9
beta_second = 0.95
adam_eps = 1e-08
weight_decay = 0.1

FSDP = ("x", "y", "core")
PLANE = ("x", "y")
f32 = jnp.float32
bf16 = jnp.bfloat16


BIG = 56 * 1024 * 1024
HALF = TOK_DEV // 2
QOWN = Q_OWN
MESH = pl.DeviceIdType.MESH
ANY = pl.BlockSpec(memory_space=pl.ANY)
VMEM = pl.BlockSpec(memory_space=pltpu.VMEM)


def dot(a, b, dims):
    return lax.dot_general(a, b, (dims, ((), ())), preferred_element_type=f32)


def greet(peers):
    barrier = pltpu.get_barrier_semaphore()
    for axis, peer in peers:
        pl.semaphore_signal(barrier, inc=1, device_id={axis: peer}, device_id_type=MESH)
    pl.semaphore_wait(barrier, len(peers))


def sender(send_sem, recv_sem):
    def send(src, dst, index, axis, peer):
        copy = pltpu.make_async_remote_copy(
            src_ref=src,
            dst_ref=dst,
            send_sem=send_sem.at[index],
            recv_sem=recv_sem.at[index],
            device_id={axis: peer},
            device_id_type=MESH,
        )
        copy.start()
        return copy

    return send


def ring(me):
    right, left = lax.rem(me + 1, N_SEQ), lax.rem(me + 3, N_SEQ)
    return right, left, lax.rem(me + 2, N_SEQ)


TOP_ROWS, LOW_ROWS = pl.ds(0, HALF), pl.ds(HALF, HALF)
GATHER_SEMS = 10


class Gather:
    def __init__(self, send, base, mine, out, me, core=None):
        self.send, self.base, self.out, self.core, self.me = send, base, out, core, me
        right, left, self.far = ring(me)
        self.right, self.left = right, left
        here = out.at[me]
        self.first = [
            send(mine.at[TOP_ROWS], here.at[TOP_ROWS], base, "seq", right),
            send(mine.at[LOW_ROWS], here.at[LOW_ROWS], base + 1, "seq", left),
            send(mine.at[LOW_ROWS], here.at[LOW_ROWS], base + 2, "seq", right),
            send(mine.at[TOP_ROWS], here.at[TOP_ROWS], base + 3, "seq", left),
        ]
        self.later = []
        self.pairs = []

    def relay(self):
        send, base, out = self.send, self.base, self.out
        self.first[0].wait_recv()
        part = out.at[self.left, TOP_ROWS]
        self.later.append(send(part, part, base + 4, "seq", self.right))
        self.first[1].wait_recv()
        part = out.at[self.right, LOW_ROWS]
        self.later.append(send(part, part, base + 5, "seq", self.left))

    def finish(self):
        self.first[2].wait_recv()
        self.first[3].wait_recv()
        for copy in self.later:
            copy.wait_recv()

    def drain(self):
        for copy in self.first + self.later:
            copy.wait_send()


def pair_blocks(send, base, mine, out, other, gather, me, core):
    copies = [send(mine, out.at[core, me], base, "core", other)]
    gather.relay()
    gather.first[2].wait_recv()
    block = out.at[core, gather.left]
    copies.append(send(block, block, base + 1, "core", other))
    gather.first[3].wait_recv()
    block = out.at[core, gather.right]
    copies.append(send(block, block, base + 2, "core", other))
    for copy in gather.later:
        copy.wait_recv()
    block = out.at[core, gather.far]
    copies.append(send(block, block, base + 3, "core", other))
    return copies


def reduce_scratch(width):
    half = pltpu.VMEM((HALF, width), bf16)
    block = pltpu.VMEM((TOK_DEV, width), bf16)
    return [half, half, half, half, block, block]


class Reduce:
    def __init__(self, send, base, part, bufs, me):
        self.send, self.base, self.part, self.bufs, self.me = send, base, part, bufs, me
        self.right, self.left, self.far = ring(me)

    def start_far(self):
        from_left, from_right = self.bufs[0], self.bufs[1]
        part = self.part
        self.copies = [
            self.send(part.at[self.far, TOP_ROWS], from_left, self.base, "seq", self.right),
            self.send(part.at[self.far, LOW_ROWS], from_right, self.base + 1, "seq", self.left),
        ]

    def start_near(self):
        got_left, got_right = self.bufs[4], self.bufs[5]
        part = self.part
        self.copies += [
            self.send(
                part.at[self.right, LOW_ROWS],
                got_left.at[LOW_ROWS],
                self.base + 2,
                "seq",
                self.right,
            ),
            self.send(
                part.at[self.left, TOP_ROWS],
                got_right.at[TOP_ROWS],
                self.base + 3,
                "seq",
                self.left,
            ),
        ]

    def relay(self):
        from_left, from_right, to_right, to_left, got_left, got_right = self.bufs
        part = self.part
        self.copies[0].wait_recv()
        to_right[...] = (
            part[self.right, :HALF].astype(f32) + from_left[...].astype(f32)
        ).astype(bf16)
        self.copies.append(
            self.send(to_right, got_left.at[TOP_ROWS], self.base + 4, "seq", self.right)
        )
        self.copies[1].wait_recv()
        to_left[...] = (
            part[self.left, HALF:].astype(f32) + from_right[...].astype(f32)
        ).astype(bf16)
        self.copies.append(
            self.send(to_left, got_right.at[LOW_ROWS], self.base + 5, "seq", self.left)
        )

    def total(self):
        for copy in self.copies[2:]:
            copy.wait_recv()
        got_left, got_right = self.bufs[4], self.bufs[5]
        return (
            self.part[self.me].astype(f32) + got_left[...].astype(f32) + got_right[...].astype(f32)
        )

    def drain(self):
        for copy in self.copies:
            copy.wait_send()


def sems(count):
    return [pltpu.SemaphoreType.DMA((count,)), pltpu.SemaphoreType.DMA((count,))]


def unit_scale(vector):
    return lax.rsqrt(jnp.mean(vector * vector, axis=-1, keepdims=True) + norm_eps)


def norm_back(vector, gain, grad):
    scale = unit_scale(vector)
    unit = vector * scale
    pulled = grad * gain
    back = scale * (pulled - unit * jnp.mean(pulled * unit, axis=-1, keepdims=True))
    return back, jnp.sum(unit * grad, axis=0, keepdims=True)


def inputs_kernel(in_ref, cot_ref, hit_ref, in_all, cot_all, hit_all, send_sem, recv_sem, copy_sem):
    me, core = lax.axis_index("seq"), lax.axis_index("core")
    right, left, _ = ring(me)
    greet([("seq", right), ("seq", left), ("core", 1 - core)])
    send = sender(send_sem, recv_sem)
    hits = Gather(send, 0, hit_ref, hit_all, me)
    rows = Gather(send, 6, in_ref, in_all, me)
    cots = Gather(send, 12, cot_ref, cot_all.at[core], me)
    local = [
        pltpu.make_async_copy(hit_ref, hit_all.at[me], copy_sem.at[0]),
        pltpu.make_async_copy(in_ref, in_all.at[me], copy_sem.at[1]),
        pltpu.make_async_copy(cot_ref, cot_all.at[core, me], copy_sem.at[2]),
    ]
    for copy in local:
        copy.start()
    hits.relay()
    rows.relay()
    pairs = pair_blocks(send, 18, cot_ref, cot_all, 1 - core, cots, me, core)
    hits.finish()
    rows.finish()
    for copy in pairs:
        copy.wait()
    for gather in (hits, rows, cots):
        gather.drain()
    for copy in local:
        copy.wait()


def gather_inputs(rows, cots, hits):
    return pl.pallas_call(
        inputs_kernel,
        out_shape=[
            jax.ShapeDtypeStruct((N_SEQ, TOK_DEV, D), bf16),
            jax.ShapeDtypeStruct((2, N_SEQ, TOK_DEV, D), bf16),
            jax.ShapeDtypeStruct((N_SEQ, TOK_DEV, 128), bf16),
        ],
        in_specs=[ANY] * 3,
        out_specs=[ANY] * 3,
        scratch_shapes=sems(22) + [pltpu.SemaphoreType.DMA((3,))],
        compiler_params=pltpu.CompilerParams(collective_id=1, has_side_effects=True),
    )(rows, cots, hits)


def middle_kernel(
    part_ref, in_ref, gain_ref, middle_ref, tokens_ref, mine, *rest
):
    bufs, (send_sem, recv_sem, copy_sem) = rest[:6], rest[6:]
    me, core = lax.axis_index("seq"), lax.axis_index("core")
    right, left, _ = ring(me)
    greet([("seq", right), ("seq", left), ("core", 1 - core)])
    send = sender(send_sem, recv_sem)
    reduce = Reduce(send, 0, part_ref, bufs, me)
    reduce.start_far()
    reduce.start_near()
    reduce.relay()
    middle = in_ref[...].astype(f32) + reduce.total()
    middle_ref[...] = middle
    mine[...] = (middle * unit_scale(middle) * gain_ref[...]).astype(bf16)
    gather = Gather(send, 6, mine, tokens_ref.at[core], me)
    local = pltpu.make_async_copy(mine, tokens_ref.at[core, me], copy_sem)
    local.start()
    pairs = pair_blocks(send, 12, mine, tokens_ref, 1 - core, gather, me, core)
    for copy in pairs:
        copy.wait()
    gather.drain()
    reduce.drain()
    local.wait()


def middle_tokens(part, rows, gain):
    return pl.pallas_call(
        middle_kernel,
        out_shape=[
            jax.ShapeDtypeStruct((TOK_DEV, D), f32),
            jax.ShapeDtypeStruct((2, N_SEQ, TOK_DEV, D), bf16),
        ],
        in_specs=[VMEM] * 3,
        out_specs=[VMEM, ANY],
        scratch_shapes=[pltpu.VMEM((TOK_DEV, D), bf16)]
        + reduce_scratch(D)
        + sems(16)
        + [pltpu.SemaphoreType.DMA],
        compiler_params=pltpu.CompilerParams(
            collective_id=2, has_side_effects=True, vmem_limit_bytes=BIG
        ),
    )(part, rows, gain)


BACK_WIDTH = D + 128


def turn_kernel(
    back_ref, middle_ref, cot_ref, gate_ref, router_ref, gain_ref,
    grad_ref, branch_ref, logit_ref, gain_grad_ref, part, from_core, mine, *rest
):
    bufs, (send_sem, recv_sem, copy_sem) = rest[:6], rest[6:]
    me, core = lax.axis_index("seq"), lax.axis_index("core")
    right, left, far = ring(me)
    greet([("seq", right), ("seq", left), ("core", 1 - core)])
    send = sender(send_sem, recv_sem)
    order = (far, right, left, me)
    swaps = [
        send(back_ref.at[1 - core, block], from_core.at[i], 12 + i, "core", 1 - core)
        for i, block in enumerate(order)
    ]
    reduce = Reduce(send, 0, part, bufs, me)
    for i, block in enumerate(order):
        swaps[i].wait_recv()
        part[block] = (back_ref[core, block].astype(f32) + from_core[i].astype(f32)).astype(bf16)
        if i == 0:
            reduce.start_far()
        if i == 2:
            reduce.start_near()
    reduce.relay()
    total = reduce.total()
    gates, gate_grad = gate_ref[...], total[:, D:]
    mean_term = jnp.sum(gates * gate_grad, axis=1, keepdims=True)
    logit_grad = (gates * (gate_grad - mean_term)).astype(bf16)
    logit_ref[...] = logit_grad
    normed_grad = total[:, :D] + dot(logit_grad, router_ref[...], ((1,), (1,)))
    back, gain_grad = norm_back(middle_ref[...], gain_ref[...], normed_grad)
    gain_grad_ref[...] = gain_grad
    middle_grad = cot_ref[...].astype(f32) + back
    grad_ref[...] = middle_grad
    mine[...] = middle_grad.astype(bf16)
    gather = Gather(send, 6, mine, branch_ref, me)
    local = pltpu.make_async_copy(mine, branch_ref.at[me], copy_sem)
    local.start()
    gather.relay()
    gather.finish()
    gather.drain()
    reduce.drain()
    for copy in swaps:
        copy.wait_send()
    local.wait()


def turn(back, middle, cot, gates, router, gain):
    return pl.pallas_call(
        turn_kernel,
        out_shape=[
            jax.ShapeDtypeStruct((TOK_DEV, D), f32),
            jax.ShapeDtypeStruct((N_SEQ, TOK_DEV, D), bf16),
            jax.ShapeDtypeStruct((TOK_DEV, 128), bf16),
            jax.ShapeDtypeStruct((1, D), f32),
        ],
        in_specs=[VMEM] * 6,
        out_specs=[VMEM, ANY, VMEM, VMEM],
        scratch_shapes=[
            pltpu.VMEM((N_SEQ, TOK_DEV, BACK_WIDTH), bf16),
            pltpu.VMEM((N_SEQ, TOK_DEV, BACK_WIDTH), bf16),
            pltpu.VMEM((TOK_DEV, D), bf16),
        ]
        + reduce_scratch(BACK_WIDTH)
        + sems(16)
        + [pltpu.SemaphoreType.DMA],
        compiler_params=pltpu.CompilerParams(
            collective_id=3, has_side_effects=True, vmem_limit_bytes=BIG
        ),
    )(back, middle, cot, gates, router, gain)


def input_kernel(part_ref, in_ref, grad_ref, gain_ref, out_ref, gain_grad_ref, *rest):
    bufs, (send_sem, recv_sem) = rest[:6], rest[6:]
    me = lax.axis_index("seq")
    right, left, _ = ring(me)
    greet([("seq", right), ("seq", left)])
    reduce = Reduce(sender(send_sem, recv_sem), 0, part_ref, bufs, me)
    reduce.start_far()
    reduce.start_near()
    reduce.relay()
    back, gain_grad = norm_back(in_ref[...].astype(f32), gain_ref[...], reduce.total())
    gain_grad_ref[...] = gain_grad
    out_ref[...] = (grad_ref[...] + back).astype(bf16)
    reduce.drain()


def input_back(part, rows, middle_grad, gain):
    return pl.pallas_call(
        input_kernel,
        out_shape=[
            jax.ShapeDtypeStruct((TOK_DEV, D), bf16),
            jax.ShapeDtypeStruct((1, D), f32),
        ],
        in_specs=[VMEM] * 4,
        out_specs=[VMEM, VMEM],
        scratch_shapes=reduce_scratch(D) + sems(6),
        compiler_params=pltpu.CompilerParams(
            collective_id=4, has_side_effects=True, vmem_limit_bytes=BIG
        ),
    )(part, rows, middle_grad, gain)


PAD_ROWS = 16
WIDE = 768


def peers_of(axis):
    me = lax.axis_index(axis)
    return [lax.rem(me + k, 4) for k in (1, 2, 3)]


def plane_greet():
    greet(
        [(axis, peer) for axis in ("seq", "x", "y") for peer in peers_of(axis)]
        + [("core", 1 - lax.axis_index("core"))]
    )


def row_pick(shape, padded_axis):
    padded = lax.broadcasted_iota(jnp.int32, shape, padded_axis)
    plain = lax.broadcasted_iota(jnp.int32, shape, 1 - padded_axis)
    row = lax.rem(padded, 16)
    return ((plain == lax.div(padded, 16) * 12 + row) & (row < 12)).astype(bf16)


def weights_kernel(
    entry_ref, exit_ref, entry_out, shared_out, exit_out, hold, full, send_sem, recv_sem, copy_sem
):
    z, x, y, c = (lax.axis_index(a) for a in ("seq", "x", "y", "core"))
    plane_greet()
    send = sender(send_sem, recv_sem)
    copies = [
        send(entry_ref.at[peer], hold.at[z], k, "seq", peer)
        for k, peer in enumerate(peers_of("seq"))
    ]
    local = [
        pltpu.make_async_copy(entry_ref.at[z], hold.at[z], copy_sem.at[0]),
        pltpu.make_async_copy(exit_ref, hold.at[pl.ds(4, 2)], copy_sem.at[1]),
    ]
    for copy in local:
        copy.start()
    for copy in local:
        copy.wait()
    for copy in copies:
        copy.wait_recv()
    own = pltpu.make_async_copy(hold, full.at[:, x, y, c], copy_sem.at[2])
    own.start()
    low, high = pl.ds(0, 3), pl.ds(3, 3)
    first_x = [
        send(hold.at[low], full.at[low, x, y, c], 3 + k, "x", peer)
        for k, peer in enumerate(peers_of("x"))
    ]
    first_y = [
        send(hold.at[high], full.at[high, x, y, c], 6 + k, "y", peer)
        for k, peer in enumerate(peers_of("y"))
    ]
    own.wait()
    for copy in first_x:
        copy.wait_recv()
    line = full.at[low, :, y, c]
    second_y = [send(line, line, 9 + k, "y", peer) for k, peer in enumerate(peers_of("y"))]
    for copy in first_y:
        copy.wait_recv()
    line = full.at[high, x, :, c]
    second_x = [send(line, line, 12 + k, "x", peer) for k, peer in enumerate(peers_of("x"))]
    for copy in second_y + second_x:
        copy.wait_recv()
    half = full.at[:, :, :, c]
    last = send(half, half, 15, "core", 1 - c)
    last.wait_recv()
    pick = row_pick((QOWN, 512), 1)
    for block in range(4):
        got = dot(pick, full[block].reshape(512, WIDE), ((1,), (0,))).astype(bf16)
        entry_out[QOWN * block : QOWN * (block + 1), :] = got[:, :640]
        shared_out[QOWN * block : QOWN * (block + 1), :] = got[:, 640:]
    for block in range(2):
        got = dot(pick, full[4 + block].reshape(512, WIDE), ((1,), (0,))).astype(bf16)
        exit_out[:, WIDE * block : WIDE * (block + 1)] = got
    for copy in copies + first_x + first_y + second_x + second_y + [last]:
        copy.wait_send()


def gather_weights(entry_cols, exit_cols):
    return pl.pallas_call(
        weights_kernel,
        out_shape=[
            jax.ShapeDtypeStruct((D, 640), bf16),
            jax.ShapeDtypeStruct((D, 128), bf16),
            jax.ShapeDtypeStruct((QOWN, D), bf16),
        ],
        in_specs=[VMEM] * 2,
        out_specs=[VMEM] * 3,
        scratch_shapes=[
            pltpu.VMEM((6, PAD_ROWS, WIDE), bf16),
            pltpu.VMEM((6, 4, 4, 2, PAD_ROWS, WIDE), bf16),
        ]
        + sems(16)
        + [pltpu.SemaphoreType.DMA((3,))],
        compiler_params=pltpu.CompilerParams(
            collective_id=5, has_side_effects=True, vmem_limit_bytes=BIG
        ),
    )(entry_cols, exit_cols)


def owners_kernel(
    normed_ref, mixed_ref, attended_ref, branch_ref, shared_ref, entry_out, exit_out,
    full, core_buf, chip, got_x, got_y, line_x, line_y, last_x, last_y, final, got_z,
    send_sem, recv_sem,
):
    z, x, y, c = (lax.axis_index(a) for a in ("seq", "x", "y", "core"))
    plane_greet()
    send = sender(send_sem, recv_sem)
    pick = row_pick((512, QOWN), 0)
    shape = (4, 4, 2, PAD_ROWS, WIDE)
    swaps = []
    for block in range(6):
        if block < 4:
            rows = slice(QOWN * block, QOWN * (block + 1))
            grad = dot(normed_ref[:, rows], mixed_ref[...], ((0,), (0,))).astype(bf16)
            grad = jnp.concatenate([grad, shared_ref[rows, :]], axis=1)
        else:
            cols = slice(WIDE * (block - 4), WIDE * (block - 3))
            grad = dot(attended_ref[...], branch_ref[:, cols], ((0,), (0,))).astype(bf16)
        full[block] = dot(pick, grad, ((1,), (0,))).astype(bf16).reshape(shape)
        swaps.append(send(full.at[block, :, :, 1 - c], core_buf.at[block], block, "core", 1 - c))
    for block in range(6):
        swaps[block].wait_recv()
        chip[block] = (full[block, :, :, c].astype(f32) + core_buf[block].astype(f32)).astype(bf16)
    low, high = pl.ds(0, 3), pl.ds(3, 3)
    first_x = [
        send(chip.at[low, peer], got_x.at[k], 6 + k, "x", peer)
        for k, peer in enumerate(peers_of("x"))
    ]
    first_y = [
        send(chip.at[high, :, peer], got_y.at[k], 9 + k, "y", peer)
        for k, peer in enumerate(peers_of("y"))
    ]
    for copy in first_x:
        copy.wait_recv()
    total = chip[low, x].astype(f32)
    for k in range(3):
        total += got_x[k].astype(f32)
    line_x[...] = total.astype(bf16)
    second_y = [
        send(line_x.at[:, peer], last_y.at[k], 12 + k, "y", peer)
        for k, peer in enumerate(peers_of("y"))
    ]
    for copy in first_y:
        copy.wait_recv()
    total = chip[high, :, y].astype(f32)
    for k in range(3):
        total += got_y[k].astype(f32)
    line_y[...] = total.astype(bf16)
    second_x = [
        send(line_y.at[:, peer], last_x.at[k], 15 + k, "x", peer)
        for k, peer in enumerate(peers_of("x"))
    ]
    for copy in second_y:
        copy.wait_recv()
    total = line_x[:, y].astype(f32)
    for k in range(3):
        total += last_y[k].astype(f32)
    final[low] = total
    for copy in second_x:
        copy.wait_recv()
    total = line_y[:, x].astype(f32)
    for k in range(3):
        total += last_x[k].astype(f32)
    final[high] = total
    third = [
        send(final.at[peer], got_z.at[k], 18 + k, "seq", peer)
        for k, peer in enumerate(peers_of("seq"))
    ]
    exit_out[...] = final[pl.ds(4, 2)]
    entry_out[z] = final[z]
    for k, copy in enumerate(third):
        copy.wait_recv()
        entry_out[lax.rem(z + 3 - k, 4)] = got_z[k]
    for copy in swaps + first_x + first_y + second_x + second_y + third:
        copy.wait_send()


def sum_to_owners(normed, mixed_grad, attended, branch_grad, shared):
    block = (PAD_ROWS, WIDE)
    return pl.pallas_call(
        owners_kernel,
        out_shape=[
            jax.ShapeDtypeStruct((4,) + block, f32),
            jax.ShapeDtypeStruct((2,) + block, f32),
        ],
        in_specs=[VMEM] * 5,
        out_specs=[VMEM] * 2,
        scratch_shapes=[
            pltpu.VMEM((6, 4, 4, 2) + block, bf16),
            pltpu.VMEM((6, 4, 4) + block, bf16),
            pltpu.VMEM((6, 4, 4) + block, bf16),
            pltpu.VMEM((3, 3, 4) + block, bf16),
            pltpu.VMEM((3, 3, 4) + block, bf16),
            pltpu.VMEM((3, 4) + block, bf16),
            pltpu.VMEM((3, 4) + block, bf16),
            pltpu.VMEM((3, 3) + block, bf16),
            pltpu.VMEM((3, 3) + block, bf16),
            pltpu.VMEM((6,) + block, f32),
            pltpu.VMEM((3,) + block, f32),
        ]
        + sems(21),
        compiler_params=pltpu.CompilerParams(
            collective_id=6, has_side_effects=True, vmem_limit_bytes=BIG
        ),
    )(normed, mixed_grad, attended, branch_grad, shared)


def dispatch_kernel(rank_ref, gate_ref, tokens_ref, cots_ref, rows_ref, cot_rows_ref, row_gate_ref):
    slot = lax.broadcasted_iota(jnp.int32, (SLOTS, PAIR_TOK), 0)
    match = rank_ref[0] == slot
    row_gate_ref[0] = jnp.sum(jnp.where(match, gate_ref[0], 0.0), axis=1, keepdims=True)
    pick = match.astype(bf16)
    for j in range(3):
        cols = slice(512 * j, 512 * (j + 1))
        rows_ref[0, :, cols] = dot(pick, tokens_ref[:, cols], ((1,), (0,))).astype(bf16)
        cot_rows_ref[0, :, cols] = dot(pick, cots_ref[:, cols], ((1,), (0,))).astype(bf16)

def dispatch(rank, gates, tokens, cots):
    one = lambda e: (e, 0, 0)
    whole = lambda e: (0, 0)
    return pl.pallas_call(
        dispatch_kernel,
        grid=(LOCAL_E,),
        in_specs=[
            pl.BlockSpec((1, 1, PAIR_TOK), one),
            pl.BlockSpec((1, 1, PAIR_TOK), one),
            pl.BlockSpec((PAIR_TOK, D), whole),
            pl.BlockSpec((PAIR_TOK, D), whole),
        ],
        out_specs=[
            pl.BlockSpec((1, SLOTS, D), one),
            pl.BlockSpec((1, SLOTS, D), one),
            pl.BlockSpec((1, SLOTS, 1), one),
        ],
        out_shape=[
            jax.ShapeDtypeStruct((LOCAL_E, SLOTS, D), bf16),
            jax.ShapeDtypeStruct((LOCAL_E, SLOTS, D), bf16),
            jax.ShapeDtypeStruct((LOCAL_E, SLOTS, 1), f32),
        ],
        compiler_params=pltpu.CompilerParams(vmem_limit_bytes=BIG),
        cost_estimate=pl.CostEstimate(
            flops=4 * LOCAL_E * SLOTS * PAIR_TOK * D, bytes_accessed=16 << 20, transcendentals=0
        ),
    )(rank[:, None], gates[:, None], tokens, cots)

def weights_of(w_ref):
    expand = w_ref[:, 0, :96, :].reshape(D, 2 * FF)
    left = w_ref[:, 0, 96:128, :].reshape(FF, 1024)
    right = jnp.concatenate([w_ref[:, 0, 128:144, :512], w_ref[:, 0, 128:144, 512:]], axis=1)
    return expand, left, right.reshape(FF, 512)

def grads_kernel(rows_ref, cot_ref, gate_ref, w_ref, hidden_ref, up_ref, out_ref):
    expand, left, right = weights_of(w_ref)
    grad_rows = (gate_ref[0] * cot_ref[0].astype(f32)).astype(bf16)
    rows = rows_ref[0]
    gate_pre = dot(rows, expand[:, :FF], ((1,), (0,)))
    up_part = dot(rows, expand[:, FF:], ((1,), (0,)))
    sig = jax.nn.sigmoid(gate_pre)
    hidden = (gate_pre * sig * up_part).astype(bf16)
    hidden_ref[0] = hidden
    hidden_grad = dot(grad_rows[:, :1024], left, ((1,), (1,))) + dot(
        grad_rows[:, 1024:], right, ((1,), (1,))
    )
    up_ref[0, :, :FF] = (hidden_grad * up_part * sig * (1.0 + gate_pre * (1.0 - sig))).astype(bf16)
    up_ref[0, :, FF:] = (hidden_grad * gate_pre * sig).astype(bf16)
    grad_left = dot(hidden, grad_rows[:, :1024], ((0,), (0,))).astype(bf16)
    out_ref[:, 0, 96:128, :] = grad_left.reshape(16, 32, 1024)
    grad_right = dot(hidden, grad_rows[:, 1024:], ((0,), (0,))).astype(bf16).reshape(16, 32, 512)
    out_ref[:, 0, 128:144, :512] = grad_right[:, :16]
    out_ref[:, 0, 128:144, 512:] = grad_right[:, 16:]
    up_grad = up_ref[0]
    for j in range(4):
        part = dot(rows[:, 384 * j : 384 * (j + 1)], up_grad, ((0,), (0,))).astype(bf16)
        out_ref[4 * j : 4 * (j + 1), 0, :96, :] = part.reshape(4, 96, 1024)

def expert_grads(rows, cot_rows, row_gates, weights):
    one = lambda e: (e, 0, 0)
    wide = lambda e: (0, e, 0, 0)
    return pl.pallas_call(
        grads_kernel,
        grid=(LOCAL_E,),
        in_specs=[
            pl.BlockSpec((1, SLOTS, D), one),
            pl.BlockSpec((1, SLOTS, D), one),
            pl.BlockSpec((1, SLOTS, 1), one),
            pl.BlockSpec((16, 1, 144, 1024), wide),
        ],
        out_specs=[
            pl.BlockSpec((1, SLOTS, FF), one),
            pl.BlockSpec((1, SLOTS, 2 * FF), one),
            pl.BlockSpec((16, 1, 144, 1024), wide),
        ],
        out_shape=[
            jax.ShapeDtypeStruct((LOCAL_E, SLOTS, FF), bf16),
            jax.ShapeDtypeStruct((LOCAL_E, SLOTS, 2 * FF), bf16),
            jax.ShapeDtypeStruct((16, LOCAL_E, 144, 1024), bf16),
        ],
        compiler_params=pltpu.CompilerParams(vmem_limit_bytes=BIG),
        cost_estimate=pl.CostEstimate(
            flops=12 * LOCAL_E * SLOTS * D * FF, bytes_accessed=60 << 20, transcendentals=0
        ),
    )(rows, cot_rows, row_gates, weights)

def combine_kernel(
    first_ref, rank_ref, up_ref, hidden_ref, gate_ref, cot_ref, w_ref, back_ref, out_ref, back_s, out_s
):
    e = pl.program_id(0)

    @pl.when(e < LOCAL_E)
    def _():
        expand, left, right = weights_of(w_ref)
        at = pl.ds(pl.multiple_of(e * SLOTS, SLOTS), SLOTS)
        back_s[at, :D] = dot(up_ref[0], expand, ((1,), (1,))).astype(bf16)
        hidden = hidden_ref[0]
        expert_out = jnp.concatenate(
            [dot(hidden, left, ((1,), (0,))), dot(hidden, right, ((1,), (0,)))], axis=1
        )
        expert_out = expert_out.astype(bf16).astype(f32)
        gate_grad = jnp.sum(expert_out * cot_ref[0].astype(f32), axis=1, keepdims=True)
        lane = lax.broadcasted_iota(jnp.int32, (SLOTS, 128), 1)
        back_s[at, D:] = jnp.where(lane == first_ref[0] + e, gate_grad, 0.0).astype(bf16)
        out_s[at, :] = (gate_ref[0] * expert_out).astype(bf16)

    @pl.when(e == LOCAL_E)
    def _():
        slot = lax.broadcasted_iota(jnp.int32, (256, SLOTS), 1)
        for i in range(4):
            toks = slice(256 * i, 256 * (i + 1))
            picks = jnp.concatenate(
                [(rank_ref[toks, k : k + 1] == slot).astype(bf16) for k in range(LOCAL_E)], axis=1
            )
            back_ref[toks, :] = dot(picks, back_s[...], ((1,), (0,))).astype(bf16)
            out_ref[toks, :] = dot(picks, out_s[...], ((1,), (0,))).astype(bf16)

def combine(first, rank_cols, up_grad, hidden, row_gates, cot_rows, weights):
    last = LOCAL_E - 1
    one = lambda e: (jnp.minimum(e, last), 0, 0)
    wide = lambda e: (0, jnp.minimum(e, last), 0, 0)
    whole = lambda e: (0, 0)
    return pl.pallas_call(
        combine_kernel,
        grid=(LOCAL_E + 1,),
        in_specs=[
            pl.BlockSpec(memory_space=pltpu.SMEM),
            pl.BlockSpec((PAIR_TOK, LOCAL_E), whole),
            pl.BlockSpec((1, SLOTS, 2 * FF), one),
            pl.BlockSpec((1, SLOTS, FF), one),
            pl.BlockSpec((1, SLOTS, 1), one),
            pl.BlockSpec((1, SLOTS, D), one),
            pl.BlockSpec((16, 1, 144, 1024), wide),
        ],
        out_specs=[
            pl.BlockSpec((PAIR_TOK, BACK_WIDTH), whole),
            pl.BlockSpec((PAIR_TOK, D), whole),
        ],
        out_shape=[
            jax.ShapeDtypeStruct((PAIR_TOK, BACK_WIDTH), bf16),
            jax.ShapeDtypeStruct((PAIR_TOK, D), bf16),
        ],
        scratch_shapes=[
            pltpu.VMEM((LOCAL_E * SLOTS, BACK_WIDTH), bf16),
            pltpu.VMEM((LOCAL_E * SLOTS, D), bf16),
        ],
        compiler_params=pltpu.CompilerParams(vmem_limit_bytes=BIG),
        cost_estimate=pl.CostEstimate(
            flops=6 * LOCAL_E * SLOTS * D * FF + 4 * LOCAL_E * SLOTS * PAIR_TOK * D,
            bytes_accessed=40 << 20,
            transcendentals=0,
        ),
    )(first, rank_cols, up_grad, hidden, row_gates, cot_rows, weights)


def core_swap(value):
    return lax.ppermute(value, "core", [(0, 1), (1, 0)])


def core_order(core, mine, other, axis):
    return jnp.concatenate(
        [jnp.where(core == 0, mine, other), jnp.where(core == 0, other, mine)], axis=axis
    )


def norm_apply(vector, gain):
    scale = lax.rsqrt(jnp.mean(vector * vector, axis=-1, keepdims=True) + norm_eps)
    return vector * scale * gain


def adamw_step(weight, gradient, mean_old, square_old, rate, decay):
    drift = beta_first * mean_old + (1.0 - beta_first) * gradient
    spread = beta_second * square_old + (1.0 - beta_second) * gradient * gradient
    mean_hat = drift / (1.0 - beta_first**STEP)
    square_hat = spread / (1.0 - beta_second**STEP)
    master = weight - rate * (mean_hat / (jnp.sqrt(square_hat) + adam_eps) + decay * weight)
    return (drift, spread, master)


def rotate(vector, cosine, sine):
    first, second = vector[..., : HD // 2], vector[..., HD // 2 :]
    return jnp.concatenate(
        [first * cosine - second * sine, second * cosine + first * sine], axis=-1
    )


def on_device(
    activations,
    cotangent,
    seq_lengths,
    deal_order,
    routes,
    entry_weight,
    entry_mean,
    entry_square,
    exit_weight,
    exit_mean,
    exit_square,
    router_weight,
    router_mean,
    router_square,
    expand_weight,
    expand_mean,
    expand_square,
    shrink_weight,
    shrink_mean,
    shrink_square,
    norm_gains,
    gains_mean,
    gains_square,
):
    seq = lax.axis_index("seq")
    core = lax.axis_index("core")
    first = (seq * 2 + core) * LOCAL_E

    expand_b = expand_weight.astype(bf16)
    shrink_b = shrink_weight.astype(bf16)
    piece = jnp.concatenate([expand_b, shrink_b[:, :, :1024]], axis=1)

    def exchange(value):
        mine = lax.dynamic_slice_in_dim(value, core * LOCAL_E, LOCAL_E, 0)
        other = core_swap(lax.dynamic_slice_in_dim(value, (1 - core) * LOCAL_E, LOCAL_E, 0))
        return jnp.where(core == 0, mine, other), jnp.where(core == 0, other, mine)

    low, high = exchange(piece)
    low_end, high_end = exchange(shrink_b[:, :, 1024:])
    packed = jnp.concatenate(
        [
            low[:, :48],
            high[:, :48],
            low[:, 48:],
            high[:, 48:],
            jnp.concatenate([low_end, high_end], axis=2),
        ],
        axis=1,
    )
    packed, rows_in, cots_in = lax.optimization_barrier((packed, activations[0], cotangent[0]))
    weights = lax.all_gather(packed, PLANE, axis=0, tiled=False)

    entry_b = entry_weight.astype(bf16)
    shared_b = jnp.concatenate([router_weight, norm_gains.T], axis=1).astype(bf16)
    shared_b = jnp.pad(shared_b, ((0, 0), (0, 128 - EXPERTS - 2)))
    entry_cols = jnp.concatenate(
        [
            entry_b[:, : QH * HD].reshape(ROWS, N_SEQ, Q_OWN).transpose(1, 0, 2),
            entry_b[:, QH * HD :].reshape(ROWS, N_SEQ, KV_OWN).transpose(1, 0, 2),
            jnp.broadcast_to(shared_b[None], (N_SEQ, ROWS, 128)),
        ],
        axis=2,
    )
    exit_cols = exit_weight.astype(bf16).reshape(ROWS, 2, WIDE).transpose(1, 0, 2)
    pad = ((0, 0), (0, PAD_ROWS - ROWS), (0, 0))
    expert_ids = jnp.arange(128, dtype=jnp.int32)
    hit_slots = jnp.any(routes[0][:, :, None] == expert_ids[None, None, :], axis=1).astype(bf16)
    in_all, cots, hit_slots = gather_inputs(rows_in, cots_in, hit_slots)
    in_all = in_all.reshape(GROUP, D)
    entry_own, shared, exit_own = gather_weights(jnp.pad(entry_cols, pad), jnp.pad(exit_cols, pad))
    gains_full = shared[:, EXPERTS : EXPERTS + 2].astype(f32).T

    order_row = deal_order[0]
    token = jnp.arange(GROUP, dtype=jnp.int32)
    back_hot = (order_row[None, :] == token[:, None]).astype(bf16)
    hit = dot(back_hot, hit_slots.reshape(GROUP, 128), ((1,), (0,))).astype(bf16)
    hits = core_order(core, hit, core_swap(hit), 0)[:, :EXPERTS]
    own_hits = lax.dynamic_slice_in_dim(hits, first, LOCAL_E, 1)
    rank = jnp.cumsum(own_hits.astype(jnp.int32), axis=0) - 1
    rank = jnp.where(own_hits > 0, rank, -1)
    seq_ends = jnp.cumsum(seq_lengths[0])
    starts = seq_ends - seq_lengths[0]
    seq_ids = jnp.sum((token[:, None] >= seq_ends[None, :]).astype(jnp.int32), axis=1)
    seq_match = seq_ids[:, None] == jnp.arange(seq_ends.shape[0], dtype=jnp.int32)[None, :]
    positions = token - jnp.sum(jnp.where(seq_match, starts[None, :], 0), axis=1)
    frequency = rope_base ** (-jnp.arange(HD // 2, dtype=f32) * 2.0 / HD)
    phase = positions.astype(f32)[:, None] * frequency[None, :]
    cosine, sine = jnp.cos(phase)[:, None, :], jnp.sin(phase)[:, None, :]
    allowed = (seq_ids[:, None] == seq_ids[None, :]) & (token[None, :] <= token[:, None])

    normed = norm_apply(in_all.astype(f32), gains_full[0]).astype(bf16)
    mixed = dot(normed, entry_own, ((1,), (0,)))
    queries = rotate(mixed[:, :Q_OWN].reshape(GROUP, HEADS_OWN, HD), cosine, sine)
    pairs = mixed[:, Q_OWN:].reshape(GROUP, KV_HEADS_OWN, 2, HD)
    keys = rotate(pairs[:, :, 0], cosine, sine)
    queries = queries.astype(bf16).reshape(GROUP, KV_HEADS_OWN, PER_KV, HD)
    keys, values = keys.astype(bf16), pairs[:, :, 1].astype(bf16)
    scores = jnp.einsum("qhgd,khd->hgqk", queries, keys, preferred_element_type=f32) * HD**-0.5
    scores = jnp.where(allowed[None, None], scores, -1e30)
    peak = jnp.max(scores, axis=-1, keepdims=True)
    expo = jnp.exp(scores - peak)
    probs = expo / jnp.sum(expo, axis=-1, keepdims=True)
    probs_b = probs.astype(bf16)
    attended = (
        jnp.einsum("hgqk,khd->qhgd", probs_b, values, preferred_element_type=f32)
        .reshape(GROUP, Q_OWN)
        .astype(bf16)
    )
    branch_part = dot(attended, exit_own, ((1,), (0,))).astype(bf16)
    middle, tokens = middle_tokens(
        branch_part.reshape(N_SEQ, TOK_DEV, D), activations[0], gains_full[1:2]
    )
    normed_two = lax.dynamic_slice(tokens, (core, seq, 0, 0), (1, 1, TOK_DEV, D))[0, 0]
    tokens = tokens.reshape(PAIR_TOK, D)

    logits = dot(tokens, shared[:, :EXPERTS], ((1,), (0,)))
    masked = jnp.where(hits > 0, logits, -jnp.inf)
    gate_expo = jnp.exp(masked - jnp.max(masked, axis=1, keepdims=True))
    gates = gate_expo / jnp.sum(gate_expo, axis=1, keepdims=True)
    own_gates = lax.dynamic_slice_in_dim(gates, first, LOCAL_E, 1)
    rows, cot_rows, row_gates = dispatch(rank.T, own_gates.T, tokens, cots.reshape(PAIR_TOK, D))
    hidden, up_grad, expert_grad = expert_grads(rows, cot_rows, row_gates, weights)
    expert_sum = lax.psum_scatter(expert_grad, PLANE, scatter_dimension=0, tiled=False)
    back_part, out_part = combine(
        first[None], rank, up_grad, hidden, row_gates, cot_rows, weights
    )
    my_gates = lax.dynamic_slice_in_dim(gates, core * GROUP + seq * TOK_DEV, TOK_DEV, 0)
    my_gates = jnp.pad(my_gates, ((0, 0), (0, 128 - EXPERTS)))
    middle_grad, branch_grad, logit_grad, gain_two_grad = turn(
        back_part.reshape(2, N_SEQ, TOK_DEV, BACK_WIDTH),
        middle,
        cotangent[0],
        my_gates,
        shared,
        gains_full[1:2],
    )
    branch_grad = branch_grad.reshape(GROUP, D)
    router_grad = dot(normed_two, logit_grad, ((0,), (0,)))

    out_part = out_part.reshape(2, GROUP, D)
    out_mine = lax.dynamic_index_in_dim(out_part, core, 0, keepdims=False)
    out_other = core_swap(lax.dynamic_index_in_dim(out_part, 1 - core, 0, keepdims=False))
    out_sum = (out_mine.astype(f32) + out_other.astype(f32)).astype(bf16)
    out_sum = out_sum.reshape(N_SEQ, TOK_DEV, D)
    out_rows = lax.dynamic_index_in_dim(out_sum, seq, 0, keepdims=False).astype(f32)
    for step in range(1, N_SEQ):
        block = lax.dynamic_index_in_dim(out_sum, (seq + step) % N_SEQ, 0, keepdims=False)
        got = lax.ppermute(block, "seq", [(i, (i + step) % N_SEQ) for i in range(N_SEQ)])
        out_rows = out_rows + got.astype(f32)
    block_output = (middle + out_rows).astype(bf16)

    attended_grad = dot(branch_grad, exit_own, ((1,), (1,))).astype(bf16)
    attended_grad = attended_grad.reshape(GROUP, KV_HEADS_OWN, PER_KV, HD)
    prob_grad = jnp.einsum("qhgd,khd->hgqk", attended_grad, values, preferred_element_type=f32)
    delta = jnp.sum(probs * prob_grad, axis=-1, keepdims=True)
    score_grad = (probs * (prob_grad - delta) * HD**-0.5).astype(bf16)
    query_grad = jnp.einsum("hgqk,khd->qhgd", score_grad, keys, preferred_element_type=f32)
    key_grad = jnp.einsum("hgqk,qhgd->khd", score_grad, queries, preferred_element_type=f32)
    value_grad = jnp.einsum("hgqk,qhgd->khd", probs_b, attended_grad, preferred_element_type=f32)
    query_grad = rotate(query_grad.reshape(GROUP, HEADS_OWN, HD), cosine, -sine)
    key_grad = rotate(key_grad, cosine, -sine)
    mixed_grad = jnp.concatenate(
        [
            query_grad.reshape(GROUP, Q_OWN),
            jnp.stack([key_grad, value_grad], axis=2).reshape(GROUP, KV_OWN),
        ],
        axis=1,
    ).astype(bf16)
    normed_part = dot(mixed_grad, entry_own, ((1,), (1,))).astype(bf16)
    input_grad, gain_one_grad = input_back(
        normed_part.reshape(N_SEQ, TOK_DEV, D), activations[0], middle_grad, gains_full[0:1]
    )

    lane = jnp.arange(128)[None, :]
    shared_grad = jnp.where(lane == EXPERTS, gain_one_grad.T, router_grad)
    shared_grad = jnp.where(lane == EXPERTS + 1, gain_two_grad.T, shared_grad).astype(bf16)
    entry_got, exit_got = sum_to_owners(normed, mixed_grad, attended, branch_grad, shared_grad)
    entry_got = entry_got[:, :ROWS]
    entry_sum = jnp.concatenate(
        [
            entry_got[:, :, :Q_OWN].transpose(1, 0, 2).reshape(ROWS, QH * HD),
            entry_got[:, :, Q_OWN:MIX_OWN].transpose(1, 0, 2).reshape(ROWS, 2 * KVH * HD),
        ],
        axis=1,
    )
    shared_sum = jnp.sum(entry_got[:, :, MIX_OWN:], axis=0)
    router_sum = shared_sum[:, :EXPERTS]
    gains_sum = shared_sum[:, EXPERTS : EXPERTS + 2].T
    exit_sum = exit_got[:, :ROWS].transpose(1, 0, 2).reshape(ROWS, D)

    ends = expert_sum[:, 128:].reshape(LOCAL_E, 16, 2, 512).transpose(2, 0, 1, 3)
    rows_of = jnp.stack(
        [
            jnp.concatenate([expert_sum[:, :48], expert_sum[:, 96:112]], axis=1),
            jnp.concatenate([expert_sum[:, 48:96], expert_sum[:, 112:128]], axis=1),
        ]
    )

    def to_owner(value):
        mine = lax.dynamic_index_in_dim(value, core, 0, keepdims=False)
        other = core_swap(lax.dynamic_index_in_dim(value, 1 - core, 0, keepdims=False))
        return core_order(core, mine, other, 0).astype(f32)

    rows_of, ends = to_owner(rows_of), to_owner(ends)
    expand_sum = rows_of[:, :48]
    shrink_sum = jnp.concatenate([rows_of[:, 48:], ends], axis=2)
    entry_new = adamw_step(entry_weight, entry_sum, entry_mean, entry_square, 0.02, weight_decay)
    exit_new = adamw_step(exit_weight, exit_sum, exit_mean, exit_square, 0.15, weight_decay)
    router_new = adamw_step(
        router_weight, router_sum, router_mean, router_square, 0.01, weight_decay
    )
    expand_new = adamw_step(
        expand_weight, expand_sum, expand_mean, expand_square, 0.02, weight_decay
    )
    shrink_new = adamw_step(
        shrink_weight, shrink_sum, shrink_mean, shrink_square, 0.12, weight_decay
    )
    gains_new = adamw_step(norm_gains, gains_sum, gains_mean, gains_square, 0.5, 0.0)
    return (
        block_output[None],
        input_grad[None],
        *entry_new,
        *exit_new,
        *router_new,
        *expand_new,
        *shrink_new,
        *gains_new,
    )


def solution(mesh):
    fine = Mesh(mesh.devices.reshape(4, 4, 4, 2), ("seq", "x", "y", "core"))
    rows = P(FSDP, "seq", None)
    lists = P(FSDP, None)
    owned = P(("seq",) + FSDP, None)
    experts = P("seq", FSDP, None)
    gains = P(None, ("seq",) + FSDP)
    return jax.shard_map(
        on_device,
        mesh=fine,
        in_specs=(rows, rows, lists, lists, rows)
        + (owned,) * 9
        + (experts,) * 6
        + (gains,) * 3,
        out_specs=(rows, rows) + (owned,) * 9 + (experts,) * 6 + (gains,) * 3,
        check_vma=False,
    )
```

```python
import jax
import jax.numpy as jnp
from jax import lax
from jax.experimental import pallas as pl
from jax.experimental.pallas import tpu as pltpu
from jax.sharding import Mesh, PartitionSpec as P

D = 1536
QH = 24
KVH = 8
HD = 64
FF = 512
EXPERTS = 40
TOP = 8
STEP = 10
CAP = 29

N_SEQ = 4
TOK_DEV = 128
GROUP = 512
PAIR_TOK = 2 * GROUP
LOCAL_E = EXPERTS // (2 * N_SEQ)
SLOTS = 256
Q_OWN = QH * HD // N_SEQ
KV_OWN = 2 * KVH * HD // N_SEQ
MIX_OWN = Q_OWN + KV_OWN
HEADS_OWN = QH // N_SEQ
KV_HEADS_OWN = KVH // N_SEQ
PER_KV = QH // KVH
ROWS = 12

norm_eps = 1e-06
rope_base = 10000.0
beta_first = 0.9
beta_second = 0.95
adam_eps = 1e-08
weight_decay = 0.1

FSDP = ("x", "y", "core")
PLANE = ("x", "y")
f32 = jnp.float32
bf16 = jnp.bfloat16


BIG = 56 * 1024 * 1024
HALF = TOK_DEV // 2
QOWN = Q_OWN
MESH = pl.DeviceIdType.MESH
ANY = pl.BlockSpec(memory_space=pl.ANY)
VMEM = pl.BlockSpec(memory_space=pltpu.VMEM)


def dot(a, b, dims):
    return lax.dot_general(a, b, (dims, ((), ())), preferred_element_type=f32)


def greet(peers):
    barrier = pltpu.get_barrier_semaphore()
    for axis, peer in peers:
        pl.semaphore_signal(barrier, inc=1, device_id={axis: peer}, device_id_type=MESH)
    pl.semaphore_wait(barrier, len(peers))


def sender(send_sem, recv_sem):
    def send(src, dst, index, axis, peer):
        copy = pltpu.make_async_remote_copy(
            src_ref=src,
            dst_ref=dst,
            send_sem=send_sem.at[index],
            recv_sem=recv_sem.at[index],
            device_id={axis: peer},
            device_id_type=MESH,
        )
        copy.start()
        return copy

    return send


def sems(count):
    return [pltpu.SemaphoreType.DMA((count,)), pltpu.SemaphoreType.DMA((count,))]


def ring(me):
    right, left = lax.rem(me + 1, 4), lax.rem(me + 3, 4)
    return right, left, lax.rem(me + 2, 4)


def near(axis):
    right, left, _ = ring(lax.axis_index(axis))
    return [(axis, right), (axis, left)]


def sibling():
    return ("core", 1 - lax.axis_index("core"))


def half_rows(ref, half):
    size = ref.shape[0] // 2
    return ref.at[pl.ds(half * size, size)]


def half_lanes(ref, half):
    size = ref.shape[-1] // 2
    return ref.at[(slice(None),) * (len(ref.shape) - 1) + (pl.ds(half * size, size),)]


class Gather:
    def __init__(self, send, base, axis, mine, slot, cut):
        self.send, self.base, self.axis, self.slot, self.cut = send, base, axis, slot, cut
        me = lax.axis_index(axis)
        self.right, self.left, self.far = ring(me)
        here = slot(me)
        self.first = [
            send(cut(mine, 0), cut(here, 0), base, axis, self.right),
            send(cut(mine, 1), cut(here, 1), base + 1, axis, self.left),
            send(cut(mine, 1), cut(here, 1), base + 2, axis, self.right),
            send(cut(mine, 0), cut(here, 0), base + 3, axis, self.left),
        ]
        self.later = []

    def relay(self):
        self.first[0].wait_recv()
        part = self.cut(self.slot(self.left), 0)
        self.later.append(self.send(part, part, self.base + 4, self.axis, self.right))
        self.first[1].wait_recv()
        part = self.cut(self.slot(self.right), 1)
        self.later.append(self.send(part, part, self.base + 5, self.axis, self.left))

    def wait_left(self):
        self.first[2].wait_recv()

    def wait_right(self):
        self.first[3].wait_recv()

    def wait_far(self):
        for copy in self.later:
            copy.wait_recv()

    def finish(self):
        self.wait_left()
        self.wait_right()
        self.wait_far()

    def drain(self):
        for copy in self.first + self.later:
            copy.wait_send()


def hand_over(send, base, mine, out, gather):
    me, core = lax.axis_index("seq"), lax.axis_index("core")
    other = 1 - core
    copies = [send(mine, out.at[core, me], base, "core", other)]
    gather.relay()
    gather.wait_left()
    block = out.at[core, gather.left]
    copies.append(send(block, block, base + 1, "core", other))
    gather.wait_right()
    block = out.at[core, gather.right]
    copies.append(send(block, block, base + 2, "core", other))
    gather.wait_far()
    block = out.at[core, gather.far]
    copies.append(send(block, block, base + 3, "core", other))
    return copies


def reduce_scratch(block, half):
    return [pltpu.VMEM(half, bf16)] * 4 + [pltpu.VMEM(block, bf16)] * 2


def added(target, first, second):
    target[...] = (first[...].astype(f32) + second[...].astype(f32)).astype(bf16)


class Reduce:
    def __init__(self, send, base, axis, block, bufs, cut):
        self.send, self.base, self.axis, self.block = send, base, axis, block
        self.bufs, self.cut = bufs, cut
        self.me = lax.axis_index(axis)
        self.right, self.left, self.far = ring(self.me)

    def start_far(self):
        far = self.block(self.far)
        self.copies = [
            self.send(self.cut(far, 0), self.bufs[0], self.base, self.axis, self.right),
            self.send(self.cut(far, 1), self.bufs[1], self.base + 1, self.axis, self.left),
        ]

    def start_near(self):
        source, target = self.cut(self.block(self.right), 1), self.cut(self.bufs[4], 1)
        self.copies.append(self.send(source, target, self.base + 2, self.axis, self.right))
        source, target = self.cut(self.block(self.left), 0), self.cut(self.bufs[5], 0)
        self.copies.append(self.send(source, target, self.base + 3, self.axis, self.left))

    def relay(self):
        from_left, from_right, to_right, to_left, got_left, got_right = self.bufs
        self.copies[0].wait_recv()
        added(to_right, self.cut(self.block(self.right), 0), from_left)
        target = self.cut(got_left, 0)
        self.copies.append(self.send(to_right, target, self.base + 4, self.axis, self.right))
        self.copies[1].wait_recv()
        added(to_left, self.cut(self.block(self.left), 1), from_right)
        target = self.cut(got_right, 1)
        self.copies.append(self.send(to_left, target, self.base + 5, self.axis, self.left))

    def total(self):
        for copy in self.copies[2:]:
            copy.wait_recv()
        mine = self.block(self.me)[...].astype(f32)
        return mine + self.bufs[4][...].astype(f32) + self.bufs[5][...].astype(f32)

    def drain(self):
        for copy in self.copies:
            copy.wait_send()


def remote_params(call_id):
    return pltpu.CompilerParams(
        collective_id=call_id, has_side_effects=True, vmem_limit_bytes=BIG
    )


def unit_scale(vector):
    return lax.rsqrt(jnp.mean(vector * vector, axis=-1, keepdims=True) + norm_eps)


def norm_back(vector, gain, grad):
    scale = unit_scale(vector)
    unit = vector * scale
    pulled = grad * gain
    back = scale * (pulled - unit * jnp.mean(pulled * unit, axis=-1, keepdims=True))
    return back, jnp.sum(unit * grad, axis=0, keepdims=True)


def pack_kernel(expand_ref, shrink_ref, out_ref, stage, stage_end, send_sem, recv_sem):
    core = lax.axis_index("core")
    greet([sibling()])
    send = sender(send_sem, recv_sem)
    other = 1 - core
    for e in range(LOCAL_E):
        theirs = other * LOCAL_E + e
        stage[e, :48] = expand_ref[theirs].astype(bf16)
        stage[e, 48:] = shrink_ref[theirs, :, :1024].astype(bf16)
        stage_end[e] = shrink_ref[theirs, :, 1024:].astype(bf16)
    main = pl.ds(pl.multiple_of(core * 48, 16), 48)
    left = pl.ds(pl.multiple_of(96 + core * 16, 16), 16)
    ends = pl.ds(pl.multiple_of(core * 512, 512), 512)
    copies = [
        send(stage.at[:, pl.ds(0, 48)], out_ref.at[:, main], 0, "core", other),
        send(stage.at[:, pl.ds(48, 16)], out_ref.at[:, left], 1, "core", other),
        send(stage_end, out_ref.at[:, pl.ds(128, 16), ends], 2, "core", other),
    ]
    for e in range(LOCAL_E):
        mine = core * LOCAL_E + e
        out_ref[e, main, :] = expand_ref[mine].astype(bf16)
        out_ref[e, left, :] = shrink_ref[mine, :, :1024].astype(bf16)
        out_ref[e, pl.ds(128, 16), ends] = shrink_ref[mine, :, 1024:].astype(bf16)
    for copy in copies:
        copy.wait()


def pack_experts(expand, shrink):
    return pl.pallas_call(
        pack_kernel,
        out_shape=jax.ShapeDtypeStruct((LOCAL_E, 144, 1024), bf16),
        in_specs=[VMEM] * 2,
        out_specs=VMEM,
        scratch_shapes=[
            pltpu.VMEM((LOCAL_E, 64, 1024), bf16),
            pltpu.VMEM((LOCAL_E, 16, 512), bf16),
        ]
        + sems(3),
        compiler_params=remote_params(1),
    )(expand, shrink)


def row_pick(shape, padded_axis):
    padded = lax.broadcasted_iota(jnp.int32, shape, padded_axis)
    plain = lax.broadcasted_iota(jnp.int32, shape, 1 - padded_axis)
    row = lax.rem(padded, 16)
    return ((plain == lax.div(padded, 16) * 12 + row) & (row < 12)).astype(bf16)


def start_kernel(
    in_ref, cot_ref, hit_ref, entry_ref, exit_ref,
    in_all, cot_all, hit_all, entry_out, shared_out, exit_out,
    hold, full, send_sem, recv_sem, copy_sem,
):
    z, x, y, c = (lax.axis_index(a) for a in ("seq", "x", "y", "core"))
    right, left, far = ring(z)
    greet(near("seq") + [("seq", far)] + near("x") + near("y") + [sibling()])
    send = sender(send_sem, recv_sem)
    columns = [
        send(entry_ref.at[peer], hold.at[z], k, "seq", peer)
        for k, peer in enumerate((right, far, left))
    ]
    hits = Gather(send, 3, "seq", hit_ref, lambda i: hit_all.at[i], half_rows)
    rows = Gather(send, 9, "seq", in_ref, lambda i: in_all.at[i], half_rows)
    local = [
        pltpu.make_async_copy(entry_ref.at[z], hold.at[z], copy_sem.at[0]),
        pltpu.make_async_copy(exit_ref, hold.at[pl.ds(4, 2)], copy_sem.at[1]),
        pltpu.make_async_copy(hit_ref, hit_all.at[z], copy_sem.at[2]),
        pltpu.make_async_copy(in_ref, in_all.at[z], copy_sem.at[3]),
        pltpu.make_async_copy(cot_ref, cot_all.at[c, z], copy_sem.at[4]),
    ]
    for copy in local:
        copy.start()
    local[0].wait()
    local[1].wait()
    for copy in columns:
        copy.wait_recv()
    own = pltpu.make_async_copy(hold, full.at[:, x, y, c], copy_sem.at[5])
    own.start()
    low, high = pl.ds(0, 3), pl.ds(3, 3)
    low_x = Gather(send, 15, "x", hold.at[low], lambda i: full.at[low, i, y, c], half_lanes)
    high_y = Gather(send, 21, "y", hold.at[high], lambda i: full.at[high, x, i, c], half_lanes)
    hits.relay()
    low_x.relay()
    high_y.relay()
    rows.relay()
    cots = Gather(send, 27, "seq", cot_ref, lambda i: cot_all.at[c, i], half_rows)
    own.wait()
    low_x.finish()

    def cut_low(ref, half):
        return ref.at[:, pl.ds(2 * half, 2)]

    low_y = Gather(
        send, 33, "y", full.at[low, :, y, c], lambda i: full.at[low, :, i, c], cut_low
    )
    high_y.finish()
    high_x = Gather(
        send, 39, "x", full.at[high, x, :, c], lambda i: full.at[high, i, :, c], cut_low
    )
    low_y.relay()
    high_x.relay()
    pairs = hand_over(send, 45, cot_ref, cot_all, cots)
    low_y.finish()
    half = full.at[low, :, :, c]
    last = [send(half, half, 49, "core", 1 - c)]
    high_x.finish()
    half = full.at[high, :, :, c]
    last.append(send(half, half, 50, "core", 1 - c))
    pick = row_pick((QOWN, 512), 1)
    for copy in last:
        copy.wait_recv()
    for block in range(4):
        got = dot(pick, full[block].reshape(512, WIDE), ((1,), (0,))).astype(bf16)
        entry_out[QOWN * block : QOWN * (block + 1), :] = got[:, :MIX_OWN]
        shared_out[QOWN * block : QOWN * (block + 1), :] = got[:, MIX_OWN:]
    for block in range(2):
        got = dot(pick, full[4 + block].reshape(512, WIDE), ((1,), (0,))).astype(bf16)
        exit_out[:, WIDE * block : WIDE * (block + 1)] = got
    hits.finish()
    rows.finish()
    for copy in pairs:
        copy.wait()
    for gather in (hits, rows, cots, low_x, high_y, low_y, high_x):
        gather.drain()
    for copy in columns + last:
        copy.wait_send()
    for copy in local[2:]:
        copy.wait()


def start(rows, cots, hits, entry_cols, exit_cols):
    return pl.pallas_call(
        start_kernel,
        out_shape=[
            jax.ShapeDtypeStruct((N_SEQ, TOK_DEV, D), bf16),
            jax.ShapeDtypeStruct((2, N_SEQ, TOK_DEV, D), bf16),
            jax.ShapeDtypeStruct((N_SEQ, TOK_DEV, 128), bf16),
            jax.ShapeDtypeStruct((D, MIX_OWN), bf16),
            jax.ShapeDtypeStruct((D, 128), bf16),
            jax.ShapeDtypeStruct((QOWN, D), bf16),
        ],
        in_specs=[ANY] * 3 + [VMEM] * 2,
        out_specs=[ANY] * 3 + [VMEM] * 3,
        scratch_shapes=[
            pltpu.VMEM((6, PAD_ROWS, WIDE), bf16),
            pltpu.VMEM((6, 4, 4, 2, PAD_ROWS, WIDE), bf16),
        ]
        + sems(51)
        + [pltpu.SemaphoreType.DMA((6,))],
        compiler_params=remote_params(2),
    )(rows, cots, hits, entry_cols, exit_cols)


def middle_kernel(part_ref, in_ref, gain_ref, middle_ref, tokens_ref, mine, *rest):
    bufs, (send_sem, recv_sem, copy_sem) = rest[:6], rest[6:]
    me, core = lax.axis_index("seq"), lax.axis_index("core")
    greet(near("seq") + [sibling()])
    send = sender(send_sem, recv_sem)
    reduce = Reduce(send, 0, "seq", lambda i: part_ref.at[i], bufs, half_rows)
    reduce.start_far()
    reduce.start_near()
    reduce.relay()
    middle = in_ref[...].astype(f32) + reduce.total()
    middle_ref[...] = middle
    mine[...] = (middle * unit_scale(middle) * gain_ref[...]).astype(bf16)
    gather = Gather(send, 6, "seq", mine, lambda i: tokens_ref.at[core, i], half_rows)
    local = pltpu.make_async_copy(mine, tokens_ref.at[core, me], copy_sem)
    local.start()
    pairs = hand_over(send, 12, mine, tokens_ref, gather)
    for copy in pairs:
        copy.wait()
    gather.drain()
    reduce.drain()
    local.wait()


def middle_tokens(part, rows, gain):
    return pl.pallas_call(
        middle_kernel,
        out_shape=[
            jax.ShapeDtypeStruct((TOK_DEV, D), f32),
            jax.ShapeDtypeStruct((2, N_SEQ, TOK_DEV, D), bf16),
        ],
        in_specs=[VMEM] * 3,
        out_specs=[VMEM, ANY],
        scratch_shapes=[pltpu.VMEM((TOK_DEV, D), bf16)]
        + reduce_scratch((TOK_DEV, D), (HALF, D))
        + sems(16)
        + [pltpu.SemaphoreType.DMA],
        compiler_params=remote_params(3),
    )(part, rows, gain)


def turn_kernel(
    rank_ref, up_ref, hidden_ref, gate_ref, cot_rows_ref, w_ref,
    middle_ref, cot_ref, my_gate_ref, router_ref, gain_ref,
    grad_ref, branch_ref, logit_ref, gain_grad_ref, out_sum_ref,
    back_s, out_s, other_back, from_core, part, other_out, out_core, mine, *rest
):
    bufs, (send_sem, recv_sem, copy_sem) = rest[:6], rest[6:]
    e = pl.program_id(0)
    me, core = lax.axis_index("seq"), lax.axis_index("core")

    @pl.when(e == 0)
    def _():
        greet(near("seq") + [sibling()])

    @pl.when(e < LOCAL_E)
    def _():
        expand, left, right = weights_of(w_ref)
        at = pl.ds(pl.multiple_of(e * SLOTS, SLOTS), SLOTS)
        back_s[at, :D] = dot(up_ref[0], expand, ((1,), (1,))).astype(bf16)
        hidden = hidden_ref[0]
        expert_out = jnp.concatenate(
            [dot(hidden, left, ((1,), (0,))), dot(hidden, right, ((1,), (0,)))], axis=1
        )
        expert_out = expert_out.astype(bf16).astype(f32)
        gate_grad = jnp.sum(expert_out * cot_rows_ref[0].astype(f32), axis=1, keepdims=True)
        lane = lax.broadcasted_iota(jnp.int32, (SLOTS, 128), 1)
        column = (me * 2 + core) * LOCAL_E + e
        back_s[at, D:] = jnp.where(lane == column, gate_grad, 0.0).astype(bf16)
        out_s[at, :] = (gate_ref[0] * expert_out).astype(bf16)

    @pl.when(e == LOCAL_E)
    def _():
        send = sender(send_sem, recv_sem)
        other = 1 - core
        right, left, far = ring(me)
        slot = lax.broadcasted_iota(jnp.int32, (GROUP, SLOTS), 1)

        def picks(group):
            at = pl.ds(pl.multiple_of(group * GROUP, GROUP), GROUP)
            ranks = rank_ref[at, :]
            return jnp.concatenate(
                [(ranks[:, k : k + 1] == slot).astype(bf16) for k in range(LOCAL_E)], axis=1
            )

        theirs, ours = picks(other), picks(core)
        order = (far, right, left, me)
        other_back[...] = (
            dot(theirs, back_s[...], ((1,), (0,))).astype(bf16).reshape(other_back.shape)
        )
        swaps = [
            send(other_back.at[block], from_core.at[block], 12 + i, "core", other)
            for i, block in enumerate(order)
        ]
        part[...] = dot(ours, back_s[...], ((1,), (0,))).astype(bf16).reshape(part.shape)
        reduce = Reduce(send, 0, "seq", lambda i: part.at[i], bufs, half_rows)
        for i, block in enumerate(order):
            swaps[i].wait_recv()
            added(part.at[block], part.at[block], from_core.at[block])
            if i == 0:
                reduce.start_far()
            if i == 2:
                reduce.start_near()
        other_out[...] = (
            dot(theirs, out_s[...], ((1,), (0,))).astype(bf16).reshape(other_out.shape)
        )
        out_swap = send(other_out, out_core, 16, "core", other)
        reduce.relay()
        out_sum_ref[...] = (
            dot(ours, out_s[...], ((1,), (0,))).astype(bf16).reshape(out_sum_ref.shape)
        )
        total = reduce.total()
        gates, gate_grad = my_gate_ref[...], total[:, D:]
        mean_term = jnp.sum(gates * gate_grad, axis=1, keepdims=True)
        logit_grad = (gates * (gate_grad - mean_term)).astype(bf16)
        logit_ref[...] = logit_grad
        normed_grad = total[:, :D] + dot(logit_grad, router_ref[...], ((1,), (1,)))
        back, gain_grad = norm_back(middle_ref[...], gain_ref[...], normed_grad)
        gain_grad_ref[...] = gain_grad
        middle_grad = cot_ref[...].astype(f32) + back
        grad_ref[...] = middle_grad
        mine[...] = middle_grad.astype(bf16)
        gather = Gather(send, 6, "seq", mine, lambda i: branch_ref.at[i], half_rows)
        local = pltpu.make_async_copy(mine, branch_ref.at[me], copy_sem)
        local.start()
        out_swap.wait_recv()
        added(out_sum_ref, out_sum_ref, out_core)
        gather.relay()
        gather.finish()
        gather.drain()
        reduce.drain()
        for copy in swaps + [out_swap]:
            copy.wait_send()
        local.wait()


BACK_WIDTH = D + 128


def turn(rank, up_grad, hidden, row_gates, cot_rows, weights, middle, cot, gates, router, gain):
    last = LOCAL_E - 1
    one = lambda e: (jnp.minimum(e, last), 0, 0)
    wide = lambda e: (0, jnp.minimum(e, last), 0, 0)
    whole = lambda e: (0, 0)
    blocks = lambda e: (0, 0, 0)
    row_block = pl.BlockSpec((TOK_DEV, D), whole)
    lane_block = pl.BlockSpec((TOK_DEV, 128), whole)
    gain_block = pl.BlockSpec((1, D), whole)
    group = pltpu.VMEM((N_SEQ, TOK_DEV, BACK_WIDTH), bf16)
    group_out = pltpu.VMEM((N_SEQ, TOK_DEV, D), bf16)
    return pl.pallas_call(
        turn_kernel,
        grid=(LOCAL_E + 1,),
        in_specs=[
            pl.BlockSpec((PAIR_TOK, LOCAL_E), whole),
            pl.BlockSpec((1, SLOTS, 2 * FF), one),
            pl.BlockSpec((1, SLOTS, FF), one),
            pl.BlockSpec((1, SLOTS, 1), one),
            pl.BlockSpec((1, SLOTS, D), one),
            pl.BlockSpec((16, 1, 144, 1024), wide),
            row_block,
            row_block,
            lane_block,
            pl.BlockSpec((D, 128), whole),
            gain_block,
        ],
        out_specs=[
            row_block,
            ANY,
            lane_block,
            gain_block,
            pl.BlockSpec((N_SEQ, TOK_DEV, D), blocks),
        ],
        out_shape=[
            jax.ShapeDtypeStruct((TOK_DEV, D), f32),
            jax.ShapeDtypeStruct((N_SEQ, TOK_DEV, D), bf16),
            jax.ShapeDtypeStruct((TOK_DEV, 128), bf16),
            jax.ShapeDtypeStruct((1, D), f32),
            jax.ShapeDtypeStruct((N_SEQ, TOK_DEV, D), bf16),
        ],
        scratch_shapes=[
            pltpu.VMEM((LOCAL_E * SLOTS, BACK_WIDTH), bf16),
            pltpu.VMEM((LOCAL_E * SLOTS, D), bf16),
            group,
            group,
            group,
            group_out,
            group_out,
            pltpu.VMEM((TOK_DEV, D), bf16),
        ]
        + reduce_scratch((TOK_DEV, BACK_WIDTH), (HALF, BACK_WIDTH))
        + sems(17)
        + [pltpu.SemaphoreType.DMA],
        compiler_params=remote_params(4),
        cost_estimate=pl.CostEstimate(
            flops=6 * LOCAL_E * SLOTS * D * FF + 4 * LOCAL_E * SLOTS * PAIR_TOK * D,
            bytes_accessed=40 << 20,
            transcendentals=0,
        ),
    )(rank, up_grad, hidden, row_gates, cot_rows, weights, middle, cot, gates, router, gain)


PAD_ROWS = 16
WIDE = 768
HALF_WIDE = 2304


def closing_kernel(
    part_ref, in_ref, grad_ref, gain_ref, normed_ref, mixed_ref, attended_ref, branch_ref,
    router_grad_ref, gain_two_ref, out_sum_ref, middle_ref,
    input_ref, block_ref, entry_out, exit_out,
    full, from_core, chip, line, final, give, got_z, *rest
):
    bufs, (send_sem, recv_sem) = [rest[6 * i : 6 * i + 6] for i in range(6)], rest[36:]
    z, x, y, c = (lax.axis_index(a) for a in ("seq", "x", "y", "core"))
    right, left, far = ring(z)
    greet(near("seq") + [("seq", far)] + near("x") + near("y") + [sibling()])
    send = sender(send_sem, recv_sem)
    rows = Reduce(send, 0, "seq", lambda i: part_ref.at[i], bufs[0], half_rows)
    rows.start_far()
    rows.start_near()
    pick = row_pick((512, QOWN), 0)

    def spread(grad):
        wide = dot(pick, grad, ((1,), (0,))).astype(bf16)
        return wide.reshape(16, 2, PAD_ROWS, grad.shape[1])

    def swap(side):
        return send(full.at[side, :, 1 - c], from_core.at[side], 36 + side, "core", 1 - c)

    def entry_rows(block):
        rows_of = slice(QOWN * block, QOWN * (block + 1))
        grad = dot(normed_ref[:, rows_of], mixed_ref[...], ((0,), (0,))).astype(bf16)
        return spread(grad)

    for block in range(3):
        cols = slice(512 * block, 512 * (block + 1))
        grad = dot(attended_ref[...], branch_ref[:, cols], ((0,), (0,))).astype(bf16)
        full[0, :, :, :, cols] = spread(grad)
    full[0, :, :, :, 1536:2176] = entry_rows(0)
    second = entry_rows(1)
    full[0, :, :, :, 2176:2304] = second[..., :128]
    swaps = [swap(0)]
    rows.relay()
    full[1, :, :, :, :512] = second[..., 128:]
    full[1, :, :, :, 512:1152] = entry_rows(2)
    full[1, :, :, :, 1152:1792] = entry_rows(3)
    back, gain_one = norm_back(in_ref[...].astype(f32), gain_ref[...], rows.total())
    input_ref[...] = (grad_ref[...] + back).astype(bf16)
    row_of = lax.broadcasted_iota(jnp.int32, (128, D), 0)
    gains = jnp.where(row_of == EXPERTS, gain_one, 0.0)
    gains = jnp.where(row_of == EXPERTS + 1, gain_two_ref[...], gains)
    shared = router_grad_ref[...] + gains.T
    for block in range(4):
        part = shared[QOWN * block : QOWN * (block + 1), :].astype(bf16)
        full[1, :, :, :, 1792 + 128 * block : 1920 + 128 * block] = spread(part)
    swaps.append(swap(1))
    outs = Reduce(send, 6, "seq", lambda i: out_sum_ref.at[i], bufs[1], half_rows)
    outs.start_far()
    outs.start_near()
    swaps[0].wait_recv()
    for plane in range(16):
        added(chip.at[0, plane // 4, plane % 4], full.at[0, plane, c], from_core.at[0, plane])
    low_x = Reduce(send, 12, "x", lambda i: chip.at[0, i], bufs[2], half_rows)
    low_x.start_far()
    low_x.start_near()
    swaps[1].wait_recv()
    for plane in range(16):
        added(chip.at[1, plane % 4, plane // 4], full.at[1, plane, c], from_core.at[1, plane])
    high_y = Reduce(send, 18, "y", lambda i: chip.at[1, i], bufs[3], half_rows)
    high_y.start_far()
    high_y.start_near()
    low_x.relay()
    high_y.relay()
    outs.relay()
    line[0] = low_x.total().astype(bf16)
    low_y = Reduce(send, 24, "y", lambda i: line.at[0, i], bufs[4], half_lanes)
    low_y.start_far()
    low_y.start_near()
    line[1] = high_y.total().astype(bf16)
    high_x = Reduce(send, 30, "x", lambda i: line.at[1, i], bufs[5], half_lanes)
    high_x.start_far()
    high_x.start_near()
    low_y.relay()
    high_x.relay()
    block_ref[...] = (middle_ref[...] + outs.total()).astype(bf16)
    final[0] = low_y.total()
    final[1] = high_x.total()
    exit_out[...] = final[0, :, :1536]
    give[0, :, :MIX_OWN] = final[0, :, 1536:2176]
    give[1, :, :128] = final[0, :, 2176:2304]
    give[1, :, 128:MIX_OWN] = final[1, :, :512]
    give[2, :, :MIX_OWN] = final[1, :, 512:1152]
    give[3, :, :MIX_OWN] = final[1, :, 1152:1792]
    for block in range(4):
        give[block, :, MIX_OWN:] = final[1, :, 1792 + 128 * block : 1920 + 128 * block]
    peers = (right, far, left)
    home = [
        send(give.at[peer], got_z.at[k], 38 + k, "seq", peer) for k, peer in enumerate(peers)
    ]
    entry_out[z] = give[z]
    for k, source in enumerate((left, far, right)):
        home[k].wait_recv()
        entry_out[source] = got_z[k]
    for copy in swaps + home:
        copy.wait_send()
    for reduce in (rows, outs, low_x, high_y, low_y, high_x):
        reduce.drain()


def closing(*operands):
    row_bufs = reduce_scratch((TOK_DEV, D), (HALF, D))
    chip_bufs = reduce_scratch((4, PAD_ROWS, HALF_WIDE), (2, PAD_ROWS, HALF_WIDE))
    line_bufs = reduce_scratch((PAD_ROWS, HALF_WIDE), (PAD_ROWS, HALF_WIDE // 2))
    tile = (PAD_ROWS, HALF_WIDE)
    return pl.pallas_call(
        closing_kernel,
        out_shape=[
            jax.ShapeDtypeStruct((TOK_DEV, D), bf16),
            jax.ShapeDtypeStruct((TOK_DEV, D), bf16),
            jax.ShapeDtypeStruct((4, PAD_ROWS, WIDE), f32),
            jax.ShapeDtypeStruct((PAD_ROWS, D), f32),
        ],
        in_specs=[VMEM] * 12,
        out_specs=[VMEM] * 4,
        scratch_shapes=[
            pltpu.VMEM((2, 16, 2) + tile, bf16),
            pltpu.VMEM((2, 16) + tile, bf16),
            pltpu.VMEM((2, 4, 4) + tile, bf16),
            pltpu.VMEM((2, 4) + tile, bf16),
            pltpu.VMEM((2,) + tile, f32),
            pltpu.VMEM((4, PAD_ROWS, WIDE), f32),
            pltpu.VMEM((3, PAD_ROWS, WIDE), f32),
        ]
        + row_bufs * 2
        + chip_bufs * 2
        + line_bufs * 2
        + sems(41),
        compiler_params=remote_params(5),
    )(*operands)


def dispatch_kernel(rank_ref, gate_ref, tokens_ref, cots_ref, rows_ref, cot_rows_ref, row_gate_ref):
    slot = lax.broadcasted_iota(jnp.int32, (SLOTS, PAIR_TOK), 0)
    match = rank_ref[0] == slot
    row_gate_ref[0] = jnp.sum(jnp.where(match, gate_ref[0], 0.0), axis=1, keepdims=True)
    pick = match.astype(bf16)
    for j in range(3):
        cols = slice(512 * j, 512 * (j + 1))
        rows_ref[0, :, cols] = dot(pick, tokens_ref[:, cols], ((1,), (0,))).astype(bf16)
        cot_rows_ref[0, :, cols] = dot(pick, cots_ref[:, cols], ((1,), (0,))).astype(bf16)

def dispatch(rank, gates, tokens, cots):
    one = lambda e: (e, 0, 0)
    whole = lambda e: (0, 0)
    return pl.pallas_call(
        dispatch_kernel,
        grid=(LOCAL_E,),
        in_specs=[
            pl.BlockSpec((1, 1, PAIR_TOK), one),
            pl.BlockSpec((1, 1, PAIR_TOK), one),
            pl.BlockSpec((PAIR_TOK, D), whole),
            pl.BlockSpec((PAIR_TOK, D), whole),
        ],
        out_specs=[
            pl.BlockSpec((1, SLOTS, D), one),
            pl.BlockSpec((1, SLOTS, D), one),
            pl.BlockSpec((1, SLOTS, 1), one),
        ],
        out_shape=[
            jax.ShapeDtypeStruct((LOCAL_E, SLOTS, D), bf16),
            jax.ShapeDtypeStruct((LOCAL_E, SLOTS, D), bf16),
            jax.ShapeDtypeStruct((LOCAL_E, SLOTS, 1), f32),
        ],
        compiler_params=pltpu.CompilerParams(vmem_limit_bytes=BIG),
        cost_estimate=pl.CostEstimate(
            flops=4 * LOCAL_E * SLOTS * PAIR_TOK * D, bytes_accessed=16 << 20, transcendentals=0
        ),
    )(rank[:, None], gates[:, None], tokens, cots)

def weights_of(w_ref):
    expand = w_ref[:, 0, :96, :].reshape(D, 2 * FF)
    left = w_ref[:, 0, 96:128, :].reshape(FF, 1024)
    right = jnp.concatenate([w_ref[:, 0, 128:144, :512], w_ref[:, 0, 128:144, 512:]], axis=1)
    return expand, left, right.reshape(FF, 512)

def grads_kernel(rows_ref, cot_ref, gate_ref, w_ref, hidden_ref, up_ref, out_ref):
    expand, left, right = weights_of(w_ref)
    grad_rows = (gate_ref[0] * cot_ref[0].astype(f32)).astype(bf16)
    rows = rows_ref[0]
    gate_pre = dot(rows, expand[:, :FF], ((1,), (0,)))
    up_part = dot(rows, expand[:, FF:], ((1,), (0,)))
    sig = jax.nn.sigmoid(gate_pre)
    hidden = (gate_pre * sig * up_part).astype(bf16)
    hidden_ref[0] = hidden
    hidden_grad = dot(grad_rows[:, :1024], left, ((1,), (1,))) + dot(
        grad_rows[:, 1024:], right, ((1,), (1,))
    )
    up_ref[0, :, :FF] = (hidden_grad * up_part * sig * (1.0 + gate_pre * (1.0 - sig))).astype(bf16)
    up_ref[0, :, FF:] = (hidden_grad * gate_pre * sig).astype(bf16)
    grad_left = dot(hidden, grad_rows[:, :1024], ((0,), (0,))).astype(bf16)
    out_ref[:, 0, 96:128, :] = grad_left.reshape(16, 32, 1024)
    grad_right = dot(hidden, grad_rows[:, 1024:], ((0,), (0,))).astype(bf16).reshape(16, 32, 512)
    out_ref[:, 0, 128:144, :512] = grad_right[:, :16]
    out_ref[:, 0, 128:144, 512:] = grad_right[:, 16:]
    up_grad = up_ref[0]
    for j in range(4):
        part = dot(rows[:, 384 * j : 384 * (j + 1)], up_grad, ((0,), (0,))).astype(bf16)
        out_ref[4 * j : 4 * (j + 1), 0, :96, :] = part.reshape(4, 96, 1024)

def expert_grads(rows, cot_rows, row_gates, weights):
    one = lambda e: (e, 0, 0)
    wide = lambda e: (0, e, 0, 0)
    return pl.pallas_call(
        grads_kernel,
        grid=(LOCAL_E,),
        in_specs=[
            pl.BlockSpec((1, SLOTS, D), one),
            pl.BlockSpec((1, SLOTS, D), one),
            pl.BlockSpec((1, SLOTS, 1), one),
            pl.BlockSpec((16, 1, 144, 1024), wide),
        ],
        out_specs=[
            pl.BlockSpec((1, SLOTS, FF), one),
            pl.BlockSpec((1, SLOTS, 2 * FF), one),
            pl.BlockSpec((16, 1, 144, 1024), wide),
        ],
        out_shape=[
            jax.ShapeDtypeStruct((LOCAL_E, SLOTS, FF), bf16),
            jax.ShapeDtypeStruct((LOCAL_E, SLOTS, 2 * FF), bf16),
            jax.ShapeDtypeStruct((16, LOCAL_E, 144, 1024), bf16),
        ],
        compiler_params=pltpu.CompilerParams(vmem_limit_bytes=BIG),
        cost_estimate=pl.CostEstimate(
            flops=12 * LOCAL_E * SLOTS * D * FF, bytes_accessed=60 << 20, transcendentals=0
        ),
    )(rows, cot_rows, row_gates, weights)


def core_swap(value):
    return lax.ppermute(value, "core", [(0, 1), (1, 0)])


def core_order(core, mine, other, axis):
    return jnp.concatenate(
        [jnp.where(core == 0, mine, other), jnp.where(core == 0, other, mine)], axis=axis
    )


def norm_apply(vector, gain):
    scale = lax.rsqrt(jnp.mean(vector * vector, axis=-1, keepdims=True) + norm_eps)
    return vector * scale * gain


def adamw_step(weight, gradient, mean_old, square_old, rate, decay):
    drift = beta_first * mean_old + (1.0 - beta_first) * gradient
    spread = beta_second * square_old + (1.0 - beta_second) * gradient * gradient
    mean_hat = drift / (1.0 - beta_first**STEP)
    square_hat = spread / (1.0 - beta_second**STEP)
    master = weight - rate * (mean_hat / (jnp.sqrt(square_hat) + adam_eps) + decay * weight)
    return (drift, spread, master)


def rotate(vector, cosine, sine):
    first, second = vector[..., : HD // 2], vector[..., HD // 2 :]
    return jnp.concatenate(
        [first * cosine - second * sine, second * cosine + first * sine], axis=-1
    )


def on_device(
    activations,
    cotangent,
    seq_lengths,
    deal_order,
    routes,
    entry_weight,
    entry_mean,
    entry_square,
    exit_weight,
    exit_mean,
    exit_square,
    router_weight,
    router_mean,
    router_square,
    expand_weight,
    expand_mean,
    expand_square,
    shrink_weight,
    shrink_mean,
    shrink_square,
    norm_gains,
    gains_mean,
    gains_square,
):
    seq = lax.axis_index("seq")
    core = lax.axis_index("core")
    first = (seq * 2 + core) * LOCAL_E

    packed = pack_experts(expand_weight, shrink_weight)
    packed, rows_in, cots_in = lax.optimization_barrier((packed, activations[0], cotangent[0]))
    weights = lax.all_gather(packed, PLANE, axis=0, tiled=False)

    entry_b = entry_weight.astype(bf16)
    shared_b = jnp.concatenate([router_weight, norm_gains.T], axis=1).astype(bf16)
    shared_b = jnp.pad(shared_b, ((0, 0), (0, 128 - EXPERTS - 2)))
    entry_cols = jnp.concatenate(
        [
            entry_b[:, : QH * HD].reshape(ROWS, N_SEQ, Q_OWN).transpose(1, 0, 2),
            entry_b[:, QH * HD :].reshape(ROWS, N_SEQ, KV_OWN).transpose(1, 0, 2),
            jnp.broadcast_to(shared_b[None], (N_SEQ, ROWS, 128)),
        ],
        axis=2,
    )
    exit_cols = exit_weight.astype(bf16).reshape(ROWS, 2, WIDE).transpose(1, 0, 2)
    pad = ((0, 0), (0, PAD_ROWS - ROWS), (0, 0))
    expert_ids = jnp.arange(128, dtype=jnp.int32)
    hit_slots = jnp.any(routes[0][:, :, None] == expert_ids[None, None, :], axis=1).astype(bf16)
    in_all, cots, hit_slots, entry_own, shared, exit_own = start(
        rows_in, cots_in, hit_slots, jnp.pad(entry_cols, pad), jnp.pad(exit_cols, pad)
    )
    in_all = in_all.reshape(GROUP, D)
    gains_full = shared[:, EXPERTS : EXPERTS + 2].astype(f32).T

    order_row = deal_order[0]
    token = jnp.arange(GROUP, dtype=jnp.int32)
    back_hot = (order_row[None, :] == token[:, None]).astype(bf16)
    hit = dot(back_hot, hit_slots.reshape(GROUP, 128), ((1,), (0,))).astype(bf16)
    hits = core_order(core, hit, core_swap(hit), 0)[:, :EXPERTS]
    own_hits = lax.dynamic_slice_in_dim(hits, first, LOCAL_E, 1)
    rank = jnp.cumsum(own_hits.astype(jnp.int32), axis=0) - 1
    rank = jnp.where(own_hits > 0, rank, -1)
    seq_ends = jnp.cumsum(seq_lengths[0])
    starts = seq_ends - seq_lengths[0]
    seq_ids = jnp.sum((token[:, None] >= seq_ends[None, :]).astype(jnp.int32), axis=1)
    seq_match = seq_ids[:, None] == jnp.arange(seq_ends.shape[0], dtype=jnp.int32)[None, :]
    positions = token - jnp.sum(jnp.where(seq_match, starts[None, :], 0), axis=1)
    frequency = rope_base ** (-jnp.arange(HD // 2, dtype=f32) * 2.0 / HD)
    phase = positions.astype(f32)[:, None] * frequency[None, :]
    cosine, sine = jnp.cos(phase)[:, None, :], jnp.sin(phase)[:, None, :]
    allowed = (seq_ids[:, None] == seq_ids[None, :]) & (token[None, :] <= token[:, None])

    normed = norm_apply(in_all.astype(f32), gains_full[0]).astype(bf16)
    mixed = dot(normed, entry_own, ((1,), (0,)))
    queries = rotate(mixed[:, :Q_OWN].reshape(GROUP, HEADS_OWN, HD), cosine, sine)
    pairs = mixed[:, Q_OWN:].reshape(GROUP, KV_HEADS_OWN, 2, HD)
    keys = rotate(pairs[:, :, 0], cosine, sine)
    queries = queries.astype(bf16).reshape(GROUP, KV_HEADS_OWN, PER_KV, HD)
    keys, values = keys.astype(bf16), pairs[:, :, 1].astype(bf16)
    scores = jnp.einsum("qhgd,khd->hgqk", queries, keys, preferred_element_type=f32) * HD**-0.5
    scores = jnp.where(allowed[None, None], scores, -1e30)
    peak = jnp.max(scores, axis=-1, keepdims=True)
    expo = jnp.exp(scores - peak)
    probs = expo / jnp.sum(expo, axis=-1, keepdims=True)
    probs_b = probs.astype(bf16)
    attended = (
        jnp.einsum("hgqk,khd->qhgd", probs_b, values, preferred_element_type=f32)
        .reshape(GROUP, Q_OWN)
        .astype(bf16)
    )
    branch_part = dot(attended, exit_own, ((1,), (0,))).astype(bf16)
    middle, tokens = middle_tokens(
        branch_part.reshape(N_SEQ, TOK_DEV, D), activations[0], gains_full[1:2]
    )
    normed_two = lax.dynamic_slice(tokens, (core, seq, 0, 0), (1, 1, TOK_DEV, D))[0, 0]
    tokens = tokens.reshape(PAIR_TOK, D)

    logits = dot(tokens, shared[:, :EXPERTS], ((1,), (0,)))
    masked = jnp.where(hits > 0, logits, -jnp.inf)
    gate_expo = jnp.exp(masked - jnp.max(masked, axis=1, keepdims=True))
    gates = gate_expo / jnp.sum(gate_expo, axis=1, keepdims=True)
    own_gates = lax.dynamic_slice_in_dim(gates, first, LOCAL_E, 1)
    rows, cot_rows, row_gates = dispatch(rank.T, own_gates.T, tokens, cots.reshape(PAIR_TOK, D))
    hidden, up_grad, expert_grad = expert_grads(rows, cot_rows, row_gates, weights)
    expert_sum = lax.psum_scatter(expert_grad, PLANE, scatter_dimension=0, tiled=False)
    my_gates = lax.dynamic_slice_in_dim(gates, core * GROUP + seq * TOK_DEV, TOK_DEV, 0)
    my_gates = jnp.pad(my_gates, ((0, 0), (0, 128 - EXPERTS)))
    middle_grad, branch_grad, logit_grad, gain_two_grad, out_sum = turn(
        rank,
        up_grad,
        hidden,
        row_gates,
        cot_rows,
        weights,
        middle,
        cotangent[0],
        my_gates,
        shared,
        gains_full[1:2],
    )
    branch_grad = branch_grad.reshape(GROUP, D)
    router_grad = dot(normed_two, logit_grad, ((0,), (0,)))

    attended_grad = dot(branch_grad, exit_own, ((1,), (1,))).astype(bf16)
    attended_grad = attended_grad.reshape(GROUP, KV_HEADS_OWN, PER_KV, HD)
    prob_grad = jnp.einsum("qhgd,khd->hgqk", attended_grad, values, preferred_element_type=f32)
    delta = jnp.sum(probs * prob_grad, axis=-1, keepdims=True)
    score_grad = (probs * (prob_grad - delta) * HD**-0.5).astype(bf16)
    query_grad = jnp.einsum("hgqk,khd->qhgd", score_grad, keys, preferred_element_type=f32)
    key_grad = jnp.einsum("hgqk,qhgd->khd", score_grad, queries, preferred_element_type=f32)
    value_grad = jnp.einsum("hgqk,qhgd->khd", probs_b, attended_grad, preferred_element_type=f32)
    query_grad = rotate(query_grad.reshape(GROUP, HEADS_OWN, HD), cosine, -sine)
    key_grad = rotate(key_grad, cosine, -sine)
    mixed_grad = jnp.concatenate(
        [
            query_grad.reshape(GROUP, Q_OWN),
            jnp.stack([key_grad, value_grad], axis=2).reshape(GROUP, KV_OWN),
        ],
        axis=1,
    ).astype(bf16)
    normed_part = dot(mixed_grad, entry_own, ((1,), (1,))).astype(bf16)
    input_grad, block_output, entry_got, exit_got = closing(
        normed_part.reshape(N_SEQ, TOK_DEV, D),
        activations[0],
        middle_grad,
        gains_full[0:1],
        normed,
        mixed_grad,
        attended,
        branch_grad,
        router_grad,
        gain_two_grad,
        out_sum,
        middle,
    )

    entry_got = entry_got[:, :ROWS]
    entry_sum = jnp.concatenate(
        [
            entry_got[:, :, :Q_OWN].transpose(1, 0, 2).reshape(ROWS, QH * HD),
            entry_got[:, :, Q_OWN:MIX_OWN].transpose(1, 0, 2).reshape(ROWS, 2 * KVH * HD),
        ],
        axis=1,
    )
    shared_sum = jnp.sum(entry_got[:, :, MIX_OWN:], axis=0)
    router_sum = shared_sum[:, :EXPERTS]
    gains_sum = shared_sum[:, EXPERTS : EXPERTS + 2].T
    exit_sum = exit_got[:ROWS]

    ends = expert_sum[:, 128:].reshape(LOCAL_E, 16, 2, 512).transpose(2, 0, 1, 3)
    rows_of = jnp.stack(
        [
            jnp.concatenate([expert_sum[:, :48], expert_sum[:, 96:112]], axis=1),
            jnp.concatenate([expert_sum[:, 48:96], expert_sum[:, 112:128]], axis=1),
        ]
    )

    def to_owner(value):
        mine = lax.dynamic_index_in_dim(value, core, 0, keepdims=False)
        other = core_swap(lax.dynamic_index_in_dim(value, 1 - core, 0, keepdims=False))
        return core_order(core, mine, other, 0).astype(f32)

    rows_of, ends = to_owner(rows_of), to_owner(ends)
    expand_sum = rows_of[:, :48]
    shrink_sum = jnp.concatenate([rows_of[:, 48:], ends], axis=2)
    entry_new = adamw_step(entry_weight, entry_sum, entry_mean, entry_square, 0.02, weight_decay)
    exit_new = adamw_step(exit_weight, exit_sum, exit_mean, exit_square, 0.15, weight_decay)
    router_new = adamw_step(
        router_weight, router_sum, router_mean, router_square, 0.01, weight_decay
    )
    expand_new = adamw_step(
        expand_weight, expand_sum, expand_mean, expand_square, 0.02, weight_decay
    )
    shrink_new = adamw_step(
        shrink_weight, shrink_sum, shrink_mean, shrink_square, 0.12, weight_decay
    )
    gains_new = adamw_step(norm_gains, gains_sum, gains_mean, gains_square, 0.5, 0.0)
    return (
        block_output[None],
        input_grad[None],
        *entry_new,
        *exit_new,
        *router_new,
        *expand_new,
        *shrink_new,
        *gains_new,
    )


def solution(mesh):
    fine = Mesh(mesh.devices.reshape(4, 4, 4, 2), ("seq", "x", "y", "core"))
    rows = P(FSDP, "seq", None)
    lists = P(FSDP, None)
    owned = P(("seq",) + FSDP, None)
    experts = P("seq", FSDP, None)
    gains = P(None, ("seq",) + FSDP)
    return jax.shard_map(
        on_device,
        mesh=fine,
        in_specs=(rows, rows, lists, lists, rows)
        + (owned,) * 9
        + (experts,) * 6
        + (gains,) * 3,
        out_specs=(rows, rows) + (owned,) * 9 + (experts,) * 6 + (gains,) * 3,
        check_vma=False,
    )
```

```python
import jax
import jax.numpy as jnp
from jax import lax
from jax.experimental import pallas as pl
from jax.experimental.pallas import tpu as pltpu
from jax.sharding import Mesh, PartitionSpec as P

D = 1536
QH = 24
KVH = 8
HD = 64
FF = 512
EXPERTS = 40
TOP = 8
STEP = 10
CAP = 29

N_SEQ = 4
TOK_DEV = 128
GROUP = 512
PAIR_TOK = 2 * GROUP
LOCAL_E = EXPERTS // (2 * N_SEQ)
SLOTS = 256
Q_OWN = QH * HD // N_SEQ
KV_OWN = 2 * KVH * HD // N_SEQ
MIX_OWN = Q_OWN + KV_OWN
HEADS_OWN = QH // N_SEQ
KV_HEADS_OWN = KVH // N_SEQ
PER_KV = QH // KVH
ROWS = 12

norm_eps = 1e-06
rope_base = 10000.0
beta_first = 0.9
beta_second = 0.95
adam_eps = 1e-08
weight_decay = 0.1

FSDP = ("x", "y", "core")
PLANE = ("x", "y")
f32 = jnp.float32
bf16 = jnp.bfloat16


BIG = 56 * 1024 * 1024
HALF = TOK_DEV // 2
QOWN = Q_OWN
MESH = pl.DeviceIdType.MESH
ANY = pl.BlockSpec(memory_space=pl.ANY)
VMEM = pl.BlockSpec(memory_space=pltpu.VMEM)


def dot(a, b, dims):
    return lax.dot_general(a, b, (dims, ((), ())), preferred_element_type=f32)


def greet(peers):
    barrier = pltpu.get_barrier_semaphore()
    for axis, peer in peers:
        pl.semaphore_signal(barrier, inc=1, device_id={axis: peer}, device_id_type=MESH)
    pl.semaphore_wait(barrier, len(peers))


def sender(send_sem, recv_sem):
    def send(src, dst, index, axis, peer):
        copy = pltpu.make_async_remote_copy(
            src_ref=src,
            dst_ref=dst,
            send_sem=send_sem.at[index],
            recv_sem=recv_sem.at[index],
            device_id={axis: peer},
            device_id_type=MESH,
        )
        copy.start()
        return copy

    return send


def sems(count):
    return [pltpu.SemaphoreType.DMA((count,)), pltpu.SemaphoreType.DMA((count,))]


def ring(me):
    right, left = lax.rem(me + 1, 4), lax.rem(me + 3, 4)
    return right, left, lax.rem(me + 2, 4)


def near(axis):
    right, left, _ = ring(lax.axis_index(axis))
    return [(axis, right), (axis, left)]


def sibling():
    return ("core", 1 - lax.axis_index("core"))


def half_rows(ref, half):
    size = ref.shape[0] // 2
    return ref.at[pl.ds(half * size, size)]


def half_lanes(ref, half):
    size = ref.shape[-1] // 2
    return ref.at[(slice(None),) * (len(ref.shape) - 1) + (pl.ds(half * size, size),)]


class Gather:
    def __init__(self, send, base, axis, mine, slot, cut):
        self.send, self.base, self.axis, self.slot, self.cut = send, base, axis, slot, cut
        me = lax.axis_index(axis)
        self.right, self.left, self.far = ring(me)
        here = slot(me)
        self.first = [
            send(cut(mine, 0), cut(here, 0), base, axis, self.right),
            send(cut(mine, 1), cut(here, 1), base + 1, axis, self.left),
            send(cut(mine, 1), cut(here, 1), base + 2, axis, self.right),
            send(cut(mine, 0), cut(here, 0), base + 3, axis, self.left),
        ]
        self.later = []

    def relay(self):
        self.first[0].wait_recv()
        part = self.cut(self.slot(self.left), 0)
        self.later.append(self.send(part, part, self.base + 4, self.axis, self.right))
        self.first[1].wait_recv()
        part = self.cut(self.slot(self.right), 1)
        self.later.append(self.send(part, part, self.base + 5, self.axis, self.left))

    def wait_left(self):
        self.first[2].wait_recv()

    def wait_right(self):
        self.first[3].wait_recv()

    def wait_far(self):
        for copy in self.later:
            copy.wait_recv()

    def finish(self):
        self.wait_left()
        self.wait_right()
        self.wait_far()

    def drain(self):
        for copy in self.first + self.later:
            copy.wait_send()


def hand_over(send, base, mine, out, gather):
    me, core = lax.axis_index("seq"), lax.axis_index("core")
    other = 1 - core
    copies = [send(mine, out.at[core, me], base, "core", other)]
    gather.relay()
    gather.wait_left()
    block = out.at[core, gather.left]
    copies.append(send(block, block, base + 1, "core", other))
    gather.wait_right()
    block = out.at[core, gather.right]
    copies.append(send(block, block, base + 2, "core", other))
    gather.wait_far()
    block = out.at[core, gather.far]
    copies.append(send(block, block, base + 3, "core", other))
    return copies


def reduce_scratch(block, half):
    return [pltpu.VMEM(half, bf16)] * 4 + [pltpu.VMEM(block, bf16)] * 2


def added(target, first, second):
    target[...] = (first[...].astype(f32) + second[...].astype(f32)).astype(bf16)


class Reduce:
    def __init__(self, send, base, axis, block, bufs, cut):
        self.send, self.base, self.axis, self.block = send, base, axis, block
        self.bufs, self.cut = bufs, cut
        self.me = lax.axis_index(axis)
        self.right, self.left, self.far = ring(self.me)

    def start_far(self):
        far = self.block(self.far)
        self.copies = [
            self.send(self.cut(far, 0), self.bufs[0], self.base, self.axis, self.right),
            self.send(self.cut(far, 1), self.bufs[1], self.base + 1, self.axis, self.left),
        ]

    def start_near(self):
        source, target = self.cut(self.block(self.right), 1), self.cut(self.bufs[4], 1)
        self.copies.append(self.send(source, target, self.base + 2, self.axis, self.right))
        source, target = self.cut(self.block(self.left), 0), self.cut(self.bufs[5], 0)
        self.copies.append(self.send(source, target, self.base + 3, self.axis, self.left))

    def relay(self):
        from_left, from_right, to_right, to_left, got_left, got_right = self.bufs
        self.copies[0].wait_recv()
        added(to_right, self.cut(self.block(self.right), 0), from_left)
        target = self.cut(got_left, 0)
        self.copies.append(self.send(to_right, target, self.base + 4, self.axis, self.right))
        self.copies[1].wait_recv()
        added(to_left, self.cut(self.block(self.left), 1), from_right)
        target = self.cut(got_right, 1)
        self.copies.append(self.send(to_left, target, self.base + 5, self.axis, self.left))

    def total(self):
        for copy in self.copies[2:]:
            copy.wait_recv()
        mine = self.block(self.me)[...].astype(f32)
        return mine + self.bufs[4][...].astype(f32) + self.bufs[5][...].astype(f32)

    def drain(self):
        for copy in self.copies:
            copy.wait_send()


def remote_params(call_id):
    return pltpu.CompilerParams(
        collective_id=call_id, has_side_effects=True, vmem_limit_bytes=BIG
    )


def unit_scale(vector):
    return lax.rsqrt(jnp.mean(vector * vector, axis=-1, keepdims=True) + norm_eps)


def norm_back(vector, gain, grad):
    scale = unit_scale(vector)
    unit = vector * scale
    pulled = grad * gain
    back = scale * (pulled - unit * jnp.mean(pulled * unit, axis=-1, keepdims=True))
    return back, jnp.sum(unit * grad, axis=0, keepdims=True)


def pack_kernel(expand_ref, shrink_ref, out_ref, stage, stage_end, send_sem, recv_sem):
    core = lax.axis_index("core")
    greet([sibling()])
    send = sender(send_sem, recv_sem)
    other = 1 - core
    for e in range(LOCAL_E):
        theirs = other * LOCAL_E + e
        stage[e, :48] = expand_ref[theirs].astype(bf16)
        stage[e, 48:] = shrink_ref[theirs, :, :1024].astype(bf16)
        stage_end[e] = shrink_ref[theirs, :, 1024:].astype(bf16)
    main = pl.ds(pl.multiple_of(core * 48, 16), 48)
    left = pl.ds(pl.multiple_of(96 + core * 16, 16), 16)
    ends = pl.ds(pl.multiple_of(core * 512, 512), 512)
    copies = [
        send(stage.at[:, pl.ds(0, 48)], out_ref.at[:, main], 0, "core", other),
        send(stage.at[:, pl.ds(48, 16)], out_ref.at[:, left], 1, "core", other),
        send(stage_end, out_ref.at[:, pl.ds(128, 16), ends], 2, "core", other),
    ]
    for e in range(LOCAL_E):
        mine = core * LOCAL_E + e
        out_ref[e, main, :] = expand_ref[mine].astype(bf16)
        out_ref[e, left, :] = shrink_ref[mine, :, :1024].astype(bf16)
        out_ref[e, pl.ds(128, 16), ends] = shrink_ref[mine, :, 1024:].astype(bf16)
    for copy in copies:
        copy.wait()


def pack_experts(expand, shrink):
    return pl.pallas_call(
        pack_kernel,
        out_shape=jax.ShapeDtypeStruct((LOCAL_E, 144, 1024), bf16),
        in_specs=[VMEM] * 2,
        out_specs=VMEM,
        scratch_shapes=[
            pltpu.VMEM((LOCAL_E, 64, 1024), bf16),
            pltpu.VMEM((LOCAL_E, 16, 512), bf16),
        ]
        + sems(3),
        compiler_params=remote_params(1),
    )(expand, shrink)


def row_pick(shape, padded_axis):
    padded = lax.broadcasted_iota(jnp.int32, shape, padded_axis)
    plain = lax.broadcasted_iota(jnp.int32, shape, 1 - padded_axis)
    row = lax.rem(padded, 16)
    return ((plain == lax.div(padded, 16) * 12 + row) & (row < 12)).astype(bf16)


def start_kernel(
    in_ref, cot_ref, hit_ref, entry_ref, exit_ref,
    in_all, cot_all, hit_all, entry_out, shared_out, exit_out,
    hold, full, send_sem, recv_sem, copy_sem,
):
    z, x, y, c = (lax.axis_index(a) for a in ("seq", "x", "y", "core"))
    right, left, far = ring(z)
    greet(near("seq") + [("seq", far)] + near("x") + near("y") + [sibling()])
    send = sender(send_sem, recv_sem)
    columns = [
        send(entry_ref.at[peer], hold.at[z], k, "seq", peer)
        for k, peer in enumerate((right, far, left))
    ]
    hits = Gather(send, 3, "seq", hit_ref, lambda i: hit_all.at[i], half_rows)
    rows = Gather(send, 9, "seq", in_ref, lambda i: in_all.at[i], half_rows)
    local = [
        pltpu.make_async_copy(entry_ref.at[z], hold.at[z], copy_sem.at[0]),
        pltpu.make_async_copy(exit_ref, hold.at[pl.ds(4, 2)], copy_sem.at[1]),
        pltpu.make_async_copy(hit_ref, hit_all.at[z], copy_sem.at[2]),
        pltpu.make_async_copy(in_ref, in_all.at[z], copy_sem.at[3]),
        pltpu.make_async_copy(cot_ref, cot_all.at[c, z], copy_sem.at[4]),
    ]
    for copy in local:
        copy.start()
    local[0].wait()
    local[1].wait()
    for copy in columns:
        copy.wait_recv()
    own = pltpu.make_async_copy(hold, full.at[:, x, y, c], copy_sem.at[5])
    own.start()
    low, high = pl.ds(0, 3), pl.ds(3, 3)
    low_x = Gather(send, 15, "x", hold.at[low], lambda i: full.at[low, i, y, c], half_lanes)
    high_y = Gather(send, 21, "y", hold.at[high], lambda i: full.at[high, x, i, c], half_lanes)
    hits.relay()
    low_x.relay()
    high_y.relay()
    rows.relay()
    cots = Gather(send, 27, "seq", cot_ref, lambda i: cot_all.at[c, i], half_rows)
    own.wait()
    low_x.finish()

    def cut_low(ref, half):
        return ref.at[:, pl.ds(2 * half, 2)]

    low_y = Gather(
        send, 33, "y", full.at[low, :, y, c], lambda i: full.at[low, :, i, c], cut_low
    )
    high_y.finish()
    high_x = Gather(
        send, 39, "x", full.at[high, x, :, c], lambda i: full.at[high, i, :, c], cut_low
    )
    low_y.relay()
    high_x.relay()
    pairs = hand_over(send, 45, cot_ref, cot_all, cots)
    low_y.finish()
    half = full.at[low, :, :, c]
    last = [send(half, half, 49, "core", 1 - c)]
    high_x.finish()
    half = full.at[high, :, :, c]
    last.append(send(half, half, 50, "core", 1 - c))
    pick = row_pick((QOWN, 512), 1)
    for copy in last:
        copy.wait_recv()
    for block in range(4):
        got = dot(pick, full[block].reshape(512, WIDE), ((1,), (0,))).astype(bf16)
        entry_out[QOWN * block : QOWN * (block + 1), :] = got[:, :MIX_OWN]
        shared_out[QOWN * block : QOWN * (block + 1), :] = got[:, MIX_OWN:]
    for block in range(2):
        got = dot(pick, full[4 + block].reshape(512, WIDE), ((1,), (0,))).astype(bf16)
        exit_out[:, WIDE * block : WIDE * (block + 1)] = got
    hits.finish()
    rows.finish()
    for copy in pairs:
        copy.wait()
    for gather in (hits, rows, cots, low_x, high_y, low_y, high_x):
        gather.drain()
    for copy in columns + last:
        copy.wait_send()
    for copy in local[2:]:
        copy.wait()


def start(rows, cots, hits, entry_cols, exit_cols):
    return pl.pallas_call(
        start_kernel,
        out_shape=[
            jax.ShapeDtypeStruct((N_SEQ, TOK_DEV, D), bf16),
            jax.ShapeDtypeStruct((2, N_SEQ, TOK_DEV, D), bf16),
            jax.ShapeDtypeStruct((N_SEQ, TOK_DEV, 128), bf16),
            jax.ShapeDtypeStruct((D, MIX_OWN), bf16),
            jax.ShapeDtypeStruct((D, 128), bf16),
            jax.ShapeDtypeStruct((QOWN, D), bf16),
        ],
        in_specs=[ANY] * 3 + [VMEM] * 2,
        out_specs=[ANY] * 3 + [VMEM] * 3,
        scratch_shapes=[
            pltpu.VMEM((6, PAD_ROWS, WIDE), bf16),
            pltpu.VMEM((6, 4, 4, 2, PAD_ROWS, WIDE), bf16),
        ]
        + sems(51)
        + [pltpu.SemaphoreType.DMA((6,))],
        compiler_params=remote_params(2),
    )(rows, cots, hits, entry_cols, exit_cols)


def swap_halves(rows, lower, upper):
    lane = lax.broadcasted_iota(jnp.int32, rows.shape, 1)
    ahead = pltpu.roll(rows, rows.shape[1] - HD // 2, 1)
    behind = pltpu.roll(rows, HD // 2, 1)
    return jnp.where(lax.rem(lane, HD) < HD // 2, lower * ahead, upper * behind)


BLOCK = 256


def block_bias(seq_col_ref, seq_row_ref, block):
    keys = BLOCK * (block + 1)
    row = lax.broadcasted_iota(jnp.int32, (BLOCK, keys), 0) + BLOCK * block
    column = lax.broadcasted_iota(jnp.int32, (BLOCK, keys), 1)
    same = seq_col_ref[BLOCK * block : keys, :] == seq_row_ref[:, :keys]
    return jnp.where(same & (column <= row), 0.0, -1e30)


def head_of(index):
    return slice(HD * index, HD * (index + 1))


def middle_kernel(
    all_ref, gain_one_ref, entry_ref, cos_ref, sin_ref, seq_col_ref, seq_row_ref, exit_ref,
    in_ref, gain_ref,
    normed_ref, qkv_ref, attended_ref, lse_ref, middle_ref, tokens_ref,
    part, mine, *rest
):
    bufs, (send_sem, recv_sem, copy_sem) = rest[:6], rest[6:]
    me, core = lax.axis_index("seq"), lax.axis_index("core")
    greet(near("seq") + [sibling()])
    send = sender(send_sem, recv_sem)
    for block in range(N_SEQ):
        rows = slice(TOK_DEV * block, TOK_DEV * (block + 1))
        vector = all_ref[block].astype(f32)
        normed_ref[rows, :] = (vector * unit_scale(vector) * gain_one_ref[...]).astype(bf16)
    mixed = dot(normed_ref[...], entry_ref[...], ((1,), (0,)))
    mixed = mixed * cos_ref[...] + swap_halves(mixed, -1.0, 1.0) * sin_ref[...]
    qkv_ref[...] = mixed.astype(bf16)
    for block in range(GROUP // BLOCK):
        bias = block_bias(seq_col_ref, seq_row_ref, block)
        keys = BLOCK * (block + 1)
        rows = slice(BLOCK * block, keys)
        for head in range(HEADS_OWN):
            pair = Q_OWN + 2 * HD * (head // PER_KV)
            key = qkv_ref[:keys, pair : pair + HD]
            value = qkv_ref[:keys, pair + HD : pair + 2 * HD]
            scores = dot(qkv_ref[rows, head_of(head)], key, ((1,), (1,))) * HD**-0.5 + bias
            peak = jnp.max(scores, axis=1, keepdims=True)
            expo = jnp.exp(scores - peak)
            total = jnp.sum(expo, axis=1, keepdims=True)
            probs = (expo / total).astype(bf16)
            attended_ref[rows, head_of(head)] = dot(probs, value, ((1,), (0,))).astype(bf16)
            lse_ref[rows, head : head + 1] = peak + jnp.log(total)
    part[...] = dot(attended_ref[...], exit_ref[...], ((1,), (0,))).astype(bf16).reshape(part.shape)
    reduce = Reduce(send, 0, "seq", lambda i: part.at[i], bufs, half_rows)
    reduce.start_far()
    reduce.start_near()
    reduce.relay()
    middle = in_ref[...].astype(f32) + reduce.total()
    middle_ref[...] = middle
    mine[...] = (middle * unit_scale(middle) * gain_ref[...]).astype(bf16)
    gather = Gather(send, 6, "seq", mine, lambda i: tokens_ref.at[core, i], half_rows)
    local = pltpu.make_async_copy(mine, tokens_ref.at[core, me], copy_sem)
    local.start()
    pairs = hand_over(send, 12, mine, tokens_ref, gather)
    for copy in pairs:
        copy.wait()
    gather.drain()
    reduce.drain()
    local.wait()


def middle_tokens(*operands):
    return pl.pallas_call(
        middle_kernel,
        out_shape=[
            jax.ShapeDtypeStruct((GROUP, D), bf16),
            jax.ShapeDtypeStruct((GROUP, MIX_OWN), bf16),
            jax.ShapeDtypeStruct((GROUP, Q_OWN), bf16),
            jax.ShapeDtypeStruct((GROUP, HEADS_OWN), f32),
            jax.ShapeDtypeStruct((TOK_DEV, D), f32),
            jax.ShapeDtypeStruct((2, N_SEQ, TOK_DEV, D), bf16),
        ],
        in_specs=[VMEM] * 10,
        out_specs=[VMEM] * 5 + [ANY],
        scratch_shapes=[pltpu.VMEM((N_SEQ, TOK_DEV, D), bf16), pltpu.VMEM((TOK_DEV, D), bf16)]
        + reduce_scratch((TOK_DEV, D), (HALF, D))
        + sems(16)
        + [pltpu.SemaphoreType.DMA],
        compiler_params=remote_params(3),
    )(*operands)


def turn_kernel(
    rank_ref, up_ref, hidden_ref, gate_ref, cot_rows_ref, w_ref,
    middle_ref, cot_ref, my_gate_ref, router_ref, gain_ref,
    grad_ref, branch_ref, logit_ref, gain_grad_ref, out_sum_ref,
    back_s, out_s, other_back, from_core, part, other_out, out_core, mine, *rest
):
    bufs, (send_sem, recv_sem, copy_sem) = rest[:6], rest[6:]
    e = pl.program_id(0)
    me, core = lax.axis_index("seq"), lax.axis_index("core")

    @pl.when(e == 0)
    def _():
        greet(near("seq") + [sibling()])

    @pl.when(e < LOCAL_E)
    def _():
        expand, left, right = weights_of(w_ref)
        at = pl.ds(pl.multiple_of(e * SLOTS, SLOTS), SLOTS)
        back_s[at, :D] = dot(up_ref[0], expand, ((1,), (1,))).astype(bf16)
        hidden = hidden_ref[0]
        expert_out = jnp.concatenate(
            [dot(hidden, left, ((1,), (0,))), dot(hidden, right, ((1,), (0,)))], axis=1
        )
        expert_out = expert_out.astype(bf16).astype(f32)
        gate_grad = jnp.sum(expert_out * cot_rows_ref[0].astype(f32), axis=1, keepdims=True)
        lane = lax.broadcasted_iota(jnp.int32, (SLOTS, 128), 1)
        column = (me * 2 + core) * LOCAL_E + e
        back_s[at, D:] = jnp.where(lane == column, gate_grad, 0.0).astype(bf16)
        out_s[at, :] = (gate_ref[0] * expert_out).astype(bf16)

    @pl.when(e == LOCAL_E)
    def _():
        send = sender(send_sem, recv_sem)
        other = 1 - core
        right, left, far = ring(me)
        slot = lax.broadcasted_iota(jnp.int32, (GROUP, SLOTS), 1)

        def picks(group):
            at = pl.ds(pl.multiple_of(group * GROUP, GROUP), GROUP)
            ranks = rank_ref[at, :]
            return jnp.concatenate(
                [(ranks[:, k : k + 1] == slot).astype(bf16) for k in range(LOCAL_E)], axis=1
            )

        theirs, ours = picks(other), picks(core)
        order = (far, right, left, me)
        other_back[...] = (
            dot(theirs, back_s[...], ((1,), (0,))).astype(bf16).reshape(other_back.shape)
        )
        swaps = [
            send(other_back.at[block], from_core.at[block], 12 + i, "core", other)
            for i, block in enumerate(order)
        ]
        part[...] = dot(ours, back_s[...], ((1,), (0,))).astype(bf16).reshape(part.shape)
        reduce = Reduce(send, 0, "seq", lambda i: part.at[i], bufs, half_rows)
        for i, block in enumerate(order):
            swaps[i].wait_recv()
            added(part.at[block], part.at[block], from_core.at[block])
            if i == 0:
                reduce.start_far()
            if i == 2:
                reduce.start_near()
        other_out[...] = (
            dot(theirs, out_s[...], ((1,), (0,))).astype(bf16).reshape(other_out.shape)
        )
        out_swap = send(other_out, out_core, 16, "core", other)
        reduce.relay()
        out_sum_ref[...] = (
            dot(ours, out_s[...], ((1,), (0,))).astype(bf16).reshape(out_sum_ref.shape)
        )
        total = reduce.total()
        gates, gate_grad = my_gate_ref[...], total[:, D:]
        mean_term = jnp.sum(gates * gate_grad, axis=1, keepdims=True)
        logit_grad = (gates * (gate_grad - mean_term)).astype(bf16)
        logit_ref[...] = logit_grad
        normed_grad = total[:, :D] + dot(logit_grad, router_ref[...], ((1,), (1,)))
        back, gain_grad = norm_back(middle_ref[...], gain_ref[...], normed_grad)
        gain_grad_ref[...] = gain_grad
        middle_grad = cot_ref[...].astype(f32) + back
        grad_ref[...] = middle_grad
        mine[...] = middle_grad.astype(bf16)
        gather = Gather(send, 6, "seq", mine, lambda i: branch_ref.at[i], half_rows)
        local = pltpu.make_async_copy(mine, branch_ref.at[me], copy_sem)
        local.start()
        out_swap.wait_recv()
        added(out_sum_ref, out_sum_ref, out_core)
        gather.relay()
        gather.finish()
        gather.drain()
        reduce.drain()
        for copy in swaps + [out_swap]:
            copy.wait_send()
        local.wait()


BACK_WIDTH = D + 128


def turn(rank, up_grad, hidden, row_gates, cot_rows, weights, middle, cot, gates, router, gain):
    last = LOCAL_E - 1
    one = lambda e: (jnp.minimum(e, last), 0, 0)
    wide = lambda e: (0, jnp.minimum(e, last), 0, 0)
    whole = lambda e: (0, 0)
    blocks = lambda e: (0, 0, 0)
    row_block = pl.BlockSpec((TOK_DEV, D), whole)
    lane_block = pl.BlockSpec((TOK_DEV, 128), whole)
    gain_block = pl.BlockSpec((1, D), whole)
    group = pltpu.VMEM((N_SEQ, TOK_DEV, BACK_WIDTH), bf16)
    group_out = pltpu.VMEM((N_SEQ, TOK_DEV, D), bf16)
    return pl.pallas_call(
        turn_kernel,
        grid=(LOCAL_E + 1,),
        in_specs=[
            pl.BlockSpec((PAIR_TOK, LOCAL_E), whole),
            pl.BlockSpec((1, SLOTS, 2 * FF), one),
            pl.BlockSpec((1, SLOTS, FF), one),
            pl.BlockSpec((1, SLOTS, 1), one),
            pl.BlockSpec((1, SLOTS, D), one),
            pl.BlockSpec((16, 1, 144, 1024), wide),
            row_block,
            row_block,
            lane_block,
            pl.BlockSpec((D, 128), whole),
            gain_block,
        ],
        out_specs=[
            row_block,
            ANY,
            lane_block,
            gain_block,
            pl.BlockSpec((N_SEQ, TOK_DEV, D), blocks),
        ],
        out_shape=[
            jax.ShapeDtypeStruct((TOK_DEV, D), f32),
            jax.ShapeDtypeStruct((N_SEQ, TOK_DEV, D), bf16),
            jax.ShapeDtypeStruct((TOK_DEV, 128), bf16),
            jax.ShapeDtypeStruct((1, D), f32),
            jax.ShapeDtypeStruct((N_SEQ, TOK_DEV, D), bf16),
        ],
        scratch_shapes=[
            pltpu.VMEM((LOCAL_E * SLOTS, BACK_WIDTH), bf16),
            pltpu.VMEM((LOCAL_E * SLOTS, D), bf16),
            group,
            group,
            group,
            group_out,
            group_out,
            pltpu.VMEM((TOK_DEV, D), bf16),
        ]
        + reduce_scratch((TOK_DEV, BACK_WIDTH), (HALF, BACK_WIDTH))
        + sems(17)
        + [pltpu.SemaphoreType.DMA],
        compiler_params=remote_params(4),
        cost_estimate=pl.CostEstimate(
            flops=6 * LOCAL_E * SLOTS * D * FF + 4 * LOCAL_E * SLOTS * PAIR_TOK * D,
            bytes_accessed=40 << 20,
            transcendentals=0,
        ),
    )(rank, up_grad, hidden, row_gates, cot_rows, weights, middle, cot, gates, router, gain)


PAD_ROWS = 16
WIDE = 768
def closing_kernel(
    qkv_ref, lse_ref, cos_ref, sin_ref, seq_col_ref, seq_row_ref, exit_ref, entry_ref,
    in_ref, grad_ref, gain_ref, normed_ref, attended_ref, branch_ref,
    router_grad_ref, gain_two_ref, out_sum_ref, middle_ref,
    input_ref, block_ref, entry_out, exit_out,
    turned, mixed_grad, part, full, from_core, chip, line, final, give, got_z, *rest
):
    bufs, (send_sem, recv_sem) = [rest[6 * i : 6 * i + 6] for i in range(8)], rest[48:]
    z, x, y, c = (lax.axis_index(a) for a in ("seq", "x", "y", "core"))
    right, left, far = ring(z)
    greet(near("seq") + [("seq", far)] + near("x") + near("y") + [sibling()])
    send = sender(send_sem, recv_sem)
    pick = row_pick((512, QOWN), 0)

    def spread(grad):
        wide = dot(pick, grad, ((1,), (0,))).astype(bf16)
        return wide.reshape(16, 2, PAD_ROWS, grad.shape[1])

    def swap(side):
        return send(full.at[side, :, 1 - c], from_core.at[side], 48 + side, "core", 1 - c)

    def chip_sum(side, copy):
        copy.wait_recv()
        for plane in range(16):
            first, second = (plane % 4, plane // 4) if side == 2 else (plane // 4, plane % 4)
            added(chip.at[side, first, second], full.at[side, plane, c], from_core.at[side, plane])

    def first_sum(side, axis):
        reduce = Reduce(send, 6 * side, axis, lambda i: chip.at[side, i], bufs[side], half_rows)
        reduce.start_far()
        reduce.start_near()
        return reduce

    def second_sum(side, axis, reduce):
        line[side] = reduce.total().astype(bf16)
        reduce = Reduce(
            send, 18 + 6 * side, axis, lambda i: line.at[side, i], bufs[3 + side], half_lanes
        )
        reduce.start_far()
        reduce.start_near()
        return reduce

    for block in range(3):
        cols = slice(512 * block, 512 * (block + 1))
        grad = dot(attended_ref[...], branch_ref[:, cols], ((0,), (0,))).astype(bf16)
        full[0, :, :, :, cols] = spread(grad)
    swaps = [swap(0)]
    outs = Reduce(send, 36, "seq", lambda i: out_sum_ref.at[i], bufs[6], half_rows)
    outs.start_far()
    outs.start_near()

    def turn_back(kv):
        pair = Q_OWN + 2 * HD * kv
        for head in range(PER_KV * kv, PER_KV * (kv + 1)):
            grad = dot(branch_ref[...], exit_ref[head_of(head), :], ((1,), (1,))).astype(bf16)
            attended = attended_ref[:, head_of(head)].astype(f32)
            delta = jnp.sum(grad.astype(f32) * attended, axis=1, keepdims=True)
            for block in range(GROUP // BLOCK):
                bias = block_bias(seq_col_ref, seq_row_ref, block)
                keys = BLOCK * (block + 1)
                rows = slice(BLOCK * block, keys)
                key = qkv_ref[:keys, pair : pair + HD]
                value = qkv_ref[:keys, pair + HD : pair + 2 * HD]
                query, grad_rows = qkv_ref[rows, head_of(head)], grad[rows]
                scores = dot(query, key, ((1,), (1,))) * HD**-0.5 + bias
                probs = jnp.exp(scores - lse_ref[rows, head : head + 1])
                prob_grad = dot(grad_rows, value, ((1,), (1,)))
                score_grad = probs * (prob_grad - delta[rows]) * HD**-0.5
                score_grad = score_grad.astype(bf16)
                turned[rows, head_of(head)] = dot(score_grad, key, ((1,), (0,)))
                key_grad = dot(score_grad, query, ((0,), (0,)))
                value_grad = dot(probs.astype(bf16), grad_rows, ((0,), (0,)))
                if head == PER_KV * kv and block == GROUP // BLOCK - 1:
                    turned[:, pair : pair + HD] = key_grad
                    turned[:, pair + HD : pair + 2 * HD] = value_grad
                    turned[:BLOCK, pair : pair + HD] += held[0]
                    turned[:BLOCK, pair + HD : pair + 2 * HD] += held[1]
                elif head == PER_KV * kv:
                    held = (key_grad, value_grad)
                else:
                    turned[:keys, pair : pair + HD] += key_grad
                    turned[:keys, pair + HD : pair + 2 * HD] += value_grad

    turn_back(0)
    chip_sum(0, swaps[0])
    first_0 = first_sum(0, "x")
    outs.relay()
    turn_back(1)
    first_0.relay()
    grads = turned[...]
    grads = grads * cos_ref[...] + swap_halves(grads, 1.0, -1.0) * sin_ref[...]
    mixed_grad[...] = grads.astype(bf16)
    part[...] = (
        dot(mixed_grad[...], entry_ref[...], ((1,), (1,))).astype(bf16).reshape(part.shape)
    )
    rows = Reduce(send, 42, "seq", lambda i: part.at[i], bufs[7], half_rows)
    rows.start_far()
    rows.start_near()

    def entry_rows(block):
        rows_of = slice(QOWN * block, QOWN * (block + 1))
        grad = dot(normed_ref[:, rows_of], mixed_grad[...], ((0,), (0,))).astype(bf16)
        return spread(grad)

    full[1, :, :, :, :640] = entry_rows(0)
    full[1, :, :, :, 640:1280] = entry_rows(1)
    third = entry_rows(2)
    full[1, :, :, :, 1280:] = third[..., :256]
    swaps.append(swap(1))
    rows.relay()
    second_0 = second_sum(0, "y", first_0)
    full[2, :, :, :, :384] = third[..., 256:]
    full[2, :, :, :, 384:1024] = entry_rows(3)
    chip_sum(1, swaps[1])
    first_1 = first_sum(1, "x")
    back, gain_one = norm_back(in_ref[...].astype(f32), gain_ref[...], rows.total())
    input_ref[...] = (grad_ref[...] + back).astype(bf16)
    row_of = lax.broadcasted_iota(jnp.int32, (128, D), 0)
    gains = jnp.where(row_of == EXPERTS, gain_one, 0.0)
    gains = jnp.where(row_of == EXPERTS + 1, gain_two_ref[...], gains)
    shared = router_grad_ref[...] + gains.T
    for block in range(4):
        shared_rows = shared[QOWN * block : QOWN * (block + 1), :].astype(bf16)
        full[2, :, :, :, 1024 + 128 * block : 1152 + 128 * block] = spread(shared_rows)
    swaps.append(swap(2))
    second_0.relay()
    block_ref[...] = (middle_ref[...] + outs.total()).astype(bf16)
    chip_sum(2, swaps[2])
    first_2 = first_sum(2, "y")
    first_1.relay()
    first_2.relay()
    exit_out[...] = second_0.total()
    second_1 = second_sum(1, "y", first_1)
    second_2 = second_sum(2, "x", first_2)
    second_1.relay()
    second_2.relay()
    final[0] = second_1.total()
    final[1] = second_2.total()
    give[0, :, :MIX_OWN] = final[0, :, :640]
    give[1, :, :MIX_OWN] = final[0, :, 640:1280]
    give[2, :, :256] = final[0, :, 1280:]
    give[2, :, 256:MIX_OWN] = final[1, :, :384]
    give[3, :, :MIX_OWN] = final[1, :, 384:1024]
    for block in range(4):
        give[block, :, MIX_OWN:] = final[1, :, 1024 + 128 * block : 1152 + 128 * block]
    home = [
        send(give.at[peer], got_z.at[k], 51 + k, "seq", peer)
        for k, peer in enumerate((right, far, left))
    ]
    entry_out[z] = give[z]
    for k, source in enumerate((left, far, right)):
        home[k].wait_recv()
        entry_out[source] = got_z[k]
    for copy in swaps + home:
        copy.wait_send()
    for reduce in (rows, outs, first_0, first_1, first_2, second_0, second_1, second_2):
        reduce.drain()


def closing(*operands):
    row_bufs = reduce_scratch((TOK_DEV, D), (HALF, D))
    chip_bufs = reduce_scratch((4, PAD_ROWS, D), (2, PAD_ROWS, D))
    line_bufs = reduce_scratch((PAD_ROWS, D), (PAD_ROWS, D // 2))
    tile = (PAD_ROWS, D)
    return pl.pallas_call(
        closing_kernel,
        out_shape=[
            jax.ShapeDtypeStruct((TOK_DEV, D), bf16),
            jax.ShapeDtypeStruct((TOK_DEV, D), bf16),
            jax.ShapeDtypeStruct((4, PAD_ROWS, WIDE), f32),
            jax.ShapeDtypeStruct((PAD_ROWS, D), f32),
        ],
        in_specs=[VMEM] * len(operands),
        out_specs=[VMEM] * 4,
        scratch_shapes=[
            pltpu.VMEM((GROUP, MIX_OWN), f32),
            pltpu.VMEM((GROUP, MIX_OWN), bf16),
            pltpu.VMEM((N_SEQ, TOK_DEV, D), bf16),
            pltpu.VMEM((3, 16, 2) + tile, bf16),
            pltpu.VMEM((3, 16) + tile, bf16),
            pltpu.VMEM((3, 4, 4) + tile, bf16),
            pltpu.VMEM((3, 4) + tile, bf16),
            pltpu.VMEM((2,) + tile, f32),
            pltpu.VMEM((4, PAD_ROWS, WIDE), f32),
            pltpu.VMEM((3, PAD_ROWS, WIDE), f32),
        ]
        + chip_bufs * 3
        + line_bufs * 3
        + row_bufs * 2
        + sems(54),
        compiler_params=remote_params(5),
    )(*operands)


def owner_kernel(sum_ref, expand_ref, shrink_ref, send_sem, recv_sem, copy_sem):
    core = lax.axis_index("core")
    greet([sibling()])
    send = sender(send_sem, recv_sem)
    experts = pl.ds(core * LOCAL_E, LOCAL_E)

    def pieces(owner):
        main = pl.ds(pl.multiple_of(owner * 48, 16), 48)
        left = pl.ds(pl.multiple_of(96 + owner * 16, 16), 16)
        ends = pl.ds(pl.multiple_of(owner * 512, 512), 512)
        return [
            (sum_ref.at[:, main], expand_ref.at[experts]),
            (sum_ref.at[:, left], shrink_ref.at[experts, :, pl.ds(0, 1024)]),
            (sum_ref.at[:, pl.ds(128, 16), ends], shrink_ref.at[experts, :, pl.ds(1024, 512)]),
        ]

    copies = [
        send(source, target, k, "core", 1 - core)
        for k, (source, target) in enumerate(pieces(1 - core))
    ]
    for k, (source, target) in enumerate(pieces(core)):
        copies.append(pltpu.make_async_copy(source, target, copy_sem.at[k]))
        copies[-1].start()
    for copy in copies:
        copy.wait()


def to_owners(summed):
    return pl.pallas_call(
        owner_kernel,
        out_shape=[
            jax.ShapeDtypeStruct((2 * LOCAL_E, 48, 1024), bf16),
            jax.ShapeDtypeStruct((2 * LOCAL_E, 16, D), bf16),
        ],
        in_specs=[VMEM],
        out_specs=[VMEM] * 2,
        scratch_shapes=sems(3) + [pltpu.SemaphoreType.DMA((3,))],
        compiler_params=remote_params(6),
    )(summed)


def dispatch_kernel(rank_ref, gate_ref, tokens_ref, cots_ref, rows_ref, cot_rows_ref, row_gate_ref):
    slot = lax.broadcasted_iota(jnp.int32, (SLOTS, PAIR_TOK), 0)
    match = rank_ref[0] == slot
    row_gate_ref[0] = jnp.sum(jnp.where(match, gate_ref[0], 0.0), axis=1, keepdims=True)
    pick = match.astype(bf16)
    for j in range(3):
        cols = slice(512 * j, 512 * (j + 1))
        rows_ref[0, :, cols] = dot(pick, tokens_ref[:, cols], ((1,), (0,))).astype(bf16)
        cot_rows_ref[0, :, cols] = dot(pick, cots_ref[:, cols], ((1,), (0,))).astype(bf16)

def dispatch(rank, gates, tokens, cots):
    one = lambda e: (e, 0, 0)
    whole = lambda e: (0, 0)
    return pl.pallas_call(
        dispatch_kernel,
        grid=(LOCAL_E,),
        in_specs=[
            pl.BlockSpec((1, 1, PAIR_TOK), one),
            pl.BlockSpec((1, 1, PAIR_TOK), one),
            pl.BlockSpec((PAIR_TOK, D), whole),
            pl.BlockSpec((PAIR_TOK, D), whole),
        ],
        out_specs=[
            pl.BlockSpec((1, SLOTS, D), one),
            pl.BlockSpec((1, SLOTS, D), one),
            pl.BlockSpec((1, SLOTS, 1), one),
        ],
        out_shape=[
            jax.ShapeDtypeStruct((LOCAL_E, SLOTS, D), bf16),
            jax.ShapeDtypeStruct((LOCAL_E, SLOTS, D), bf16),
            jax.ShapeDtypeStruct((LOCAL_E, SLOTS, 1), f32),
        ],
        compiler_params=pltpu.CompilerParams(vmem_limit_bytes=BIG),
        cost_estimate=pl.CostEstimate(
            flops=4 * LOCAL_E * SLOTS * PAIR_TOK * D, bytes_accessed=16 << 20, transcendentals=0
        ),
    )(rank[:, None], gates[:, None], tokens, cots)

def weights_of(w_ref):
    expand = w_ref[:, 0, :96, :].reshape(D, 2 * FF)
    left = w_ref[:, 0, 96:128, :].reshape(FF, 1024)
    right = jnp.concatenate([w_ref[:, 0, 128:144, :512], w_ref[:, 0, 128:144, 512:]], axis=1)
    return expand, left, right.reshape(FF, 512)

def grads_kernel(rows_ref, cot_ref, gate_ref, w_ref, hidden_ref, up_ref, out_ref):
    expand, left, right = weights_of(w_ref)
    grad_rows = (gate_ref[0] * cot_ref[0].astype(f32)).astype(bf16)
    rows = rows_ref[0]
    gate_pre = dot(rows, expand[:, :FF], ((1,), (0,)))
    up_part = dot(rows, expand[:, FF:], ((1,), (0,)))
    sig = jax.nn.sigmoid(gate_pre)
    hidden = (gate_pre * sig * up_part).astype(bf16)
    hidden_ref[0] = hidden
    hidden_grad = dot(grad_rows[:, :1024], left, ((1,), (1,))) + dot(
        grad_rows[:, 1024:], right, ((1,), (1,))
    )
    up_ref[0, :, :FF] = (hidden_grad * up_part * sig * (1.0 + gate_pre * (1.0 - sig))).astype(bf16)
    up_ref[0, :, FF:] = (hidden_grad * gate_pre * sig).astype(bf16)
    grad_left = dot(hidden, grad_rows[:, :1024], ((0,), (0,))).astype(bf16)
    out_ref[:, 0, 96:128, :] = grad_left.reshape(16, 32, 1024)
    grad_right = dot(hidden, grad_rows[:, 1024:], ((0,), (0,))).astype(bf16).reshape(16, 32, 512)
    out_ref[:, 0, 128:144, :512] = grad_right[:, :16]
    out_ref[:, 0, 128:144, 512:] = grad_right[:, 16:]
    up_grad = up_ref[0]
    for j in range(4):
        part = dot(rows[:, 384 * j : 384 * (j + 1)], up_grad, ((0,), (0,))).astype(bf16)
        out_ref[4 * j : 4 * (j + 1), 0, :96, :] = part.reshape(4, 96, 1024)

def expert_grads(rows, cot_rows, row_gates, weights):
    one = lambda e: (e, 0, 0)
    wide = lambda e: (0, e, 0, 0)
    return pl.pallas_call(
        grads_kernel,
        grid=(LOCAL_E,),
        in_specs=[
            pl.BlockSpec((1, SLOTS, D), one),
            pl.BlockSpec((1, SLOTS, D), one),
            pl.BlockSpec((1, SLOTS, 1), one),
            pl.BlockSpec((16, 1, 144, 1024), wide),
        ],
        out_specs=[
            pl.BlockSpec((1, SLOTS, FF), one),
            pl.BlockSpec((1, SLOTS, 2 * FF), one),
            pl.BlockSpec((16, 1, 144, 1024), wide),
        ],
        out_shape=[
            jax.ShapeDtypeStruct((LOCAL_E, SLOTS, FF), bf16),
            jax.ShapeDtypeStruct((LOCAL_E, SLOTS, 2 * FF), bf16),
            jax.ShapeDtypeStruct((16, LOCAL_E, 144, 1024), bf16),
        ],
        compiler_params=pltpu.CompilerParams(vmem_limit_bytes=BIG),
        cost_estimate=pl.CostEstimate(
            flops=12 * LOCAL_E * SLOTS * D * FF, bytes_accessed=60 << 20, transcendentals=0
        ),
    )(rows, cot_rows, row_gates, weights)


def core_swap(value):
    return lax.ppermute(value, "core", [(0, 1), (1, 0)])


def core_order(core, mine, other, axis):
    return jnp.concatenate(
        [jnp.where(core == 0, mine, other), jnp.where(core == 0, other, mine)], axis=axis
    )


def norm_apply(vector, gain):
    scale = lax.rsqrt(jnp.mean(vector * vector, axis=-1, keepdims=True) + norm_eps)
    return vector * scale * gain


def adamw_step(weight, gradient, mean_old, square_old, rate, decay):
    drift = beta_first * mean_old + (1.0 - beta_first) * gradient
    spread = beta_second * square_old + (1.0 - beta_second) * gradient * gradient
    mean_hat = drift / (1.0 - beta_first**STEP)
    square_hat = spread / (1.0 - beta_second**STEP)
    master = weight - rate * (mean_hat / (jnp.sqrt(square_hat) + adam_eps) + decay * weight)
    return (drift, spread, master)


def rotate(vector, cosine, sine):
    first, second = vector[..., : HD // 2], vector[..., HD // 2 :]
    return jnp.concatenate(
        [first * cosine - second * sine, second * cosine + first * sine], axis=-1
    )


def on_device(
    activations,
    cotangent,
    seq_lengths,
    deal_order,
    routes,
    entry_weight,
    entry_mean,
    entry_square,
    exit_weight,
    exit_mean,
    exit_square,
    router_weight,
    router_mean,
    router_square,
    expand_weight,
    expand_mean,
    expand_square,
    shrink_weight,
    shrink_mean,
    shrink_square,
    norm_gains,
    gains_mean,
    gains_square,
):
    seq = lax.axis_index("seq")
    core = lax.axis_index("core")
    first = (seq * 2 + core) * LOCAL_E

    packed = pack_experts(expand_weight, shrink_weight)
    packed, rows_in, cots_in = lax.optimization_barrier((packed, activations[0], cotangent[0]))
    weights = lax.all_gather(packed, PLANE, axis=0, tiled=False)

    entry_b = entry_weight.astype(bf16)
    shared_b = jnp.concatenate([router_weight, norm_gains.T], axis=1).astype(bf16)
    shared_b = jnp.pad(shared_b, ((0, 0), (0, 128 - EXPERTS - 2)))
    entry_cols = jnp.concatenate(
        [
            entry_b[:, : QH * HD].reshape(ROWS, N_SEQ, Q_OWN).transpose(1, 0, 2),
            entry_b[:, QH * HD :].reshape(ROWS, N_SEQ, KV_OWN).transpose(1, 0, 2),
            jnp.broadcast_to(shared_b[None], (N_SEQ, ROWS, 128)),
        ],
        axis=2,
    )
    exit_cols = exit_weight.astype(bf16).reshape(ROWS, 2, WIDE).transpose(1, 0, 2)
    pad = ((0, 0), (0, PAD_ROWS - ROWS), (0, 0))
    expert_ids = jnp.arange(128, dtype=jnp.int32)
    hit_slots = jnp.any(routes[0][:, :, None] == expert_ids[None, None, :], axis=1).astype(bf16)
    in_all, cots, hit_slots, entry_own, shared, exit_own = start(
        rows_in, cots_in, hit_slots, jnp.pad(entry_cols, pad), jnp.pad(exit_cols, pad)
    )
    gains_full = shared[:, EXPERTS : EXPERTS + 2].astype(f32).T

    order_row = deal_order[0]
    token = jnp.arange(GROUP, dtype=jnp.int32)
    back_hot = (order_row[None, :] == token[:, None]).astype(bf16)
    hit = dot(back_hot, hit_slots.reshape(GROUP, 128), ((1,), (0,))).astype(bf16)
    hits = core_order(core, hit, core_swap(hit), 0)[:, :EXPERTS]
    own_hits = lax.dynamic_slice_in_dim(hits, first, LOCAL_E, 1)
    rank = jnp.cumsum(own_hits.astype(jnp.int32), axis=0) - 1
    rank = jnp.where(own_hits > 0, rank, -1)
    seq_ends = jnp.cumsum(seq_lengths[0])
    starts = seq_ends - seq_lengths[0]
    seq_ids = jnp.sum((token[:, None] >= seq_ends[None, :]).astype(jnp.int32), axis=1)
    seq_match = seq_ids[:, None] == jnp.arange(seq_ends.shape[0], dtype=jnp.int32)[None, :]
    positions = token - jnp.sum(jnp.where(seq_match, starts[None, :], 0), axis=1)
    frequency = rope_base ** (-jnp.arange(HD // 2, dtype=f32) * 2.0 / HD)
    phase = positions.astype(f32)[:, None] * frequency[None, :]
    ones = jnp.ones((GROUP, HD), f32)
    cosine, sine = jnp.tile(jnp.cos(phase), (1, 2)), jnp.tile(jnp.sin(phase), (1, 2))
    cosine = jnp.concatenate(
        [jnp.tile(cosine, (1, HEADS_OWN))] + [cosine, ones] * KV_HEADS_OWN, axis=1
    )
    sine = jnp.concatenate(
        [jnp.tile(sine, (1, HEADS_OWN))] + [sine, 0.0 * ones] * KV_HEADS_OWN, axis=1
    )
    angles = (cosine, sine, seq_ids[:, None], seq_ids[None, :])

    normed, qkv, attended, lse, middle, tokens = middle_tokens(
        in_all,
        gains_full[0:1],
        entry_own,
        *angles,
        exit_own,
        activations[0],
        gains_full[1:2],
    )
    normed_two = lax.dynamic_slice(tokens, (core, seq, 0, 0), (1, 1, TOK_DEV, D))[0, 0]
    tokens = tokens.reshape(PAIR_TOK, D)

    logits = dot(tokens, shared[:, :EXPERTS], ((1,), (0,)))
    masked = jnp.where(hits > 0, logits, -jnp.inf)
    gate_expo = jnp.exp(masked - jnp.max(masked, axis=1, keepdims=True))
    gates = gate_expo / jnp.sum(gate_expo, axis=1, keepdims=True)
    own_gates = lax.dynamic_slice_in_dim(gates, first, LOCAL_E, 1)
    rows, cot_rows, row_gates = dispatch(rank.T, own_gates.T, tokens, cots.reshape(PAIR_TOK, D))
    hidden, up_grad, expert_grad = expert_grads(rows, cot_rows, row_gates, weights)
    expert_sum = lax.psum_scatter(expert_grad, PLANE, scatter_dimension=0, tiled=False)
    my_gates = lax.dynamic_slice_in_dim(gates, core * GROUP + seq * TOK_DEV, TOK_DEV, 0)
    my_gates = jnp.pad(my_gates, ((0, 0), (0, 128 - EXPERTS)))
    middle_grad, branch_grad, logit_grad, gain_two_grad, out_sum = turn(
        rank,
        up_grad,
        hidden,
        row_gates,
        cot_rows,
        weights,
        middle,
        cotangent[0],
        my_gates,
        shared,
        gains_full[1:2],
    )
    branch_grad = branch_grad.reshape(GROUP, D)
    router_grad = dot(normed_two, logit_grad, ((0,), (0,)))

    input_grad, block_output, entry_got, exit_got = closing(
        qkv,
        lse,
        *angles,
        exit_own,
        entry_own,
        activations[0],
        middle_grad,
        gains_full[0:1],
        normed,
        attended,
        branch_grad,
        router_grad,
        gain_two_grad,
        out_sum,
        middle,
    )

    entry_got = entry_got[:, :ROWS]
    entry_sum = jnp.concatenate(
        [
            entry_got[:, :, :Q_OWN].transpose(1, 0, 2).reshape(ROWS, QH * HD),
            entry_got[:, :, Q_OWN:MIX_OWN].transpose(1, 0, 2).reshape(ROWS, 2 * KVH * HD),
        ],
        axis=1,
    )
    shared_sum = jnp.sum(entry_got[:, :, MIX_OWN:], axis=0)
    router_sum = shared_sum[:, :EXPERTS]
    gains_sum = shared_sum[:, EXPERTS : EXPERTS + 2].T
    exit_sum = exit_got[:ROWS]

    expand_sum, shrink_sum = to_owners(expert_sum)
    expand_sum, shrink_sum = expand_sum.astype(f32), shrink_sum.astype(f32)
    entry_new = adamw_step(entry_weight, entry_sum, entry_mean, entry_square, 0.02, weight_decay)
    exit_new = adamw_step(exit_weight, exit_sum, exit_mean, exit_square, 0.15, weight_decay)
    router_new = adamw_step(
        router_weight, router_sum, router_mean, router_square, 0.01, weight_decay
    )
    expand_new = adamw_step(
        expand_weight, expand_sum, expand_mean, expand_square, 0.02, weight_decay
    )
    shrink_new = adamw_step(
        shrink_weight, shrink_sum, shrink_mean, shrink_square, 0.12, weight_decay
    )
    gains_new = adamw_step(norm_gains, gains_sum, gains_mean, gains_square, 0.5, 0.0)
    return (
        block_output[None],
        input_grad[None],
        *entry_new,
        *exit_new,
        *router_new,
        *expand_new,
        *shrink_new,
        *gains_new,
    )


def solution(mesh):
    fine = Mesh(mesh.devices.reshape(4, 4, 4, 2), ("seq", "x", "y", "core"))
    rows = P(FSDP, "seq", None)
    lists = P(FSDP, None)
    owned = P(("seq",) + FSDP, None)
    experts = P("seq", FSDP, None)
    gains = P(None, ("seq",) + FSDP)
    return jax.shard_map(
        on_device,
        mesh=fine,
        in_specs=(rows, rows, lists, lists, rows)
        + (owned,) * 9
        + (experts,) * 6
        + (gains,) * 3,
        out_specs=(rows, rows) + (owned,) * 9 + (experts,) * 6 + (gains,) * 3,
        check_vma=False,
    )
```

```python
import jax
import jax.numpy as jnp
from jax import lax
from jax.experimental import pallas as pl
from jax.experimental.pallas import tpu as pltpu
from jax.sharding import Mesh, PartitionSpec as P

D = 1536
QH = 24
KVH = 8
HD = 64
FF = 512
EXPERTS = 40
TOP = 8
STEP = 10
CAP = 29

N_SEQ = 4
TOK_DEV = 128
GROUP = 512
PAIR_TOK = 2 * GROUP
LOCAL_E = EXPERTS // (2 * N_SEQ)
SLOTS = 256
Q_OWN = QH * HD // N_SEQ
KV_OWN = 2 * KVH * HD // N_SEQ
MIX_OWN = Q_OWN + KV_OWN
HEADS_OWN = QH // N_SEQ
KV_HEADS_OWN = KVH // N_SEQ
PER_KV = QH // KVH
ROWS = 12

norm_eps = 1e-06
rope_base = 10000.0
beta_first = 0.9
beta_second = 0.95
adam_eps = 1e-08
weight_decay = 0.1

FSDP = ("x", "y", "core")
PLANE = ("x", "y")
f32 = jnp.float32
bf16 = jnp.bfloat16


BIG = 60 * 1024 * 1024
HALF = TOK_DEV // 2
QOWN = Q_OWN
MESH = pl.DeviceIdType.MESH
ANY = pl.BlockSpec(memory_space=pl.ANY)
VMEM = pl.BlockSpec(memory_space=pltpu.VMEM)


def dot(a, b, dims):
    return lax.dot_general(a, b, (dims, ((), ())), preferred_element_type=f32)


def greet(peers):
    barrier = pltpu.get_barrier_semaphore()
    for axis, peer in peers:
        pl.semaphore_signal(barrier, inc=1, device_id={axis: peer}, device_id_type=MESH)
    pl.semaphore_wait(barrier, len(peers))


def planner(send_sem, recv_sem):
    def plan(src, dst, index, axis, peer):
        return pltpu.make_async_remote_copy(
            src_ref=src,
            dst_ref=dst,
            send_sem=send_sem.at[index],
            recv_sem=recv_sem.at[index],
            device_id={axis: peer},
            device_id_type=MESH,
        )

    return plan


def sender(send_sem, recv_sem):
    plan = planner(send_sem, recv_sem)

    def send(*args):
        copy = plan(*args)
        copy.start()
        return copy

    return send


def sems(count):
    return [pltpu.SemaphoreType.DMA((count,)), pltpu.SemaphoreType.DMA((count,))]


def ring(me):
    right, left = lax.rem(me + 1, 4), lax.rem(me + 3, 4)
    return right, left, lax.rem(me + 2, 4)


def near(axis):
    right, left, _ = ring(lax.axis_index(axis))
    return [(axis, right), (axis, left)]


def sibling():
    return ("core", 1 - lax.axis_index("core"))


def half_rows(ref, half):
    size = ref.shape[0] // 2
    return ref.at[pl.ds(half * size, size)]


def half_lanes(ref, half):
    size = ref.shape[-1] // 2
    return ref.at[(slice(None),) * (len(ref.shape) - 1) + (pl.ds(half * size, size),)]


class Gather:
    def __init__(self, plan, base, axis, mine, slot, cut):
        me = lax.axis_index(axis)
        right, left, self.far = ring(me)
        self.right, self.left = right, left
        here, from_left, from_right = slot(me), cut(slot(left), 0), cut(slot(right), 1)
        self.first = [
            plan(cut(mine, 0), cut(here, 0), base, axis, right),
            plan(cut(mine, 1), cut(here, 1), base + 1, axis, left),
            plan(cut(mine, 1), cut(here, 1), base + 2, axis, right),
            plan(cut(mine, 0), cut(here, 0), base + 3, axis, left),
        ]
        self.later = [
            plan(from_left, from_left, base + 4, axis, right),
            plan(from_right, from_right, base + 5, axis, left),
        ]

    def start(self):
        for copy in self.first:
            copy.start()
        return self

    def relay(self):
        for got, on in zip(self.first, self.later):
            got.wait_recv()
            on.start()

    def wait_left(self):
        self.first[2].wait_recv()

    def wait_right(self):
        self.first[3].wait_recv()

    def wait_far(self):
        for copy in self.later:
            copy.wait_recv()

    def finish(self):
        self.wait_left()
        self.wait_right()
        self.wait_far()

    def drain(self):
        for copy in self.first + self.later:
            copy.wait_send()


def hand_over(send, base, mine, out, gather):
    me, core = lax.axis_index("seq"), lax.axis_index("core")
    other = 1 - core
    copies = [send(mine, out.at[core, me], base, "core", other)]
    gather.relay()
    gather.wait_left()
    block = out.at[core, gather.left]
    copies.append(send(block, block, base + 1, "core", other))
    gather.wait_right()
    block = out.at[core, gather.right]
    copies.append(send(block, block, base + 2, "core", other))
    gather.wait_far()
    block = out.at[core, gather.far]
    copies.append(send(block, block, base + 3, "core", other))
    return copies


def reduce_scratch(block, half):
    return [pltpu.VMEM(half, bf16)] * 4 + [pltpu.VMEM(block, bf16)] * 2


def added(target, first, second):
    target[...] = (first[...].astype(f32) + second[...].astype(f32)).astype(bf16)


class Reduce:
    def __init__(self, plan, base, axis, block, bufs, cut):
        me = lax.axis_index(axis)
        right, left, far = ring(me)
        from_left, from_right, to_right, to_left, got_left, got_right = bufs
        far, on_right, on_left = block(far), block(right), block(left)
        self.mine, self.got = block(me), (got_left, got_right)
        self.hops = (
            (to_right, cut(on_right, 0), from_left),
            (to_left, cut(on_left, 1), from_right),
        )
        self.far = [
            plan(cut(far, 0), from_left, base, axis, right),
            plan(cut(far, 1), from_right, base + 1, axis, left),
        ]
        self.near = [
            plan(cut(on_right, 1), cut(got_left, 1), base + 2, axis, right),
            plan(cut(on_left, 0), cut(got_right, 0), base + 3, axis, left),
        ]
        self.later = [
            plan(to_right, cut(got_left, 0), base + 4, axis, right),
            plan(to_left, cut(got_right, 1), base + 5, axis, left),
        ]

    def start_far(self):
        for copy in self.far:
            copy.start()

    def start_near(self):
        for copy in self.near:
            copy.start()

    def start(self):
        self.start_far()
        self.start_near()
        return self

    def relay(self):
        for got, hop, on in zip(self.far, self.hops, self.later):
            got.wait_recv()
            added(*hop)
            on.start()

    def total(self):
        for copy in self.near + self.later:
            copy.wait_recv()
        total = self.mine[...].astype(f32)
        for part in self.got:
            total += part[...].astype(f32)
        return total

    def drain(self):
        for copy in self.far + self.near + self.later:
            copy.wait_send()


def remote_params(call_id):
    return pltpu.CompilerParams(
        collective_id=call_id, has_side_effects=True, vmem_limit_bytes=BIG
    )


def unit_scale(vector):
    return lax.rsqrt(jnp.mean(vector * vector, axis=-1, keepdims=True) + norm_eps)


def norm_back(vector, gain, grad):
    scale = unit_scale(vector)
    unit = vector * scale
    pulled = grad * gain
    back = scale * (pulled - unit * jnp.mean(pulled * unit, axis=-1, keepdims=True))
    return back, jnp.sum(unit * grad, axis=0, keepdims=True)


MAIN_E = LOCAL_E - 1


def pack_kernel(expand_ref, shrink_ref, main_ref, extra_ref, stage, stage_end, send_sem, recv_sem):
    core = lax.axis_index("core")
    greet([sibling()])
    send = sender(send_sem, recv_sem)
    other = 1 - core
    for e in range(LOCAL_E):
        theirs = other * LOCAL_E + e
        stage[e, :48] = expand_ref[theirs].astype(bf16)
        stage[e, 48:] = shrink_ref[theirs, :, :1024].astype(bf16)
        stage_end[e] = shrink_ref[theirs, :, 1024:].astype(bf16)
    rows = pl.ds(pl.multiple_of(core * 48, 16), 48)
    left = pl.ds(pl.multiple_of(96 + core * 16, 16), 16)
    ends = pl.ds(pl.multiple_of(core * 512, 512), 512)
    low, most = pl.ds(128, 16), pl.ds(0, MAIN_E)
    copies = [
        send(stage.at[most, pl.ds(0, 48)], main_ref.at[:, rows], 0, "core", other),
        send(stage.at[most, pl.ds(48, 16)], main_ref.at[:, left], 1, "core", other),
        send(stage_end.at[most], main_ref.at[:, low, ends], 2, "core", other),
        send(stage.at[MAIN_E, pl.ds(0, 48)], extra_ref.at[rows], 3, "core", other),
        send(stage.at[MAIN_E, pl.ds(48, 16)], extra_ref.at[left], 4, "core", other),
        send(stage_end.at[MAIN_E], extra_ref.at[low, ends], 5, "core", other),
    ]
    for e in range(LOCAL_E):
        mine = core * LOCAL_E + e
        out = main_ref.at[e] if e < MAIN_E else extra_ref
        out[rows, :] = expand_ref[mine].astype(bf16)
        out[left, :] = shrink_ref[mine, :, :1024].astype(bf16)
        out[low, ends] = shrink_ref[mine, :, 1024:].astype(bf16)
    for copy in copies:
        copy.wait()


def pack_experts(expand, shrink):
    return pl.pallas_call(
        pack_kernel,
        out_shape=[
            jax.ShapeDtypeStruct((MAIN_E, 144, 1024), bf16),
            jax.ShapeDtypeStruct((144, 1024), bf16),
        ],
        in_specs=[VMEM] * 2,
        out_specs=[VMEM] * 2,
        scratch_shapes=[
            pltpu.VMEM((LOCAL_E, 64, 1024), bf16),
            pltpu.VMEM((LOCAL_E, 16, 512), bf16),
        ]
        + sems(6),
        compiler_params=remote_params(1),
    )(expand, shrink)


def row_pick(shape, padded_axis):
    padded = lax.broadcasted_iota(jnp.int32, shape, padded_axis)
    plain = lax.broadcasted_iota(jnp.int32, shape, 1 - padded_axis)
    row = lax.rem(padded, 16)
    return ((plain == lax.div(padded, 16) * 12 + row) & (row < 12)).astype(bf16)


def start_kernel(
    in_ref, cot_ref, hit_ref, entry_ref, exit_ref,
    in_all, cot_all, hit_all, entry_out, shared_out, exit_out,
    hold, full, send_sem, recv_sem, copy_sem,
):
    z, x, y, c = (lax.axis_index(a) for a in ("seq", "x", "y", "core"))
    right, left, far = ring(z)
    greet(near("seq") + [("seq", far)] + near("x") + near("y") + [sibling()])
    send, plan = sender(send_sem, recv_sem), planner(send_sem, recv_sem)
    columns = [
        send(entry_ref.at[peer], hold.at[z], k, "seq", peer)
        for k, peer in enumerate((right, far, left))
    ]
    hits = Gather(plan, 3, "seq", hit_ref, lambda i: hit_all.at[i], half_rows).start()
    rows = Gather(plan, 9, "seq", in_ref, lambda i: in_all.at[i], half_rows).start()
    local = [
        pltpu.make_async_copy(entry_ref.at[z], hold.at[z], copy_sem.at[0]),
        pltpu.make_async_copy(exit_ref, hold.at[pl.ds(4, 2)], copy_sem.at[1]),
        pltpu.make_async_copy(hit_ref, hit_all.at[z], copy_sem.at[2]),
        pltpu.make_async_copy(in_ref, in_all.at[z], copy_sem.at[3]),
        pltpu.make_async_copy(cot_ref, cot_all.at[c, z], copy_sem.at[4]),
    ]
    for copy in local:
        copy.start()
    local[0].wait()
    local[1].wait()
    for copy in columns:
        copy.wait_recv()
    own = pltpu.make_async_copy(hold, full.at[:, x, y, c], copy_sem.at[5])
    own.start()
    low, high = pl.ds(0, 3), pl.ds(3, 3)
    low_x = Gather(plan, 15, "x", hold.at[low], lambda i: full.at[low, i, y, c], half_lanes)
    low_x.start()
    high_y = Gather(plan, 21, "y", hold.at[high], lambda i: full.at[high, x, i, c], half_lanes)
    high_y.start()
    hits.relay()
    low_x.relay()
    high_y.relay()
    rows.relay()
    cots = Gather(plan, 27, "seq", cot_ref, lambda i: cot_all.at[c, i], half_rows).start()
    own.wait()
    low_x.finish()

    def cut_low(ref, half):
        return ref.at[:, pl.ds(2 * half, 2)]

    low_y = Gather(
        plan, 33, "y", full.at[low, :, y, c], lambda i: full.at[low, :, i, c], cut_low
    ).start()
    high_y.finish()
    high_x = Gather(
        plan, 39, "x", full.at[high, x, :, c], lambda i: full.at[high, i, :, c], cut_low
    ).start()
    low_y.relay()
    high_x.relay()
    pairs = hand_over(send, 45, cot_ref, cot_all, cots)
    low_y.finish()
    half = full.at[low, :, :, c]
    last = [send(half, half, 49, "core", 1 - c)]
    high_x.finish()
    half = full.at[high, :, :, c]
    last.append(send(half, half, 50, "core", 1 - c))
    pick = row_pick((QOWN, 512), 1)
    for copy in last:
        copy.wait_recv()
    for block in range(4):
        got = dot(pick, full[block].reshape(512, WIDE), ((1,), (0,))).astype(bf16)
        entry_out[QOWN * block : QOWN * (block + 1), :] = got[:, :MIX_OWN]
        shared_out[QOWN * block : QOWN * (block + 1), :] = got[:, MIX_OWN:]
    for block in range(2):
        got = dot(pick, full[4 + block].reshape(512, WIDE), ((1,), (0,))).astype(bf16)
        exit_out[:, WIDE * block : WIDE * (block + 1)] = got
    hits.finish()
    rows.finish()
    for copy in pairs:
        copy.wait()
    for gather in (hits, rows, cots, low_x, high_y, low_y, high_x):
        gather.drain()
    for copy in columns + last:
        copy.wait_send()
    for copy in local[2:]:
        copy.wait()


def start(rows, cots, hits, entry_cols, exit_cols):
    return pl.pallas_call(
        start_kernel,
        out_shape=[
            jax.ShapeDtypeStruct((N_SEQ, TOK_DEV, D), bf16),
            jax.ShapeDtypeStruct((2, N_SEQ, TOK_DEV, D), bf16),
            jax.ShapeDtypeStruct((N_SEQ, TOK_DEV, 128), bf16),
            jax.ShapeDtypeStruct((D, MIX_OWN), bf16),
            jax.ShapeDtypeStruct((D, 128), bf16),
            jax.ShapeDtypeStruct((QOWN, D), bf16),
        ],
        in_specs=[ANY] * 3 + [VMEM] * 2,
        out_specs=[ANY] * 3 + [VMEM] * 3,
        scratch_shapes=[
            pltpu.VMEM((6, PAD_ROWS, WIDE), bf16),
            pltpu.VMEM((6, 4, 4, 2, PAD_ROWS, WIDE), bf16),
        ]
        + sems(51)
        + [pltpu.SemaphoreType.DMA((6,))],
        compiler_params=remote_params(2),
    )(rows, cots, hits, entry_cols, exit_cols)


def swap_halves(rows, lower, upper):
    lane = lax.broadcasted_iota(jnp.int32, rows.shape, 1)
    ahead = pltpu.roll(rows, rows.shape[1] - HD // 2, 1)
    behind = pltpu.roll(rows, HD // 2, 1)
    return jnp.where(lax.rem(lane, HD) < HD // 2, lower * ahead, upper * behind)


BLOCK = 256


def block_bias(seq_col_ref, seq_row_ref, block):
    keys = BLOCK * (block + 1)
    row = lax.broadcasted_iota(jnp.int32, (BLOCK, keys), 0) + BLOCK * block
    column = lax.broadcasted_iota(jnp.int32, (BLOCK, keys), 1)
    same = seq_col_ref[BLOCK * block : keys, :] == seq_row_ref[:, :keys]
    return jnp.where(same & (column <= row), 0.0, -1e30)


def head_of(index):
    return slice(HD * index, HD * (index + 1))


def middle_kernel(
    all_ref, gain_one_ref, entry_ref, cos_ref, sin_ref, seq_col_ref, seq_row_ref, exit_ref,
    in_ref, gain_ref, extra_ref,
    normed_ref, qkv_ref, attended_ref, lse_ref, middle_ref, tokens_ref, extra_all,
    part, mine, *rest
):
    bufs, (send_sem, recv_sem, copy_sem) = rest[:6], rest[6:]
    me, core = lax.axis_index("seq"), lax.axis_index("core")
    x, y = lax.axis_index("x"), lax.axis_index("y")
    greet(near("seq") + near("x") + near("y") + [sibling()])
    send, plan = sender(send_sem, recv_sem), planner(send_sem, recv_sem)
    low, high = pl.ds(0, 512), pl.ds(512, 512)
    own = pltpu.make_async_copy(extra_ref, extra_all.at[x, y], copy_sem.at[1])
    own.start()
    low_x = Gather(
        plan, 16, "x", extra_ref.at[:, low], lambda i: extra_all.at[i, y, :, low], half_lanes
    ).start()
    high_y = Gather(
        plan, 22, "y", extra_ref.at[:, high], lambda i: extra_all.at[x, i, :, high], half_lanes
    ).start()
    for block in range(N_SEQ):
        rows = slice(TOK_DEV * block, TOK_DEV * (block + 1))
        vector = all_ref[block].astype(f32)
        normed_ref[rows, :] = (vector * unit_scale(vector) * gain_one_ref[...]).astype(bf16)
    low_x.relay()
    high_y.relay()
    mixed = dot(normed_ref[...], entry_ref[...], ((1,), (0,)))
    mixed = mixed * cos_ref[...] + swap_halves(mixed, -1.0, 1.0) * sin_ref[...]
    qkv_ref[...] = mixed.astype(bf16)
    own.wait()
    low_x.finish()
    low_y = Gather(
        plan,
        28,
        "y",
        extra_all.at[:, y, :, low],
        lambda i: extra_all.at[:, i, :, low],
        half_rows,
    ).start()
    high_y.finish()
    high_x = Gather(
        plan,
        34,
        "x",
        extra_all.at[x, :, :, high],
        lambda i: extra_all.at[i, :, :, high],
        half_rows,
    ).start()
    for block in range(GROUP // BLOCK):
        bias = block_bias(seq_col_ref, seq_row_ref, block)
        keys = BLOCK * (block + 1)
        rows = slice(BLOCK * block, keys)
        for head in range(HEADS_OWN):
            pair = Q_OWN + 2 * HD * (head // PER_KV)
            key = qkv_ref[:keys, pair : pair + HD]
            value = qkv_ref[:keys, pair + HD : pair + 2 * HD]
            scores = dot(qkv_ref[rows, head_of(head)], key, ((1,), (1,))) * HD**-0.5 + bias
            peak = jnp.max(scores, axis=1, keepdims=True)
            expo = jnp.exp(scores - peak)
            total = jnp.sum(expo, axis=1, keepdims=True)
            probs = (expo / total).astype(bf16)
            attended_ref[rows, head_of(head)] = dot(probs, value, ((1,), (0,))).astype(bf16)
            lse_ref[rows, head : head + 1] = peak + jnp.log(total)
    part[...] = dot(attended_ref[...], exit_ref[...], ((1,), (0,))).astype(bf16).reshape(part.shape)
    reduce = Reduce(plan, 0, "seq", lambda i: part.at[i], bufs, half_rows).start()
    low_y.relay()
    high_x.relay()
    reduce.relay()
    middle = in_ref[...].astype(f32) + reduce.total()
    middle_ref[...] = middle
    mine[...] = (middle * unit_scale(middle) * gain_ref[...]).astype(bf16)
    gather = Gather(plan, 6, "seq", mine, lambda i: tokens_ref.at[core, i], half_rows).start()
    local = pltpu.make_async_copy(mine, tokens_ref.at[core, me], copy_sem.at[0])
    local.start()
    pairs = hand_over(send, 12, mine, tokens_ref, gather)
    for copy in pairs:
        copy.wait()
    low_y.finish()
    high_x.finish()
    for transfer in (gather, reduce, low_x, high_y, low_y, high_x):
        transfer.drain()
    local.wait()


def middle_tokens(*operands):
    return pl.pallas_call(
        middle_kernel,
        out_shape=[
            jax.ShapeDtypeStruct((GROUP, D), bf16),
            jax.ShapeDtypeStruct((GROUP, MIX_OWN), bf16),
            jax.ShapeDtypeStruct((GROUP, Q_OWN), bf16),
            jax.ShapeDtypeStruct((GROUP, HEADS_OWN), f32),
            jax.ShapeDtypeStruct((TOK_DEV, D), f32),
            jax.ShapeDtypeStruct((2, N_SEQ, TOK_DEV, D), bf16),
            jax.ShapeDtypeStruct((4, 4, 144, 1024), bf16),
        ],
        in_specs=[VMEM] * 10 + [ANY],
        out_specs=[VMEM] * 5 + [ANY] * 2,
        scratch_shapes=[pltpu.VMEM((N_SEQ, TOK_DEV, D), bf16), pltpu.VMEM((TOK_DEV, D), bf16)]
        + reduce_scratch((TOK_DEV, D), (HALF, D))
        + sems(40)
        + [pltpu.SemaphoreType.DMA((2,))],
        compiler_params=remote_params(3),
    )(*operands)


def turn_kernel(
    rank_ref, up_ref, hidden_ref, gate_ref, cot_rows_ref, w_ref,
    extra_up_ref, extra_hidden_ref, extra_w_ref, extra_grad_ref, middle_ref, cot_ref, my_gate_ref, router_ref, gain_ref,
    grad_ref, branch_ref, logit_ref, gain_grad_ref, out_sum_ref, extra_sum_ref,
    back_s, out_s, other_back, from_core, part, other_out, out_core, mine, line, *rest
):
    bufs, (send_sem, recv_sem, copy_sem) = [rest[6 * i : 6 * i + 6] for i in range(5)], rest[30:]
    e = pl.program_id(0)
    me, core = lax.axis_index("seq"), lax.axis_index("core")
    send, plan = sender(send_sem, recv_sem), planner(send_sem, recv_sem)
    low, high = pl.ds(0, 512), pl.ds(512, 512)
    low_x = Reduce(
        plan, 17, "x", lambda i: extra_grad_ref.at[i, :, :, low], bufs[1], half_rows
    )
    high_y = Reduce(
        plan, 23, "y", lambda i: extra_grad_ref.at[:, i, :, high], bufs[2], half_rows
    )
    low_y = Reduce(plan, 29, "y", lambda i: line.at[0, i], bufs[3], half_lanes)
    high_x = Reduce(plan, 35, "x", lambda i: line.at[1, i], bufs[4], half_lanes)

    @pl.when(e == 0)
    def _():
        greet(near("seq") + near("x") + near("y") + [sibling()])
        low_x.start()
        high_y.start()

    @pl.when(e == 2)
    def _():
        low_x.relay()
        high_y.relay()

    def expert_rows(up_ref, hidden_ref, w_ref):
        expand, left, right = weights_of(w_ref)
        at = pl.ds(pl.multiple_of(e * SLOTS, SLOTS), SLOTS)
        back_s[at, :D] = dot(up_ref[0], expand, ((1,), (1,))).astype(bf16)
        hidden = hidden_ref[0]
        expert_out = jnp.concatenate(
            [dot(hidden, left, ((1,), (0,))), dot(hidden, right, ((1,), (0,)))], axis=1
        )
        expert_out = expert_out.astype(bf16).astype(f32)
        gate_grad = jnp.sum(expert_out * cot_rows_ref[0].astype(f32), axis=1, keepdims=True)
        lane = lax.broadcasted_iota(jnp.int32, (SLOTS, 128), 1)
        column = (me * 2 + core) * LOCAL_E + e
        back_s[at, D:] = jnp.where(lane == column, gate_grad, 0.0).astype(bf16)
        out_s[at, :] = (gate_ref[0] * expert_out).astype(bf16)

    @pl.when(e < MAIN_E)
    def _():
        expert_rows(up_ref, hidden_ref, w_ref)

    @pl.when(e == MAIN_E)
    def _():
        expert_rows(extra_up_ref, extra_hidden_ref, extra_w_ref)

    @pl.when(e == LOCAL_E)
    def _():
        other = 1 - core
        right, left, far = ring(me)
        slot = lax.broadcasted_iota(jnp.int32, (GROUP, SLOTS), 1)

        def picks(group):
            at = pl.ds(pl.multiple_of(group * GROUP, GROUP), GROUP)
            ranks = rank_ref[at, :]
            return jnp.concatenate(
                [(ranks[:, k : k + 1] == slot).astype(bf16) for k in range(LOCAL_E)], axis=1
            )

        theirs, ours = picks(other), picks(core)
        order = (far, right, left, me)
        other_back[...] = (
            dot(theirs, back_s[...], ((1,), (0,))).astype(bf16).reshape(other_back.shape)
        )
        swaps = [
            send(other_back.at[block], from_core.at[block], 12 + i, "core", other)
            for i, block in enumerate(order)
        ]
        line[0] = low_x.total().astype(bf16)
        low_y.start()
        line[1] = high_y.total().astype(bf16)
        high_x.start()
        part[...] = dot(ours, back_s[...], ((1,), (0,))).astype(bf16).reshape(part.shape)
        reduce = Reduce(plan, 0, "seq", lambda i: part.at[i], bufs[0], half_rows)
        for i, block in enumerate(order):
            swaps[i].wait_recv()
            added(part.at[block], part.at[block], from_core.at[block])
            if i == 0:
                reduce.start_far()
            if i == 2:
                reduce.start_near()
        other_out[...] = (
            dot(theirs, out_s[...], ((1,), (0,))).astype(bf16).reshape(other_out.shape)
        )
        out_swap = send(other_out, out_core, 16, "core", other)
        reduce.relay()
        low_y.relay()
        high_x.relay()
        out_sum_ref[...] = (
            dot(ours, out_s[...], ((1,), (0,))).astype(bf16).reshape(out_sum_ref.shape)
        )
        total = reduce.total()
        gates, gate_grad = my_gate_ref[...], total[:, D:]
        mean_term = jnp.sum(gates * gate_grad, axis=1, keepdims=True)
        logit_grad = (gates * (gate_grad - mean_term)).astype(bf16)
        logit_ref[...] = logit_grad
        normed_grad = total[:, :D] + dot(logit_grad, router_ref[...], ((1,), (1,)))
        back, gain_grad = norm_back(middle_ref[...], gain_ref[...], normed_grad)
        gain_grad_ref[...] = gain_grad
        middle_grad = cot_ref[...].astype(f32) + back
        grad_ref[...] = middle_grad
        mine[...] = middle_grad.astype(bf16)
        gather = Gather(plan, 6, "seq", mine, lambda i: branch_ref.at[i], half_rows).start()
        local = pltpu.make_async_copy(mine, branch_ref.at[me], copy_sem)
        local.start()
        out_swap.wait_recv()
        added(out_sum_ref, out_sum_ref, out_core)
        gather.relay()
        extra_sum_ref[:, :512] = low_y.total().astype(bf16)
        extra_sum_ref[:, 512:] = high_x.total().astype(bf16)
        gather.finish()
        for transfer in (gather, reduce, low_x, high_y, low_y, high_x):
            transfer.drain()
        for copy in swaps + [out_swap]:
            copy.wait_send()
        local.wait()


BACK_WIDTH = D + 128


def turn(*operands):
    one = lambda e: (jnp.minimum(e, MAIN_E - 1), 0, 0)
    each = lambda e: (jnp.minimum(e, LOCAL_E - 1), 0, 0)
    wide = lambda e: (0, jnp.minimum(e, MAIN_E - 1), 0, 0)
    cubes = lambda e: (0, 0, 0, 0)
    whole = lambda e: (0, 0)
    blocks = lambda e: (0, 0, 0)
    row_block = pl.BlockSpec((TOK_DEV, D), whole)
    lane_block = pl.BlockSpec((TOK_DEV, 128), whole)
    gain_block = pl.BlockSpec((1, D), whole)
    group = pltpu.VMEM((N_SEQ, TOK_DEV, BACK_WIDTH), bf16)
    group_out = pltpu.VMEM((N_SEQ, TOK_DEV, D), bf16)
    return pl.pallas_call(
        turn_kernel,
        grid=(LOCAL_E + 1,),
        in_specs=[
            pl.BlockSpec((PAIR_TOK, LOCAL_E), whole),
            pl.BlockSpec((1, SLOTS, 2 * FF), one),
            pl.BlockSpec((1, SLOTS, FF), one),
            pl.BlockSpec((1, SLOTS, 1), each),
            pl.BlockSpec((1, SLOTS, D), each),
            pl.BlockSpec((16, 1, 144, 1024), wide),
            pl.BlockSpec((1, SLOTS, 2 * FF), blocks),
            pl.BlockSpec((1, SLOTS, FF), blocks),
            pl.BlockSpec((16, 1, 144, 1024), cubes, pipeline_mode=pl.Buffered(1)),
            pl.BlockSpec((4, 4, 144, 1024), cubes, pipeline_mode=pl.Buffered(1)),
            row_block,
            row_block,
            lane_block,
            pl.BlockSpec((D, 128), whole),
            gain_block,
        ],
        out_specs=[
            row_block,
            ANY,
            lane_block,
            gain_block,
            pl.BlockSpec((N_SEQ, TOK_DEV, D), blocks),
            pl.BlockSpec((144, 1024), whole),
        ],
        out_shape=[
            jax.ShapeDtypeStruct((TOK_DEV, D), f32),
            jax.ShapeDtypeStruct((N_SEQ, TOK_DEV, D), bf16),
            jax.ShapeDtypeStruct((TOK_DEV, 128), bf16),
            jax.ShapeDtypeStruct((1, D), f32),
            jax.ShapeDtypeStruct((N_SEQ, TOK_DEV, D), bf16),
            jax.ShapeDtypeStruct((144, 1024), bf16),
        ],
        scratch_shapes=[
            pltpu.VMEM((LOCAL_E * SLOTS, BACK_WIDTH), bf16),
            pltpu.VMEM((LOCAL_E * SLOTS, D), bf16),
            group,
            group,
            group,
            group_out,
            group_out,
            pltpu.VMEM((TOK_DEV, D), bf16),
            pltpu.VMEM((2, 4, 144, 512), bf16),
        ]
        + reduce_scratch((TOK_DEV, BACK_WIDTH), (HALF, BACK_WIDTH))
        + reduce_scratch((4, 144, 512), (2, 144, 512)) * 2
        + reduce_scratch((144, 512), (144, 256)) * 2
        + sems(41)
        + [pltpu.SemaphoreType.DMA],
        compiler_params=remote_params(4),
        cost_estimate=pl.CostEstimate(
            flops=6 * LOCAL_E * SLOTS * D * FF + 4 * LOCAL_E * SLOTS * PAIR_TOK * D,
            bytes_accessed=40 << 20,
            transcendentals=0,
        ),
    )(*operands)


PAD_ROWS = 16
WIDE = 768
def closing_kernel(
    qkv_ref, lse_ref, cos_ref, sin_ref, seq_col_ref, seq_row_ref, exit_ref, entry_ref,
    in_ref, grad_ref, gain_ref, normed_ref, attended_ref, branch_ref,
    router_grad_ref, gain_two_ref, out_sum_ref, middle_ref,
    input_ref, block_ref, entry_out, exit_out,
    turned, mixed_grad, part, full, from_core, chip, line, final, give, got_z, *rest
):
    bufs, (send_sem, recv_sem) = [rest[6 * i : 6 * i + 6] for i in range(8)], rest[48:]
    z, x, y, c = (lax.axis_index(a) for a in ("seq", "x", "y", "core"))
    right, left, far = ring(z)
    greet(near("seq") + [("seq", far)] + near("x") + near("y") + [sibling()])
    send, plan = sender(send_sem, recv_sem), planner(send_sem, recv_sem)
    pick = row_pick((512, QOWN), 0)

    def spread(grad):
        wide = dot(pick, grad, ((1,), (0,))).astype(bf16)
        return wide.reshape(16, 2, PAD_ROWS, grad.shape[1])

    def swap(side):
        return send(full.at[side, :, 1 - c], from_core.at[side], 48 + side, "core", 1 - c)

    def chip_sum(side, copy):
        copy.wait_recv()
        for plane in range(16):
            first, second = (plane % 4, plane // 4) if side == 2 else (plane // 4, plane % 4)
            added(chip.at[side, first, second], full.at[side, plane, c], from_core.at[side, plane])

    def first_sum(side, axis):
        return Reduce(
            plan, 6 * side, axis, lambda i: chip.at[side, i], bufs[side], half_rows
        ).start()

    def second_sum(side, axis, reduce):
        line[side] = reduce.total().astype(bf16)
        return Reduce(
            plan, 18 + 6 * side, axis, lambda i: line.at[side, i], bufs[3 + side], half_lanes
        ).start()

    for block in range(3):
        cols = slice(512 * block, 512 * (block + 1))
        grad = dot(attended_ref[...], branch_ref[:, cols], ((0,), (0,))).astype(bf16)
        full[0, :, :, :, cols] = spread(grad)
    swaps = [swap(0)]
    outs = Reduce(plan, 36, "seq", lambda i: out_sum_ref.at[i], bufs[6], half_rows).start()

    def turn_back(kv):
        pair = Q_OWN + 2 * HD * kv
        for head in range(PER_KV * kv, PER_KV * (kv + 1)):
            grad = dot(branch_ref[...], exit_ref[head_of(head), :], ((1,), (1,))).astype(bf16)
            attended = attended_ref[:, head_of(head)].astype(f32)
            delta = jnp.sum(grad.astype(f32) * attended, axis=1, keepdims=True)
            for block in range(GROUP // BLOCK):
                bias = block_bias(seq_col_ref, seq_row_ref, block)
                keys = BLOCK * (block + 1)
                rows = slice(BLOCK * block, keys)
                key = qkv_ref[:keys, pair : pair + HD]
                value = qkv_ref[:keys, pair + HD : pair + 2 * HD]
                query, grad_rows = qkv_ref[rows, head_of(head)], grad[rows]
                scores = dot(query, key, ((1,), (1,))) * HD**-0.5 + bias
                probs = jnp.exp(scores - lse_ref[rows, head : head + 1])
                prob_grad = dot(grad_rows, value, ((1,), (1,)))
                score_grad = probs * (prob_grad - delta[rows]) * HD**-0.5
                score_grad = score_grad.astype(bf16)
                turned[rows, head_of(head)] = dot(score_grad, key, ((1,), (0,)))
                key_grad = dot(score_grad, query, ((0,), (0,)))
                value_grad = dot(probs.astype(bf16), grad_rows, ((0,), (0,)))
                if head == PER_KV * kv and block == GROUP // BLOCK - 1:
                    turned[:, pair : pair + HD] = key_grad
                    turned[:, pair + HD : pair + 2 * HD] = value_grad
                    turned[:BLOCK, pair : pair + HD] += held[0]
                    turned[:BLOCK, pair + HD : pair + 2 * HD] += held[1]
                elif head == PER_KV * kv:
                    held = (key_grad, value_grad)
                else:
                    turned[:keys, pair : pair + HD] += key_grad
                    turned[:keys, pair + HD : pair + 2 * HD] += value_grad

    turn_back(0)
    chip_sum(0, swaps[0])
    first_0 = first_sum(0, "x")
    outs.relay()
    turn_back(1)
    first_0.relay()
    grads = turned[...]
    grads = grads * cos_ref[...] + swap_halves(grads, 1.0, -1.0) * sin_ref[...]
    mixed_grad[...] = grads.astype(bf16)
    part[...] = (
        dot(mixed_grad[...], entry_ref[...], ((1,), (1,))).astype(bf16).reshape(part.shape)
    )
    rows = Reduce(plan, 42, "seq", lambda i: part.at[i], bufs[7], half_rows).start()

    def entry_rows(block):
        rows_of = slice(QOWN * block, QOWN * (block + 1))
        grad = dot(normed_ref[:, rows_of], mixed_grad[...], ((0,), (0,))).astype(bf16)
        return spread(grad)

    full[1, :, :, :, :640] = entry_rows(0)
    full[1, :, :, :, 640:1280] = entry_rows(1)
    third = entry_rows(2)
    full[1, :, :, :, 1280:] = third[..., :256]
    swaps.append(swap(1))
    rows.relay()
    second_0 = second_sum(0, "y", first_0)
    full[2, :, :, :, :384] = third[..., 256:]
    full[2, :, :, :, 384:1024] = entry_rows(3)
    chip_sum(1, swaps[1])
    first_1 = first_sum(1, "x")
    back, gain_one = norm_back(in_ref[...].astype(f32), gain_ref[...], rows.total())
    input_ref[...] = grad_ref[...] + back
    row_of = lax.broadcasted_iota(jnp.int32, (128, D), 0)
    gains = jnp.where(row_of == EXPERTS, gain_one, 0.0)
    gains = jnp.where(row_of == EXPERTS + 1, gain_two_ref[...], gains)
    shared = router_grad_ref[...] + gains.T
    for block in range(4):
        shared_rows = shared[QOWN * block : QOWN * (block + 1), :].astype(bf16)
        full[2, :, :, :, 1024 + 128 * block : 1152 + 128 * block] = spread(shared_rows)
    swaps.append(swap(2))
    second_0.relay()
    block_ref[...] = middle_ref[...] + outs.total()
    chip_sum(2, swaps[2])
    first_2 = first_sum(2, "y")
    first_1.relay()
    first_2.relay()
    exit_out[...] = second_0.total()
    second_1 = second_sum(1, "y", first_1)
    second_2 = second_sum(2, "x", first_2)
    second_1.relay()
    second_2.relay()
    final[0] = second_1.total()
    final[1] = second_2.total()
    give[0, :, :MIX_OWN] = final[0, :, :640]
    give[1, :, :MIX_OWN] = final[0, :, 640:1280]
    give[2, :, :256] = final[0, :, 1280:]
    give[2, :, 256:MIX_OWN] = final[1, :, :384]
    give[3, :, :MIX_OWN] = final[1, :, 384:1024]
    for block in range(4):
        give[block, :, MIX_OWN:] = final[1, :, 1024 + 128 * block : 1152 + 128 * block]
    home = [
        send(give.at[peer], got_z.at[k], 51 + k, "seq", peer)
        for k, peer in enumerate((right, far, left))
    ]
    entry_out[z] = give[z]
    for k, source in enumerate((left, far, right)):
        home[k].wait_recv()
        entry_out[source] = got_z[k]
    for copy in swaps + home:
        copy.wait_send()
    for reduce in (rows, outs, first_0, first_1, first_2, second_0, second_1, second_2):
        reduce.drain()


def closing(*operands):
    row_bufs = reduce_scratch((TOK_DEV, D), (HALF, D))
    chip_bufs = reduce_scratch((4, PAD_ROWS, D), (2, PAD_ROWS, D))
    line_bufs = reduce_scratch((PAD_ROWS, D), (PAD_ROWS, D // 2))
    tile = (PAD_ROWS, D)
    return pl.pallas_call(
        closing_kernel,
        out_shape=[
            jax.ShapeDtypeStruct((TOK_DEV, D), f32),
            jax.ShapeDtypeStruct((TOK_DEV, D), f32),
            jax.ShapeDtypeStruct((4, PAD_ROWS, WIDE), f32),
            jax.ShapeDtypeStruct((PAD_ROWS, D), f32),
        ],
        in_specs=[VMEM] * len(operands),
        out_specs=[VMEM] * 4,
        scratch_shapes=[
            pltpu.VMEM((GROUP, MIX_OWN), f32),
            pltpu.VMEM((GROUP, MIX_OWN), bf16),
            pltpu.VMEM((N_SEQ, TOK_DEV, D), bf16),
            pltpu.VMEM((3, 16, 2) + tile, bf16),
            pltpu.VMEM((3, 16) + tile, bf16),
            pltpu.VMEM((3, 4, 4) + tile, bf16),
            pltpu.VMEM((3, 4) + tile, bf16),
            pltpu.VMEM((2,) + tile, f32),
            pltpu.VMEM((4, PAD_ROWS, WIDE), f32),
            pltpu.VMEM((3, PAD_ROWS, WIDE), f32),
        ]
        + chip_bufs * 3
        + line_bufs * 3
        + row_bufs * 2
        + sems(54),
        compiler_params=remote_params(5),
    )(*operands)


def owner_kernel(sum_ref, extra_ref, expand_ref, shrink_ref, send_sem, recv_sem, copy_sem):
    core = lax.axis_index("core")
    greet([sibling()])
    send = sender(send_sem, recv_sem)
    most, last = pl.ds(core * LOCAL_E, MAIN_E), core * LOCAL_E + MAIN_E

    def pieces(owner):
        rows = pl.ds(pl.multiple_of(owner * 48, 16), 48)
        left = pl.ds(pl.multiple_of(96 + owner * 16, 16), 16)
        ends = pl.ds(pl.multiple_of(owner * 512, 512), 512)
        low, start, end = pl.ds(128, 16), pl.ds(0, 1024), pl.ds(1024, 512)
        return [
            (sum_ref.at[:, rows], expand_ref.at[most]),
            (sum_ref.at[:, left], shrink_ref.at[most, :, start]),
            (sum_ref.at[:, low, ends], shrink_ref.at[most, :, end]),
            (extra_ref.at[rows], expand_ref.at[last]),
            (extra_ref.at[left], shrink_ref.at[last, :, start]),
            (extra_ref.at[low, ends], shrink_ref.at[last, :, end]),
        ]

    copies = [
        send(source, target, k, "core", 1 - core)
        for k, (source, target) in enumerate(pieces(1 - core))
    ]
    for k, (source, target) in enumerate(pieces(core)):
        copies.append(pltpu.make_async_copy(source, target, copy_sem.at[k]))
        copies[-1].start()
    for copy in copies:
        copy.wait()


def to_owners(summed, extra):
    return pl.pallas_call(
        owner_kernel,
        out_shape=[
            jax.ShapeDtypeStruct((2 * LOCAL_E, 48, 1024), bf16),
            jax.ShapeDtypeStruct((2 * LOCAL_E, 16, D), bf16),
        ],
        in_specs=[VMEM] * 2,
        out_specs=[VMEM] * 2,
        scratch_shapes=sems(6) + [pltpu.SemaphoreType.DMA((6,))],
        compiler_params=remote_params(6),
    )(summed, extra)


def dispatch_kernel(rank_ref, gate_ref, tokens_ref, cots_ref, rows_ref, cot_rows_ref, row_gate_ref):
    slot = lax.broadcasted_iota(jnp.int32, (SLOTS, PAIR_TOK), 0)
    match = rank_ref[0] == slot
    row_gate_ref[0] = jnp.sum(jnp.where(match, gate_ref[0], 0.0), axis=1, keepdims=True)
    pick = match.astype(bf16)
    for j in range(3):
        cols = slice(512 * j, 512 * (j + 1))
        rows_ref[0, :, cols] = dot(pick, tokens_ref[:, cols], ((1,), (0,))).astype(bf16)
        cot_rows_ref[0, :, cols] = dot(pick, cots_ref[:, cols], ((1,), (0,))).astype(bf16)

def dispatch(rank, gates, tokens, cots):
    one = lambda e: (e, 0, 0)
    whole = lambda e: (0, 0)
    return pl.pallas_call(
        dispatch_kernel,
        grid=(LOCAL_E,),
        in_specs=[
            pl.BlockSpec((1, 1, PAIR_TOK), one),
            pl.BlockSpec((1, 1, PAIR_TOK), one),
            pl.BlockSpec((PAIR_TOK, D), whole),
            pl.BlockSpec((PAIR_TOK, D), whole),
        ],
        out_specs=[
            pl.BlockSpec((1, SLOTS, D), one),
            pl.BlockSpec((1, SLOTS, D), one),
            pl.BlockSpec((1, SLOTS, 1), one),
        ],
        out_shape=[
            jax.ShapeDtypeStruct((LOCAL_E, SLOTS, D), bf16),
            jax.ShapeDtypeStruct((LOCAL_E, SLOTS, D), bf16),
            jax.ShapeDtypeStruct((LOCAL_E, SLOTS, 1), f32),
        ],
        compiler_params=pltpu.CompilerParams(vmem_limit_bytes=BIG),
        cost_estimate=pl.CostEstimate(
            flops=4 * LOCAL_E * SLOTS * PAIR_TOK * D, bytes_accessed=16 << 20, transcendentals=0
        ),
    )(rank[:, None], gates[:, None], tokens, cots)

def weights_of(w_ref):
    expand = w_ref[:, 0, :96, :].reshape(D, 2 * FF)
    left = w_ref[:, 0, 96:128, :].reshape(FF, 1024)
    right = jnp.concatenate([w_ref[:, 0, 128:144, :512], w_ref[:, 0, 128:144, 512:]], axis=1)
    return expand, left, right.reshape(FF, 512)

def grads_kernel(rows_ref, cot_ref, gate_ref, w_ref, hidden_ref, up_ref, out_ref):
    expand, left, right = weights_of(w_ref)
    grad_rows = (gate_ref[0] * cot_ref[0].astype(f32)).astype(bf16)
    rows = rows_ref[0]
    gate_pre = dot(rows, expand[:, :FF], ((1,), (0,)))
    up_part = dot(rows, expand[:, FF:], ((1,), (0,)))
    sig = jax.nn.sigmoid(gate_pre)
    hidden = (gate_pre * sig * up_part).astype(bf16)
    hidden_ref[0] = hidden
    hidden_grad = dot(grad_rows[:, :1024], left, ((1,), (1,))) + dot(
        grad_rows[:, 1024:], right, ((1,), (1,))
    )
    up_ref[0, :, :FF] = (hidden_grad * up_part * sig * (1.0 + gate_pre * (1.0 - sig))).astype(bf16)
    up_ref[0, :, FF:] = (hidden_grad * gate_pre * sig).astype(bf16)
    grad_left = dot(hidden, grad_rows[:, :1024], ((0,), (0,))).astype(bf16)
    out_ref[:, 0, 96:128, :] = grad_left.reshape(16, 32, 1024)
    grad_right = dot(hidden, grad_rows[:, 1024:], ((0,), (0,))).astype(bf16).reshape(16, 32, 512)
    out_ref[:, 0, 128:144, :512] = grad_right[:, :16]
    out_ref[:, 0, 128:144, 512:] = grad_right[:, 16:]
    up_grad = up_ref[0]
    for j in range(4):
        part = dot(rows[:, 384 * j : 384 * (j + 1)], up_grad, ((0,), (0,))).astype(bf16)
        out_ref[4 * j : 4 * (j + 1), 0, :96, :] = part.reshape(4, 96, 1024)

def expert_grads(rows, cot_rows, row_gates, weights, first):
    count = weights.shape[1]
    at = lambda e: (e + first, 0, 0)
    one = lambda e: (e, 0, 0)
    wide = lambda e: (0, e, 0, 0)
    return pl.pallas_call(
        grads_kernel,
        grid=(count,),
        in_specs=[
            pl.BlockSpec((1, SLOTS, D), at),
            pl.BlockSpec((1, SLOTS, D), at),
            pl.BlockSpec((1, SLOTS, 1), at),
            pl.BlockSpec((16, 1, 144, 1024), wide),
        ],
        out_specs=[
            pl.BlockSpec((1, SLOTS, FF), one),
            pl.BlockSpec((1, SLOTS, 2 * FF), one),
            pl.BlockSpec((16, 1, 144, 1024), wide),
        ],
        out_shape=[
            jax.ShapeDtypeStruct((count, SLOTS, FF), bf16),
            jax.ShapeDtypeStruct((count, SLOTS, 2 * FF), bf16),
            jax.ShapeDtypeStruct((16, count, 144, 1024), bf16),
        ],
        compiler_params=pltpu.CompilerParams(vmem_limit_bytes=BIG),
        cost_estimate=pl.CostEstimate(
            flops=12 * count * SLOTS * D * FF, bytes_accessed=count * (12 << 20), transcendentals=0
        ),
    )(rows, cot_rows, row_gates, weights)


def core_swap(value):
    return lax.ppermute(value, "core", [(0, 1), (1, 0)])


def core_order(core, mine, other, axis):
    return jnp.concatenate(
        [jnp.where(core == 0, mine, other), jnp.where(core == 0, other, mine)], axis=axis
    )


def norm_apply(vector, gain):
    scale = lax.rsqrt(jnp.mean(vector * vector, axis=-1, keepdims=True) + norm_eps)
    return vector * scale * gain


def adamw_step(weight, gradient, mean_old, square_old, rate, decay):
    drift = beta_first * mean_old + (1.0 - beta_first) * gradient
    spread = beta_second * square_old + (1.0 - beta_second) * gradient * gradient
    mean_hat = drift / (1.0 - beta_first**STEP)
    square_hat = spread / (1.0 - beta_second**STEP)
    master = weight - rate * (mean_hat / (jnp.sqrt(square_hat) + adam_eps) + decay * weight)
    return (drift, spread, master)


def rotate(vector, cosine, sine):
    first, second = vector[..., : HD // 2], vector[..., HD // 2 :]
    return jnp.concatenate(
        [first * cosine - second * sine, second * cosine + first * sine], axis=-1
    )


def on_device(
    activations,
    cotangent,
    seq_lengths,
    deal_order,
    routes,
    entry_weight,
    entry_mean,
    entry_square,
    exit_weight,
    exit_mean,
    exit_square,
    router_weight,
    router_mean,
    router_square,
    expand_weight,
    expand_mean,
    expand_square,
    shrink_weight,
    shrink_mean,
    shrink_square,
    norm_gains,
    gains_mean,
    gains_square,
):
    seq = lax.axis_index("seq")
    core = lax.axis_index("core")
    first = (seq * 2 + core) * LOCAL_E

    packed, extra = pack_experts(expand_weight, shrink_weight)
    packed, rows_in, cots_in = lax.optimization_barrier((packed, activations[0], cotangent[0]))
    weights = lax.all_gather(packed, PLANE, axis=0, tiled=False)

    entry_b = entry_weight.astype(bf16)
    shared_b = jnp.concatenate([router_weight, norm_gains.T], axis=1).astype(bf16)
    shared_b = jnp.pad(shared_b, ((0, 0), (0, 128 - EXPERTS - 2)))
    entry_cols = jnp.concatenate(
        [
            entry_b[:, : QH * HD].reshape(ROWS, N_SEQ, Q_OWN).transpose(1, 0, 2),
            entry_b[:, QH * HD :].reshape(ROWS, N_SEQ, KV_OWN).transpose(1, 0, 2),
            jnp.broadcast_to(shared_b[None], (N_SEQ, ROWS, 128)),
        ],
        axis=2,
    )
    exit_cols = exit_weight.astype(bf16).reshape(ROWS, 2, WIDE).transpose(1, 0, 2)
    pad = ((0, 0), (0, PAD_ROWS - ROWS), (0, 0))
    expert_ids = jnp.arange(128, dtype=jnp.int32)
    hit_slots = jnp.any(routes[0][:, :, None] == expert_ids[None, None, :], axis=1).astype(bf16)
    in_all, cots, hit_slots, entry_own, shared, exit_own = start(
        rows_in, cots_in, hit_slots, jnp.pad(entry_cols, pad), jnp.pad(exit_cols, pad)
    )
    gains_full = shared[:, EXPERTS : EXPERTS + 2].astype(f32).T

    order_row = deal_order[0]
    token = jnp.arange(GROUP, dtype=jnp.int32)
    back_hot = (order_row[None, :] == token[:, None]).astype(bf16)
    hit = dot(back_hot, hit_slots.reshape(GROUP, 128), ((1,), (0,))).astype(bf16)
    hits = core_order(core, hit, core_swap(hit), 0)[:, :EXPERTS]
    own_hits = lax.dynamic_slice_in_dim(hits, first, LOCAL_E, 1)
    rank = jnp.cumsum(own_hits.astype(jnp.int32), axis=0) - 1
    rank = jnp.where(own_hits > 0, rank, -1)
    seq_ends = jnp.cumsum(seq_lengths[0])
    starts = seq_ends - seq_lengths[0]
    seq_ids = jnp.sum((token[:, None] >= seq_ends[None, :]).astype(jnp.int32), axis=1)
    seq_match = seq_ids[:, None] == jnp.arange(seq_ends.shape[0], dtype=jnp.int32)[None, :]
    positions = token - jnp.sum(jnp.where(seq_match, starts[None, :], 0), axis=1)
    frequency = rope_base ** (-jnp.arange(HD // 2, dtype=f32) * 2.0 / HD)
    phase = positions.astype(f32)[:, None] * frequency[None, :]
    ones = jnp.ones((GROUP, HD), f32)
    cosine, sine = jnp.tile(jnp.cos(phase), (1, 2)), jnp.tile(jnp.sin(phase), (1, 2))
    cosine = jnp.concatenate(
        [jnp.tile(cosine, (1, HEADS_OWN))] + [cosine, ones] * KV_HEADS_OWN, axis=1
    )
    sine = jnp.concatenate(
        [jnp.tile(sine, (1, HEADS_OWN))] + [sine, 0.0 * ones] * KV_HEADS_OWN, axis=1
    )
    angles = (cosine, sine, seq_ids[:, None], seq_ids[None, :])

    normed, qkv, attended, lse, middle, tokens, extra_weights = middle_tokens(
        in_all,
        gains_full[0:1],
        entry_own,
        *angles,
        exit_own,
        activations[0],
        gains_full[1:2],
        extra,
    )
    extra_weights = extra_weights.reshape(16, 1, 144, 1024)
    normed_two = lax.dynamic_slice(tokens, (core, seq, 0, 0), (1, 1, TOK_DEV, D))[0, 0]
    tokens = tokens.reshape(PAIR_TOK, D)

    logits = dot(tokens, shared[:, :EXPERTS], ((1,), (0,)))
    masked = jnp.where(hits > 0, logits, -jnp.inf)
    gate_expo = jnp.exp(masked - jnp.max(masked, axis=1, keepdims=True))
    gates = gate_expo / jnp.sum(gate_expo, axis=1, keepdims=True)
    own_gates = lax.dynamic_slice_in_dim(gates, first, LOCAL_E, 1)
    rows, cot_rows, row_gates = dispatch(rank.T, own_gates.T, tokens, cots.reshape(PAIR_TOK, D))
    extra_hidden, extra_up, extra_grad = expert_grads(
        rows, cot_rows, row_gates, extra_weights, MAIN_E
    )
    hidden, up_grad, expert_grad = expert_grads(rows, cot_rows, row_gates, weights, 0)
    expert_sum = lax.psum_scatter(expert_grad, PLANE, scatter_dimension=0, tiled=False)
    my_gates = lax.dynamic_slice_in_dim(gates, core * GROUP + seq * TOK_DEV, TOK_DEV, 0)
    my_gates = jnp.pad(my_gates, ((0, 0), (0, 128 - EXPERTS)))
    middle_grad, branch_grad, logit_grad, gain_two_grad, out_sum, extra_sum = turn(
        rank,
        up_grad,
        hidden,
        row_gates,
        cot_rows,
        weights,
        extra_up,
        extra_hidden,
        extra_weights,
        extra_grad.reshape(4, 4, 144, 1024),
        middle,
        cotangent[0],
        my_gates,
        shared,
        gains_full[1:2],
    )
    branch_grad = branch_grad.reshape(GROUP, D)
    router_grad = dot(normed_two, logit_grad, ((0,), (0,)))

    input_rows, block_rows, entry_got, exit_got = closing(
        qkv,
        lse,
        *angles,
        exit_own,
        entry_own,
        activations[0],
        middle_grad,
        gains_full[0:1],
        normed,
        attended,
        branch_grad,
        router_grad,
        gain_two_grad,
        out_sum,
        middle,
    )

    input_grad, block_output = input_rows.astype(bf16), block_rows.astype(bf16)

    entry_got = entry_got[:, :ROWS]
    entry_sum = jnp.concatenate(
        [
            entry_got[:, :, :Q_OWN].transpose(1, 0, 2).reshape(ROWS, QH * HD),
            entry_got[:, :, Q_OWN:MIX_OWN].transpose(1, 0, 2).reshape(ROWS, 2 * KVH * HD),
        ],
        axis=1,
    )
    shared_sum = jnp.sum(entry_got[:, :, MIX_OWN:], axis=0)
    router_sum = shared_sum[:, :EXPERTS]
    gains_sum = shared_sum[:, EXPERTS : EXPERTS + 2].T
    exit_sum = exit_got[:ROWS]

    expand_sum, shrink_sum = to_owners(expert_sum, extra_sum)
    expand_sum, shrink_sum = expand_sum.astype(f32), shrink_sum.astype(f32)
    entry_new = adamw_step(entry_weight, entry_sum, entry_mean, entry_square, 0.02, weight_decay)
    exit_new = adamw_step(exit_weight, exit_sum, exit_mean, exit_square, 0.15, weight_decay)
    router_new = adamw_step(
        router_weight, router_sum, router_mean, router_square, 0.01, weight_decay
    )
    expand_new = adamw_step(
        expand_weight, expand_sum, expand_mean, expand_square, 0.02, weight_decay
    )
    shrink_new = adamw_step(
        shrink_weight, shrink_sum, shrink_mean, shrink_square, 0.12, weight_decay
    )
    gains_new = adamw_step(norm_gains, gains_sum, gains_mean, gains_square, 0.5, 0.0)
    return (
        block_output[None],
        input_grad[None],
        *entry_new,
        *exit_new,
        *router_new,
        *expand_new,
        *shrink_new,
        *gains_new,
    )


def solution(mesh):
    fine = Mesh(mesh.devices.reshape(4, 4, 4, 2), ("seq", "x", "y", "core"))
    rows = P(FSDP, "seq", None)
    lists = P(FSDP, None)
    owned = P(("seq",) + FSDP, None)
    experts = P("seq", FSDP, None)
    gains = P(None, ("seq",) + FSDP)
    return jax.shard_map(
        on_device,
        mesh=fine,
        in_specs=(rows, rows, lists, lists, rows)
        + (owned,) * 9
        + (experts,) * 6
        + (gains,) * 3,
        out_specs=(rows, rows) + (owned,) * 9 + (experts,) * 6 + (gains,) * 3,
        check_vma=False,
    )
```

```python
import jax
import jax.numpy as jnp
from jax import lax
from jax.experimental import pallas as pl
from jax.experimental.pallas import tpu as pltpu
from jax.sharding import Mesh, PartitionSpec as P

D = 1536
QH = 24
KVH = 8
HD = 64
FF = 512
EXPERTS = 40
TOP = 8
STEP = 10
CAP = 29

N_SEQ = 4
TOK_DEV = 128
GROUP = 512
PAIR_TOK = 2 * GROUP
LOCAL_E = EXPERTS // (2 * N_SEQ)
SLOTS = 256
Q_OWN = QH * HD // N_SEQ
KV_OWN = 2 * KVH * HD // N_SEQ
MIX_OWN = Q_OWN + KV_OWN
HEADS_OWN = QH // N_SEQ
KV_HEADS_OWN = KVH // N_SEQ
PER_KV = QH // KVH
ROWS = 12

norm_eps = 1e-06
rope_base = 10000.0
beta_first = 0.9
beta_second = 0.95
adam_eps = 1e-08
weight_decay = 0.1

FSDP = ("x", "y", "core")
PLANE = ("x", "y")
f32 = jnp.float32
bf16 = jnp.bfloat16


BIG = 60 * 1024 * 1024
HALF = TOK_DEV // 2
QOWN = Q_OWN
MESH = pl.DeviceIdType.MESH
ANY = pl.BlockSpec(memory_space=pl.ANY)
VMEM = pl.BlockSpec(memory_space=pltpu.VMEM)


def dot(a, b, dims):
    return lax.dot_general(a, b, (dims, ((), ())), preferred_element_type=f32)


def greet(peers):
    barrier = pltpu.get_barrier_semaphore()
    for axis, peer in peers:
        pl.semaphore_signal(barrier, inc=1, device_id={axis: peer}, device_id_type=MESH)
    pl.semaphore_wait(barrier, len(peers))


def planner(send_sem, recv_sem):
    def plan(src, dst, index, axis, peer):
        return pltpu.make_async_remote_copy(
            src_ref=src,
            dst_ref=dst,
            send_sem=send_sem.at[index],
            recv_sem=recv_sem.at[index],
            device_id={axis: peer},
            device_id_type=MESH,
        )

    return plan


def sender(send_sem, recv_sem):
    plan = planner(send_sem, recv_sem)

    def send(*args):
        copy = plan(*args)
        copy.start()
        return copy

    return send


def sems(count):
    return [pltpu.SemaphoreType.DMA((count,)), pltpu.SemaphoreType.DMA((count,))]


def ring(me):
    right, left = lax.rem(me + 1, 4), lax.rem(me + 3, 4)
    return right, left, lax.rem(me + 2, 4)


def near(axis):
    right, left, _ = ring(lax.axis_index(axis))
    return [(axis, right), (axis, left)]


def sibling():
    return ("core", 1 - lax.axis_index("core"))


def half_rows(ref, half):
    size = ref.shape[0] // 2
    return ref.at[pl.ds(half * size, size)]


def half_lanes(ref, half):
    size = ref.shape[-1] // 2
    return ref.at[(slice(None),) * (len(ref.shape) - 1) + (pl.ds(half * size, size),)]


class Gather:
    def __init__(self, plan, base, axis, mine, slot, cut):
        me = lax.axis_index(axis)
        right, left, self.far = ring(me)
        self.right, self.left = right, left
        here, from_left, from_right = slot(me), cut(slot(left), 0), cut(slot(right), 1)
        self.first = [
            plan(cut(mine, 0), cut(here, 0), base, axis, right),
            plan(cut(mine, 1), cut(here, 1), base + 1, axis, left),
            plan(cut(mine, 1), cut(here, 1), base + 2, axis, right),
            plan(cut(mine, 0), cut(here, 0), base + 3, axis, left),
        ]
        self.later = [
            plan(from_left, from_left, base + 4, axis, right),
            plan(from_right, from_right, base + 5, axis, left),
        ]

    def start(self):
        for copy in self.first:
            copy.start()
        return self

    def relay(self):
        for got, on in zip(self.first, self.later):
            got.wait_recv()
            on.start()

    def wait_left(self):
        self.first[2].wait_recv()

    def wait_right(self):
        self.first[3].wait_recv()

    def wait_far(self):
        for copy in self.later:
            copy.wait_recv()

    def finish(self):
        self.wait_left()
        self.wait_right()
        self.wait_far()

    def drain(self):
        for copy in self.first + self.later:
            copy.wait_send()


def hand_over(send, base, mine, out, gather):
    me, core = lax.axis_index("seq"), lax.axis_index("core")
    other = 1 - core
    copies = [send(mine, out.at[core, me], base, "core", other)]
    gather.relay()
    gather.wait_left()
    block = out.at[core, gather.left]
    copies.append(send(block, block, base + 1, "core", other))
    gather.wait_right()
    block = out.at[core, gather.right]
    copies.append(send(block, block, base + 2, "core", other))
    gather.wait_far()
    block = out.at[core, gather.far]
    copies.append(send(block, block, base + 3, "core", other))
    return copies


def reduce_scratch(block, half):
    return [pltpu.VMEM(half, bf16)] * 4 + [pltpu.VMEM(block, bf16)] * 2


def added(target, first, second):
    target[...] = (first[...].astype(f32) + second[...].astype(f32)).astype(bf16)


class Reduce:
    def __init__(self, plan, base, axis, block, bufs, cut):
        me = lax.axis_index(axis)
        right, left, far = ring(me)
        from_left, from_right, to_right, to_left, got_left, got_right = bufs
        far, on_right, on_left = block(far), block(right), block(left)
        self.mine, self.got = block(me), (got_left, got_right)
        self.hops = (
            (to_right, cut(on_right, 0), from_left),
            (to_left, cut(on_left, 1), from_right),
        )
        self.far = [
            plan(cut(far, 0), from_left, base, axis, right),
            plan(cut(far, 1), from_right, base + 1, axis, left),
        ]
        self.near = [
            plan(cut(on_right, 1), cut(got_left, 1), base + 2, axis, right),
            plan(cut(on_left, 0), cut(got_right, 0), base + 3, axis, left),
        ]
        self.later = [
            plan(to_right, cut(got_left, 0), base + 4, axis, right),
            plan(to_left, cut(got_right, 1), base + 5, axis, left),
        ]

    def start_far(self):
        for copy in self.far:
            copy.start()

    def start_near(self):
        for copy in self.near:
            copy.start()

    def start(self):
        self.start_far()
        self.start_near()
        return self

    def relay(self):
        for got, hop, on in zip(self.far, self.hops, self.later):
            got.wait_recv()
            added(*hop)
            on.start()

    def total(self):
        for copy in self.near + self.later:
            copy.wait_recv()
        total = self.mine[...].astype(f32)
        for part in self.got:
            total += part[...].astype(f32)
        return total

    def drain(self):
        for copy in self.far + self.near + self.later:
            copy.wait_send()


def remote_params(call_id):
    return pltpu.CompilerParams(
        collective_id=call_id, has_side_effects=True, vmem_limit_bytes=BIG
    )


def unit_scale(vector):
    return lax.rsqrt(jnp.mean(vector * vector, axis=-1, keepdims=True) + norm_eps)


def norm_back(vector, gain, grad):
    scale = unit_scale(vector)
    unit = vector * scale
    pulled = grad * gain
    back = scale * (pulled - unit * jnp.mean(pulled * unit, axis=-1, keepdims=True))
    return back, jnp.sum(unit * grad, axis=0, keepdims=True)


MAIN_E = LOCAL_E - 1


def pack_kernel(expand_ref, shrink_ref, out_ref, stage, stage_end, send_sem, recv_sem):
    core = lax.axis_index("core")
    greet([sibling()])
    send = sender(send_sem, recv_sem)
    other = 1 - core
    for e in range(LOCAL_E):
        theirs = other * LOCAL_E + e
        stage[e, :48] = expand_ref[theirs].astype(bf16)
        stage[e, 48:] = shrink_ref[theirs, :, :1024].astype(bf16)
        stage_end[e] = shrink_ref[theirs, :, 1024:].astype(bf16)
    main = pl.ds(pl.multiple_of(core * 48, 16), 48)
    left = pl.ds(pl.multiple_of(96 + core * 16, 16), 16)
    ends = pl.ds(pl.multiple_of(core * 512, 512), 512)
    copies = [
        send(stage.at[:, pl.ds(0, 48)], out_ref.at[:, main], 0, "core", other),
        send(stage.at[:, pl.ds(48, 16)], out_ref.at[:, left], 1, "core", other),
        send(stage_end, out_ref.at[:, pl.ds(128, 16), ends], 2, "core", other),
    ]
    for e in range(LOCAL_E):
        mine = core * LOCAL_E + e
        out_ref[e, main, :] = expand_ref[mine].astype(bf16)
        out_ref[e, left, :] = shrink_ref[mine, :, :1024].astype(bf16)
        out_ref[e, pl.ds(128, 16), ends] = shrink_ref[mine, :, 1024:].astype(bf16)
    for copy in copies:
        copy.wait()


def pack_experts(expand, shrink):
    return pl.pallas_call(
        pack_kernel,
        out_shape=jax.ShapeDtypeStruct((LOCAL_E, 144, 1024), bf16),
        in_specs=[VMEM] * 2,
        out_specs=VMEM,
        scratch_shapes=[
            pltpu.VMEM((LOCAL_E, 64, 1024), bf16),
            pltpu.VMEM((LOCAL_E, 16, 512), bf16),
        ]
        + sems(3),
        compiler_params=remote_params(1),
    )(expand, shrink)


def row_pick(shape, padded_axis):
    padded = lax.broadcasted_iota(jnp.int32, shape, padded_axis)
    plain = lax.broadcasted_iota(jnp.int32, shape, 1 - padded_axis)
    row = lax.rem(padded, 16)
    return ((plain == lax.div(padded, 16) * 12 + row) & (row < 12)).astype(bf16)


def start_kernel(
    in_ref, cot_ref, hit_ref, entry_ref, exit_ref,
    in_all, cot_all, hit_all, entry_out, shared_out, exit_out,
    hold, full, send_sem, recv_sem, copy_sem,
):
    z, x, y, c = (lax.axis_index(a) for a in ("seq", "x", "y", "core"))
    right, left, far = ring(z)
    greet(near("seq") + [("seq", far)] + near("x") + near("y") + [sibling()])
    send, plan = sender(send_sem, recv_sem), planner(send_sem, recv_sem)
    columns = [
        send(entry_ref.at[peer], hold.at[z], k, "seq", peer)
        for k, peer in enumerate((right, far, left))
    ]
    hits = Gather(plan, 3, "seq", hit_ref, lambda i: hit_all.at[i], half_rows).start()
    rows = Gather(plan, 9, "seq", in_ref, lambda i: in_all.at[i], half_rows).start()
    local = [
        pltpu.make_async_copy(entry_ref.at[z], hold.at[z], copy_sem.at[0]),
        pltpu.make_async_copy(exit_ref, hold.at[pl.ds(4, 2)], copy_sem.at[1]),
        pltpu.make_async_copy(hit_ref, hit_all.at[z], copy_sem.at[2]),
        pltpu.make_async_copy(in_ref, in_all.at[z], copy_sem.at[3]),
        pltpu.make_async_copy(cot_ref, cot_all.at[c, z], copy_sem.at[4]),
    ]
    for copy in local:
        copy.start()
    local[0].wait()
    local[1].wait()
    for copy in columns:
        copy.wait_recv()
    own = pltpu.make_async_copy(hold, full.at[:, x, y, c], copy_sem.at[5])
    own.start()
    low, high = pl.ds(0, 3), pl.ds(3, 3)
    low_x = Gather(plan, 15, "x", hold.at[low], lambda i: full.at[low, i, y, c], half_lanes)
    low_x.start()
    high_y = Gather(plan, 21, "y", hold.at[high], lambda i: full.at[high, x, i, c], half_lanes)
    high_y.start()
    hits.relay()
    low_x.relay()
    high_y.relay()
    rows.relay()
    cots = Gather(plan, 27, "seq", cot_ref, lambda i: cot_all.at[c, i], half_rows).start()
    own.wait()
    low_x.finish()

    def cut_low(ref, half):
        return ref.at[:, pl.ds(2 * half, 2)]

    low_y = Gather(
        plan, 33, "y", full.at[low, :, y, c], lambda i: full.at[low, :, i, c], cut_low
    ).start()
    high_y.finish()
    high_x = Gather(
        plan, 39, "x", full.at[high, x, :, c], lambda i: full.at[high, i, :, c], cut_low
    ).start()
    low_y.relay()
    high_x.relay()
    pairs = hand_over(send, 45, cot_ref, cot_all, cots)
    low_y.finish()
    half = full.at[low, :, :, c]
    last = [send(half, half, 49, "core", 1 - c)]
    high_x.finish()
    half = full.at[high, :, :, c]
    last.append(send(half, half, 50, "core", 1 - c))
    pick = row_pick((QOWN, 512), 1)
    for copy in last:
        copy.wait_recv()
    for block in range(4):
        got = dot(pick, full[block].reshape(512, WIDE), ((1,), (0,))).astype(bf16)
        entry_out[QOWN * block : QOWN * (block + 1), :] = got[:, :MIX_OWN]
        shared_out[QOWN * block : QOWN * (block + 1), :] = got[:, MIX_OWN:]
    for block in range(2):
        got = dot(pick, full[4 + block].reshape(512, WIDE), ((1,), (0,))).astype(bf16)
        exit_out[:, WIDE * block : WIDE * (block + 1)] = got
    hits.finish()
    rows.finish()
    for copy in pairs:
        copy.wait()
    for gather in (hits, rows, cots, low_x, high_y, low_y, high_x):
        gather.drain()
    for copy in columns + last:
        copy.wait_send()
    for copy in local[2:]:
        copy.wait()


def start(rows, cots, hits, entry_cols, exit_cols):
    return pl.pallas_call(
        start_kernel,
        out_shape=[
            jax.ShapeDtypeStruct((N_SEQ, TOK_DEV, D), bf16),
            jax.ShapeDtypeStruct((2, N_SEQ, TOK_DEV, D), bf16),
            jax.ShapeDtypeStruct((N_SEQ, TOK_DEV, 128), bf16),
            jax.ShapeDtypeStruct((D, MIX_OWN), bf16),
            jax.ShapeDtypeStruct((D, 128), bf16),
            jax.ShapeDtypeStruct((QOWN, D), bf16),
        ],
        in_specs=[ANY] * 3 + [VMEM] * 2,
        out_specs=[ANY] * 3 + [VMEM] * 3,
        scratch_shapes=[
            pltpu.VMEM((6, PAD_ROWS, WIDE), bf16),
            pltpu.VMEM((6, 4, 4, 2, PAD_ROWS, WIDE), bf16),
        ]
        + sems(51)
        + [pltpu.SemaphoreType.DMA((6,))],
        compiler_params=remote_params(2),
    )(rows, cots, hits, entry_cols, exit_cols)


def swap_halves(rows, lower, upper):
    lane = lax.broadcasted_iota(jnp.int32, rows.shape, 1)
    ahead = pltpu.roll(rows, rows.shape[1] - HD // 2, 1)
    behind = pltpu.roll(rows, HD // 2, 1)
    return jnp.where(lax.rem(lane, HD) < HD // 2, lower * ahead, upper * behind)


BLOCK = 256


def block_bias(seq_col_ref, seq_row_ref, block):
    keys = BLOCK * (block + 1)
    row = lax.broadcasted_iota(jnp.int32, (BLOCK, keys), 0) + BLOCK * block
    column = lax.broadcasted_iota(jnp.int32, (BLOCK, keys), 1)
    same = seq_col_ref[BLOCK * block : keys, :] == seq_row_ref[:, :keys]
    return jnp.where(same & (column <= row), 0.0, -1e30)


def head_of(index):
    return slice(HD * index, HD * (index + 1))


def middle_kernel(
    all_ref, gain_one_ref, entry_ref, cos_ref, sin_ref, seq_col_ref, seq_row_ref, exit_ref,
    in_ref, gain_ref,
    normed_ref, qkv_ref, attended_ref, lse_ref, middle_ref, tokens_ref,
    part, mine, *rest
):
    bufs, (send_sem, recv_sem, copy_sem) = rest[:6], rest[6:]
    me, core = lax.axis_index("seq"), lax.axis_index("core")
    greet(near("seq") + [sibling()])
    send, plan = sender(send_sem, recv_sem), planner(send_sem, recv_sem)
    for block in range(N_SEQ):
        rows = slice(TOK_DEV * block, TOK_DEV * (block + 1))
        vector = all_ref[block].astype(f32)
        normed_ref[rows, :] = (vector * unit_scale(vector) * gain_one_ref[...]).astype(bf16)
    mixed = dot(normed_ref[...], entry_ref[...], ((1,), (0,)))
    mixed = mixed * cos_ref[...] + swap_halves(mixed, -1.0, 1.0) * sin_ref[...]
    qkv_ref[...] = mixed.astype(bf16)
    for block in range(GROUP // BLOCK):
        bias = block_bias(seq_col_ref, seq_row_ref, block)
        keys = BLOCK * (block + 1)
        rows = slice(BLOCK * block, keys)
        for head in range(HEADS_OWN):
            pair = Q_OWN + 2 * HD * (head // PER_KV)
            key = qkv_ref[:keys, pair : pair + HD]
            value = qkv_ref[:keys, pair + HD : pair + 2 * HD]
            scores = dot(qkv_ref[rows, head_of(head)], key, ((1,), (1,))) * HD**-0.5 + bias
            peak = jnp.max(scores, axis=1, keepdims=True)
            expo = jnp.exp(scores - peak)
            total = jnp.sum(expo, axis=1, keepdims=True)
            probs = (expo / total).astype(bf16)
            attended_ref[rows, head_of(head)] = dot(probs, value, ((1,), (0,))).astype(bf16)
            lse_ref[rows, head : head + 1] = peak + jnp.log(total)
    part[...] = dot(attended_ref[...], exit_ref[...], ((1,), (0,))).astype(bf16).reshape(part.shape)
    reduce = Reduce(plan, 0, "seq", lambda i: part.at[i], bufs, half_rows).start()
    reduce.relay()
    middle = in_ref[...].astype(f32) + reduce.total()
    middle_ref[...] = middle
    mine[...] = (middle * unit_scale(middle) * gain_ref[...]).astype(bf16)
    gather = Gather(plan, 6, "seq", mine, lambda i: tokens_ref.at[core, i], half_rows).start()
    local = pltpu.make_async_copy(mine, tokens_ref.at[core, me], copy_sem)
    local.start()
    pairs = hand_over(send, 12, mine, tokens_ref, gather)
    for copy in pairs:
        copy.wait()
    for transfer in (gather, reduce):
        transfer.drain()
    local.wait()


def middle_tokens(*operands):
    return pl.pallas_call(
        middle_kernel,
        out_shape=[
            jax.ShapeDtypeStruct((GROUP, D), bf16),
            jax.ShapeDtypeStruct((GROUP, MIX_OWN), bf16),
            jax.ShapeDtypeStruct((GROUP, Q_OWN), bf16),
            jax.ShapeDtypeStruct((GROUP, HEADS_OWN), f32),
            jax.ShapeDtypeStruct((TOK_DEV, D), f32),
            jax.ShapeDtypeStruct((2, N_SEQ, TOK_DEV, D), bf16),
        ],
        in_specs=[VMEM] * 10,
        out_specs=[VMEM] * 5 + [ANY],
        scratch_shapes=[pltpu.VMEM((N_SEQ, TOK_DEV, D), bf16), pltpu.VMEM((TOK_DEV, D), bf16)]
        + reduce_scratch((TOK_DEV, D), (HALF, D))
        + sems(16)
        + [pltpu.SemaphoreType.DMA],
        compiler_params=remote_params(3),
    )(*operands)


def turn_kernel(
    rank_ref, up_ref, hidden_ref, gate_ref, cot_rows_ref, w_ref,
    line, middle_ref, cot_ref, my_gate_ref, router_ref, gain_ref,
    grad_ref, branch_ref, logit_ref, gain_grad_ref, out_sum_ref, extra_sum_ref,
    back_s, out_s, other_back, from_core, part, other_out, out_core, mine, *rest
):
    bufs, (send_sem, recv_sem, copy_sem) = [rest[6 * i : 6 * i + 6] for i in range(3)], rest[18:]
    e = pl.program_id(0)
    me, core = lax.axis_index("seq"), lax.axis_index("core")
    send, plan = sender(send_sem, recv_sem), planner(send_sem, recv_sem)
    low_y = Reduce(plan, 17, "y", lambda i: line.at[0, i], bufs[1], half_lanes)
    high_x = Reduce(plan, 23, "x", lambda i: line.at[1, i], bufs[2], half_lanes)

    @pl.when(e == 0)
    def _():
        greet(near("seq") + near("x") + near("y") + [sibling()])
        low_y.start()
        high_x.start()

    @pl.when(e == 2)
    def _():
        low_y.relay()
        high_x.relay()

    @pl.when(e < LOCAL_E)
    def _():
        expand, left, right = weights_of(w_ref)
        at = pl.ds(pl.multiple_of(e * SLOTS, SLOTS), SLOTS)
        back_s[at, :D] = dot(up_ref[0], expand, ((1,), (1,))).astype(bf16)
        hidden = hidden_ref[0]
        expert_out = jnp.concatenate(
            [dot(hidden, left, ((1,), (0,))), dot(hidden, right, ((1,), (0,)))], axis=1
        )
        expert_out = expert_out.astype(bf16).astype(f32)
        gate_grad = jnp.sum(expert_out * cot_rows_ref[0].astype(f32), axis=1, keepdims=True)
        lane = lax.broadcasted_iota(jnp.int32, (SLOTS, 128), 1)
        column = (me * 2 + core) * LOCAL_E + e
        back_s[at, D:] = jnp.where(lane == column, gate_grad, 0.0).astype(bf16)
        out_s[at, :] = (gate_ref[0] * expert_out).astype(bf16)

    @pl.when(e == LOCAL_E)
    def _():
        other = 1 - core
        right, left, far = ring(me)
        slot = lax.broadcasted_iota(jnp.int32, (GROUP, SLOTS), 1)

        def picks(group):
            at = pl.ds(pl.multiple_of(group * GROUP, GROUP), GROUP)
            ranks = rank_ref[at, :]
            return jnp.concatenate(
                [(ranks[:, k : k + 1] == slot).astype(bf16) for k in range(LOCAL_E)], axis=1
            )

        theirs, ours = picks(other), picks(core)
        order = (far, right, left, me)
        other_back[...] = (
            dot(theirs, back_s[...], ((1,), (0,))).astype(bf16).reshape(other_back.shape)
        )
        swaps = [
            send(other_back.at[block], from_core.at[block], 12 + i, "core", other)
            for i, block in enumerate(order)
        ]
        part[...] = dot(ours, back_s[...], ((1,), (0,))).astype(bf16).reshape(part.shape)
        reduce = Reduce(plan, 0, "seq", lambda i: part.at[i], bufs[0], half_rows)
        for i, block in enumerate(order):
            swaps[i].wait_recv()
            added(part.at[block], part.at[block], from_core.at[block])
            if i == 0:
                reduce.start_far()
            if i == 2:
                reduce.start_near()
        other_out[...] = (
            dot(theirs, out_s[...], ((1,), (0,))).astype(bf16).reshape(other_out.shape)
        )
        out_swap = send(other_out, out_core, 16, "core", other)
        reduce.relay()
        out_sum_ref[...] = (
            dot(ours, out_s[...], ((1,), (0,))).astype(bf16).reshape(out_sum_ref.shape)
        )
        total = reduce.total()
        gates, gate_grad = my_gate_ref[...], total[:, D:]
        mean_term = jnp.sum(gates * gate_grad, axis=1, keepdims=True)
        logit_grad = (gates * (gate_grad - mean_term)).astype(bf16)
        logit_ref[...] = logit_grad
        normed_grad = total[:, :D] + dot(logit_grad, router_ref[...], ((1,), (1,)))
        back, gain_grad = norm_back(middle_ref[...], gain_ref[...], normed_grad)
        gain_grad_ref[...] = gain_grad
        middle_grad = cot_ref[...].astype(f32) + back
        grad_ref[...] = middle_grad
        mine[...] = middle_grad.astype(bf16)
        gather = Gather(plan, 6, "seq", mine, lambda i: branch_ref.at[i], half_rows).start()
        local = pltpu.make_async_copy(mine, branch_ref.at[me], copy_sem)
        local.start()
        out_swap.wait_recv()
        added(out_sum_ref, out_sum_ref, out_core)
        gather.relay()
        extra_sum_ref[:, :512] = low_y.total().astype(bf16)
        extra_sum_ref[:, 512:] = high_x.total().astype(bf16)
        gather.finish()
        for transfer in (gather, reduce, low_y, high_x):
            transfer.drain()
        for copy in swaps + [out_swap]:
            copy.wait_send()
        local.wait()


BACK_WIDTH = D + 128


def turn(*operands):
    one = lambda e: (jnp.minimum(e, LOCAL_E - 1), 0, 0)
    wide = lambda e: (0, jnp.minimum(e, LOCAL_E - 1), 0, 0)
    cubes = lambda e: (0, 0, 0, 0)
    whole = lambda e: (0, 0)
    blocks = lambda e: (0, 0, 0)
    row_block = pl.BlockSpec((TOK_DEV, D), whole)
    lane_block = pl.BlockSpec((TOK_DEV, 128), whole)
    gain_block = pl.BlockSpec((1, D), whole)
    group = pltpu.VMEM((N_SEQ, TOK_DEV, BACK_WIDTH), bf16)
    group_out = pltpu.VMEM((N_SEQ, TOK_DEV, D), bf16)
    return pl.pallas_call(
        turn_kernel,
        grid=(LOCAL_E + 1,),
        in_specs=[
            pl.BlockSpec((PAIR_TOK, LOCAL_E), whole),
            pl.BlockSpec((1, SLOTS, 2 * FF), one),
            pl.BlockSpec((1, SLOTS, FF), one),
            pl.BlockSpec((1, SLOTS, 1), one),
            pl.BlockSpec((1, SLOTS, D), one),
            pl.BlockSpec((16, 1, 144, 1024), wide),
            pl.BlockSpec((2, 4, 144, 512), cubes),
            row_block,
            row_block,
            lane_block,
            pl.BlockSpec((D, 128), whole),
            gain_block,
        ],
        out_specs=[
            row_block,
            ANY,
            lane_block,
            gain_block,
            pl.BlockSpec((N_SEQ, TOK_DEV, D), blocks),
            pl.BlockSpec((144, 1024), whole),
        ],
        out_shape=[
            jax.ShapeDtypeStruct((TOK_DEV, D), f32),
            jax.ShapeDtypeStruct((N_SEQ, TOK_DEV, D), bf16),
            jax.ShapeDtypeStruct((TOK_DEV, 128), bf16),
            jax.ShapeDtypeStruct((1, D), f32),
            jax.ShapeDtypeStruct((N_SEQ, TOK_DEV, D), bf16),
            jax.ShapeDtypeStruct((144, 1024), bf16),
        ],
        scratch_shapes=[
            pltpu.VMEM((LOCAL_E * SLOTS, BACK_WIDTH), bf16),
            pltpu.VMEM((LOCAL_E * SLOTS, D), bf16),
            group,
            group,
            group,
            group_out,
            group_out,
            pltpu.VMEM((TOK_DEV, D), bf16),
        ]
        + reduce_scratch((TOK_DEV, BACK_WIDTH), (HALF, BACK_WIDTH))
        + reduce_scratch((144, 512), (144, 256)) * 2
        + sems(29)
        + [pltpu.SemaphoreType.DMA],
        compiler_params=remote_params(4),
        cost_estimate=pl.CostEstimate(
            flops=6 * LOCAL_E * SLOTS * D * FF + 4 * LOCAL_E * SLOTS * PAIR_TOK * D,
            bytes_accessed=40 << 20,
            transcendentals=0,
        ),
    )(*operands)


PAD_ROWS = 16
WIDE = 768
def closing_kernel(
    qkv_ref, lse_ref, cos_ref, sin_ref, seq_col_ref, seq_row_ref, exit_ref, entry_ref,
    in_ref, grad_ref, gain_ref, normed_ref, attended_ref, branch_ref,
    router_grad_ref, gain_two_ref, out_sum_ref, middle_ref,
    input_ref, block_ref, entry_out, exit_out,
    turned, mixed_grad, part, full, from_core, chip, line, final, give, got_z, *rest
):
    bufs, (send_sem, recv_sem) = [rest[6 * i : 6 * i + 6] for i in range(8)], rest[48:]
    z, x, y, c = (lax.axis_index(a) for a in ("seq", "x", "y", "core"))
    right, left, far = ring(z)
    greet(near("seq") + [("seq", far)] + near("x") + near("y") + [sibling()])
    send, plan = sender(send_sem, recv_sem), planner(send_sem, recv_sem)
    pick = row_pick((512, QOWN), 0)

    def spread(grad):
        wide = dot(pick, grad, ((1,), (0,))).astype(bf16)
        return wide.reshape(16, 2, PAD_ROWS, grad.shape[1])

    def swap(side):
        return send(full.at[side, :, 1 - c], from_core.at[side], 48 + side, "core", 1 - c)

    def chip_sum(side, copy):
        copy.wait_recv()
        for plane in range(16):
            first, second = (plane % 4, plane // 4) if side == 2 else (plane // 4, plane % 4)
            added(chip.at[side, first, second], full.at[side, plane, c], from_core.at[side, plane])

    def first_sum(side, axis):
        return Reduce(
            plan, 6 * side, axis, lambda i: chip.at[side, i], bufs[side], half_rows
        ).start()

    def second_sum(side, axis, reduce):
        line[side] = reduce.total().astype(bf16)
        return Reduce(
            plan, 18 + 6 * side, axis, lambda i: line.at[side, i], bufs[3 + side], half_lanes
        ).start()

    for block in range(3):
        cols = slice(512 * block, 512 * (block + 1))
        grad = dot(attended_ref[...], branch_ref[:, cols], ((0,), (0,))).astype(bf16)
        full[0, :, :, :, cols] = spread(grad)
    swaps = [swap(0)]
    outs = Reduce(plan, 36, "seq", lambda i: out_sum_ref.at[i], bufs[6], half_rows).start()

    def turn_back(kv):
        pair = Q_OWN + 2 * HD * kv
        for head in range(PER_KV * kv, PER_KV * (kv + 1)):
            grad = dot(branch_ref[...], exit_ref[head_of(head), :], ((1,), (1,))).astype(bf16)
            attended = attended_ref[:, head_of(head)].astype(f32)
            delta = jnp.sum(grad.astype(f32) * attended, axis=1, keepdims=True)
            for block in range(GROUP // BLOCK):
                bias = block_bias(seq_col_ref, seq_row_ref, block)
                keys = BLOCK * (block + 1)
                rows = slice(BLOCK * block, keys)
                key = qkv_ref[:keys, pair : pair + HD]
                value = qkv_ref[:keys, pair + HD : pair + 2 * HD]
                query, grad_rows = qkv_ref[rows, head_of(head)], grad[rows]
                scores = dot(query, key, ((1,), (1,))) * HD**-0.5 + bias
                probs = jnp.exp(scores - lse_ref[rows, head : head + 1])
                prob_grad = dot(grad_rows, value, ((1,), (1,)))
                score_grad = probs * (prob_grad - delta[rows]) * HD**-0.5
                score_grad = score_grad.astype(bf16)
                turned[rows, head_of(head)] = dot(score_grad, key, ((1,), (0,)))
                key_grad = dot(score_grad, query, ((0,), (0,)))
                value_grad = dot(probs.astype(bf16), grad_rows, ((0,), (0,)))
                if head == PER_KV * kv and block == GROUP // BLOCK - 1:
                    turned[:, pair : pair + HD] = key_grad
                    turned[:, pair + HD : pair + 2 * HD] = value_grad
                    turned[:BLOCK, pair : pair + HD] += held[0]
                    turned[:BLOCK, pair + HD : pair + 2 * HD] += held[1]
                elif head == PER_KV * kv:
                    held = (key_grad, value_grad)
                else:
                    turned[:keys, pair : pair + HD] += key_grad
                    turned[:keys, pair + HD : pair + 2 * HD] += value_grad

    turn_back(0)
    chip_sum(0, swaps[0])
    first_0 = first_sum(0, "x")
    outs.relay()
    turn_back(1)
    first_0.relay()
    grads = turned[...]
    grads = grads * cos_ref[...] + swap_halves(grads, 1.0, -1.0) * sin_ref[...]
    mixed_grad[...] = grads.astype(bf16)
    part[...] = (
        dot(mixed_grad[...], entry_ref[...], ((1,), (1,))).astype(bf16).reshape(part.shape)
    )
    rows = Reduce(plan, 42, "seq", lambda i: part.at[i], bufs[7], half_rows).start()

    def entry_rows(block):
        rows_of = slice(QOWN * block, QOWN * (block + 1))
        grad = dot(normed_ref[:, rows_of], mixed_grad[...], ((0,), (0,))).astype(bf16)
        return spread(grad)

    full[1, :, :, :, :640] = entry_rows(0)
    full[1, :, :, :, 640:1280] = entry_rows(1)
    third = entry_rows(2)
    full[1, :, :, :, 1280:] = third[..., :256]
    swaps.append(swap(1))
    rows.relay()
    second_0 = second_sum(0, "y", first_0)
    full[2, :, :, :, :384] = third[..., 256:]
    full[2, :, :, :, 384:1024] = entry_rows(3)
    chip_sum(1, swaps[1])
    first_1 = first_sum(1, "x")
    back, gain_one = norm_back(in_ref[...].astype(f32), gain_ref[...], rows.total())
    input_ref[...] = grad_ref[...] + back
    row_of = lax.broadcasted_iota(jnp.int32, (128, D), 0)
    gains = jnp.where(row_of == EXPERTS, gain_one, 0.0)
    gains = jnp.where(row_of == EXPERTS + 1, gain_two_ref[...], gains)
    shared = router_grad_ref[...] + gains.T
    for block in range(4):
        shared_rows = shared[QOWN * block : QOWN * (block + 1), :].astype(bf16)
        full[2, :, :, :, 1024 + 128 * block : 1152 + 128 * block] = spread(shared_rows)
    swaps.append(swap(2))
    second_0.relay()
    block_ref[...] = middle_ref[...] + outs.total()
    chip_sum(2, swaps[2])
    first_2 = first_sum(2, "y")
    first_1.relay()
    first_2.relay()
    exit_out[...] = second_0.total()
    second_1 = second_sum(1, "y", first_1)
    second_2 = second_sum(2, "x", first_2)
    second_1.relay()
    second_2.relay()
    final[0] = second_1.total()
    final[1] = second_2.total()
    give[0, :, :MIX_OWN] = final[0, :, :640]
    give[1, :, :MIX_OWN] = final[0, :, 640:1280]
    give[2, :, :256] = final[0, :, 1280:]
    give[2, :, 256:MIX_OWN] = final[1, :, :384]
    give[3, :, :MIX_OWN] = final[1, :, 384:1024]
    for block in range(4):
        give[block, :, MIX_OWN:] = final[1, :, 1024 + 128 * block : 1152 + 128 * block]
    home = [
        send(give.at[peer], got_z.at[k], 51 + k, "seq", peer)
        for k, peer in enumerate((right, far, left))
    ]
    entry_out[z] = give[z]
    for k, source in enumerate((left, far, right)):
        home[k].wait_recv()
        entry_out[source] = got_z[k]
    for copy in swaps + home:
        copy.wait_send()
    for reduce in (rows, outs, first_0, first_1, first_2, second_0, second_1, second_2):
        reduce.drain()


def closing(*operands):
    row_bufs = reduce_scratch((TOK_DEV, D), (HALF, D))
    chip_bufs = reduce_scratch((4, PAD_ROWS, D), (2, PAD_ROWS, D))
    line_bufs = reduce_scratch((PAD_ROWS, D), (PAD_ROWS, D // 2))
    tile = (PAD_ROWS, D)
    return pl.pallas_call(
        closing_kernel,
        out_shape=[
            jax.ShapeDtypeStruct((TOK_DEV, D), f32),
            jax.ShapeDtypeStruct((TOK_DEV, D), f32),
            jax.ShapeDtypeStruct((4, PAD_ROWS, WIDE), f32),
            jax.ShapeDtypeStruct((PAD_ROWS, D), f32),
        ],
        in_specs=[VMEM] * len(operands),
        out_specs=[VMEM] * 4,
        scratch_shapes=[
            pltpu.VMEM((GROUP, MIX_OWN), f32),
            pltpu.VMEM((GROUP, MIX_OWN), bf16),
            pltpu.VMEM((N_SEQ, TOK_DEV, D), bf16),
            pltpu.VMEM((3, 16, 2) + tile, bf16),
            pltpu.VMEM((3, 16) + tile, bf16),
            pltpu.VMEM((3, 4, 4) + tile, bf16),
            pltpu.VMEM((3, 4) + tile, bf16),
            pltpu.VMEM((2,) + tile, f32),
            pltpu.VMEM((4, PAD_ROWS, WIDE), f32),
            pltpu.VMEM((3, PAD_ROWS, WIDE), f32),
        ]
        + chip_bufs * 3
        + line_bufs * 3
        + row_bufs * 2
        + sems(54),
        compiler_params=remote_params(5),
    )(*operands)


def owner_kernel(sum_ref, extra_ref, expand_ref, shrink_ref, send_sem, recv_sem, copy_sem):
    core = lax.axis_index("core")
    greet([sibling()])
    send = sender(send_sem, recv_sem)
    most, single = pl.ds(core * LOCAL_E + 1, MAIN_E), core * LOCAL_E

    def pieces(owner):
        rows = pl.ds(pl.multiple_of(owner * 48, 16), 48)
        left = pl.ds(pl.multiple_of(96 + owner * 16, 16), 16)
        ends = pl.ds(pl.multiple_of(owner * 512, 512), 512)
        low, start, end = pl.ds(128, 16), pl.ds(0, 1024), pl.ds(1024, 512)
        return [
            (sum_ref.at[:, rows], expand_ref.at[most]),
            (sum_ref.at[:, left], shrink_ref.at[most, :, start]),
            (sum_ref.at[:, low, ends], shrink_ref.at[most, :, end]),
            (extra_ref.at[rows], expand_ref.at[single]),
            (extra_ref.at[left], shrink_ref.at[single, :, start]),
            (extra_ref.at[low, ends], shrink_ref.at[single, :, end]),
        ]

    copies = [
        send(source, target, k, "core", 1 - core)
        for k, (source, target) in enumerate(pieces(1 - core))
    ]
    for k, (source, target) in enumerate(pieces(core)):
        copies.append(pltpu.make_async_copy(source, target, copy_sem.at[k]))
        copies[-1].start()
    for copy in copies:
        copy.wait()


def to_owners(summed, extra):
    return pl.pallas_call(
        owner_kernel,
        out_shape=[
            jax.ShapeDtypeStruct((2 * LOCAL_E, 48, 1024), bf16),
            jax.ShapeDtypeStruct((2 * LOCAL_E, 16, D), bf16),
        ],
        in_specs=[VMEM] * 2,
        out_specs=[VMEM] * 2,
        scratch_shapes=sems(6) + [pltpu.SemaphoreType.DMA((6,))],
        compiler_params=remote_params(6),
    )(summed, extra)


def dispatch_kernel(rank_ref, gate_ref, tokens_ref, cots_ref, rows_ref, cot_rows_ref, row_gate_ref):
    slot = lax.broadcasted_iota(jnp.int32, (SLOTS, PAIR_TOK), 0)
    match = rank_ref[0] == slot
    row_gate_ref[0] = jnp.sum(jnp.where(match, gate_ref[0], 0.0), axis=1, keepdims=True)
    pick = match.astype(bf16)
    for j in range(3):
        cols = slice(512 * j, 512 * (j + 1))
        rows_ref[0, :, cols] = dot(pick, tokens_ref[:, cols], ((1,), (0,))).astype(bf16)
        cot_rows_ref[0, :, cols] = dot(pick, cots_ref[:, cols], ((1,), (0,))).astype(bf16)

def dispatch(rank, gates, tokens, cots):
    one = lambda e: (e, 0, 0)
    whole = lambda e: (0, 0)
    return pl.pallas_call(
        dispatch_kernel,
        grid=(LOCAL_E,),
        in_specs=[
            pl.BlockSpec((1, 1, PAIR_TOK), one),
            pl.BlockSpec((1, 1, PAIR_TOK), one),
            pl.BlockSpec((PAIR_TOK, D), whole),
            pl.BlockSpec((PAIR_TOK, D), whole),
        ],
        out_specs=[
            pl.BlockSpec((1, SLOTS, D), one),
            pl.BlockSpec((1, SLOTS, D), one),
            pl.BlockSpec((1, SLOTS, 1), one),
        ],
        out_shape=[
            jax.ShapeDtypeStruct((LOCAL_E, SLOTS, D), bf16),
            jax.ShapeDtypeStruct((LOCAL_E, SLOTS, D), bf16),
            jax.ShapeDtypeStruct((LOCAL_E, SLOTS, 1), f32),
        ],
        compiler_params=pltpu.CompilerParams(vmem_limit_bytes=BIG),
        cost_estimate=pl.CostEstimate(
            flops=4 * LOCAL_E * SLOTS * PAIR_TOK * D, bytes_accessed=16 << 20, transcendentals=0
        ),
    )(rank[:, None], gates[:, None], tokens, cots)

def weights_of(w_ref):
    expand = w_ref[:, 0, :96, :].reshape(D, 2 * FF)
    left = w_ref[:, 0, 96:128, :].reshape(FF, 1024)
    right = jnp.concatenate([w_ref[:, 0, 128:144, :512], w_ref[:, 0, 128:144, 512:]], axis=1)
    return expand, left, right.reshape(FF, 512)

def grads_kernel(
    rows_ref, cot_ref, gate_ref, w_ref, hidden_ref, up_ref, out_ref, line_ref, own, *rest
):
    bufs, (send_sem, recv_sem) = [rest[6 * i : 6 * i + 6] for i in range(2)], rest[12:]
    e = pl.program_id(0)
    plan = planner(send_sem, recv_sem)
    low, high = pl.ds(0, 512), pl.ds(512, 512)
    low_x = Reduce(plan, 0, "x", lambda i: own.at[i, :, :, low], bufs[0], half_rows)
    high_y = Reduce(plan, 6, "y", lambda i: own.at[:, i, :, high], bufs[1], half_rows)

    @pl.when(e == 0)
    def _():
        greet(near("x") + near("y"))

    expand, left, right = weights_of(w_ref)
    grad_rows = (gate_ref[0] * cot_ref[0].astype(f32)).astype(bf16)
    rows = rows_ref[0]
    gate_pre = dot(rows, expand[:, :FF], ((1,), (0,)))
    up_part = dot(rows, expand[:, FF:], ((1,), (0,)))
    sig = jax.nn.sigmoid(gate_pre)
    hidden = (gate_pre * sig * up_part).astype(bf16)
    hidden_ref[0] = hidden

    @pl.when(e == 2)
    def _():
        low_x.relay()
        high_y.relay()

    hidden_grad = dot(grad_rows[:, :1024], left, ((1,), (1,))) + dot(
        grad_rows[:, 1024:], right, ((1,), (1,))
    )
    up_ref[0, :, :FF] = (hidden_grad * up_part * sig * (1.0 + gate_pre * (1.0 - sig))).astype(bf16)
    up_ref[0, :, FF:] = (hidden_grad * gate_pre * sig).astype(bf16)

    def write(shrink_at, end_at, expand_at):
        grad_left = dot(hidden, grad_rows[:, :1024], ((0,), (0,))).astype(bf16)
        grad_right = dot(hidden, grad_rows[:, 1024:], ((0,), (0,))).astype(bf16)
        grad_right = grad_right.reshape(4, 4, 32, 512)
        shrink_at(grad_left.reshape(4, 4, 32, 1024))
        end_at(grad_right[:, :, :16], grad_right[:, :, 16:])
        up_grad = up_ref[0]
        for j in range(4):
            part = dot(rows[:, 384 * j : 384 * (j + 1)], up_grad, ((0,), (0,))).astype(bf16)
            expand_at(j, part.reshape(4, 96, 1024))

    @pl.when(e == 0)
    def _():
        def shrink_at(value):
            own[:, :, 96:128, :] = value

        def end_at(first, second):
            own[:, :, 128:144, :512] = first
            own[:, :, 128:144, 512:] = second

        def expand_at(j, value):
            own[j, :, :96, :] = value

        write(shrink_at, end_at, expand_at)
        low_x.start()
        high_y.start()

    @pl.when(e > 0)
    def _():
        def shrink_at(value):
            out_ref[:, :, 0, 96:128, :] = value

        def end_at(first, second):
            out_ref[:, :, 0, 128:144, :512] = first
            out_ref[:, :, 0, 128:144, 512:] = second

        def expand_at(j, value):
            out_ref[j, :, 0, :96, :] = value

        write(shrink_at, end_at, expand_at)

    @pl.when(e == LOCAL_E - 1)
    def _():
        line_ref[0] = low_x.total().astype(bf16)
        line_ref[1] = high_y.total().astype(bf16)
        low_x.drain()
        high_y.drain()


def expert_grads(rows, cot_rows, row_gates, weights):
    one = lambda e: (e, 0, 0)
    wide = lambda e: (0, e, 0, 0)
    out = lambda e: (0, 0, jnp.maximum(e - 1, 0), 0, 0)
    return pl.pallas_call(
        grads_kernel,
        grid=(LOCAL_E,),
        in_specs=[
            pl.BlockSpec((1, SLOTS, D), one),
            pl.BlockSpec((1, SLOTS, D), one),
            pl.BlockSpec((1, SLOTS, 1), one),
            pl.BlockSpec((16, 1, 144, 1024), wide),
        ],
        out_specs=[
            pl.BlockSpec((1, SLOTS, FF), one),
            pl.BlockSpec((1, SLOTS, 2 * FF), one),
            pl.BlockSpec((4, 4, 1, 144, 1024), out),
            pl.BlockSpec((2, 4, 144, 512), lambda e: (0, 0, 0, 0)),
        ],
        out_shape=[
            jax.ShapeDtypeStruct((LOCAL_E, SLOTS, FF), bf16),
            jax.ShapeDtypeStruct((LOCAL_E, SLOTS, 2 * FF), bf16),
            jax.ShapeDtypeStruct((4, 4, MAIN_E, 144, 1024), bf16),
            jax.ShapeDtypeStruct((2, 4, 144, 512), bf16),
        ],
        scratch_shapes=[pltpu.VMEM((4, 4, 144, 1024), bf16)]
        + reduce_scratch((4, 144, 512), (2, 144, 512)) * 2
        + sems(12),
        compiler_params=remote_params(7),
        cost_estimate=pl.CostEstimate(
            flops=12 * LOCAL_E * SLOTS * D * FF, bytes_accessed=60 << 20, transcendentals=0
        ),
    )(rows, cot_rows, row_gates, weights)


def core_swap(value):
    return lax.ppermute(value, "core", [(0, 1), (1, 0)])


def core_order(core, mine, other, axis):
    return jnp.concatenate(
        [jnp.where(core == 0, mine, other), jnp.where(core == 0, other, mine)], axis=axis
    )


def norm_apply(vector, gain):
    scale = lax.rsqrt(jnp.mean(vector * vector, axis=-1, keepdims=True) + norm_eps)
    return vector * scale * gain


def adamw_step(weight, gradient, mean_old, square_old, rate, decay):
    drift = beta_first * mean_old + (1.0 - beta_first) * gradient
    spread = beta_second * square_old + (1.0 - beta_second) * gradient * gradient
    mean_hat = drift / (1.0 - beta_first**STEP)
    square_hat = spread / (1.0 - beta_second**STEP)
    master = weight - rate * (mean_hat / (jnp.sqrt(square_hat) + adam_eps) + decay * weight)
    return (drift, spread, master)


def rotate(vector, cosine, sine):
    first, second = vector[..., : HD // 2], vector[..., HD // 2 :]
    return jnp.concatenate(
        [first * cosine - second * sine, second * cosine + first * sine], axis=-1
    )


def on_device(
    activations,
    cotangent,
    seq_lengths,
    deal_order,
    routes,
    entry_weight,
    entry_mean,
    entry_square,
    exit_weight,
    exit_mean,
    exit_square,
    router_weight,
    router_mean,
    router_square,
    expand_weight,
    expand_mean,
    expand_square,
    shrink_weight,
    shrink_mean,
    shrink_square,
    norm_gains,
    gains_mean,
    gains_square,
):
    seq = lax.axis_index("seq")
    core = lax.axis_index("core")
    first = (seq * 2 + core) * LOCAL_E

    packed = pack_experts(expand_weight, shrink_weight)
    packed, rows_in, cots_in = lax.optimization_barrier((packed, activations[0], cotangent[0]))
    weights = lax.all_gather(packed, PLANE, axis=0, tiled=False)

    entry_b = entry_weight.astype(bf16)
    shared_b = jnp.concatenate([router_weight, norm_gains.T], axis=1).astype(bf16)
    shared_b = jnp.pad(shared_b, ((0, 0), (0, 128 - EXPERTS - 2)))
    entry_cols = jnp.concatenate(
        [
            entry_b[:, : QH * HD].reshape(ROWS, N_SEQ, Q_OWN).transpose(1, 0, 2),
            entry_b[:, QH * HD :].reshape(ROWS, N_SEQ, KV_OWN).transpose(1, 0, 2),
            jnp.broadcast_to(shared_b[None], (N_SEQ, ROWS, 128)),
        ],
        axis=2,
    )
    exit_cols = exit_weight.astype(bf16).reshape(ROWS, 2, WIDE).transpose(1, 0, 2)
    pad = ((0, 0), (0, PAD_ROWS - ROWS), (0, 0))
    expert_ids = jnp.arange(128, dtype=jnp.int32)
    hit_slots = jnp.any(routes[0][:, :, None] == expert_ids[None, None, :], axis=1).astype(bf16)
    in_all, cots, hit_slots, entry_own, shared, exit_own = start(
        rows_in, cots_in, hit_slots, jnp.pad(entry_cols, pad), jnp.pad(exit_cols, pad)
    )
    gains_full = shared[:, EXPERTS : EXPERTS + 2].astype(f32).T

    order_row = deal_order[0]
    token = jnp.arange(GROUP, dtype=jnp.int32)
    back_hot = (order_row[None, :] == token[:, None]).astype(bf16)
    hit = dot(back_hot, hit_slots.reshape(GROUP, 128), ((1,), (0,))).astype(bf16)
    hits = core_order(core, hit, core_swap(hit), 0)[:, :EXPERTS]
    own_hits = lax.dynamic_slice_in_dim(hits, first, LOCAL_E, 1)
    rank = jnp.cumsum(own_hits.astype(jnp.int32), axis=0) - 1
    rank = jnp.where(own_hits > 0, rank, -1)
    seq_ends = jnp.cumsum(seq_lengths[0])
    starts = seq_ends - seq_lengths[0]
    seq_ids = jnp.sum((token[:, None] >= seq_ends[None, :]).astype(jnp.int32), axis=1)
    seq_match = seq_ids[:, None] == jnp.arange(seq_ends.shape[0], dtype=jnp.int32)[None, :]
    positions = token - jnp.sum(jnp.where(seq_match, starts[None, :], 0), axis=1)
    frequency = rope_base ** (-jnp.arange(HD // 2, dtype=f32) * 2.0 / HD)
    phase = positions.astype(f32)[:, None] * frequency[None, :]
    ones = jnp.ones((GROUP, HD), f32)
    cosine, sine = jnp.tile(jnp.cos(phase), (1, 2)), jnp.tile(jnp.sin(phase), (1, 2))
    cosine = jnp.concatenate(
        [jnp.tile(cosine, (1, HEADS_OWN))] + [cosine, ones] * KV_HEADS_OWN, axis=1
    )
    sine = jnp.concatenate(
        [jnp.tile(sine, (1, HEADS_OWN))] + [sine, 0.0 * ones] * KV_HEADS_OWN, axis=1
    )
    angles = (cosine, sine, seq_ids[:, None], seq_ids[None, :])

    normed, qkv, attended, lse, middle, tokens = middle_tokens(
        in_all,
        gains_full[0:1],
        entry_own,
        *angles,
        exit_own,
        activations[0],
        gains_full[1:2],
    )
    normed_two = lax.dynamic_slice(tokens, (core, seq, 0, 0), (1, 1, TOK_DEV, D))[0, 0]
    tokens = tokens.reshape(PAIR_TOK, D)

    logits = dot(tokens, shared[:, :EXPERTS], ((1,), (0,)))
    masked = jnp.where(hits > 0, logits, -jnp.inf)
    gate_expo = jnp.exp(masked - jnp.max(masked, axis=1, keepdims=True))
    gates = gate_expo / jnp.sum(gate_expo, axis=1, keepdims=True)
    own_gates = lax.dynamic_slice_in_dim(gates, first, LOCAL_E, 1)
    rows, cot_rows, row_gates = dispatch(rank.T, own_gates.T, tokens, cots.reshape(PAIR_TOK, D))
    hidden, up_grad, expert_grad, line = expert_grads(rows, cot_rows, row_gates, weights)
    expert_grad = expert_grad.reshape(16, MAIN_E, 144, 1024)
    expert_sum = lax.psum_scatter(expert_grad, PLANE, scatter_dimension=0, tiled=False)
    my_gates = lax.dynamic_slice_in_dim(gates, core * GROUP + seq * TOK_DEV, TOK_DEV, 0)
    my_gates = jnp.pad(my_gates, ((0, 0), (0, 128 - EXPERTS)))
    middle_grad, branch_grad, logit_grad, gain_two_grad, out_sum, extra_sum = turn(
        rank,
        up_grad,
        hidden,
        row_gates,
        cot_rows,
        weights,
        line,
        middle,
        cotangent[0],
        my_gates,
        shared,
        gains_full[1:2],
    )
    branch_grad = branch_grad.reshape(GROUP, D)
    router_grad = dot(normed_two, logit_grad, ((0,), (0,)))

    input_rows, block_rows, entry_got, exit_got = closing(
        qkv,
        lse,
        *angles,
        exit_own,
        entry_own,
        activations[0],
        middle_grad,
        gains_full[0:1],
        normed,
        attended,
        branch_grad,
        router_grad,
        gain_two_grad,
        out_sum,
        middle,
    )

    input_grad, block_output = input_rows.astype(bf16), block_rows.astype(bf16)

    entry_got = entry_got[:, :ROWS]
    entry_sum = jnp.concatenate(
        [
            entry_got[:, :, :Q_OWN].transpose(1, 0, 2).reshape(ROWS, QH * HD),
            entry_got[:, :, Q_OWN:MIX_OWN].transpose(1, 0, 2).reshape(ROWS, 2 * KVH * HD),
        ],
        axis=1,
    )
    shared_sum = jnp.sum(entry_got[:, :, MIX_OWN:], axis=0)
    router_sum = shared_sum[:, :EXPERTS]
    gains_sum = shared_sum[:, EXPERTS : EXPERTS + 2].T
    exit_sum = exit_got[:ROWS]

    expand_sum, shrink_sum = to_owners(expert_sum, extra_sum)
    expand_sum, shrink_sum = expand_sum.astype(f32), shrink_sum.astype(f32)
    entry_new = adamw_step(entry_weight, entry_sum, entry_mean, entry_square, 0.02, weight_decay)
    exit_new = adamw_step(exit_weight, exit_sum, exit_mean, exit_square, 0.15, weight_decay)
    router_new = adamw_step(
        router_weight, router_sum, router_mean, router_square, 0.01, weight_decay
    )
    expand_new = adamw_step(
        expand_weight, expand_sum, expand_mean, expand_square, 0.02, weight_decay
    )
    shrink_new = adamw_step(
        shrink_weight, shrink_sum, shrink_mean, shrink_square, 0.12, weight_decay
    )
    gains_new = adamw_step(norm_gains, gains_sum, gains_mean, gains_square, 0.5, 0.0)
    return (
        block_output[None],
        input_grad[None],
        *entry_new,
        *exit_new,
        *router_new,
        *expand_new,
        *shrink_new,
        *gains_new,
    )


def solution(mesh):
    fine = Mesh(mesh.devices.reshape(4, 4, 4, 2), ("seq", "x", "y", "core"))
    rows = P(FSDP, "seq", None)
    lists = P(FSDP, None)
    owned = P(("seq",) + FSDP, None)
    experts = P("seq", FSDP, None)
    gains = P(None, ("seq",) + FSDP)
    return jax.shard_map(
        on_device,
        mesh=fine,
        in_specs=(rows, rows, lists, lists, rows)
        + (owned,) * 9
        + (experts,) * 6
        + (gains,) * 3,
        out_specs=(rows, rows) + (owned,) * 9 + (experts,) * 6 + (gains,) * 3,
        check_vma=False,
    )
```

```python
import jax
import jax.numpy as jnp
from jax import lax
from jax.experimental import pallas as pl
from jax.experimental.pallas import tpu as pltpu
from jax.sharding import Mesh, PartitionSpec as P

D = 1536
QH = 24
KVH = 8
HD = 64
FF = 512
EXPERTS = 40
TOP = 8
STEP = 10
CAP = 29

N_SEQ = 4
TOK_DEV = 128
GROUP = 512
PAIR_TOK = 2 * GROUP
LOCAL_E = EXPERTS // (2 * N_SEQ)
SLOTS = 256
Q_OWN = QH * HD // N_SEQ
KV_OWN = 2 * KVH * HD // N_SEQ
MIX_OWN = Q_OWN + KV_OWN
HEADS_OWN = QH // N_SEQ
KV_HEADS_OWN = KVH // N_SEQ
PER_KV = QH // KVH
ROWS = 12

norm_eps = 1e-06
rope_base = 10000.0
beta_first = 0.9
beta_second = 0.95
adam_eps = 1e-08
weight_decay = 0.1

FSDP = ("x", "y", "core")
PLANE = ("x", "y")
f32 = jnp.float32
bf16 = jnp.bfloat16


BIG = 60 * 1024 * 1024
HALF = TOK_DEV // 2
QOWN = Q_OWN
MESH = pl.DeviceIdType.MESH
ANY = pl.BlockSpec(memory_space=pl.ANY)
VMEM = pl.BlockSpec(memory_space=pltpu.VMEM)


def dot(a, b, dims):
    return lax.dot_general(a, b, (dims, ((), ())), preferred_element_type=f32)


def greet(peers):
    barrier = pltpu.get_barrier_semaphore()
    for axis, peer in peers:
        pl.semaphore_signal(barrier, inc=1, device_id={axis: peer}, device_id_type=MESH)
    pl.semaphore_wait(barrier, len(peers))


def planner(send_sem, recv_sem):
    def plan(src, dst, index, axis, peer):
        return pltpu.make_async_remote_copy(
            src_ref=src,
            dst_ref=dst,
            send_sem=send_sem.at[index],
            recv_sem=recv_sem.at[index],
            device_id={axis: peer},
            device_id_type=MESH,
        )

    return plan


def sender(send_sem, recv_sem):
    plan = planner(send_sem, recv_sem)

    def send(*args):
        copy = plan(*args)
        copy.start()
        return copy

    return send


def sems(count):
    return [pltpu.SemaphoreType.DMA((count,)), pltpu.SemaphoreType.DMA((count,))]


def ring(me):
    right, left = lax.rem(me + 1, 4), lax.rem(me + 3, 4)
    return right, left, lax.rem(me + 2, 4)


def near(axis):
    right, left, _ = ring(lax.axis_index(axis))
    return [(axis, right), (axis, left)]


def sibling():
    return ("core", 1 - lax.axis_index("core"))


def half_rows(ref, half):
    size = ref.shape[0] // 2
    return ref.at[pl.ds(half * size, size)]


def half_lanes(ref, half):
    size = ref.shape[-1] // 2
    return ref.at[(slice(None),) * (len(ref.shape) - 1) + (pl.ds(half * size, size),)]


class Gather:
    def __init__(self, plan, base, axis, mine, slot, cut):
        me = lax.axis_index(axis)
        right, left, self.far = ring(me)
        self.right, self.left = right, left
        here, from_left, from_right = slot(me), cut(slot(left), 0), cut(slot(right), 1)
        self.first = [
            plan(cut(mine, 0), cut(here, 0), base, axis, right),
            plan(cut(mine, 1), cut(here, 1), base + 1, axis, left),
            plan(cut(mine, 1), cut(here, 1), base + 2, axis, right),
            plan(cut(mine, 0), cut(here, 0), base + 3, axis, left),
        ]
        self.later = [
            plan(from_left, from_left, base + 4, axis, right),
            plan(from_right, from_right, base + 5, axis, left),
        ]

    def start(self):
        for copy in self.first:
            copy.start()
        return self

    def relay(self):
        for got, on in zip(self.first, self.later):
            got.wait_recv()
            on.start()

    def wait_left(self):
        self.first[2].wait_recv()

    def wait_right(self):
        self.first[3].wait_recv()

    def wait_far(self):
        for copy in self.later:
            copy.wait_recv()

    def finish(self):
        self.wait_left()
        self.wait_right()
        self.wait_far()

    def drain(self):
        for copy in self.first + self.later:
            copy.wait_send()


def hand_over(send, base, mine, out, gather):
    me, core = lax.axis_index("seq"), lax.axis_index("core")
    other = 1 - core
    copies = [send(mine, out.at[core, me], base, "core", other)]
    gather.relay()
    gather.wait_left()
    block = out.at[core, gather.left]
    copies.append(send(block, block, base + 1, "core", other))
    gather.wait_right()
    block = out.at[core, gather.right]
    copies.append(send(block, block, base + 2, "core", other))
    gather.wait_far()
    block = out.at[core, gather.far]
    copies.append(send(block, block, base + 3, "core", other))
    return copies


def reduce_scratch(block, half):
    return [pltpu.VMEM(half, bf16)] * 4 + [pltpu.VMEM(block, bf16)] * 2


def added(target, first, second):
    target[...] = (first[...].astype(f32) + second[...].astype(f32)).astype(bf16)


class Reduce:
    def __init__(self, plan, base, axis, block, bufs, cut):
        me = lax.axis_index(axis)
        right, left, far = ring(me)
        from_left, from_right, to_right, to_left, got_left, got_right = bufs
        far, on_right, on_left = block(far), block(right), block(left)
        self.mine, self.got = block(me), (got_left, got_right)
        self.hops = (
            (to_right, cut(on_right, 0), from_left),
            (to_left, cut(on_left, 1), from_right),
        )
        self.far = [
            plan(cut(far, 0), from_left, base, axis, right),
            plan(cut(far, 1), from_right, base + 1, axis, left),
        ]
        self.near = [
            plan(cut(on_right, 1), cut(got_left, 1), base + 2, axis, right),
            plan(cut(on_left, 0), cut(got_right, 0), base + 3, axis, left),
        ]
        self.later = [
            plan(to_right, cut(got_left, 0), base + 4, axis, right),
            plan(to_left, cut(got_right, 1), base + 5, axis, left),
        ]

    def start_far(self):
        for copy in self.far:
            copy.start()

    def start_near(self):
        for copy in self.near:
            copy.start()

    def start(self):
        self.start_far()
        self.start_near()
        return self

    def relay(self):
        for got, hop, on in zip(self.far, self.hops, self.later):
            got.wait_recv()
            added(*hop)
            on.start()

    def total(self):
        for copy in self.near + self.later:
            copy.wait_recv()
        total = self.mine[...].astype(f32)
        for part in self.got:
            total += part[...].astype(f32)
        return total

    def drain(self):
        for copy in self.far + self.near + self.later:
            copy.wait_send()


def remote_params(call_id):
    return pltpu.CompilerParams(
        collective_id=call_id, has_side_effects=True, vmem_limit_bytes=BIG
    )


def unit_scale(vector):
    return lax.rsqrt(jnp.mean(vector * vector, axis=-1, keepdims=True) + norm_eps)


def norm_back(vector, gain, grad):
    scale = unit_scale(vector)
    unit = vector * scale
    pulled = grad * gain
    back = scale * (pulled - unit * jnp.mean(pulled * unit, axis=-1, keepdims=True))
    return back, jnp.sum(unit * grad, axis=0, keepdims=True)


MAIN_E = LOCAL_E - 1


def row_pick(shape, padded_axis):
    padded = lax.broadcasted_iota(jnp.int32, shape, padded_axis)
    plain = lax.broadcasted_iota(jnp.int32, shape, 1 - padded_axis)
    row = lax.rem(padded, 16)
    return ((plain == lax.div(padded, 16) * 12 + row) & (row < 12)).astype(bf16)


def swap_halves(rows, lower, upper):
    lane = lax.broadcasted_iota(jnp.int32, rows.shape, 1)
    ahead = pltpu.roll(rows, rows.shape[1] - HD // 2, 1)
    behind = pltpu.roll(rows, HD // 2, 1)
    return jnp.where(lax.rem(lane, HD) < HD // 2, lower * ahead, upper * behind)


BLOCK = 256


def sequence_of(lengths_ref, token):
    first_end = lengths_ref[0, 0]
    second_end = first_end + lengths_ref[0, 1]
    return (token >= first_end).astype(jnp.int32) + (token >= second_end).astype(jnp.int32)


def block_bias(lengths_ref, block):
    keys = BLOCK * (block + 1)
    row = lax.broadcasted_iota(jnp.int32, (BLOCK, keys), 0) + BLOCK * block
    column = lax.broadcasted_iota(jnp.int32, (BLOCK, keys), 1)
    same = sequence_of(lengths_ref, row) == sequence_of(lengths_ref, column)
    return jnp.where(same & (column <= row), 0.0, -1e30)


def rope_tables(lengths_ref, trig_ref, start_ref):
    seq = sequence_of(lengths_ref, lax.broadcasted_iota(jnp.int32, (GROUP, 128), 0))

    def of_start(row):
        later = jnp.where(seq == 1, start_ref[row + 1 : row + 2], start_ref[row + 2 : row + 3])
        return jnp.where(seq == 0, start_ref[row : row + 1], later)

    start_cos, start_sin = of_start(0), of_start(3)
    cosine = trig_ref[0] * start_cos + trig_ref[1] * start_sin
    sine = trig_ref[1] * start_cos - trig_ref[0] * start_sin
    is_key = lax.broadcasted_iota(jnp.int32, (GROUP, 128), 1) < HD
    pair_cos, pair_sin = jnp.where(is_key, cosine, 1.0), jnp.where(is_key, sine, 0.0)
    return (
        jnp.concatenate([cosine] * 3 + [pair_cos] * 2, axis=1),
        jnp.concatenate([sine] * 3 + [pair_sin] * 2, axis=1),
    )


def head_of(index):
    return slice(HD * index, HD * (index + 1))


def lane_pick(first, rows):
    row = lax.broadcasted_iota(jnp.int32, (rows, 128), 0)
    lane = lax.broadcasted_iota(jnp.int32, (rows, 128), 1)
    return (lane == row + first).astype(bf16)


def forward_kernel(
    in_hbm, cot_hbm, in_ref, route_ref, order_ref, lengths_ref, trig_ref, start_ref,
    entry_ref, exit_ref, shared_ref, expand_ref, shrink_ref,
    weights_out, entry_out, shared_out, exit_out, gains_out, normed_ref, qkv_ref, attended_ref,
    lse_ref, middle_ref, mine, rows_out, cot_rows_out, row_gate_out, rank_out, my_gate_out,
    stage, stage_end, packed, columns, exit_cols, hit_mine, hold, full,
    in_all, cot_all, hit_all, hit_pair, tokens, part, gates, *rest
):
    bufs, (send_sem, recv_sem, copy_sem) = rest[:6], rest[6:]
    z, x, y, c = (lax.axis_index(a) for a in ("seq", "x", "y", "core"))
    right, left, far = ring(z)
    other = 1 - c
    greet(near("seq") + [("seq", far)] + near("x") + near("y") + [sibling()])
    send, plan = sender(send_sem, recv_sem), planner(send_sem, recv_sem)

    empty = jnp.zeros((PAD_ROWS - ROWS, WIDE), f32)
    for block in range(4):
        cols = jnp.concatenate(
            [
                entry_ref[:, Q_OWN * block : Q_OWN * (block + 1)],
                entry_ref[:, QH * HD + KV_OWN * block : QH * HD + KV_OWN * (block + 1)],
                shared_ref[...],
            ],
            axis=1,
        )
        columns[block] = jnp.concatenate([cols, empty], axis=0).astype(bf16)
    for block in range(2):
        cols = exit_ref[:, WIDE * block : WIDE * (block + 1)]
        exit_cols[block] = jnp.concatenate([cols, empty], axis=0).astype(bf16)
    to_seq = [
        send(columns.at[peer], hold.at[z], k, "seq", peer)
        for k, peer in enumerate((right, far, left))
    ]
    lane = lax.broadcasted_iota(jnp.int32, (TOK_DEV, 128), 1)
    hit = route_ref[:, 0:1] == lane
    for k in range(1, TOP):
        hit = hit | (route_ref[:, k : k + 1] == lane)
    hit_mine[...] = hit.astype(bf16)
    hits = Gather(plan, 3, "seq", hit_mine, lambda i: hit_all.at[i], half_rows).start()
    rows = Gather(plan, 9, "seq", in_hbm, lambda i: in_all.at[i], half_rows).start()
    local = [
        pltpu.make_async_copy(columns.at[z], hold.at[z], copy_sem.at[0]),
        pltpu.make_async_copy(exit_cols, hold.at[pl.ds(4, 2)], copy_sem.at[1]),
        pltpu.make_async_copy(hit_mine, hit_all.at[z], copy_sem.at[2]),
        pltpu.make_async_copy(in_hbm, in_all.at[z], copy_sem.at[3]),
        pltpu.make_async_copy(cot_hbm, cot_all.at[c, z], copy_sem.at[4]),
    ]
    for copy in local:
        copy.start()

    for e in range(LOCAL_E):
        theirs = other * LOCAL_E + e
        stage[e, :48] = expand_ref[theirs].astype(bf16)
        stage[e, 48:] = shrink_ref[theirs, :, :1024].astype(bf16)
        stage_end[e] = shrink_ref[theirs, :, 1024:].astype(bf16)
    of_core = pl.ds(pl.multiple_of(c * 48, 16), 48)
    lefts = pl.ds(pl.multiple_of(96 + c * 16, 16), 16)
    ends = pl.ds(pl.multiple_of(c * 512, 512), 512)
    to_core = [
        send(stage.at[:, pl.ds(0, 48)], packed.at[:, of_core], 51, "core", other),
        send(stage.at[:, pl.ds(48, 16)], packed.at[:, lefts], 52, "core", other),
        send(stage_end, packed.at[:, pl.ds(128, 16), ends], 53, "core", other),
    ]
    for e in range(LOCAL_E):
        own_e = c * LOCAL_E + e
        packed[e, of_core, :] = expand_ref[own_e].astype(bf16)
        packed[e, lefts, :] = shrink_ref[own_e, :, :1024].astype(bf16)
        packed[e, pl.ds(128, 16), ends] = shrink_ref[own_e, :, 1024:].astype(bf16)
    local[0].wait()
    local[1].wait()
    for copy in to_seq:
        copy.wait_recv()
    own = pltpu.make_async_copy(hold, full.at[:, x, y, c], copy_sem.at[5])
    own.start()
    low, high = pl.ds(0, 3), pl.ds(3, 3)
    low_x = Gather(plan, 15, "x", hold.at[low], lambda i: full.at[low, i, y, c], half_lanes)
    low_x.start()
    high_y = Gather(plan, 21, "y", hold.at[high], lambda i: full.at[high, x, i, c], half_lanes)
    high_y.start()
    for copy in to_core:
        copy.wait_recv()
    own_weights = pltpu.make_async_copy(packed, weights_out.at[x, y], copy_sem.at[6])
    own_weights.start()
    start, end = pl.ds(0, 512), pl.ds(512, 512)
    expert_x = Gather(
        plan,
        54,
        "x",
        packed.at[:, :, start],
        lambda i: weights_out.at[i, y, :, :, start],
        half_lanes,
    ).start()
    expert_y = Gather(
        plan,
        60,
        "y",
        packed.at[:, :, end],
        lambda i: weights_out.at[x, i, :, :, end],
        half_lanes,
    ).start()

    def cut_low(ref, half):
        return ref.at[:, pl.ds(2 * half, 2)]

    hits.relay()
    low_x.relay()
    high_y.relay()
    rows.relay()
    cots = Gather(plan, 27, "seq", cot_hbm, lambda i: cot_all.at[c, i], half_rows).start()
    own.wait()
    low_x.finish()
    low_y = Gather(
        plan, 33, "y", full.at[low, :, y, c], lambda i: full.at[low, :, i, c], cut_low
    ).start()
    high_y.finish()
    high_x = Gather(
        plan, 39, "x", full.at[high, x, :, c], lambda i: full.at[high, i, :, c], cut_low
    ).start()
    expert_x.relay()
    expert_y.relay()

    local[2].wait()
    hits.finish()
    token = lax.broadcasted_iota(jnp.int32, (GROUP, GROUP), 0)
    back_hot = (order_ref[...] == token).astype(bf16)
    hit_slots = hit_all[...].reshape(GROUP, 128)
    hit_pair[c] = dot(back_hot, hit_slots, ((1,), (0,))).astype(bf16)
    hit_swap = send(hit_pair.at[c], hit_pair.at[c], 66, "core", other)
    low_y.relay()
    high_x.relay()
    hit_swap.wait_recv()
    hit_both = hit_pair[...].reshape(PAIR_TOK, 128)
    first = (z * 2 + c) * LOCAL_E
    lower = lax.broadcasted_iota(jnp.int32, (PAIR_TOK, PAIR_TOK), 0)
    lower = (lower >= lax.broadcasted_iota(jnp.int32, (PAIR_TOK, PAIR_TOK), 1)).astype(bf16)
    rank = dot(lower, hit_both, ((1,), (0,))) - 1.0
    rank = jnp.where(hit_both.astype(f32) > 0.0, rank, -1.0).astype(bf16)
    mine_of = lane_pick(first, 8)
    rank_out[...] = dot(rank, mine_of, ((1,), (1,))).astype(jnp.int32)
    rank_rows = dot(mine_of, rank, ((1,), (1,))).astype(jnp.int32)

    low_y.finish()
    half = full.at[low, :, :, c]
    last = [send(half, half, 49, "core", other)]
    high_x.finish()
    half = full.at[high, :, :, c]
    last.append(send(half, half, 50, "core", other))
    cosine, sine = rope_tables(lengths_ref, trig_ref, start_ref)
    rows.finish()
    local[3].wait()
    for copy in last:
        copy.wait_recv()
    own_weights.wait()
    expert_x.finish()
    expert_low = Gather(
        plan,
        67,
        "y",
        weights_out.at[:, y, :, :, start],
        lambda i: weights_out.at[:, i, :, :, start],
        half_rows,
    ).start()
    expert_y.finish()
    expert_high = Gather(
        plan,
        73,
        "x",
        weights_out.at[x, :, :, :, end],
        lambda i: weights_out.at[i, :, :, :, end],
        half_rows,
    ).start()
    pick = row_pick((QOWN, 512), 1)
    for block in range(4):
        got = dot(pick, full[block].reshape(512, WIDE), ((1,), (0,))).astype(bf16)
        entry_out[QOWN * block : QOWN * (block + 1), :] = got[:, :MIX_OWN]
        shared_out[QOWN * block : QOWN * (block + 1), :] = got[:, MIX_OWN:]
    for block in range(2):
        got = dot(pick, full[4 + block].reshape(512, WIDE), ((1,), (0,))).astype(bf16)
        exit_out[:, WIDE * block : WIDE * (block + 1)] = got
    gains = dot(lane_pick(EXPERTS, 8), shared_out[...], ((1,), (1,)))
    gains_out[...] = gains
    for block in range(N_SEQ):
        at = slice(TOK_DEV * block, TOK_DEV * (block + 1))
        vector = in_all[block].astype(f32)
        normed_ref[at, :] = (vector * unit_scale(vector) * gains[0:1]).astype(bf16)
    mixed = dot(normed_ref[...], entry_out[...], ((1,), (0,)))
    mixed = mixed * cosine + swap_halves(mixed, -1.0, 1.0) * sine
    qkv_ref[...] = mixed.astype(bf16)
    for block in range(GROUP // BLOCK):
        bias = block_bias(lengths_ref, block)
        keys = BLOCK * (block + 1)
        at = slice(BLOCK * block, keys)
        for head in range(HEADS_OWN):
            pair = Q_OWN + 2 * HD * (head // PER_KV)
            key = qkv_ref[:keys, pair : pair + HD]
            value = qkv_ref[:keys, pair + HD : pair + 2 * HD]
            scores = dot(qkv_ref[at, head_of(head)], key, ((1,), (1,))) * HD**-0.5 + bias
            peak = jnp.max(scores, axis=1, keepdims=True)
            expo = jnp.exp(scores - peak)
            total = jnp.sum(expo, axis=1, keepdims=True)
            probs = (expo / total).astype(bf16)
            attended_ref[at, head_of(head)] = dot(probs, value, ((1,), (0,))).astype(bf16)
            lse_ref[at, head : head + 1] = peak + jnp.log(total)
    part[...] = dot(attended_ref[...], exit_out[...], ((1,), (0,))).astype(bf16).reshape(part.shape)
    reduce = Reduce(plan, 79, "seq", lambda i: part.at[i], bufs, half_rows).start()
    pairs = hand_over(send, 45, cot_hbm, cot_all, cots)
    reduce.relay()
    middle = in_ref[...].astype(f32) + reduce.total()
    middle_ref[...] = middle
    mine[...] = (middle * unit_scale(middle) * gains[1:2]).astype(bf16)
    gather = Gather(plan, 85, "seq", mine, lambda i: tokens.at[c, i], half_rows).start()
    tokens[c, z] = mine[...]
    expert_low.relay()
    expert_high.relay()
    pairs += hand_over(send, 91, mine, tokens, gather)
    for copy in pairs:
        copy.wait()
    local[4].wait()

    logits = dot(tokens[...].reshape(PAIR_TOK, D), shared_out[...], ((1,), (0,)))
    masked = jnp.where(hit_both.astype(f32) > 0.0, logits, -jnp.inf)
    gate_expo = jnp.exp(masked - jnp.max(masked, axis=1, keepdims=True))
    gates[...] = gate_expo / jnp.sum(gate_expo, axis=1, keepdims=True)
    my_gate_out[...] = gates[pl.ds(pl.multiple_of(c * GROUP + z * TOK_DEV, TOK_DEV), TOK_DEV), :]
    rest_of = gates[...]
    gate_rows = jnp.zeros((8, PAIR_TOK), f32)
    for _ in range(3):
        piece = rest_of.astype(bf16)
        gate_rows += dot(mine_of, piece, ((1,), (1,)))
        rest_of -= piece.astype(f32)
    slot = lax.broadcasted_iota(jnp.int32, (SLOTS, PAIR_TOK), 0)
    for e in range(LOCAL_E):
        match = rank_rows[e : e + 1] == slot
        row_gate_out[e] = jnp.sum(
            jnp.where(match, gate_rows[e : e + 1], 0.0), axis=1, keepdims=True
        )
        match = match.astype(bf16)
        for half in range(2):
            lanes = slice(768 * half, 768 * (half + 1))
            table = tokens[:, :, :, lanes].reshape(PAIR_TOK, 768)
            rows_out[e, :, lanes] = dot(match, table, ((1,), (0,))).astype(bf16)
            table = cot_all[:, :, :, lanes].reshape(PAIR_TOK, 768)
            cot_rows_out[e, :, lanes] = dot(match, table, ((1,), (0,))).astype(bf16)
    expert_low.finish()
    expert_high.finish()
    for copy in to_seq + to_core + last + [hit_swap]:
        copy.wait_send()
    for transfer in (hits, rows, cots, low_x, high_y, low_y, high_x, reduce, gather):
        transfer.drain()
    for transfer in (expert_x, expert_y, expert_low, expert_high):
        transfer.drain()


def forward(*operands):
    scalar = pl.BlockSpec(memory_space=pltpu.SMEM)
    block = (PAD_ROWS, WIDE)
    group = (N_SEQ, TOK_DEV, D)
    return pl.pallas_call(
        forward_kernel,
        out_shape=[
            jax.ShapeDtypeStruct((4, 4, LOCAL_E, 144, 1024), bf16),
            jax.ShapeDtypeStruct((D, MIX_OWN), bf16),
            jax.ShapeDtypeStruct((D, 128), bf16),
            jax.ShapeDtypeStruct((QOWN, D), bf16),
            jax.ShapeDtypeStruct((8, D), f32),
            jax.ShapeDtypeStruct((GROUP, D), bf16),
            jax.ShapeDtypeStruct((GROUP, MIX_OWN), bf16),
            jax.ShapeDtypeStruct((GROUP, Q_OWN), bf16),
            jax.ShapeDtypeStruct((GROUP, HEADS_OWN), f32),
            jax.ShapeDtypeStruct((TOK_DEV, D), f32),
            jax.ShapeDtypeStruct((TOK_DEV, D), bf16),
            jax.ShapeDtypeStruct((LOCAL_E, SLOTS, D), bf16),
            jax.ShapeDtypeStruct((LOCAL_E, SLOTS, D), bf16),
            jax.ShapeDtypeStruct((LOCAL_E, SLOTS, 1), f32),
            jax.ShapeDtypeStruct((PAIR_TOK, 8), jnp.int32),
            jax.ShapeDtypeStruct((TOK_DEV, 128), f32),
        ],
        in_specs=[ANY] * 2 + [VMEM] * 3 + [scalar] + [VMEM] * 7,
        out_specs=[ANY] + [VMEM] * 15,
        scratch_shapes=[
            pltpu.VMEM((LOCAL_E, 64, 1024), bf16),
            pltpu.VMEM((LOCAL_E, 16, 512), bf16),
            pltpu.VMEM((LOCAL_E, 144, 1024), bf16),
            pltpu.VMEM((4,) + block, bf16),
            pltpu.VMEM((2,) + block, bf16),
            pltpu.VMEM((TOK_DEV, 128), bf16),
            pltpu.VMEM((6,) + block, bf16),
            pltpu.VMEM((6, 4, 4, 2) + block, bf16),
            pltpu.VMEM(group, bf16),
            pltpu.VMEM((2,) + group, bf16),
            pltpu.VMEM((N_SEQ, TOK_DEV, 128), bf16),
            pltpu.VMEM((2, GROUP, 128), bf16),
            pltpu.VMEM((2,) + group, bf16),
            pltpu.VMEM(group, bf16),
            pltpu.VMEM((PAIR_TOK, 128), f32),
        ]
        + reduce_scratch((TOK_DEV, D), (HALF, D))
        + sems(95)
        + [pltpu.SemaphoreType.DMA((7,))],
        compiler_params=remote_params(2),
    )(*operands)


def turn_kernel(
    rank_ref, up_ref, hidden_ref, gate_ref, cot_rows_ref, w_ref,
    line, middle_ref, cot_ref, my_gate_ref, router_ref, gain_ref,
    grad_ref, branch_ref, logit_ref, gain_grad_ref, out_sum_ref, extra_sum_ref,
    back_s, out_s, other_back, from_core, part, other_out, out_core, mine, *rest
):
    bufs, (send_sem, recv_sem, copy_sem) = [rest[6 * i : 6 * i + 6] for i in range(3)], rest[18:]
    e = pl.program_id(0)
    me, core = lax.axis_index("seq"), lax.axis_index("core")
    send, plan = sender(send_sem, recv_sem), planner(send_sem, recv_sem)
    low_y = Reduce(plan, 17, "y", lambda i: line.at[0, i], bufs[1], half_lanes)
    high_x = Reduce(plan, 23, "x", lambda i: line.at[1, i], bufs[2], half_lanes)

    @pl.when(e == 0)
    def _():
        greet(near("seq") + near("x") + near("y") + [sibling()])
        low_y.start()
        high_x.start()

    @pl.when(e == 2)
    def _():
        low_y.relay()
        high_x.relay()

    @pl.when(e < LOCAL_E)
    def _():
        expand, left, right = weights_of(w_ref)
        at = pl.ds(pl.multiple_of(e * SLOTS, SLOTS), SLOTS)
        back_s[at, :D] = dot(up_ref[0], expand, ((1,), (1,))).astype(bf16)
        hidden = hidden_ref[0]
        expert_out = jnp.concatenate(
            [dot(hidden, left, ((1,), (0,))), dot(hidden, right, ((1,), (0,)))], axis=1
        )
        expert_out = expert_out.astype(bf16).astype(f32)
        gate_grad = jnp.sum(expert_out * cot_rows_ref[0].astype(f32), axis=1, keepdims=True)
        lane = lax.broadcasted_iota(jnp.int32, (SLOTS, 128), 1)
        column = (me * 2 + core) * LOCAL_E + e
        back_s[at, D:] = jnp.where(lane == column, gate_grad, 0.0).astype(bf16)
        out_s[at, :] = (gate_ref[0] * expert_out).astype(bf16)

    @pl.when(e == LOCAL_E)
    def _():
        other = 1 - core
        right, left, far = ring(me)
        slot = lax.broadcasted_iota(jnp.int32, (GROUP, SLOTS), 1)

        def picks(group):
            at = pl.ds(pl.multiple_of(group * GROUP, GROUP), GROUP)
            ranks = rank_ref[at, :]
            return jnp.concatenate(
                [(ranks[:, k : k + 1] == slot).astype(bf16) for k in range(LOCAL_E)], axis=1
            )

        theirs, ours = picks(other), picks(core)
        order = (far, right, left, me)
        other_back[...] = (
            dot(theirs, back_s[...], ((1,), (0,))).astype(bf16).reshape(other_back.shape)
        )
        swaps = [
            send(other_back.at[block], from_core.at[block], 12 + i, "core", other)
            for i, block in enumerate(order)
        ]
        part[...] = dot(ours, back_s[...], ((1,), (0,))).astype(bf16).reshape(part.shape)
        reduce = Reduce(plan, 0, "seq", lambda i: part.at[i], bufs[0], half_rows)
        for i, block in enumerate(order):
            swaps[i].wait_recv()
            added(part.at[block], part.at[block], from_core.at[block])
            if i == 0:
                reduce.start_far()
            if i == 2:
                reduce.start_near()
        other_out[...] = (
            dot(theirs, out_s[...], ((1,), (0,))).astype(bf16).reshape(other_out.shape)
        )
        out_swap = send(other_out, out_core, 16, "core", other)
        reduce.relay()
        out_sum_ref[...] = (
            dot(ours, out_s[...], ((1,), (0,))).astype(bf16).reshape(out_sum_ref.shape)
        )
        total = reduce.total()
        gates, gate_grad = my_gate_ref[...], total[:, D:]
        mean_term = jnp.sum(gates * gate_grad, axis=1, keepdims=True)
        logit_grad = (gates * (gate_grad - mean_term)).astype(bf16)
        logit_ref[...] = logit_grad
        normed_grad = total[:, :D] + dot(logit_grad, router_ref[...], ((1,), (1,)))
        back, gain_grad = norm_back(middle_ref[...], gain_ref[...], normed_grad)
        gain_grad_ref[...] = gain_grad
        middle_grad = cot_ref[...].astype(f32) + back
        grad_ref[...] = middle_grad
        mine[...] = middle_grad.astype(bf16)
        gather = Gather(plan, 6, "seq", mine, lambda i: branch_ref.at[i], half_rows).start()
        local = pltpu.make_async_copy(mine, branch_ref.at[me], copy_sem)
        local.start()
        out_swap.wait_recv()
        added(out_sum_ref, out_sum_ref, out_core)
        gather.relay()
        extra_sum_ref[:, :512] = low_y.total().astype(bf16)
        extra_sum_ref[:, 512:] = high_x.total().astype(bf16)
        gather.finish()
        for transfer in (gather, reduce, low_y, high_x):
            transfer.drain()
        for copy in swaps + [out_swap]:
            copy.wait_send()
        local.wait()


BACK_WIDTH = D + 128


def turn(*operands):
    one = lambda e: (jnp.minimum(e, LOCAL_E - 1), 0, 0)
    wide = lambda e: (0, jnp.minimum(e, LOCAL_E - 1), 0, 0)
    cubes = lambda e: (0, 0, 0, 0)
    whole = lambda e: (0, 0)
    blocks = lambda e: (0, 0, 0)
    row_block = pl.BlockSpec((TOK_DEV, D), whole)
    lane_block = pl.BlockSpec((TOK_DEV, 128), whole)
    gain_block = pl.BlockSpec((1, D), whole)
    group = pltpu.VMEM((N_SEQ, TOK_DEV, BACK_WIDTH), bf16)
    group_out = pltpu.VMEM((N_SEQ, TOK_DEV, D), bf16)
    return pl.pallas_call(
        turn_kernel,
        grid=(LOCAL_E + 1,),
        in_specs=[
            pl.BlockSpec((PAIR_TOK, 8), whole),
            pl.BlockSpec((1, SLOTS, 2 * FF), one),
            pl.BlockSpec((1, SLOTS, FF), one),
            pl.BlockSpec((1, SLOTS, 1), one),
            pl.BlockSpec((1, SLOTS, D), one),
            pl.BlockSpec((16, 1, 144, 1024), wide),
            pl.BlockSpec((2, 4, 144, 512), cubes),
            row_block,
            row_block,
            lane_block,
            pl.BlockSpec((D, 128), whole),
            gain_block,
        ],
        out_specs=[
            row_block,
            ANY,
            lane_block,
            gain_block,
            pl.BlockSpec((N_SEQ, TOK_DEV, D), blocks),
            pl.BlockSpec((144, 1024), whole),
        ],
        out_shape=[
            jax.ShapeDtypeStruct((TOK_DEV, D), f32),
            jax.ShapeDtypeStruct((N_SEQ, TOK_DEV, D), bf16),
            jax.ShapeDtypeStruct((TOK_DEV, 128), bf16),
            jax.ShapeDtypeStruct((1, D), f32),
            jax.ShapeDtypeStruct((N_SEQ, TOK_DEV, D), bf16),
            jax.ShapeDtypeStruct((144, 1024), bf16),
        ],
        scratch_shapes=[
            pltpu.VMEM((LOCAL_E * SLOTS, BACK_WIDTH), bf16),
            pltpu.VMEM((LOCAL_E * SLOTS, D), bf16),
            group,
            group,
            group,
            group_out,
            group_out,
            pltpu.VMEM((TOK_DEV, D), bf16),
        ]
        + reduce_scratch((TOK_DEV, BACK_WIDTH), (HALF, BACK_WIDTH))
        + reduce_scratch((144, 512), (144, 256)) * 2
        + sems(29)
        + [pltpu.SemaphoreType.DMA],
        compiler_params=remote_params(4),
        cost_estimate=pl.CostEstimate(
            flops=6 * LOCAL_E * SLOTS * D * FF + 4 * LOCAL_E * SLOTS * PAIR_TOK * D,
            bytes_accessed=40 << 20,
            transcendentals=0,
        ),
    )(*operands)


PAD_ROWS = 16
WIDE = 768
def closing_kernel(
    qkv_ref, lse_ref, lengths_ref, trig_ref, start_ref, exit_ref, entry_ref,
    in_ref, grad_ref, gain_ref, normed_ref, attended_ref, branch_ref,
    router_grad_ref, gain_two_ref, out_sum_ref, middle_ref,
    input_ref, block_ref, entry_out, exit_out,
    turned, mixed_grad, part, full, from_core, chip, line, final, give, got_z, *rest
):
    bufs, (send_sem, recv_sem) = [rest[6 * i : 6 * i + 6] for i in range(8)], rest[48:]
    z, x, y, c = (lax.axis_index(a) for a in ("seq", "x", "y", "core"))
    right, left, far = ring(z)
    greet(near("seq") + [("seq", far)] + near("x") + near("y") + [sibling()])
    send, plan = sender(send_sem, recv_sem), planner(send_sem, recv_sem)
    pick = row_pick((512, QOWN), 0)

    def spread(grad):
        wide = dot(pick, grad, ((1,), (0,))).astype(bf16)
        return wide.reshape(16, 2, PAD_ROWS, grad.shape[1])

    def swap(side):
        return send(full.at[side, :, 1 - c], from_core.at[side], 48 + side, "core", 1 - c)

    def chip_sum(side, copy):
        copy.wait_recv()
        for plane in range(16):
            first, second = (plane % 4, plane // 4) if side == 2 else (plane // 4, plane % 4)
            added(chip.at[side, first, second], full.at[side, plane, c], from_core.at[side, plane])

    def first_sum(side, axis):
        return Reduce(
            plan, 6 * side, axis, lambda i: chip.at[side, i], bufs[side], half_rows
        ).start()

    def second_sum(side, axis, reduce):
        line[side] = reduce.total().astype(bf16)
        return Reduce(
            plan, 18 + 6 * side, axis, lambda i: line.at[side, i], bufs[3 + side], half_lanes
        ).start()

    for block in range(3):
        cols = slice(512 * block, 512 * (block + 1))
        grad = dot(attended_ref[...], branch_ref[:, cols], ((0,), (0,))).astype(bf16)
        full[0, :, :, :, cols] = spread(grad)
    swaps = [swap(0)]
    outs = Reduce(plan, 36, "seq", lambda i: out_sum_ref.at[i], bufs[6], half_rows).start()

    def turn_back(kv):
        pair = Q_OWN + 2 * HD * kv
        for head in range(PER_KV * kv, PER_KV * (kv + 1)):
            grad = dot(branch_ref[...], exit_ref[head_of(head), :], ((1,), (1,))).astype(bf16)
            attended = attended_ref[:, head_of(head)].astype(f32)
            delta = jnp.sum(grad.astype(f32) * attended, axis=1, keepdims=True)
            for block in range(GROUP // BLOCK):
                bias = block_bias(lengths_ref, block)
                keys = BLOCK * (block + 1)
                rows = slice(BLOCK * block, keys)
                key = qkv_ref[:keys, pair : pair + HD]
                value = qkv_ref[:keys, pair + HD : pair + 2 * HD]
                query, grad_rows = qkv_ref[rows, head_of(head)], grad[rows]
                scores = dot(query, key, ((1,), (1,))) * HD**-0.5 + bias
                probs = jnp.exp(scores - lse_ref[rows, head : head + 1])
                prob_grad = dot(grad_rows, value, ((1,), (1,)))
                score_grad = probs * (prob_grad - delta[rows]) * HD**-0.5
                score_grad = score_grad.astype(bf16)
                turned[rows, head_of(head)] = dot(score_grad, key, ((1,), (0,)))
                key_grad = dot(score_grad, query, ((0,), (0,)))
                value_grad = dot(probs.astype(bf16), grad_rows, ((0,), (0,)))
                if head == PER_KV * kv and block == GROUP // BLOCK - 1:
                    turned[:, pair : pair + HD] = key_grad
                    turned[:, pair + HD : pair + 2 * HD] = value_grad
                    turned[:BLOCK, pair : pair + HD] += held[0]
                    turned[:BLOCK, pair + HD : pair + 2 * HD] += held[1]
                elif head == PER_KV * kv:
                    held = (key_grad, value_grad)
                else:
                    turned[:keys, pair : pair + HD] += key_grad
                    turned[:keys, pair + HD : pair + 2 * HD] += value_grad

    turn_back(0)
    chip_sum(0, swaps[0])
    first_0 = first_sum(0, "x")
    outs.relay()
    turn_back(1)
    first_0.relay()
    grads = turned[...]
    cosine, sine = rope_tables(lengths_ref, trig_ref, start_ref)
    grads = grads * cosine + swap_halves(grads, 1.0, -1.0) * sine
    mixed_grad[...] = grads.astype(bf16)
    part[...] = (
        dot(mixed_grad[...], entry_ref[...], ((1,), (1,))).astype(bf16).reshape(part.shape)
    )
    rows = Reduce(plan, 42, "seq", lambda i: part.at[i], bufs[7], half_rows).start()

    def entry_rows(block):
        rows_of = slice(QOWN * block, QOWN * (block + 1))
        grad = dot(normed_ref[:, rows_of], mixed_grad[...], ((0,), (0,))).astype(bf16)
        return spread(grad)

    full[1, :, :, :, :640] = entry_rows(0)
    full[1, :, :, :, 640:1280] = entry_rows(1)
    third = entry_rows(2)
    full[1, :, :, :, 1280:] = third[..., :256]
    swaps.append(swap(1))
    rows.relay()
    second_0 = second_sum(0, "y", first_0)
    full[2, :, :, :, :384] = third[..., 256:]
    full[2, :, :, :, 384:1024] = entry_rows(3)
    chip_sum(1, swaps[1])
    first_1 = first_sum(1, "x")
    back, gain_one = norm_back(in_ref[...].astype(f32), gain_ref[...], rows.total())
    input_ref[...] = grad_ref[...] + back
    row_of = lax.broadcasted_iota(jnp.int32, (128, D), 0)
    gains = jnp.where(row_of == EXPERTS, gain_one, 0.0)
    gains = jnp.where(row_of == EXPERTS + 1, gain_two_ref[...], gains)
    shared = router_grad_ref[...] + gains.T
    for block in range(4):
        shared_rows = shared[QOWN * block : QOWN * (block + 1), :].astype(bf16)
        full[2, :, :, :, 1024 + 128 * block : 1152 + 128 * block] = spread(shared_rows)
    swaps.append(swap(2))
    second_0.relay()
    block_ref[...] = middle_ref[...] + outs.total()
    chip_sum(2, swaps[2])
    first_2 = first_sum(2, "y")
    first_1.relay()
    first_2.relay()
    exit_out[...] = second_0.total()
    second_1 = second_sum(1, "y", first_1)
    second_2 = second_sum(2, "x", first_2)
    second_1.relay()
    second_2.relay()
    final[0] = second_1.total()
    final[1] = second_2.total()
    give[0, :, :MIX_OWN] = final[0, :, :640]
    give[1, :, :MIX_OWN] = final[0, :, 640:1280]
    give[2, :, :256] = final[0, :, 1280:]
    give[2, :, 256:MIX_OWN] = final[1, :, :384]
    give[3, :, :MIX_OWN] = final[1, :, 384:1024]
    for block in range(4):
        give[block, :, MIX_OWN:] = final[1, :, 1024 + 128 * block : 1152 + 128 * block]
    home = [
        send(give.at[peer], got_z.at[k], 51 + k, "seq", peer)
        for k, peer in enumerate((right, far, left))
    ]
    entry_out[z] = give[z]
    for k, source in enumerate((left, far, right)):
        home[k].wait_recv()
        entry_out[source] = got_z[k]
    for copy in swaps + home:
        copy.wait_send()
    for reduce in (rows, outs, first_0, first_1, first_2, second_0, second_1, second_2):
        reduce.drain()


def closing(*operands):
    row_bufs = reduce_scratch((TOK_DEV, D), (HALF, D))
    chip_bufs = reduce_scratch((4, PAD_ROWS, D), (2, PAD_ROWS, D))
    line_bufs = reduce_scratch((PAD_ROWS, D), (PAD_ROWS, D // 2))
    tile = (PAD_ROWS, D)
    return pl.pallas_call(
        closing_kernel,
        out_shape=[
            jax.ShapeDtypeStruct((TOK_DEV, D), f32),
            jax.ShapeDtypeStruct((TOK_DEV, D), f32),
            jax.ShapeDtypeStruct((4, PAD_ROWS, WIDE), f32),
            jax.ShapeDtypeStruct((PAD_ROWS, D), f32),
        ],
        in_specs=[VMEM] * 2
        + [pl.BlockSpec(memory_space=pltpu.SMEM)]
        + [VMEM] * (len(operands) - 3),
        out_specs=[VMEM] * 4,
        scratch_shapes=[
            pltpu.VMEM((GROUP, MIX_OWN), f32),
            pltpu.VMEM((GROUP, MIX_OWN), bf16),
            pltpu.VMEM((N_SEQ, TOK_DEV, D), bf16),
            pltpu.VMEM((3, 16, 2) + tile, bf16),
            pltpu.VMEM((3, 16) + tile, bf16),
            pltpu.VMEM((3, 4, 4) + tile, bf16),
            pltpu.VMEM((3, 4) + tile, bf16),
            pltpu.VMEM((2,) + tile, f32),
            pltpu.VMEM((4, PAD_ROWS, WIDE), f32),
            pltpu.VMEM((3, PAD_ROWS, WIDE), f32),
        ]
        + chip_bufs * 3
        + line_bufs * 3
        + row_bufs * 2
        + sems(54),
        compiler_params=remote_params(5),
    )(*operands)


def owner_kernel(sum_ref, extra_ref, expand_ref, shrink_ref, send_sem, recv_sem, copy_sem):
    core = lax.axis_index("core")
    greet([sibling()])
    send = sender(send_sem, recv_sem)
    most, single = pl.ds(core * LOCAL_E + 1, MAIN_E), core * LOCAL_E

    def pieces(owner):
        rows = pl.ds(pl.multiple_of(owner * 48, 16), 48)
        left = pl.ds(pl.multiple_of(96 + owner * 16, 16), 16)
        ends = pl.ds(pl.multiple_of(owner * 512, 512), 512)
        low, start, end = pl.ds(128, 16), pl.ds(0, 1024), pl.ds(1024, 512)
        return [
            (sum_ref.at[:, rows], expand_ref.at[most]),
            (sum_ref.at[:, left], shrink_ref.at[most, :, start]),
            (sum_ref.at[:, low, ends], shrink_ref.at[most, :, end]),
            (extra_ref.at[rows], expand_ref.at[single]),
            (extra_ref.at[left], shrink_ref.at[single, :, start]),
            (extra_ref.at[low, ends], shrink_ref.at[single, :, end]),
        ]

    copies = [
        send(source, target, k, "core", 1 - core)
        for k, (source, target) in enumerate(pieces(1 - core))
    ]
    for k, (source, target) in enumerate(pieces(core)):
        copies.append(pltpu.make_async_copy(source, target, copy_sem.at[k]))
        copies[-1].start()
    for copy in copies:
        copy.wait()


def to_owners(summed, extra):
    return pl.pallas_call(
        owner_kernel,
        out_shape=[
            jax.ShapeDtypeStruct((2 * LOCAL_E, 48, 1024), bf16),
            jax.ShapeDtypeStruct((2 * LOCAL_E, 16, D), bf16),
        ],
        in_specs=[VMEM] * 2,
        out_specs=[VMEM] * 2,
        scratch_shapes=sems(6) + [pltpu.SemaphoreType.DMA((6,))],
        compiler_params=remote_params(6),
    )(summed, extra)


def weights_of(w_ref):
    expand = w_ref[:, 0, :96, :].reshape(D, 2 * FF)
    left = w_ref[:, 0, 96:128, :].reshape(FF, 1024)
    right = jnp.concatenate([w_ref[:, 0, 128:144, :512], w_ref[:, 0, 128:144, 512:]], axis=1)
    return expand, left, right.reshape(FF, 512)

def grads_kernel(
    rows_ref, cot_ref, gate_ref, w_ref, hidden_ref, up_ref, out_ref, line_ref, own, *rest
):
    bufs, (send_sem, recv_sem) = [rest[6 * i : 6 * i + 6] for i in range(2)], rest[12:]
    e = pl.program_id(0)
    plan = planner(send_sem, recv_sem)
    low, high = pl.ds(0, 512), pl.ds(512, 512)
    low_x = Reduce(plan, 0, "x", lambda i: own.at[i, :, :, low], bufs[0], half_rows)
    high_y = Reduce(plan, 6, "y", lambda i: own.at[:, i, :, high], bufs[1], half_rows)

    @pl.when(e == 0)
    def _():
        greet(near("x") + near("y"))

    expand, left, right = weights_of(w_ref)
    grad_rows = (gate_ref[0] * cot_ref[0].astype(f32)).astype(bf16)
    rows = rows_ref[0]
    gate_pre = dot(rows, expand[:, :FF], ((1,), (0,)))
    up_part = dot(rows, expand[:, FF:], ((1,), (0,)))
    sig = jax.nn.sigmoid(gate_pre)
    hidden = (gate_pre * sig * up_part).astype(bf16)
    hidden_ref[0] = hidden

    @pl.when(e == 2)
    def _():
        low_x.relay()
        high_y.relay()

    hidden_grad = dot(grad_rows[:, :1024], left, ((1,), (1,))) + dot(
        grad_rows[:, 1024:], right, ((1,), (1,))
    )
    up_ref[0, :, :FF] = (hidden_grad * up_part * sig * (1.0 + gate_pre * (1.0 - sig))).astype(bf16)
    up_ref[0, :, FF:] = (hidden_grad * gate_pre * sig).astype(bf16)

    def write(shrink_at, end_at, expand_at):
        grad_left = dot(hidden, grad_rows[:, :1024], ((0,), (0,))).astype(bf16)
        grad_right = dot(hidden, grad_rows[:, 1024:], ((0,), (0,))).astype(bf16)
        grad_right = grad_right.reshape(4, 4, 32, 512)
        shrink_at(grad_left.reshape(4, 4, 32, 1024))
        end_at(grad_right[:, :, :16], grad_right[:, :, 16:])
        up_grad = up_ref[0]
        for j in range(4):
            part = dot(rows[:, 384 * j : 384 * (j + 1)], up_grad, ((0,), (0,))).astype(bf16)
            expand_at(j, part.reshape(4, 96, 1024))

    @pl.when(e == 0)
    def _():
        def shrink_at(value):
            own[:, :, 96:128, :] = value

        def end_at(first, second):
            own[:, :, 128:144, :512] = first
            own[:, :, 128:144, 512:] = second

        def expand_at(j, value):
            own[j, :, :96, :] = value

        write(shrink_at, end_at, expand_at)
        low_x.start()
        high_y.start()

    @pl.when(e > 0)
    def _():
        def shrink_at(value):
            out_ref[:, :, 0, 96:128, :] = value

        def end_at(first, second):
            out_ref[:, :, 0, 128:144, :512] = first
            out_ref[:, :, 0, 128:144, 512:] = second

        def expand_at(j, value):
            out_ref[j, :, 0, :96, :] = value

        write(shrink_at, end_at, expand_at)

    @pl.when(e == LOCAL_E - 1)
    def _():
        line_ref[0] = low_x.total().astype(bf16)
        line_ref[1] = high_y.total().astype(bf16)
        low_x.drain()
        high_y.drain()


def expert_grads(rows, cot_rows, row_gates, weights):
    one = lambda e: (e, 0, 0)
    wide = lambda e: (0, e, 0, 0)
    out = lambda e: (0, 0, jnp.maximum(e - 1, 0), 0, 0)
    return pl.pallas_call(
        grads_kernel,
        grid=(LOCAL_E,),
        in_specs=[
            pl.BlockSpec((1, SLOTS, D), one),
            pl.BlockSpec((1, SLOTS, D), one),
            pl.BlockSpec((1, SLOTS, 1), one),
            pl.BlockSpec((16, 1, 144, 1024), wide),
        ],
        out_specs=[
            pl.BlockSpec((1, SLOTS, FF), one),
            pl.BlockSpec((1, SLOTS, 2 * FF), one),
            pl.BlockSpec((4, 4, 1, 144, 1024), out),
            pl.BlockSpec((2, 4, 144, 512), lambda e: (0, 0, 0, 0)),
        ],
        out_shape=[
            jax.ShapeDtypeStruct((LOCAL_E, SLOTS, FF), bf16),
            jax.ShapeDtypeStruct((LOCAL_E, SLOTS, 2 * FF), bf16),
            jax.ShapeDtypeStruct((4, 4, MAIN_E, 144, 1024), bf16),
            jax.ShapeDtypeStruct((2, 4, 144, 512), bf16),
        ],
        scratch_shapes=[pltpu.VMEM((4, 4, 144, 1024), bf16)]
        + reduce_scratch((4, 144, 512), (2, 144, 512)) * 2
        + sems(12),
        compiler_params=remote_params(7),
        cost_estimate=pl.CostEstimate(
            flops=12 * LOCAL_E * SLOTS * D * FF, bytes_accessed=60 << 20, transcendentals=0
        ),
    )(rows, cot_rows, row_gates, weights)


def adamw_step(weight, gradient, mean_old, square_old, rate, decay):
    drift = beta_first * mean_old + (1.0 - beta_first) * gradient
    spread = beta_second * square_old + (1.0 - beta_second) * gradient * gradient
    mean_hat = drift / (1.0 - beta_first**STEP)
    square_hat = spread / (1.0 - beta_second**STEP)
    master = weight - rate * (mean_hat / (jnp.sqrt(square_hat) + adam_eps) + decay * weight)
    return (drift, spread, master)


def on_device(
    activations,
    cotangent,
    seq_lengths,
    deal_order,
    routes,
    entry_weight,
    entry_mean,
    entry_square,
    exit_weight,
    exit_mean,
    exit_square,
    router_weight,
    router_mean,
    router_square,
    expand_weight,
    expand_mean,
    expand_square,
    shrink_weight,
    shrink_mean,
    shrink_square,
    norm_gains,
    gains_mean,
    gains_square,
):
    frequency = rope_base ** (-jnp.arange(HD // 2, dtype=f32) * 2.0 / HD)
    seq_starts = jnp.cumsum(seq_lengths[0]) - seq_lengths[0]

    def trig(positions):
        phase = jnp.tile(positions.astype(f32)[:, None] * frequency[None, :], (1, 4))
        return jnp.cos(phase), jnp.sin(phase)

    token_trig = jnp.stack(trig(jnp.arange(GROUP, dtype=jnp.int32)))
    start_trig = jnp.concatenate(trig(seq_starts), axis=0)
    angles = (seq_lengths, token_trig, start_trig)
    shared_own = jnp.concatenate([router_weight, norm_gains.T], axis=1)
    shared_own = jnp.pad(shared_own, ((0, 0), (0, 128 - EXPERTS - 2)))
    (
        weights, entry_own, shared, exit_own, gains, normed, qkv, attended, lse, middle,
        normed_two, rows, cot_rows, row_gates, rank, my_gates,
    ) = forward(
        activations[0],
        cotangent[0],
        activations[0],
        routes[0],
        deal_order,
        *angles,
        entry_weight,
        exit_weight,
        shared_own,
        expand_weight,
        shrink_weight,
    )
    weights = weights.reshape(16, LOCAL_E, 144, 1024)
    hidden, up_grad, expert_grad, line = expert_grads(rows, cot_rows, row_gates, weights)
    expert_grad = expert_grad.reshape(16, MAIN_E, 144, 1024)
    expert_sum = lax.psum_scatter(expert_grad, PLANE, scatter_dimension=0, tiled=False)
    middle_grad, branch_grad, logit_grad, gain_two_grad, out_sum, extra_sum = turn(
        rank,
        up_grad,
        hidden,
        row_gates,
        cot_rows,
        weights,
        line,
        middle,
        cotangent[0],
        my_gates,
        shared,
        gains[1:2],
    )
    branch_grad = branch_grad.reshape(GROUP, D)
    router_grad = dot(normed_two, logit_grad, ((0,), (0,)))

    input_rows, block_rows, entry_got, exit_got = closing(
        qkv,
        lse,
        *angles,
        exit_own,
        entry_own,
        activations[0],
        middle_grad,
        gains[0:1],
        normed,
        attended,
        branch_grad,
        router_grad,
        gain_two_grad,
        out_sum,
        middle,
    )

    input_grad, block_output = input_rows.astype(bf16), block_rows.astype(bf16)

    entry_got = entry_got[:, :ROWS]
    entry_sum = jnp.concatenate(
        [
            entry_got[:, :, :Q_OWN].transpose(1, 0, 2).reshape(ROWS, QH * HD),
            entry_got[:, :, Q_OWN:MIX_OWN].transpose(1, 0, 2).reshape(ROWS, 2 * KVH * HD),
        ],
        axis=1,
    )
    shared_sum = jnp.sum(entry_got[:, :, MIX_OWN:], axis=0)
    router_sum = shared_sum[:, :EXPERTS]
    gains_sum = shared_sum[:, EXPERTS : EXPERTS + 2].T
    exit_sum = exit_got[:ROWS]

    expand_sum, shrink_sum = to_owners(expert_sum, extra_sum)
    expand_sum, shrink_sum = expand_sum.astype(f32), shrink_sum.astype(f32)
    entry_new = adamw_step(entry_weight, entry_sum, entry_mean, entry_square, 0.02, weight_decay)
    exit_new = adamw_step(exit_weight, exit_sum, exit_mean, exit_square, 0.15, weight_decay)
    router_new = adamw_step(
        router_weight, router_sum, router_mean, router_square, 0.01, weight_decay
    )
    expand_new = adamw_step(
        expand_weight, expand_sum, expand_mean, expand_square, 0.02, weight_decay
    )
    shrink_new = adamw_step(
        shrink_weight, shrink_sum, shrink_mean, shrink_square, 0.12, weight_decay
    )
    gains_new = adamw_step(norm_gains, gains_sum, gains_mean, gains_square, 0.5, 0.0)
    return (
        block_output[None],
        input_grad[None],
        *entry_new,
        *exit_new,
        *router_new,
        *expand_new,
        *shrink_new,
        *gains_new,
    )


def solution(mesh):
    fine = Mesh(mesh.devices.reshape(4, 4, 4, 2), ("seq", "x", "y", "core"))
    rows = P(FSDP, "seq", None)
    lists = P(FSDP, None)
    owned = P(("seq",) + FSDP, None)
    experts = P("seq", FSDP, None)
    gains = P(None, ("seq",) + FSDP)
    return jax.shard_map(
        on_device,
        mesh=fine,
        in_specs=(rows, rows, lists, lists, rows)
        + (owned,) * 9
        + (experts,) * 6
        + (gains,) * 3,
        out_specs=(rows, rows) + (owned,) * 9 + (experts,) * 6 + (gains,) * 3,
        check_vma=False,
    )
```

```python
import jax
import jax.numpy as jnp
import numpy as np
from jax import lax
from jax.experimental import pallas as pl
from jax.experimental.pallas import tpu as pltpu
from jax.sharding import Mesh, PartitionSpec as P

D = 1536
QH = 24
KVH = 8
HD = 64
FF = 512
EXPERTS = 40
TOP = 8
STEP = 10
CAP = 29

N_SEQ = 4
TOK_DEV = 128
GROUP = 512
PAIR_TOK = 2 * GROUP
LOCAL_E = EXPERTS // (2 * N_SEQ)
SLOTS = 256
Q_OWN = QH * HD // N_SEQ
KV_OWN = 2 * KVH * HD // N_SEQ
MIX_OWN = Q_OWN + KV_OWN
HEADS_OWN = QH // N_SEQ
KV_HEADS_OWN = KVH // N_SEQ
PER_KV = QH // KVH
ROWS = 12

norm_eps = 1e-06
rope_base = 10000.0
beta_first = 0.9
beta_second = 0.95
adam_eps = 1e-08
weight_decay = 0.1

FSDP = ("x", "y", "core")
PLANE = ("x", "y")
f32 = jnp.float32
bf16 = jnp.bfloat16


BIG = 60 * 1024 * 1024
HALF = TOK_DEV // 2
QOWN = Q_OWN
MESH = pl.DeviceIdType.MESH
ANY = pl.BlockSpec(memory_space=pl.ANY)
VMEM = pl.BlockSpec(memory_space=pltpu.VMEM)


def dot(a, b, dims):
    return lax.dot_general(a, b, (dims, ((), ())), preferred_element_type=f32)


def greet(peers):
    barrier = pltpu.get_barrier_semaphore()
    for axis, peer in peers:
        pl.semaphore_signal(barrier, inc=1, device_id={axis: peer}, device_id_type=MESH)
    pl.semaphore_wait(barrier, len(peers))


def planner(send_sem, recv_sem):
    def plan(src, dst, index, axis, peer):
        return pltpu.make_async_remote_copy(
            src_ref=src,
            dst_ref=dst,
            send_sem=send_sem.at[index],
            recv_sem=recv_sem.at[index],
            device_id={axis: peer},
            device_id_type=MESH,
        )

    return plan


def sender(send_sem, recv_sem):
    plan = planner(send_sem, recv_sem)

    def send(*args):
        copy = plan(*args)
        copy.start()
        return copy

    return send


def sems(count):
    return [pltpu.SemaphoreType.DMA((count,)), pltpu.SemaphoreType.DMA((count,))]


def ring(me):
    right, left = lax.rem(me + 1, 4), lax.rem(me + 3, 4)
    return right, left, lax.rem(me + 2, 4)


def near(axis):
    right, left, _ = ring(lax.axis_index(axis))
    return [(axis, right), (axis, left)]


def sibling():
    return ("core", 1 - lax.axis_index("core"))


def half_rows(ref, half):
    size = ref.shape[0] // 2
    return ref.at[pl.ds(half * size, size)]


def half_lanes(ref, half):
    size = ref.shape[-1] // 2
    return ref.at[(slice(None),) * (len(ref.shape) - 1) + (pl.ds(half * size, size),)]


class Gather:
    def __init__(self, plan, base, axis, mine, slot, cut):
        me = lax.axis_index(axis)
        right, left, self.far = ring(me)
        self.right, self.left = right, left
        here, from_left, from_right = slot(me), cut(slot(left), 0), cut(slot(right), 1)
        self.first = [
            plan(cut(mine, 0), cut(here, 0), base, axis, right),
            plan(cut(mine, 1), cut(here, 1), base + 1, axis, left),
            plan(cut(mine, 1), cut(here, 1), base + 2, axis, right),
            plan(cut(mine, 0), cut(here, 0), base + 3, axis, left),
        ]
        self.later = [
            plan(from_left, from_left, base + 4, axis, right),
            plan(from_right, from_right, base + 5, axis, left),
        ]

    def start(self):
        for copy in self.first:
            copy.start()
        return self

    def relay(self):
        for got, on in zip(self.first, self.later):
            got.wait_recv()
            on.start()

    def wait_left(self):
        self.first[2].wait_recv()

    def wait_right(self):
        self.first[3].wait_recv()

    def wait_far(self):
        for copy in self.later:
            copy.wait_recv()

    def finish(self):
        self.wait_left()
        self.wait_right()
        self.wait_far()

    def drain(self):
        for copy in self.first + self.later:
            copy.wait_send()


def hand_over(send, base, mine, out, gather):
    me, core = lax.axis_index("seq"), lax.axis_index("core")
    other = 1 - core
    copies = [send(mine, out.at[core, me], base, "core", other)]
    gather.relay()
    gather.wait_left()
    block = out.at[core, gather.left]
    copies.append(send(block, block, base + 1, "core", other))
    gather.wait_right()
    block = out.at[core, gather.right]
    copies.append(send(block, block, base + 2, "core", other))
    gather.wait_far()
    block = out.at[core, gather.far]
    copies.append(send(block, block, base + 3, "core", other))
    return copies


def reduce_scratch(block, half):
    return [pltpu.VMEM(half, bf16)] * 4 + [pltpu.VMEM(block, bf16)] * 2


def added(target, first, second):
    target[...] = (first[...].astype(f32) + second[...].astype(f32)).astype(bf16)


class Reduce:
    def __init__(self, plan, base, axis, block, bufs, cut):
        me = lax.axis_index(axis)
        right, left, far = ring(me)
        from_left, from_right, to_right, to_left, got_left, got_right = bufs
        far, on_right, on_left = block(far), block(right), block(left)
        self.mine, self.got = block(me), (got_left, got_right)
        self.hops = (
            (to_right, cut(on_right, 0), from_left),
            (to_left, cut(on_left, 1), from_right),
        )
        self.far = [
            plan(cut(far, 0), from_left, base, axis, right),
            plan(cut(far, 1), from_right, base + 1, axis, left),
        ]
        self.near = [
            plan(cut(on_right, 1), cut(got_left, 1), base + 2, axis, right),
            plan(cut(on_left, 0), cut(got_right, 0), base + 3, axis, left),
        ]
        self.later = [
            plan(to_right, cut(got_left, 0), base + 4, axis, right),
            plan(to_left, cut(got_right, 1), base + 5, axis, left),
        ]

    def start_far(self):
        for copy in self.far:
            copy.start()

    def start_near(self):
        for copy in self.near:
            copy.start()

    def start(self):
        self.start_far()
        self.start_near()
        return self

    def relay(self):
        for got, hop, on in zip(self.far, self.hops, self.later):
            got.wait_recv()
            added(*hop)
            on.start()

    def total(self):
        for copy in self.near + self.later:
            copy.wait_recv()
        total = self.mine[...].astype(f32)
        for part in self.got:
            total += part[...].astype(f32)
        return total

    def drain(self):
        for copy in self.far + self.near + self.later:
            copy.wait_send()


def remote_params(call_id):
    return pltpu.CompilerParams(
        collective_id=call_id, has_side_effects=True, vmem_limit_bytes=BIG
    )


def unit_scale(vector):
    return lax.rsqrt(jnp.mean(vector * vector, axis=-1, keepdims=True) + norm_eps)


def norm_back(vector, gain, grad):
    scale = unit_scale(vector)
    unit = vector * scale
    pulled = grad * gain
    back = scale * (pulled - unit * jnp.mean(pulled * unit, axis=-1, keepdims=True))
    return back, jnp.sum(unit * grad, axis=0, keepdims=True)


MAIN_E = LOCAL_E - 1


def row_pick(shape, padded_axis):
    padded = lax.broadcasted_iota(jnp.int32, shape, padded_axis)
    plain = lax.broadcasted_iota(jnp.int32, shape, 1 - padded_axis)
    row = lax.rem(padded, 16)
    return ((plain == lax.div(padded, 16) * 12 + row) & (row < 12)).astype(bf16)


def swap_halves(rows, lower, upper):
    lane = lax.broadcasted_iota(jnp.int32, rows.shape, 1)
    ahead = pltpu.roll(rows, rows.shape[1] - HD // 2, 1)
    behind = pltpu.roll(rows, HD // 2, 1)
    return jnp.where(lax.rem(lane, HD) < HD // 2, lower * ahead, upper * behind)


BLOCK = 256


def sequence_of(lengths_ref, token):
    first_end = lengths_ref[0, 0]
    second_end = first_end + lengths_ref[0, 1]
    return (token >= first_end).astype(jnp.int32) + (token >= second_end).astype(jnp.int32)


def block_bias(lengths_ref, block):
    keys = BLOCK * (block + 1)
    row = lax.broadcasted_iota(jnp.int32, (BLOCK, keys), 0) + BLOCK * block
    column = lax.broadcasted_iota(jnp.int32, (BLOCK, keys), 1)
    same = sequence_of(lengths_ref, row) == sequence_of(lengths_ref, column)
    return jnp.where(same & (column <= row), 0.0, -1e30)


def rope_tables(lengths_ref, trig_ref):
    seq = sequence_of(lengths_ref, lax.broadcasted_iota(jnp.int32, (GROUP, 128), 0))
    second = lengths_ref[0, 0]
    third = second + lengths_ref[0, 1]

    def of_start(table):
        later = jnp.where(
            seq == 1, trig_ref[table, pl.ds(second, 1)], trig_ref[table, pl.ds(third, 1)]
        )
        return jnp.where(seq == 0, trig_ref[table, 0:1], later)

    start_cos, start_sin = of_start(0), of_start(1)
    cosine = trig_ref[0] * start_cos + trig_ref[1] * start_sin
    sine = trig_ref[1] * start_cos - trig_ref[0] * start_sin
    is_key = lax.broadcasted_iota(jnp.int32, (GROUP, 128), 1) < HD
    pair_cos, pair_sin = jnp.where(is_key, cosine, 1.0), jnp.where(is_key, sine, 0.0)
    return (
        jnp.concatenate([cosine] * 3 + [pair_cos] * 2, axis=1),
        jnp.concatenate([sine] * 3 + [pair_sin] * 2, axis=1),
    )


def head_of(index):
    return slice(HD * index, HD * (index + 1))


def lane_pick(first, rows):
    row = lax.broadcasted_iota(jnp.int32, (rows, 128), 0)
    lane = lax.broadcasted_iota(jnp.int32, (rows, 128), 1)
    return (lane == row + first).astype(bf16)


def forward_kernel(
    in_hbm, cot_hbm, in_ref, route_ref, order_ref, lengths_ref, trig_ref,
    entry_ref, exit_ref, router_ref, gain_ref, expand_ref, shrink_ref,
    weights_out, entry_out, shared_out, exit_out, gains_out, normed_ref, qkv_ref, attended_ref,
    lse_ref, middle_ref, mine, rows_out, cot_rows_out, row_gate_out, rank_out, my_gate_out,
    stage, stage_end, packed, shared, columns, hold, full,
    in_all, cot_all, hit_all, hit_pair, tokens, part, gates, *rest
):
    bufs, (send_sem, recv_sem, copy_sem) = rest[:6], rest[6:]
    z, x, y, c = (lax.axis_index(a) for a in ("seq", "x", "y", "core"))
    right, left, far = ring(z)
    other = 1 - c
    greet(near("seq") + [("seq", far)] + near("x") + near("y") + [sibling()])
    send, plan = sender(send_sem, recv_sem), planner(send_sem, recv_sem)

    rows = Gather(plan, 9, "seq", in_hbm, lambda i: in_all.at[i], half_rows).start()
    expert = lax.broadcasted_iota(jnp.int32, (128, TOK_DEV), 0)
    hit = route_ref[0:1] == expert
    for k in range(1, TOP):
        hit = hit | (route_ref[k : k + 1] == expert)
    hit_all[z] = hit.astype(bf16)
    hits = Gather(plan, 3, "seq", hit_all.at[z], lambda i: hit_all.at[i], half_rows).start()

    lane = lax.broadcasted_iota(jnp.int32, (ROWS, 128), 1)
    square = lax.broadcasted_iota(jnp.int32, (ROWS, ROWS), 0)
    square = square == lax.broadcasted_iota(jnp.int32, (ROWS, ROWS), 1)
    shared[...] = jnp.zeros_like(shared)
    shared[:, :EXPERTS] = router_ref[...]
    block_of = shared[...]
    for k in range(2):
        column = jnp.sum(jnp.where(square, gain_ref[k : k + 1], 0.0), axis=1, keepdims=True)
        block_of = jnp.where(lane == EXPERTS + k, column, block_of)
    empty = jnp.zeros((PAD_ROWS - ROWS, WIDE), f32)
    for block in range(4):
        cols = jnp.concatenate(
            [
                entry_ref[:, Q_OWN * block : Q_OWN * (block + 1)],
                entry_ref[:, QH * HD + KV_OWN * block : QH * HD + KV_OWN * (block + 1)],
                block_of,
            ],
            axis=1,
        )
        columns[block] = jnp.concatenate([cols, empty], axis=0).astype(bf16)
    to_seq = [
        send(columns.at[peer], hold.at[z], k, "seq", peer)
        for k, peer in enumerate((right, far, left))
    ]
    for block in range(2):
        cols = exit_ref[:, WIDE * block : WIDE * (block + 1)]
        hold[4 + block] = jnp.concatenate([cols, empty], axis=0).astype(bf16)
    hold[z] = columns[z]
    local = [
        pltpu.make_async_copy(in_hbm, in_all.at[z], copy_sem.at[0]),
        pltpu.make_async_copy(cot_hbm, cot_all.at[c, z], copy_sem.at[1]),
    ]
    for copy in local:
        copy.start()

    for e in range(LOCAL_E):
        theirs = other * LOCAL_E + e
        stage[e, :48] = expand_ref[theirs].astype(bf16)
        stage[e, 48:] = shrink_ref[theirs, :, :1024].astype(bf16)
        stage_end[e] = shrink_ref[theirs, :, 1024:].astype(bf16)
    of_core = pl.ds(pl.multiple_of(c * 48, 16), 48)
    lefts = pl.ds(pl.multiple_of(96 + c * 16, 16), 16)
    ends = pl.ds(pl.multiple_of(c * 512, 512), 512)
    to_core = [
        send(stage.at[:, pl.ds(0, 48)], packed.at[:, of_core], 51, "core", other),
        send(stage.at[:, pl.ds(48, 16)], packed.at[:, lefts], 52, "core", other),
        send(stage_end, packed.at[:, pl.ds(128, 16), ends], 53, "core", other),
    ]
    for e in range(LOCAL_E):
        own_e = c * LOCAL_E + e
        packed[e, of_core, :] = expand_ref[own_e].astype(bf16)
        packed[e, lefts, :] = shrink_ref[own_e, :, :1024].astype(bf16)
        packed[e, pl.ds(128, 16), ends] = shrink_ref[own_e, :, 1024:].astype(bf16)
    for copy in to_seq:
        copy.wait_recv()
    for block in range(6):
        full[block, x, y, c] = hold[block]
    low, high = pl.ds(0, 3), pl.ds(3, 3)
    low_x = Gather(plan, 15, "x", hold.at[low], lambda i: full.at[low, i, y, c], half_lanes)
    low_x.start()
    high_y = Gather(plan, 21, "y", hold.at[high], lambda i: full.at[high, x, i, c], half_lanes)
    high_y.start()
    for copy in to_core:
        copy.wait_recv()
    own_weights = pltpu.make_async_copy(packed, weights_out.at[x, y], copy_sem.at[2])
    own_weights.start()
    start, end = pl.ds(0, 512), pl.ds(512, 512)
    expert_x = Gather(
        plan,
        54,
        "x",
        packed.at[:, :, start],
        lambda i: weights_out.at[i, y, :, :, start],
        half_lanes,
    ).start()
    expert_y = Gather(
        plan,
        60,
        "y",
        packed.at[:, :, end],
        lambda i: weights_out.at[x, i, :, :, end],
        half_lanes,
    ).start()

    def cut_low(ref, half):
        return ref.at[:, pl.ds(2 * half, 2)]

    hits.relay()
    low_x.relay()
    high_y.relay()
    rows.relay()
    cots = Gather(plan, 27, "seq", cot_hbm, lambda i: cot_all.at[c, i], half_rows).start()
    low_x.finish()
    low_y = Gather(
        plan, 33, "y", full.at[low, :, y, c], lambda i: full.at[low, :, i, c], cut_low
    ).start()
    high_y.finish()
    high_x = Gather(
        plan, 39, "x", full.at[high, x, :, c], lambda i: full.at[high, i, :, c], cut_low
    ).start()
    expert_x.relay()
    expert_y.relay()

    hits.finish()
    token = lax.broadcasted_iota(jnp.int32, (GROUP, GROUP), 0)
    back_hot = (order_ref[...] == token).astype(bf16)
    natural = jnp.zeros((GROUP, 128), f32)
    for block in range(N_SEQ):
        slots = back_hot[:, TOK_DEV * block : TOK_DEV * (block + 1)]
        natural += dot(slots, hit_all[block], ((1,), (1,)))
    hit_pair[c] = natural.astype(bf16)
    hit_swap = send(hit_pair.at[c], hit_pair.at[c], 66, "core", other)
    low_y.relay()
    high_x.relay()
    hit_swap.wait_recv()
    hit_both = hit_pair[...].reshape(PAIR_TOK, 128)
    first = (z * 2 + c) * LOCAL_E
    lower = lax.broadcasted_iota(jnp.int32, (PAIR_TOK, PAIR_TOK), 0)
    lower = (lower >= lax.broadcasted_iota(jnp.int32, (PAIR_TOK, PAIR_TOK), 1)).astype(bf16)
    rank = dot(lower, hit_both, ((1,), (0,))) - 1.0
    rank = jnp.where(hit_both.astype(f32) > 0.0, rank, -1.0).astype(bf16)
    mine_of = lane_pick(first, 8)
    rank_out[...] = dot(rank, mine_of, ((1,), (1,))).astype(jnp.int32)
    rank_rows = dot(mine_of, rank, ((1,), (1,))).astype(jnp.int32)

    low_y.finish()
    half = full.at[low, :, :, c]
    last = [send(half, half, 49, "core", other)]
    high_x.finish()
    half = full.at[high, :, :, c]
    last.append(send(half, half, 50, "core", other))
    own_weights.wait()
    expert_x.finish()
    expert_low = Gather(
        plan,
        67,
        "y",
        weights_out.at[:, y, :, :, start],
        lambda i: weights_out.at[:, i, :, :, start],
        half_rows,
    ).start()
    expert_y.finish()
    expert_high = Gather(
        plan,
        73,
        "x",
        weights_out.at[x, :, :, :, end],
        lambda i: weights_out.at[i, :, :, :, end],
        half_rows,
    ).start()
    cosine, sine = rope_tables(lengths_ref, trig_ref)
    rows.finish()
    local[0].wait()
    for copy in last:
        copy.wait_recv()
    pick = row_pick((QOWN, 512), 1)
    for block in range(4):
        got = dot(pick, full[block].reshape(512, WIDE), ((1,), (0,))).astype(bf16)
        entry_out[QOWN * block : QOWN * (block + 1), :] = got[:, :MIX_OWN]
        shared_out[QOWN * block : QOWN * (block + 1), :] = got[:, MIX_OWN:]
    for block in range(2):
        got = dot(pick, full[4 + block].reshape(512, WIDE), ((1,), (0,))).astype(bf16)
        exit_out[:, WIDE * block : WIDE * (block + 1)] = got
    gains = dot(lane_pick(EXPERTS, 8), shared_out[...], ((1,), (1,)))
    gains_out[...] = gains
    for block in range(N_SEQ):
        at = slice(TOK_DEV * block, TOK_DEV * (block + 1))
        vector = in_all[block].astype(f32)
        normed_ref[at, :] = (vector * unit_scale(vector) * gains[0:1]).astype(bf16)
    mixed = dot(normed_ref[...], entry_out[...], ((1,), (0,)))
    mixed = mixed * cosine + swap_halves(mixed, -1.0, 1.0) * sine
    qkv_ref[...] = mixed.astype(bf16)
    for block in range(GROUP // BLOCK):
        bias = block_bias(lengths_ref, block)
        keys = BLOCK * (block + 1)
        at = slice(BLOCK * block, keys)
        for head in range(HEADS_OWN):
            pair = Q_OWN + 2 * HD * (head // PER_KV)
            key = qkv_ref[:keys, pair : pair + HD]
            value = qkv_ref[:keys, pair + HD : pair + 2 * HD]
            scores = dot(qkv_ref[at, head_of(head)], key, ((1,), (1,))) * HD**-0.5 + bias
            peak = jnp.max(scores, axis=1, keepdims=True)
            expo = jnp.exp(scores - peak)
            total = jnp.sum(expo, axis=1, keepdims=True)
            probs = (expo / total).astype(bf16)
            attended_ref[at, head_of(head)] = dot(probs, value, ((1,), (0,))).astype(bf16)
            lse_ref[at, head : head + 1] = peak + jnp.log(total)
    part[...] = dot(attended_ref[...], exit_out[...], ((1,), (0,))).astype(bf16).reshape(part.shape)
    reduce = Reduce(plan, 79, "seq", lambda i: part.at[i], bufs, half_rows).start()
    pairs = hand_over(send, 45, cot_hbm, cot_all, cots)
    reduce.relay()
    middle = in_ref[...].astype(f32) + reduce.total()
    middle_ref[...] = middle
    mine[...] = (middle * unit_scale(middle) * gains[1:2]).astype(bf16)
    gather = Gather(plan, 85, "seq", mine, lambda i: tokens.at[c, i], half_rows).start()
    tokens[c, z] = mine[...]
    pairs += hand_over(send, 91, mine, tokens, gather)
    for copy in pairs:
        copy.wait()
    local[1].wait()

    logits = dot(tokens[...].reshape(PAIR_TOK, D), shared_out[...], ((1,), (0,)))
    masked = jnp.where(hit_both.astype(f32) > 0.0, logits, -jnp.inf)
    gate_expo = jnp.exp(masked - jnp.max(masked, axis=1, keepdims=True))
    gates[...] = gate_expo / jnp.sum(gate_expo, axis=1, keepdims=True)
    my_gate_out[...] = gates[pl.ds(pl.multiple_of(c * GROUP + z * TOK_DEV, TOK_DEV), TOK_DEV), :]
    rest_of = gates[...]
    gate_rows = jnp.zeros((8, PAIR_TOK), f32)
    for _ in range(3):
        piece = rest_of.astype(bf16)
        gate_rows += dot(mine_of, piece, ((1,), (1,)))
        rest_of -= piece.astype(f32)
    slot = lax.broadcasted_iota(jnp.int32, (SLOTS, PAIR_TOK), 0)
    for e in range(LOCAL_E):
        if e == 3:
            expert_low.relay()
            expert_high.relay()
        match = rank_rows[e : e + 1] == slot
        row_gate_out[e] = jnp.sum(
            jnp.where(match, gate_rows[e : e + 1], 0.0), axis=1, keepdims=True
        )
        match = match.astype(bf16)
        for half in range(2):
            lanes = slice(768 * half, 768 * (half + 1))
            table = tokens[:, :, :, lanes].reshape(PAIR_TOK, 768)
            rows_out[e, :, lanes] = dot(match, table, ((1,), (0,))).astype(bf16)
            table = cot_all[:, :, :, lanes].reshape(PAIR_TOK, 768)
            cot_rows_out[e, :, lanes] = dot(match, table, ((1,), (0,))).astype(bf16)
    expert_low.finish()
    expert_high.finish()
    for copy in to_seq + to_core + last + [hit_swap]:
        copy.wait_send()
    for transfer in (hits, rows, cots, low_x, high_y, low_y, high_x, reduce, gather):
        transfer.drain()
    for transfer in (expert_x, expert_y, expert_low, expert_high):
        transfer.drain()


def forward(*operands):
    scalar = pl.BlockSpec(memory_space=pltpu.SMEM)
    block = (PAD_ROWS, WIDE)
    group = (N_SEQ, TOK_DEV, D)
    return pl.pallas_call(
        forward_kernel,
        out_shape=[
            jax.ShapeDtypeStruct((4, 4, LOCAL_E, 144, 1024), bf16),
            jax.ShapeDtypeStruct((D, MIX_OWN), bf16),
            jax.ShapeDtypeStruct((D, 128), bf16),
            jax.ShapeDtypeStruct((QOWN, D), bf16),
            jax.ShapeDtypeStruct((8, D), f32),
            jax.ShapeDtypeStruct((GROUP, D), bf16),
            jax.ShapeDtypeStruct((GROUP, MIX_OWN), bf16),
            jax.ShapeDtypeStruct((GROUP, Q_OWN), bf16),
            jax.ShapeDtypeStruct((GROUP, HEADS_OWN), f32),
            jax.ShapeDtypeStruct((TOK_DEV, D), f32),
            jax.ShapeDtypeStruct((TOK_DEV, D), bf16),
            jax.ShapeDtypeStruct((LOCAL_E, SLOTS, D), bf16),
            jax.ShapeDtypeStruct((LOCAL_E, SLOTS, D), bf16),
            jax.ShapeDtypeStruct((LOCAL_E, SLOTS, 1), f32),
            jax.ShapeDtypeStruct((PAIR_TOK, 8), jnp.int32),
            jax.ShapeDtypeStruct((TOK_DEV, 128), f32),
        ],
        in_specs=[ANY] * 2 + [VMEM] * 3 + [scalar] + [VMEM] * 7,
        out_specs=[ANY] + [VMEM] * 15,
        scratch_shapes=[
            pltpu.VMEM((LOCAL_E, 64, 1024), bf16),
            pltpu.VMEM((LOCAL_E, 16, 512), bf16),
            pltpu.VMEM((LOCAL_E, 144, 1024), bf16),
            pltpu.VMEM((ROWS, 128), f32),
            pltpu.VMEM((4,) + block, bf16),
            pltpu.VMEM((6,) + block, bf16),
            pltpu.VMEM((6, 4, 4, 2) + block, bf16),
            pltpu.VMEM(group, bf16),
            pltpu.VMEM((2,) + group, bf16),
            pltpu.VMEM((N_SEQ, TOK_DEV, 128), bf16),
            pltpu.VMEM((2, GROUP, 128), bf16),
            pltpu.VMEM((2,) + group, bf16),
            pltpu.VMEM(group, bf16),
            pltpu.VMEM((PAIR_TOK, 128), f32),
        ]
        + reduce_scratch((TOK_DEV, D), (HALF, D))
        + sems(95)
        + [pltpu.SemaphoreType.DMA((3,))],
        compiler_params=remote_params(2),
    )(*operands)


def turn_kernel(
    rank_ref, up_ref, hidden_ref, gate_ref, cot_rows_ref, w_ref,
    line, middle_ref, cot_ref, my_gate_ref, router_ref, gain_ref,
    grad_ref, branch_ref, logit_ref, gain_grad_ref, out_sum_ref, extra_sum_ref,
    back_s, out_s, other_back, from_core, part, other_out, out_core, mine, *rest
):
    bufs, (send_sem, recv_sem, copy_sem) = [rest[6 * i : 6 * i + 6] for i in range(3)], rest[18:]
    e = pl.program_id(0)
    me, core = lax.axis_index("seq"), lax.axis_index("core")
    send, plan = sender(send_sem, recv_sem), planner(send_sem, recv_sem)
    low_y = Reduce(plan, 17, "y", lambda i: line.at[0, i], bufs[1], half_lanes)
    high_x = Reduce(plan, 23, "x", lambda i: line.at[1, i], bufs[2], half_lanes)

    @pl.when(e == 0)
    def _():
        greet(near("seq") + near("x") + near("y") + [sibling()])
        low_y.start()
        high_x.start()

    @pl.when(e == 2)
    def _():
        low_y.relay()
        high_x.relay()

    @pl.when(e < LOCAL_E)
    def _():
        expand, left, right = weights_of(w_ref)
        at = pl.ds(pl.multiple_of(e * SLOTS, SLOTS), SLOTS)
        back_s[at, :D] = dot(up_ref[0], expand, ((1,), (1,))).astype(bf16)
        hidden = hidden_ref[0]
        expert_out = jnp.concatenate(
            [dot(hidden, left, ((1,), (0,))), dot(hidden, right, ((1,), (0,)))], axis=1
        )
        expert_out = expert_out.astype(bf16).astype(f32)
        gate_grad = jnp.sum(expert_out * cot_rows_ref[0].astype(f32), axis=1, keepdims=True)
        lane = lax.broadcasted_iota(jnp.int32, (SLOTS, 128), 1)
        column = (me * 2 + core) * LOCAL_E + e
        back_s[at, D:] = jnp.where(lane == column, gate_grad, 0.0).astype(bf16)
        out_s[at, :] = (gate_ref[0] * expert_out).astype(bf16)

    @pl.when(e == LOCAL_E)
    def _():
        other = 1 - core
        right, left, far = ring(me)
        slot = lax.broadcasted_iota(jnp.int32, (GROUP, SLOTS), 1)

        def picks(group):
            at = pl.ds(pl.multiple_of(group * GROUP, GROUP), GROUP)
            ranks = rank_ref[at, :]
            return jnp.concatenate(
                [(ranks[:, k : k + 1] == slot).astype(bf16) for k in range(LOCAL_E)], axis=1
            )

        theirs, ours = picks(other), picks(core)
        order = (far, right, left, me)
        other_back[...] = (
            dot(theirs, back_s[...], ((1,), (0,))).astype(bf16).reshape(other_back.shape)
        )
        swaps = [
            send(other_back.at[block], from_core.at[block], 12 + i, "core", other)
            for i, block in enumerate(order)
        ]
        part[...] = dot(ours, back_s[...], ((1,), (0,))).astype(bf16).reshape(part.shape)
        reduce = Reduce(plan, 0, "seq", lambda i: part.at[i], bufs[0], half_rows)
        for i, block in enumerate(order):
            swaps[i].wait_recv()
            added(part.at[block], part.at[block], from_core.at[block])
            if i == 0:
                reduce.start_far()
            if i == 2:
                reduce.start_near()
        other_out[...] = (
            dot(theirs, out_s[...], ((1,), (0,))).astype(bf16).reshape(other_out.shape)
        )
        out_swap = send(other_out, out_core, 16, "core", other)
        reduce.relay()
        out_sum_ref[...] = (
            dot(ours, out_s[...], ((1,), (0,))).astype(bf16).reshape(out_sum_ref.shape)
        )
        total = reduce.total()
        gates, gate_grad = my_gate_ref[...], total[:, D:]
        mean_term = jnp.sum(gates * gate_grad, axis=1, keepdims=True)
        logit_grad = (gates * (gate_grad - mean_term)).astype(bf16)
        logit_ref[...] = logit_grad
        normed_grad = total[:, :D] + dot(logit_grad, router_ref[...], ((1,), (1,)))
        back, gain_grad = norm_back(middle_ref[...], gain_ref[...], normed_grad)
        gain_grad_ref[...] = gain_grad
        middle_grad = cot_ref[...].astype(f32) + back
        grad_ref[...] = middle_grad
        mine[...] = middle_grad.astype(bf16)
        gather = Gather(plan, 6, "seq", mine, lambda i: branch_ref.at[i], half_rows).start()
        local = pltpu.make_async_copy(mine, branch_ref.at[me], copy_sem)
        local.start()
        out_swap.wait_recv()
        added(out_sum_ref, out_sum_ref, out_core)
        gather.relay()
        extra_sum_ref[:, :512] = low_y.total().astype(bf16)
        extra_sum_ref[:, 512:] = high_x.total().astype(bf16)
        gather.finish()
        for transfer in (gather, reduce, low_y, high_x):
            transfer.drain()
        for copy in swaps + [out_swap]:
            copy.wait_send()
        local.wait()


BACK_WIDTH = D + 128


def turn(*operands):
    one = lambda e: (jnp.minimum(e, LOCAL_E - 1), 0, 0)
    wide = lambda e: (0, jnp.minimum(e, LOCAL_E - 1), 0, 0)
    cubes = lambda e: (0, 0, 0, 0)
    whole = lambda e: (0, 0)
    blocks = lambda e: (0, 0, 0)
    row_block = pl.BlockSpec((TOK_DEV, D), whole)
    lane_block = pl.BlockSpec((TOK_DEV, 128), whole)
    gain_block = pl.BlockSpec((1, D), whole)
    group = pltpu.VMEM((N_SEQ, TOK_DEV, BACK_WIDTH), bf16)
    group_out = pltpu.VMEM((N_SEQ, TOK_DEV, D), bf16)
    return pl.pallas_call(
        turn_kernel,
        grid=(LOCAL_E + 1,),
        in_specs=[
            pl.BlockSpec((PAIR_TOK, 8), whole),
            pl.BlockSpec((1, SLOTS, 2 * FF), one),
            pl.BlockSpec((1, SLOTS, FF), one),
            pl.BlockSpec((1, SLOTS, 1), one),
            pl.BlockSpec((1, SLOTS, D), one),
            pl.BlockSpec((16, 1, 144, 1024), wide),
            pl.BlockSpec((2, 4, 144, 512), cubes),
            row_block,
            row_block,
            lane_block,
            pl.BlockSpec((D, 128), whole),
            gain_block,
        ],
        out_specs=[
            row_block,
            ANY,
            lane_block,
            gain_block,
            pl.BlockSpec((N_SEQ, TOK_DEV, D), blocks),
            pl.BlockSpec((144, 1024), whole),
        ],
        out_shape=[
            jax.ShapeDtypeStruct((TOK_DEV, D), f32),
            jax.ShapeDtypeStruct((N_SEQ, TOK_DEV, D), bf16),
            jax.ShapeDtypeStruct((TOK_DEV, 128), bf16),
            jax.ShapeDtypeStruct((1, D), f32),
            jax.ShapeDtypeStruct((N_SEQ, TOK_DEV, D), bf16),
            jax.ShapeDtypeStruct((144, 1024), bf16),
        ],
        scratch_shapes=[
            pltpu.VMEM((LOCAL_E * SLOTS, BACK_WIDTH), bf16),
            pltpu.VMEM((LOCAL_E * SLOTS, D), bf16),
            group,
            group,
            group,
            group_out,
            group_out,
            pltpu.VMEM((TOK_DEV, D), bf16),
        ]
        + reduce_scratch((TOK_DEV, BACK_WIDTH), (HALF, BACK_WIDTH))
        + reduce_scratch((144, 512), (144, 256)) * 2
        + sems(29)
        + [pltpu.SemaphoreType.DMA],
        compiler_params=remote_params(4),
        cost_estimate=pl.CostEstimate(
            flops=6 * LOCAL_E * SLOTS * D * FF + 4 * LOCAL_E * SLOTS * PAIR_TOK * D,
            bytes_accessed=40 << 20,
            transcendentals=0,
        ),
    )(*operands)


PAD_ROWS = 16
WIDE = 768
def closing_kernel(
    qkv_ref, lse_ref, lengths_ref, trig_ref, exit_ref, entry_ref,
    in_ref, grad_ref, gain_ref, normed_ref, attended_ref, branch_ref,
    router_grad_ref, gain_two_ref, out_sum_ref, middle_ref,
    input_ref, block_ref, entry_out, exit_out,
    turned, mixed_grad, part, full, from_core, chip, line, final, give, got_z, *rest
):
    bufs, (send_sem, recv_sem) = [rest[6 * i : 6 * i + 6] for i in range(8)], rest[48:]
    z, x, y, c = (lax.axis_index(a) for a in ("seq", "x", "y", "core"))
    right, left, far = ring(z)
    greet(near("seq") + [("seq", far)] + near("x") + near("y") + [sibling()])
    send, plan = sender(send_sem, recv_sem), planner(send_sem, recv_sem)
    pick = row_pick((512, QOWN), 0)

    def spread(grad):
        wide = dot(pick, grad, ((1,), (0,))).astype(bf16)
        return wide.reshape(16, 2, PAD_ROWS, grad.shape[1])

    def swap(side):
        return send(full.at[side, :, 1 - c], from_core.at[side], 48 + side, "core", 1 - c)

    def chip_sum(side, copy):
        copy.wait_recv()
        for plane in range(16):
            first, second = (plane % 4, plane // 4) if side == 2 else (plane // 4, plane % 4)
            added(chip.at[side, first, second], full.at[side, plane, c], from_core.at[side, plane])

    def first_sum(side, axis):
        return Reduce(
            plan, 6 * side, axis, lambda i: chip.at[side, i], bufs[side], half_rows
        ).start()

    def second_sum(side, axis, reduce):
        line[side] = reduce.total().astype(bf16)
        return Reduce(
            plan, 18 + 6 * side, axis, lambda i: line.at[side, i], bufs[3 + side], half_lanes
        ).start()

    for block in range(3):
        cols = slice(512 * block, 512 * (block + 1))
        grad = dot(attended_ref[...], branch_ref[:, cols], ((0,), (0,))).astype(bf16)
        full[0, :, :, :, cols] = spread(grad)
    swaps = [swap(0)]
    outs = Reduce(plan, 36, "seq", lambda i: out_sum_ref.at[i], bufs[6], half_rows).start()

    def turn_back(kv):
        pair = Q_OWN + 2 * HD * kv
        for head in range(PER_KV * kv, PER_KV * (kv + 1)):
            grad = dot(branch_ref[...], exit_ref[head_of(head), :], ((1,), (1,))).astype(bf16)
            attended = attended_ref[:, head_of(head)].astype(f32)
            delta = jnp.sum(grad.astype(f32) * attended, axis=1, keepdims=True)
            for block in range(GROUP // BLOCK):
                bias = block_bias(lengths_ref, block)
                keys = BLOCK * (block + 1)
                rows = slice(BLOCK * block, keys)
                key = qkv_ref[:keys, pair : pair + HD]
                value = qkv_ref[:keys, pair + HD : pair + 2 * HD]
                query, grad_rows = qkv_ref[rows, head_of(head)], grad[rows]
                scores = dot(query, key, ((1,), (1,))) * HD**-0.5 + bias
                probs = jnp.exp(scores - lse_ref[rows, head : head + 1])
                prob_grad = dot(grad_rows, value, ((1,), (1,)))
                score_grad = probs * (prob_grad - delta[rows]) * HD**-0.5
                score_grad = score_grad.astype(bf16)
                turned[rows, head_of(head)] = dot(score_grad, key, ((1,), (0,)))
                key_grad = dot(score_grad, query, ((0,), (0,)))
                value_grad = dot(probs.astype(bf16), grad_rows, ((0,), (0,)))
                if head == PER_KV * kv and block == GROUP // BLOCK - 1:
                    turned[:, pair : pair + HD] = key_grad
                    turned[:, pair + HD : pair + 2 * HD] = value_grad
                    turned[:BLOCK, pair : pair + HD] += held[0]
                    turned[:BLOCK, pair + HD : pair + 2 * HD] += held[1]
                elif head == PER_KV * kv:
                    held = (key_grad, value_grad)
                else:
                    turned[:keys, pair : pair + HD] += key_grad
                    turned[:keys, pair + HD : pair + 2 * HD] += value_grad

    turn_back(0)
    chip_sum(0, swaps[0])
    first_0 = first_sum(0, "x")
    outs.relay()
    turn_back(1)
    first_0.relay()
    grads = turned[...]
    cosine, sine = rope_tables(lengths_ref, trig_ref)
    grads = grads * cosine + swap_halves(grads, 1.0, -1.0) * sine
    mixed_grad[...] = grads.astype(bf16)
    part[...] = (
        dot(mixed_grad[...], entry_ref[...], ((1,), (1,))).astype(bf16).reshape(part.shape)
    )
    rows = Reduce(plan, 42, "seq", lambda i: part.at[i], bufs[7], half_rows).start()

    def entry_rows(block):
        rows_of = slice(QOWN * block, QOWN * (block + 1))
        grad = dot(normed_ref[:, rows_of], mixed_grad[...], ((0,), (0,))).astype(bf16)
        return spread(grad)

    full[1, :, :, :, :640] = entry_rows(0)
    full[1, :, :, :, 640:1280] = entry_rows(1)
    third = entry_rows(2)
    full[1, :, :, :, 1280:] = third[..., :256]
    swaps.append(swap(1))
    rows.relay()
    second_0 = second_sum(0, "y", first_0)
    full[2, :, :, :, :384] = third[..., 256:]
    full[2, :, :, :, 384:1024] = entry_rows(3)
    chip_sum(1, swaps[1])
    first_1 = first_sum(1, "x")
    back, gain_one = norm_back(in_ref[...].astype(f32), gain_ref[...], rows.total())
    input_ref[...] = grad_ref[...] + back
    row_of = lax.broadcasted_iota(jnp.int32, (128, D), 0)
    gains = jnp.where(row_of == EXPERTS, gain_one, 0.0)
    gains = jnp.where(row_of == EXPERTS + 1, gain_two_ref[...], gains)
    shared = router_grad_ref[...] + gains.T
    for block in range(4):
        shared_rows = shared[QOWN * block : QOWN * (block + 1), :].astype(bf16)
        full[2, :, :, :, 1024 + 128 * block : 1152 + 128 * block] = spread(shared_rows)
    swaps.append(swap(2))
    second_0.relay()
    block_ref[...] = middle_ref[...] + outs.total()
    chip_sum(2, swaps[2])
    first_2 = first_sum(2, "y")
    first_1.relay()
    first_2.relay()
    exit_out[...] = second_0.total()
    second_1 = second_sum(1, "y", first_1)
    second_2 = second_sum(2, "x", first_2)
    second_1.relay()
    second_2.relay()
    final[0] = second_1.total()
    final[1] = second_2.total()
    give[0, :, :MIX_OWN] = final[0, :, :640]
    give[1, :, :MIX_OWN] = final[0, :, 640:1280]
    give[2, :, :256] = final[0, :, 1280:]
    give[2, :, 256:MIX_OWN] = final[1, :, :384]
    give[3, :, :MIX_OWN] = final[1, :, 384:1024]
    for block in range(4):
        give[block, :, MIX_OWN:] = final[1, :, 1024 + 128 * block : 1152 + 128 * block]
    home = [
        send(give.at[peer], got_z.at[k], 51 + k, "seq", peer)
        for k, peer in enumerate((right, far, left))
    ]
    entry_out[z] = give[z]
    for k, source in enumerate((left, far, right)):
        home[k].wait_recv()
        entry_out[source] = got_z[k]
    for copy in swaps + home:
        copy.wait_send()
    for reduce in (rows, outs, first_0, first_1, first_2, second_0, second_1, second_2):
        reduce.drain()


def closing(*operands):
    row_bufs = reduce_scratch((TOK_DEV, D), (HALF, D))
    chip_bufs = reduce_scratch((4, PAD_ROWS, D), (2, PAD_ROWS, D))
    line_bufs = reduce_scratch((PAD_ROWS, D), (PAD_ROWS, D // 2))
    tile = (PAD_ROWS, D)
    return pl.pallas_call(
        closing_kernel,
        out_shape=[
            jax.ShapeDtypeStruct((TOK_DEV, D), f32),
            jax.ShapeDtypeStruct((TOK_DEV, D), f32),
            jax.ShapeDtypeStruct((4, PAD_ROWS, WIDE), f32),
            jax.ShapeDtypeStruct((PAD_ROWS, D), f32),
        ],
        in_specs=[VMEM] * 2
        + [pl.BlockSpec(memory_space=pltpu.SMEM)]
        + [VMEM] * (len(operands) - 3),
        out_specs=[VMEM] * 4,
        scratch_shapes=[
            pltpu.VMEM((GROUP, MIX_OWN), f32),
            pltpu.VMEM((GROUP, MIX_OWN), bf16),
            pltpu.VMEM((N_SEQ, TOK_DEV, D), bf16),
            pltpu.VMEM((3, 16, 2) + tile, bf16),
            pltpu.VMEM((3, 16) + tile, bf16),
            pltpu.VMEM((3, 4, 4) + tile, bf16),
            pltpu.VMEM((3, 4) + tile, bf16),
            pltpu.VMEM((2,) + tile, f32),
            pltpu.VMEM((4, PAD_ROWS, WIDE), f32),
            pltpu.VMEM((3, PAD_ROWS, WIDE), f32),
        ]
        + chip_bufs * 3
        + line_bufs * 3
        + row_bufs * 2
        + sems(54),
        compiler_params=remote_params(5),
    )(*operands)


def owner_kernel(sum_ref, extra_ref, expand_ref, shrink_ref, send_sem, recv_sem):
    core = lax.axis_index("core")
    greet([sibling()])
    send = sender(send_sem, recv_sem)
    most, single = pl.ds(core * LOCAL_E + 1, MAIN_E), core * LOCAL_E

    def parts(owner):
        return (
            pl.ds(pl.multiple_of(owner * 48, 16), 48),
            pl.ds(pl.multiple_of(96 + owner * 16, 16), 16),
            pl.ds(pl.multiple_of(owner * 512, 512), 512),
        )

    rows, left, ends = parts(1 - core)
    low, start, end = pl.ds(128, 16), pl.ds(0, 1024), pl.ds(1024, 512)
    pieces = [
        (sum_ref.at[:, rows], expand_ref.at[most]),
        (sum_ref.at[:, left], shrink_ref.at[most, :, start]),
        (sum_ref.at[:, low, ends], shrink_ref.at[most, :, end]),
        (extra_ref.at[rows], expand_ref.at[single]),
        (extra_ref.at[left], shrink_ref.at[single, :, start]),
        (extra_ref.at[low, ends], shrink_ref.at[single, :, end]),
    ]
    copies = [
        send(source, target, k, "core", 1 - core) for k, (source, target) in enumerate(pieces)
    ]
    rows, left, ends = parts(core)
    for e in range(LOCAL_E):
        source = extra_ref if e == 0 else sum_ref.at[e - 1]
        expert = core * LOCAL_E + e
        expand_ref[expert] = source[rows, :]
        shrink_ref[expert, :, :1024] = source[left, :]
        shrink_ref[expert, :, 1024:] = source[low, ends]
    for copy in copies:
        copy.wait()


def to_owners(summed, extra):
    return pl.pallas_call(
        owner_kernel,
        out_shape=[
            jax.ShapeDtypeStruct((2 * LOCAL_E, 48, 1024), bf16),
            jax.ShapeDtypeStruct((2 * LOCAL_E, 16, D), bf16),
        ],
        in_specs=[VMEM] * 2,
        out_specs=[VMEM] * 2,
        scratch_shapes=sems(6),
        compiler_params=remote_params(6),
    )(summed, extra)


def weights_of(w_ref):
    expand = w_ref[:, 0, :96, :].reshape(D, 2 * FF)
    left = w_ref[:, 0, 96:128, :].reshape(FF, 1024)
    right = jnp.concatenate([w_ref[:, 0, 128:144, :512], w_ref[:, 0, 128:144, 512:]], axis=1)
    return expand, left, right.reshape(FF, 512)

def grads_kernel(
    rows_ref, cot_ref, gate_ref, w_ref, hidden_ref, up_ref, out_ref, line_ref, own, *rest
):
    bufs, (send_sem, recv_sem) = [rest[6 * i : 6 * i + 6] for i in range(2)], rest[12:]
    e = pl.program_id(0)
    plan = planner(send_sem, recv_sem)
    low, high = pl.ds(0, 512), pl.ds(512, 512)
    low_x = Reduce(plan, 0, "x", lambda i: own.at[i, :, :, low], bufs[0], half_rows)
    high_y = Reduce(plan, 6, "y", lambda i: own.at[:, i, :, high], bufs[1], half_rows)

    @pl.when(e == 0)
    def _():
        greet(near("x") + near("y"))

    expand, left, right = weights_of(w_ref)
    grad_rows = (gate_ref[0] * cot_ref[0].astype(f32)).astype(bf16)
    rows = rows_ref[0]
    gate_pre = dot(rows, expand[:, :FF], ((1,), (0,)))
    up_part = dot(rows, expand[:, FF:], ((1,), (0,)))
    sig = jax.nn.sigmoid(gate_pre)
    hidden = (gate_pre * sig * up_part).astype(bf16)
    hidden_ref[0] = hidden

    @pl.when(e == 2)
    def _():
        low_x.relay()
        high_y.relay()

    hidden_grad = dot(grad_rows[:, :1024], left, ((1,), (1,))) + dot(
        grad_rows[:, 1024:], right, ((1,), (1,))
    )
    up_ref[0, :, :FF] = (hidden_grad * up_part * sig * (1.0 + gate_pre * (1.0 - sig))).astype(bf16)
    up_ref[0, :, FF:] = (hidden_grad * gate_pre * sig).astype(bf16)

    def write(shrink_at, end_at, expand_at):
        grad_left = dot(hidden, grad_rows[:, :1024], ((0,), (0,))).astype(bf16)
        grad_right = dot(hidden, grad_rows[:, 1024:], ((0,), (0,))).astype(bf16)
        grad_right = grad_right.reshape(4, 4, 32, 512)
        shrink_at(grad_left.reshape(4, 4, 32, 1024))
        end_at(grad_right[:, :, :16], grad_right[:, :, 16:])
        up_grad = up_ref[0]
        for j in range(4):
            part = dot(rows[:, 384 * j : 384 * (j + 1)], up_grad, ((0,), (0,))).astype(bf16)
            expand_at(j, part.reshape(4, 96, 1024))

    @pl.when(e == 0)
    def _():
        def shrink_at(value):
            own[:, :, 96:128, :] = value

        def end_at(first, second):
            own[:, :, 128:144, :512] = first
            own[:, :, 128:144, 512:] = second

        def expand_at(j, value):
            own[j, :, :96, :] = value

        write(shrink_at, end_at, expand_at)
        low_x.start()
        high_y.start()

    @pl.when(e > 0)
    def _():
        def shrink_at(value):
            out_ref[:, :, 0, 96:128, :] = value

        def end_at(first, second):
            out_ref[:, :, 0, 128:144, :512] = first
            out_ref[:, :, 0, 128:144, 512:] = second

        def expand_at(j, value):
            out_ref[j, :, 0, :96, :] = value

        write(shrink_at, end_at, expand_at)

    @pl.when(e == LOCAL_E - 1)
    def _():
        line_ref[0] = low_x.total().astype(bf16)
        line_ref[1] = high_y.total().astype(bf16)
        low_x.drain()
        high_y.drain()


def expert_grads(rows, cot_rows, row_gates, weights):
    one = lambda e: (e, 0, 0)
    wide = lambda e: (0, e, 0, 0)
    out = lambda e: (0, 0, jnp.maximum(e - 1, 0), 0, 0)
    return pl.pallas_call(
        grads_kernel,
        grid=(LOCAL_E,),
        in_specs=[
            pl.BlockSpec((1, SLOTS, D), one),
            pl.BlockSpec((1, SLOTS, D), one),
            pl.BlockSpec((1, SLOTS, 1), one),
            pl.BlockSpec((16, 1, 144, 1024), wide),
        ],
        out_specs=[
            pl.BlockSpec((1, SLOTS, FF), one),
            pl.BlockSpec((1, SLOTS, 2 * FF), one),
            pl.BlockSpec((4, 4, 1, 144, 1024), out),
            pl.BlockSpec((2, 4, 144, 512), lambda e: (0, 0, 0, 0)),
        ],
        out_shape=[
            jax.ShapeDtypeStruct((LOCAL_E, SLOTS, FF), bf16),
            jax.ShapeDtypeStruct((LOCAL_E, SLOTS, 2 * FF), bf16),
            jax.ShapeDtypeStruct((4, 4, MAIN_E, 144, 1024), bf16),
            jax.ShapeDtypeStruct((2, 4, 144, 512), bf16),
        ],
        scratch_shapes=[pltpu.VMEM((4, 4, 144, 1024), bf16)]
        + reduce_scratch((4, 144, 512), (2, 144, 512)) * 2
        + sems(12),
        compiler_params=remote_params(7),
        cost_estimate=pl.CostEstimate(
            flops=12 * LOCAL_E * SLOTS * D * FF, bytes_accessed=60 << 20, transcendentals=0
        ),
    )(rows, cot_rows, row_gates, weights)


def token_trig():
    frequency = rope_base ** (-np.arange(HD // 2, dtype=np.float64) * 2.0 / HD)
    phase = np.arange(GROUP, dtype=np.float64)[:, None] * np.tile(frequency, 4)[None, :]
    return np.stack([np.cos(phase), np.sin(phase)]).astype(np.float32)


def adamw_step(weight, gradient, mean_old, square_old, rate, decay):
    drift = beta_first * mean_old + (1.0 - beta_first) * gradient
    spread = beta_second * square_old + (1.0 - beta_second) * gradient * gradient
    mean_hat = drift / (1.0 - beta_first**STEP)
    square_hat = spread / (1.0 - beta_second**STEP)
    master = weight - rate * (mean_hat / (jnp.sqrt(square_hat) + adam_eps) + decay * weight)
    return (drift, spread, master)


def on_device(
    activations,
    cotangent,
    seq_lengths,
    deal_order,
    routes,
    entry_weight,
    entry_mean,
    entry_square,
    exit_weight,
    exit_mean,
    exit_square,
    router_weight,
    router_mean,
    router_square,
    expand_weight,
    expand_mean,
    expand_square,
    shrink_weight,
    shrink_mean,
    shrink_square,
    norm_gains,
    gains_mean,
    gains_square,
):
    angles = (seq_lengths, token_trig())
    (
        weights, entry_own, shared, exit_own, gains, normed, qkv, attended, lse, middle,
        normed_two, rows, cot_rows, row_gates, rank, my_gates,
    ) = forward(
        activations[0],
        cotangent[0],
        activations[0],
        routes[0].T,
        deal_order,
        *angles,
        entry_weight,
        exit_weight,
        router_weight,
        norm_gains,
        expand_weight,
        shrink_weight,
    )
    weights = weights.reshape(16, LOCAL_E, 144, 1024)
    hidden, up_grad, expert_grad, line = expert_grads(rows, cot_rows, row_gates, weights)
    expert_grad = expert_grad.reshape(16, MAIN_E, 144, 1024)
    expert_sum = lax.psum_scatter(expert_grad, PLANE, scatter_dimension=0, tiled=False)
    middle_grad, branch_grad, logit_grad, gain_two_grad, out_sum, extra_sum = turn(
        rank,
        up_grad,
        hidden,
        row_gates,
        cot_rows,
        weights,
        line,
        middle,
        cotangent[0],
        my_gates,
        shared,
        gains[1:2],
    )
    branch_grad = branch_grad.reshape(GROUP, D)
    router_grad = dot(normed_two, logit_grad, ((0,), (0,)))

    input_rows, block_rows, entry_got, exit_got = closing(
        qkv,
        lse,
        *angles,
        exit_own,
        entry_own,
        activations[0],
        middle_grad,
        gains[0:1],
        normed,
        attended,
        branch_grad,
        router_grad,
        gain_two_grad,
        out_sum,
        middle,
    )

    input_grad, block_output = input_rows.astype(bf16), block_rows.astype(bf16)

    entry_got = entry_got[:, :ROWS]
    entry_sum = jnp.concatenate(
        [
            entry_got[:, :, :Q_OWN].transpose(1, 0, 2).reshape(ROWS, QH * HD),
            entry_got[:, :, Q_OWN:MIX_OWN].transpose(1, 0, 2).reshape(ROWS, 2 * KVH * HD),
        ],
        axis=1,
    )
    shared_sum = jnp.sum(entry_got[:, :, MIX_OWN:], axis=0)
    router_sum = shared_sum[:, :EXPERTS]
    gains_sum = shared_sum[:, EXPERTS : EXPERTS + 2].T
    exit_sum = exit_got[:ROWS]

    expand_sum, shrink_sum = to_owners(expert_sum, extra_sum)
    expand_sum, shrink_sum = expand_sum.astype(f32), shrink_sum.astype(f32)
    entry_new = adamw_step(entry_weight, entry_sum, entry_mean, entry_square, 0.02, weight_decay)
    exit_new = adamw_step(exit_weight, exit_sum, exit_mean, exit_square, 0.15, weight_decay)
    router_new = adamw_step(
        router_weight, router_sum, router_mean, router_square, 0.01, weight_decay
    )
    expand_new = adamw_step(
        expand_weight, expand_sum, expand_mean, expand_square, 0.02, weight_decay
    )
    shrink_new = adamw_step(
        shrink_weight, shrink_sum, shrink_mean, shrink_square, 0.12, weight_decay
    )
    gains_new = adamw_step(norm_gains, gains_sum, gains_mean, gains_square, 0.5, 0.0)
    return (
        block_output[None],
        input_grad[None],
        *entry_new,
        *exit_new,
        *router_new,
        *expand_new,
        *shrink_new,
        *gains_new,
    )


def solution(mesh):
    fine = Mesh(mesh.devices.reshape(4, 4, 4, 2), ("seq", "x", "y", "core"))
    rows = P(FSDP, "seq", None)
    lists = P(FSDP, None)
    owned = P(("seq",) + FSDP, None)
    experts = P("seq", FSDP, None)
    gains = P(None, ("seq",) + FSDP)
    return jax.shard_map(
        on_device,
        mesh=fine,
        in_specs=(rows, rows, lists, lists, rows)
        + (owned,) * 9
        + (experts,) * 6
        + (gains,) * 3,
        out_specs=(rows, rows) + (owned,) * 9 + (experts,) * 6 + (gains,) * 3,
        check_vma=False,
    )
```

```python
import jax
import jax.numpy as jnp
import numpy as np
from jax import lax
from jax.experimental import pallas as pl
from jax.experimental.pallas import tpu as pltpu
from jax.sharding import Mesh, PartitionSpec as P

D = 1536
QH = 24
KVH = 8
HD = 64
FF = 512
EXPERTS = 40
TOP = 8
STEP = 10
CAP = 29

N_SEQ = 4
TOK_DEV = 128
GROUP = 512
PAIR_TOK = 2 * GROUP
LOCAL_E = EXPERTS // (2 * N_SEQ)
SLOTS = 256
Q_OWN = QH * HD // N_SEQ
KV_OWN = 2 * KVH * HD // N_SEQ
MIX_OWN = Q_OWN + KV_OWN
HEADS_OWN = QH // N_SEQ
KV_HEADS_OWN = KVH // N_SEQ
PER_KV = QH // KVH
ROWS = 12

norm_eps = 1e-06
rope_base = 10000.0
beta_first = 0.9
beta_second = 0.95
adam_eps = 1e-08
weight_decay = 0.1

FSDP = ("x", "y", "core")
PLANE = ("x", "y")
f32 = jnp.float32
bf16 = jnp.bfloat16


BIG = 60 * 1024 * 1024
HALF = TOK_DEV // 2
QOWN = Q_OWN
MESH = pl.DeviceIdType.MESH
ANY = pl.BlockSpec(memory_space=pl.ANY)
VMEM = pl.BlockSpec(memory_space=pltpu.VMEM)


def dot(a, b, dims):
    return lax.dot_general(a, b, (dims, ((), ())), preferred_element_type=f32)


def greet(peers):
    barrier = pltpu.get_barrier_semaphore()
    for axis, peer in peers:
        pl.semaphore_signal(barrier, inc=1, device_id={axis: peer}, device_id_type=MESH)
    pl.semaphore_wait(barrier, len(peers))


def planner(send_sem, recv_sem):
    def plan(src, dst, index, axis, peer):
        return pltpu.make_async_remote_copy(
            src_ref=src,
            dst_ref=dst,
            send_sem=send_sem.at[index],
            recv_sem=recv_sem.at[index],
            device_id={axis: peer},
            device_id_type=MESH,
        )

    return plan


def sender(send_sem, recv_sem):
    plan = planner(send_sem, recv_sem)

    def send(*args):
        copy = plan(*args)
        copy.start()
        return copy

    return send


def sems(count):
    return [pltpu.SemaphoreType.DMA((count,)), pltpu.SemaphoreType.DMA((count,))]


def ring(me):
    right, left = lax.rem(me + 1, 4), lax.rem(me + 3, 4)
    return right, left, lax.rem(me + 2, 4)


def near(axis):
    right, left, _ = ring(lax.axis_index(axis))
    return [(axis, right), (axis, left)]


def sibling():
    return ("core", 1 - lax.axis_index("core"))


def half_rows(ref, half):
    size = ref.shape[0] // 2
    return ref.at[pl.ds(half * size, size)]


def half_lanes(ref, half):
    size = ref.shape[-1] // 2
    return ref.at[(slice(None),) * (len(ref.shape) - 1) + (pl.ds(half * size, size),)]


class Gather:
    def __init__(self, plan, base, axis, mine, slot, cut):
        me = lax.axis_index(axis)
        right, left, self.far = ring(me)
        self.right, self.left = right, left
        here, from_left, from_right = slot(me), cut(slot(left), 0), cut(slot(right), 1)
        self.first = [
            plan(cut(mine, 0), cut(here, 0), base, axis, right),
            plan(cut(mine, 1), cut(here, 1), base + 1, axis, left),
            plan(cut(mine, 1), cut(here, 1), base + 2, axis, right),
            plan(cut(mine, 0), cut(here, 0), base + 3, axis, left),
        ]
        self.later = [
            plan(from_left, from_left, base + 4, axis, right),
            plan(from_right, from_right, base + 5, axis, left),
        ]

    def start(self):
        for copy in self.first:
            copy.start()
        return self

    def relay(self):
        for got, on in zip(self.first, self.later):
            got.wait_recv()
            on.start()

    def wait_left(self):
        self.first[2].wait_recv()

    def wait_right(self):
        self.first[3].wait_recv()

    def wait_far(self):
        for copy in self.later:
            copy.wait_recv()

    def finish(self):
        self.wait_left()
        self.wait_right()
        self.wait_far()

    def drain(self):
        for copy in self.first + self.later:
            copy.wait_send()


def hand_over(send, base, mine, out, gather):
    me, core = lax.axis_index("seq"), lax.axis_index("core")
    other = 1 - core
    copies = [send(mine, out.at[core, me], base, "core", other)]
    gather.relay()
    gather.wait_left()
    block = out.at[core, gather.left]
    copies.append(send(block, block, base + 1, "core", other))
    gather.wait_right()
    block = out.at[core, gather.right]
    copies.append(send(block, block, base + 2, "core", other))
    gather.wait_far()
    block = out.at[core, gather.far]
    copies.append(send(block, block, base + 3, "core", other))
    return copies


def reduce_scratch(block, half):
    return [pltpu.VMEM(half, bf16)] * 4 + [pltpu.VMEM(block, bf16)] * 2


def added(target, first, second):
    target[...] = (first[...].astype(f32) + second[...].astype(f32)).astype(bf16)


class Reduce:
    def __init__(self, plan, base, axis, block, bufs, cut):
        me = lax.axis_index(axis)
        right, left, far = ring(me)
        from_left, from_right, to_right, to_left, got_left, got_right = bufs
        far, on_right, on_left = block(far), block(right), block(left)
        self.mine, self.got = block(me), (got_left, got_right)
        self.hops = (
            (to_right, cut(on_right, 0), from_left),
            (to_left, cut(on_left, 1), from_right),
        )
        self.far = [
            plan(cut(far, 0), from_left, base, axis, right),
            plan(cut(far, 1), from_right, base + 1, axis, left),
        ]
        self.near = [
            plan(cut(on_right, 1), cut(got_left, 1), base + 2, axis, right),
            plan(cut(on_left, 0), cut(got_right, 0), base + 3, axis, left),
        ]
        self.later = [
            plan(to_right, cut(got_left, 0), base + 4, axis, right),
            plan(to_left, cut(got_right, 1), base + 5, axis, left),
        ]

    def start_far(self):
        for copy in self.far:
            copy.start()

    def start_near(self):
        for copy in self.near:
            copy.start()

    def start(self):
        self.start_far()
        self.start_near()
        return self

    def relay(self):
        for got, hop, on in zip(self.far, self.hops, self.later):
            got.wait_recv()
            added(*hop)
            on.start()

    def total(self):
        for copy in self.near + self.later:
            copy.wait_recv()
        total = self.mine[...].astype(f32)
        for part in self.got:
            total += part[...].astype(f32)
        return total

    def drain(self):
        for copy in self.far + self.near + self.later:
            copy.wait_send()


LOW_LANES, HIGH_LANES = pl.ds(0, 512), pl.ds(512, 512)


def plane_scratch():
    return (
        reduce_scratch((4, 144, 512), (2, 144, 512)) * 2
        + reduce_scratch((144, 512), (144, 256)) * 2
    )


PLANE_BUFS = 24


class PlaneSum:
    def __init__(self, plan, base, grads, bufs):
        every = slice(None)
        self.line = low, high = bufs[4], bufs[10]
        self.first = (
            Reduce(plan, base, "x", lambda i: grads(i, every, LOW_LANES), bufs[:6], half_rows),
            Reduce(
                plan, base + 6, "y", lambda i: grads(every, i, HIGH_LANES), bufs[6:12], half_rows
            ),
        )
        self.second = (
            Reduce(plan, base + 12, "y", lambda i: low.at[i], bufs[12:18], half_lanes),
            Reduce(plan, base + 18, "x", lambda i: high.at[i], bufs[18:24], half_lanes),
        )

    def start(self):
        for reduce in self.first:
            reduce.start()

    def relay(self):
        for reduce in self.first:
            reduce.relay()

    def turn(self):
        for side in range(2):
            self.line[side][...] = self.first[side].total().astype(bf16)
            self.second[side].start()

    def relay_again(self):
        for reduce in self.second:
            reduce.relay()

    def finish(self, out):
        out[:, LOW_LANES] = self.second[0].total().astype(bf16)
        out[:, HIGH_LANES] = self.second[1].total().astype(bf16)

    def drain(self):
        for reduce in self.first + self.second:
            reduce.drain()


def remote_params(call_id):
    return pltpu.CompilerParams(
        collective_id=call_id, has_side_effects=True, vmem_limit_bytes=BIG
    )


def unit_scale(vector):
    return lax.rsqrt(jnp.mean(vector * vector, axis=-1, keepdims=True) + norm_eps)


def norm_back(vector, gain, grad):
    scale = unit_scale(vector)
    unit = vector * scale
    pulled = grad * gain
    back = scale * (pulled - unit * jnp.mean(pulled * unit, axis=-1, keepdims=True))
    return back, jnp.sum(unit * grad, axis=0, keepdims=True)


MAIN_E = LOCAL_E - 1


def row_pick(shape, padded_axis):
    padded = lax.broadcasted_iota(jnp.int32, shape, padded_axis)
    plain = lax.broadcasted_iota(jnp.int32, shape, 1 - padded_axis)
    row = lax.rem(padded, 16)
    return ((plain == lax.div(padded, 16) * 12 + row) & (row < 12)).astype(bf16)


def swap_halves(rows, lower, upper):
    lane = lax.broadcasted_iota(jnp.int32, rows.shape, 1)
    ahead = pltpu.roll(rows, rows.shape[1] - HD // 2, 1)
    behind = pltpu.roll(rows, HD // 2, 1)
    return jnp.where(lax.rem(lane, HD) < HD // 2, lower * ahead, upper * behind)


BLOCK = 256


def sequence_of(lengths_ref, token):
    first_end = lengths_ref[0, 0]
    second_end = first_end + lengths_ref[0, 1]
    return (token >= first_end).astype(jnp.int32) + (token >= second_end).astype(jnp.int32)


def block_bias(lengths_ref, block):
    keys = BLOCK * (block + 1)
    row = lax.broadcasted_iota(jnp.int32, (BLOCK, keys), 0) + BLOCK * block
    column = lax.broadcasted_iota(jnp.int32, (BLOCK, keys), 1)
    same = sequence_of(lengths_ref, row) == sequence_of(lengths_ref, column)
    return jnp.where(same & (column <= row), 0.0, -1e30)


def rope_tables(lengths_ref, trig_ref):
    seq = sequence_of(lengths_ref, lax.broadcasted_iota(jnp.int32, (GROUP, 128), 0))
    second = lengths_ref[0, 0]
    third = second + lengths_ref[0, 1]

    def of_start(table):
        later = jnp.where(
            seq == 1, trig_ref[table, pl.ds(second, 1)], trig_ref[table, pl.ds(third, 1)]
        )
        return jnp.where(seq == 0, trig_ref[table, 0:1], later)

    start_cos, start_sin = of_start(0), of_start(1)
    cosine = trig_ref[0] * start_cos + trig_ref[1] * start_sin
    sine = trig_ref[1] * start_cos - trig_ref[0] * start_sin
    is_key = lax.broadcasted_iota(jnp.int32, (GROUP, 128), 1) < HD
    pair_cos, pair_sin = jnp.where(is_key, cosine, 1.0), jnp.where(is_key, sine, 0.0)
    return (
        jnp.concatenate([cosine] * 3 + [pair_cos] * 2, axis=1),
        jnp.concatenate([sine] * 3 + [pair_sin] * 2, axis=1),
    )


def head_of(index):
    return slice(HD * index, HD * (index + 1))


def lane_pick(first, rows):
    row = lax.broadcasted_iota(jnp.int32, (rows, 128), 0)
    lane = lax.broadcasted_iota(jnp.int32, (rows, 128), 1)
    return (lane == row + first).astype(bf16)


def forward_kernel(
    in_hbm, cot_hbm, in_ref, route_ref, order_ref, lengths_ref, trig_ref,
    entry_ref, exit_ref, router_ref, gain_ref, expand_ref, shrink_ref,
    weights_out, entry_out, shared_out, exit_out, gains_out, normed_ref, qkv_ref, attended_ref,
    lse_ref, middle_ref, mine, rows_out, cot_rows_out, row_gate_out, rank_out, my_gate_out,
    stage, stage_end, packed, shared, columns, hold, full,
    in_all, cot_all, hit_all, hit_pair, tokens, part, gates, *rest
):
    bufs, (send_sem, recv_sem, copy_sem) = rest[:6], rest[6:]
    z, x, y, c = (lax.axis_index(a) for a in ("seq", "x", "y", "core"))
    right, left, far = ring(z)
    other = 1 - c
    greet(near("seq") + [("seq", far)] + near("x") + near("y") + [sibling()])
    send, plan = sender(send_sem, recv_sem), planner(send_sem, recv_sem)

    rows = Gather(plan, 9, "seq", in_hbm, lambda i: in_all.at[i], half_rows).start()
    expert = lax.broadcasted_iota(jnp.int32, (128, TOK_DEV), 0)
    hit = route_ref[0:1] == expert
    for k in range(1, TOP):
        hit = hit | (route_ref[k : k + 1] == expert)
    hit_all[z] = hit.astype(bf16)
    hits = Gather(plan, 3, "seq", hit_all.at[z], lambda i: hit_all.at[i], half_rows).start()

    lane = lax.broadcasted_iota(jnp.int32, (ROWS, 128), 1)
    square = lax.broadcasted_iota(jnp.int32, (ROWS, ROWS), 0)
    square = square == lax.broadcasted_iota(jnp.int32, (ROWS, ROWS), 1)
    shared[...] = jnp.zeros_like(shared)
    shared[:, :EXPERTS] = router_ref[...]
    block_of = shared[...]
    for k in range(2):
        column = jnp.sum(jnp.where(square, gain_ref[k : k + 1], 0.0), axis=1, keepdims=True)
        block_of = jnp.where(lane == EXPERTS + k, column, block_of)
    empty = jnp.zeros((PAD_ROWS - ROWS, WIDE), f32)
    for block in range(4):
        cols = jnp.concatenate(
            [
                entry_ref[:, Q_OWN * block : Q_OWN * (block + 1)],
                entry_ref[:, QH * HD + KV_OWN * block : QH * HD + KV_OWN * (block + 1)],
                block_of,
            ],
            axis=1,
        )
        columns[block] = jnp.concatenate([cols, empty], axis=0).astype(bf16)
    to_seq = [
        send(columns.at[peer], hold.at[z], k, "seq", peer)
        for k, peer in enumerate((right, far, left))
    ]
    for block in range(2):
        cols = exit_ref[:, WIDE * block : WIDE * (block + 1)]
        hold[4 + block] = jnp.concatenate([cols, empty], axis=0).astype(bf16)
    hold[z] = columns[z]
    local = [
        pltpu.make_async_copy(in_hbm, in_all.at[z], copy_sem.at[0]),
        pltpu.make_async_copy(cot_hbm, cot_all.at[c, z], copy_sem.at[1]),
    ]
    for copy in local:
        copy.start()

    for e in range(LOCAL_E):
        theirs = other * LOCAL_E + e
        stage[e, :48] = expand_ref[theirs].astype(bf16)
        stage[e, 48:] = shrink_ref[theirs, :, :1024].astype(bf16)
        stage_end[e] = shrink_ref[theirs, :, 1024:].astype(bf16)
    of_core = pl.ds(pl.multiple_of(c * 48, 16), 48)
    lefts = pl.ds(pl.multiple_of(96 + c * 16, 16), 16)
    ends = pl.ds(pl.multiple_of(c * 512, 512), 512)
    to_core = [
        send(stage.at[:, pl.ds(0, 48)], packed.at[:, of_core], 51, "core", other),
        send(stage.at[:, pl.ds(48, 16)], packed.at[:, lefts], 52, "core", other),
        send(stage_end, packed.at[:, pl.ds(128, 16), ends], 53, "core", other),
    ]
    for e in range(LOCAL_E):
        own_e = c * LOCAL_E + e
        packed[e, of_core, :] = expand_ref[own_e].astype(bf16)
        packed[e, lefts, :] = shrink_ref[own_e, :, :1024].astype(bf16)
        packed[e, pl.ds(128, 16), ends] = shrink_ref[own_e, :, 1024:].astype(bf16)
    for copy in to_seq:
        copy.wait_recv()
    for block in range(6):
        full[block, x, y, c] = hold[block]
    low, high = pl.ds(0, 3), pl.ds(3, 3)
    low_x = Gather(plan, 15, "x", hold.at[low], lambda i: full.at[low, i, y, c], half_lanes)
    low_x.start()
    high_y = Gather(plan, 21, "y", hold.at[high], lambda i: full.at[high, x, i, c], half_lanes)
    high_y.start()
    for copy in to_core:
        copy.wait_recv()
    own_weights = pltpu.make_async_copy(packed, weights_out.at[x, y], copy_sem.at[2])
    own_weights.start()
    start, end = pl.ds(0, 512), pl.ds(512, 512)
    expert_x = Gather(
        plan,
        54,
        "x",
        packed.at[:, :, start],
        lambda i: weights_out.at[i, y, :, :, start],
        half_lanes,
    ).start()
    expert_y = Gather(
        plan,
        60,
        "y",
        packed.at[:, :, end],
        lambda i: weights_out.at[x, i, :, :, end],
        half_lanes,
    ).start()

    def cut_low(ref, half):
        return ref.at[:, pl.ds(2 * half, 2)]

    hits.relay()
    low_x.relay()
    high_y.relay()
    rows.relay()
    cots = Gather(plan, 27, "seq", cot_hbm, lambda i: cot_all.at[c, i], half_rows).start()
    low_x.finish()
    low_y = Gather(
        plan, 33, "y", full.at[low, :, y, c], lambda i: full.at[low, :, i, c], cut_low
    ).start()
    high_y.finish()
    high_x = Gather(
        plan, 39, "x", full.at[high, x, :, c], lambda i: full.at[high, i, :, c], cut_low
    ).start()
    expert_x.relay()
    expert_y.relay()

    hits.finish()
    token = lax.broadcasted_iota(jnp.int32, (GROUP, GROUP), 0)
    back_hot = (order_ref[...] == token).astype(bf16)
    natural = jnp.zeros((GROUP, 128), f32)
    for block in range(N_SEQ):
        slots = back_hot[:, TOK_DEV * block : TOK_DEV * (block + 1)]
        natural += dot(slots, hit_all[block], ((1,), (1,)))
    hit_pair[c] = natural.astype(bf16)
    hit_swap = send(hit_pair.at[c], hit_pair.at[c], 66, "core", other)
    low_y.relay()
    high_x.relay()
    hit_swap.wait_recv()
    hit_both = hit_pair[...].reshape(PAIR_TOK, 128)
    first = (z * 2 + c) * LOCAL_E
    lower = lax.broadcasted_iota(jnp.int32, (PAIR_TOK, PAIR_TOK), 0)
    lower = (lower >= lax.broadcasted_iota(jnp.int32, (PAIR_TOK, PAIR_TOK), 1)).astype(bf16)
    rank = dot(lower, hit_both, ((1,), (0,))) - 1.0
    rank = jnp.where(hit_both.astype(f32) > 0.0, rank, -1.0).astype(bf16)
    mine_of = lane_pick(first, 8)
    rank_out[...] = dot(rank, mine_of, ((1,), (1,))).astype(jnp.int32)
    rank_rows = dot(mine_of, rank, ((1,), (1,))).astype(jnp.int32)

    low_y.finish()
    half = full.at[low, :, :, c]
    last = [send(half, half, 49, "core", other)]
    high_x.finish()
    half = full.at[high, :, :, c]
    last.append(send(half, half, 50, "core", other))
    own_weights.wait()
    expert_x.finish()
    expert_low = Gather(
        plan,
        67,
        "y",
        weights_out.at[:, y, :, :, start],
        lambda i: weights_out.at[:, i, :, :, start],
        half_rows,
    ).start()
    expert_y.finish()
    expert_high = Gather(
        plan,
        73,
        "x",
        weights_out.at[x, :, :, :, end],
        lambda i: weights_out.at[i, :, :, :, end],
        half_rows,
    ).start()
    cosine, sine = rope_tables(lengths_ref, trig_ref)
    rows.finish()
    local[0].wait()
    for copy in last:
        copy.wait_recv()
    pick = row_pick((QOWN, 512), 1)
    for block in range(4):
        got = dot(pick, full[block].reshape(512, WIDE), ((1,), (0,))).astype(bf16)
        entry_out[QOWN * block : QOWN * (block + 1), :] = got[:, :MIX_OWN]
        shared_out[QOWN * block : QOWN * (block + 1), :] = got[:, MIX_OWN:]
    for block in range(2):
        got = dot(pick, full[4 + block].reshape(512, WIDE), ((1,), (0,))).astype(bf16)
        exit_out[:, WIDE * block : WIDE * (block + 1)] = got
    gains = dot(lane_pick(EXPERTS, 8), shared_out[...], ((1,), (1,)))
    gains_out[...] = gains
    for block in range(N_SEQ):
        at = slice(TOK_DEV * block, TOK_DEV * (block + 1))
        vector = in_all[block].astype(f32)
        normed_ref[at, :] = (vector * unit_scale(vector) * gains[0:1]).astype(bf16)
    mixed = dot(normed_ref[...], entry_out[...], ((1,), (0,)))
    mixed = mixed * cosine + swap_halves(mixed, -1.0, 1.0) * sine
    qkv_ref[...] = mixed.astype(bf16)
    for block in range(GROUP // BLOCK):
        bias = block_bias(lengths_ref, block)
        keys = BLOCK * (block + 1)
        at = slice(BLOCK * block, keys)
        for head in range(HEADS_OWN):
            pair = Q_OWN + 2 * HD * (head // PER_KV)
            key = qkv_ref[:keys, pair : pair + HD]
            value = qkv_ref[:keys, pair + HD : pair + 2 * HD]
            scores = dot(qkv_ref[at, head_of(head)], key, ((1,), (1,))) * HD**-0.5 + bias
            peak = jnp.max(scores, axis=1, keepdims=True)
            expo = jnp.exp(scores - peak)
            total = jnp.sum(expo, axis=1, keepdims=True)
            probs = (expo / total).astype(bf16)
            attended_ref[at, head_of(head)] = dot(probs, value, ((1,), (0,))).astype(bf16)
            lse_ref[at, head : head + 1] = peak + jnp.log(total)
    part[...] = dot(attended_ref[...], exit_out[...], ((1,), (0,))).astype(bf16).reshape(part.shape)
    reduce = Reduce(plan, 79, "seq", lambda i: part.at[i], bufs, half_rows).start()
    pairs = hand_over(send, 45, cot_hbm, cot_all, cots)
    reduce.relay()
    middle = in_ref[...].astype(f32) + reduce.total()
    middle_ref[...] = middle
    mine[...] = (middle * unit_scale(middle) * gains[1:2]).astype(bf16)
    gather = Gather(plan, 85, "seq", mine, lambda i: tokens.at[c, i], half_rows).start()
    tokens[c, z] = mine[...]
    pairs += hand_over(send, 91, mine, tokens, gather)
    for copy in pairs:
        copy.wait()
    local[1].wait()

    logits = dot(tokens[...].reshape(PAIR_TOK, D), shared_out[...], ((1,), (0,)))
    masked = jnp.where(hit_both.astype(f32) > 0.0, logits, -jnp.inf)
    gate_expo = jnp.exp(masked - jnp.max(masked, axis=1, keepdims=True))
    gates[...] = gate_expo / jnp.sum(gate_expo, axis=1, keepdims=True)
    my_gate_out[...] = gates[pl.ds(pl.multiple_of(c * GROUP + z * TOK_DEV, TOK_DEV), TOK_DEV), :]
    rest_of = gates[...]
    gate_rows = jnp.zeros((8, PAIR_TOK), f32)
    for _ in range(3):
        piece = rest_of.astype(bf16)
        gate_rows += dot(mine_of, piece, ((1,), (1,)))
        rest_of -= piece.astype(f32)
    slot = lax.broadcasted_iota(jnp.int32, (SLOTS, PAIR_TOK), 0)
    for e in range(LOCAL_E):
        if e == 3:
            expert_low.relay()
            expert_high.relay()
        match = rank_rows[e : e + 1] == slot
        row_gate_out[e] = jnp.sum(
            jnp.where(match, gate_rows[e : e + 1], 0.0), axis=1, keepdims=True
        )
        match = match.astype(bf16)
        for half in range(2):
            lanes = slice(768 * half, 768 * (half + 1))
            table = tokens[:, :, :, lanes].reshape(PAIR_TOK, 768)
            rows_out[e, :, lanes] = dot(match, table, ((1,), (0,))).astype(bf16)
            table = cot_all[:, :, :, lanes].reshape(PAIR_TOK, 768)
            cot_rows_out[e, :, lanes] = dot(match, table, ((1,), (0,))).astype(bf16)
    expert_low.finish()
    expert_high.finish()
    for copy in to_seq + to_core + last + [hit_swap]:
        copy.wait_send()
    for transfer in (hits, rows, cots, low_x, high_y, low_y, high_x, reduce, gather):
        transfer.drain()
    for transfer in (expert_x, expert_y, expert_low, expert_high):
        transfer.drain()


def forward(*operands):
    scalar = pl.BlockSpec(memory_space=pltpu.SMEM)
    block = (PAD_ROWS, WIDE)
    group = (N_SEQ, TOK_DEV, D)
    return pl.pallas_call(
        forward_kernel,
        out_shape=[
            jax.ShapeDtypeStruct((4, 4, LOCAL_E, 144, 1024), bf16),
            jax.ShapeDtypeStruct((D, MIX_OWN), bf16),
            jax.ShapeDtypeStruct((D, 128), bf16),
            jax.ShapeDtypeStruct((QOWN, D), bf16),
            jax.ShapeDtypeStruct((8, D), f32),
            jax.ShapeDtypeStruct((GROUP, D), bf16),
            jax.ShapeDtypeStruct((GROUP, MIX_OWN), bf16),
            jax.ShapeDtypeStruct((GROUP, Q_OWN), bf16),
            jax.ShapeDtypeStruct((GROUP, HEADS_OWN), f32),
            jax.ShapeDtypeStruct((TOK_DEV, D), f32),
            jax.ShapeDtypeStruct((TOK_DEV, D), bf16),
            jax.ShapeDtypeStruct((LOCAL_E, SLOTS, D), bf16),
            jax.ShapeDtypeStruct((LOCAL_E, SLOTS, D), bf16),
            jax.ShapeDtypeStruct((LOCAL_E, SLOTS, 1), f32),
            jax.ShapeDtypeStruct((PAIR_TOK, 8), jnp.int32),
            jax.ShapeDtypeStruct((TOK_DEV, 128), f32),
        ],
        in_specs=[ANY] * 2 + [VMEM] * 3 + [scalar] + [VMEM] * 7,
        out_specs=[ANY] + [VMEM] * 15,
        scratch_shapes=[
            pltpu.VMEM((LOCAL_E, 64, 1024), bf16),
            pltpu.VMEM((LOCAL_E, 16, 512), bf16),
            pltpu.VMEM((LOCAL_E, 144, 1024), bf16),
            pltpu.VMEM((ROWS, 128), f32),
            pltpu.VMEM((4,) + block, bf16),
            pltpu.VMEM((6,) + block, bf16),
            pltpu.VMEM((6, 4, 4, 2) + block, bf16),
            pltpu.VMEM(group, bf16),
            pltpu.VMEM((2,) + group, bf16),
            pltpu.VMEM((N_SEQ, TOK_DEV, 128), bf16),
            pltpu.VMEM((2, GROUP, 128), bf16),
            pltpu.VMEM((2,) + group, bf16),
            pltpu.VMEM(group, bf16),
            pltpu.VMEM((PAIR_TOK, 128), f32),
        ]
        + reduce_scratch((TOK_DEV, D), (HALF, D))
        + sems(95)
        + [pltpu.SemaphoreType.DMA((3,))],
        compiler_params=remote_params(2),
    )(*operands)


def turn_kernel(
    rank_ref, up_ref, hidden_ref, gate_ref, cot_rows_ref, w_ref,
    line, pair_grad_ref, middle_ref, cot_ref, my_gate_ref, router_ref, gain_ref,
    grad_ref, branch_ref, logit_ref, gain_grad_ref, out_sum_ref, sums_ref,
    back_s, out_s, other_back, from_core, part, out_core, mine, *rest
):
    bufs, (send_sem, recv_sem, copy_sem) = [rest[6 * i : 6 * i + 6] for i in range(3)], rest[-3:]
    e = pl.program_id(0)
    me, core = lax.axis_index("seq"), lax.axis_index("core")
    send, plan = sender(send_sem, recv_sem), planner(send_sem, recv_sem)
    low_y = Reduce(plan, 17, "y", lambda i: line.at[0, i], bufs[1], half_lanes)
    high_x = Reduce(plan, 23, "x", lambda i: line.at[1, i], bufs[2], half_lanes)
    first_sum, second_sum = (
        PlaneSum(
            plan,
            29 + 24 * k,
            lambda i, j, lanes, k=k: pair_grad_ref.at[i, j, k, :, lanes],
            rest[18 + PLANE_BUFS * k : 18 + PLANE_BUFS * (k + 1)],
        )
        for k in range(2)
    )

    @pl.when(e == 0)
    def _():
        greet(near("seq") + near("x") + near("y") + [sibling()])
        low_y.start()
        high_x.start()
        first_sum.start()

    @pl.when(e == 2)
    def _():
        low_y.relay()
        high_x.relay()

    @pl.when(e < LOCAL_E)
    def _():
        expand, left, right = weights_of(w_ref)
        at = pl.ds(pl.multiple_of(e * SLOTS, SLOTS), SLOTS)
        back_s[at, :D] = dot(up_ref[0], expand, ((1,), (1,))).astype(bf16)
        hidden = hidden_ref[0]
        expert_out = jnp.concatenate(
            [dot(hidden, left, ((1,), (0,))), dot(hidden, right, ((1,), (0,)))], axis=1
        )
        expert_out = expert_out.astype(bf16).astype(f32)
        gate_grad = jnp.sum(expert_out * cot_rows_ref[0].astype(f32), axis=1, keepdims=True)
        lane = lax.broadcasted_iota(jnp.int32, (SLOTS, 128), 1)
        column = (me * 2 + core) * LOCAL_E + e
        back_s[at, D:] = jnp.where(lane == column, gate_grad, 0.0).astype(bf16)
        out_s[at, :] = (gate_ref[0] * expert_out).astype(bf16)

    @pl.when(e == LOCAL_E - 1)
    def _():
        first_sum.relay()
        second_sum.start()

    @pl.when(e == LOCAL_E)
    def _():
        other = 1 - core
        right, left, far = ring(me)
        slot = lax.broadcasted_iota(jnp.int32, (GROUP // 2, SLOTS), 1)

        def combine(group, table, target):
            for half in range(2):
                at = group * GROUP + half * (GROUP // 2)
                ranks = rank_ref[pl.ds(pl.multiple_of(at, GROUP // 2), GROUP // 2), :]
                picks = jnp.concatenate(
                    [(ranks[:, k : k + 1] == slot).astype(bf16) for k in range(LOCAL_E)], axis=1
                )
                got = dot(picks, table[...], ((1,), (0,))).astype(bf16)
                target[pl.ds(2 * half, 2)] = got.reshape(2, TOK_DEV, got.shape[1])

        order = (far, right, left, me)
        combine(other, back_s, other_back)
        swaps = [
            send(other_back.at[block], from_core.at[block], 12 + i, "core", other)
            for i, block in enumerate(order)
        ]
        first_sum.turn()
        combine(core, back_s, part)
        reduce = Reduce(plan, 0, "seq", lambda i: part.at[i], bufs[0], half_rows)
        for i, block in enumerate(order):
            swaps[i].wait_recv()
            added(part.at[block], part.at[block], from_core.at[block])
            if i == 0:
                reduce.start_far()
            if i == 2:
                reduce.start_near()
        for copy in swaps:
            copy.wait_send()
        other_out = other_back.at[:, :, pl.ds(0, D)]
        combine(other, out_s, other_out)
        out_swap = send(other_out, out_core, 16, "core", other)
        reduce.relay()
        first_sum.relay_again()
        combine(core, out_s, out_sum_ref)
        total = reduce.total()
        gates, gate_grad = my_gate_ref[...], total[:, D:]
        mean_term = jnp.sum(gates * gate_grad, axis=1, keepdims=True)
        logit_grad = (gates * (gate_grad - mean_term)).astype(bf16)
        logit_ref[...] = logit_grad
        normed_grad = total[:, :D] + dot(logit_grad, router_ref[...], ((1,), (1,)))
        back, gain_grad = norm_back(middle_ref[...], gain_ref[...], normed_grad)
        gain_grad_ref[...] = gain_grad
        middle_grad = cot_ref[...].astype(f32) + back
        grad_ref[...] = middle_grad
        mine[...] = middle_grad.astype(bf16)
        gather = Gather(plan, 6, "seq", mine, lambda i: branch_ref.at[i], half_rows).start()
        local = pltpu.make_async_copy(mine, branch_ref.at[me], copy_sem)
        local.start()
        second_sum.relay()
        out_swap.wait_recv()
        added(out_sum_ref, out_sum_ref, out_core)
        gather.relay()
        sums_ref[0, :, :512] = low_y.total().astype(bf16)
        sums_ref[0, :, 512:] = high_x.total().astype(bf16)
        first_sum.finish(sums_ref.at[1])
        second_sum.turn()
        gather.finish()
        second_sum.relay_again()
        second_sum.finish(sums_ref.at[2])
        first_sum.drain()
        second_sum.drain()
        for transfer in (gather, reduce, low_y, high_x):
            transfer.drain()
        out_swap.wait_send()
        local.wait()


BACK_WIDTH = D + 128


def turn(*operands):
    one = lambda e: (jnp.minimum(e, LOCAL_E - 1), 0, 0)
    wide = lambda e: (0, jnp.minimum(e, LOCAL_E - 1), 0, 0)
    cubes = lambda e: (0, 0, 0, 0)
    whole = lambda e: (0, 0)
    blocks = lambda e: (0, 0, 0)
    once = pl.Buffered(1)
    lane_block = pl.BlockSpec((TOK_DEV, 128), whole)
    gain_block = pl.BlockSpec((1, D), whole)
    group = pltpu.VMEM((N_SEQ, TOK_DEV, BACK_WIDTH), bf16)
    group_out = pltpu.VMEM((N_SEQ, TOK_DEV, D), bf16)
    return pl.pallas_call(
        turn_kernel,
        grid=(LOCAL_E + 1,),
        in_specs=[
            pl.BlockSpec((PAIR_TOK, 8), whole, pipeline_mode=once),
            pl.BlockSpec((1, SLOTS, 2 * FF), one),
            pl.BlockSpec((1, SLOTS, FF), one),
            pl.BlockSpec((1, SLOTS, 1), one),
            pl.BlockSpec((1, SLOTS, D), one),
            pl.BlockSpec((16, 1, 144, 1024), wide),
            pl.BlockSpec((2, 4, 144, 512), cubes, pipeline_mode=once),
            pl.BlockSpec((4, 4, 2, 144, 1024), lambda e: (0, 0, 0, 0, 0), pipeline_mode=once),
            pl.BlockSpec((TOK_DEV, D), whole, pipeline_mode=once),
            pl.BlockSpec((TOK_DEV, D), whole, pipeline_mode=once),
            lane_block,
            pl.BlockSpec((D, 128), whole, pipeline_mode=once),
            gain_block,
        ],
        out_specs=[
            pl.BlockSpec((TOK_DEV, D), whole, pipeline_mode=once),
            ANY,
            lane_block,
            gain_block,
            pl.BlockSpec((N_SEQ, TOK_DEV, D), blocks, pipeline_mode=once),
            pl.BlockSpec((3, 144, 1024), blocks, pipeline_mode=once),
        ],
        out_shape=[
            jax.ShapeDtypeStruct((TOK_DEV, D), f32),
            jax.ShapeDtypeStruct((N_SEQ, TOK_DEV, D), bf16),
            jax.ShapeDtypeStruct((TOK_DEV, 128), bf16),
            jax.ShapeDtypeStruct((1, D), f32),
            jax.ShapeDtypeStruct((N_SEQ, TOK_DEV, D), bf16),
            jax.ShapeDtypeStruct((3, 144, 1024), bf16),
        ],
        scratch_shapes=[
            pltpu.VMEM((LOCAL_E * SLOTS, BACK_WIDTH), bf16),
            pltpu.VMEM((LOCAL_E * SLOTS, D), bf16),
            group,
            group,
            group,
            group_out,
            pltpu.VMEM((TOK_DEV, D), bf16),
        ]
        + reduce_scratch((TOK_DEV, BACK_WIDTH), (HALF, BACK_WIDTH))
        + reduce_scratch((144, 512), (144, 256)) * 2
        + plane_scratch() * 2
        + sems(77)
        + [pltpu.SemaphoreType.DMA],
        compiler_params=remote_params(4),
        cost_estimate=pl.CostEstimate(
            flops=6 * LOCAL_E * SLOTS * D * FF + 4 * LOCAL_E * SLOTS * PAIR_TOK * D,
            bytes_accessed=40 << 20,
            transcendentals=0,
        ),
    )(*operands)


PAD_ROWS = 16
WIDE = 768
def closing_kernel(
    qkv_ref, lse_ref, lengths_ref, trig_ref, exit_ref, entry_ref,
    in_ref, grad_ref, gain_ref, normed_ref, attended_ref, branch_ref,
    router_grad_ref, gain_two_ref, out_sum_ref, middle_ref, pair_grad_ref, sums_ref,
    input_ref, block_ref, entry_out, exit_out, expand_ref, shrink_ref,
    last_sums, turned, mixed_grad, part, full, from_core, chip, line, final, give, got_z, *rest
):
    bufs, (send_sem, recv_sem) = [rest[6 * i : 6 * i + 6] for i in range(8)], rest[-2:]
    z, x, y, c = (lax.axis_index(a) for a in ("seq", "x", "y", "core"))
    right, left, far = ring(z)
    greet(near("seq") + [("seq", far)] + near("x") + near("y") + [sibling()])
    send, plan = sender(send_sem, recv_sem), planner(send_sem, recv_sem)
    pick = row_pick((512, QOWN), 0)
    expert_sums = [
        PlaneSum(
            plan,
            54 + 24 * k,
            lambda i, j, lanes, k=k: pair_grad_ref.at[i, j, k, :, lanes],
            rest[48 + PLANE_BUFS * k : 48 + PLANE_BUFS * (k + 1)],
        )
        for k in range(2)
    ]
    expert_sums[0].start()

    def parts(owner):
        return (
            pl.ds(pl.multiple_of(owner * 48, 16), 48),
            pl.ds(pl.multiple_of(96 + owner * 16, 16), 16),
            pl.ds(pl.multiple_of(owner * 512, 512), 512),
        )

    def to_owner(e, source):
        expert = c * LOCAL_E + e
        rows, left, ends = parts(1 - c)
        low, main, end = pl.ds(128, 16), pl.ds(0, 1024), pl.ds(1024, 512)
        pieces = (
            (source.at[rows], expand_ref.at[expert]),
            (source.at[left], shrink_ref.at[expert, :, main]),
            (source.at[low, ends], shrink_ref.at[expert, :, end]),
        )
        copies = [
            send(part, place, 102 + 3 * e + k, "core", 1 - c)
            for k, (part, place) in enumerate(pieces)
        ]
        rows, left, ends = parts(c)
        expand_ref[expert] = source[rows, :]
        shrink_ref[expert, :, main] = source[left, :]
        shrink_ref[expert, :, end] = source[low, ends]
        return copies

    def spread(grad):
        wide = dot(pick, grad, ((1,), (0,))).astype(bf16)
        return wide.reshape(16, 2, PAD_ROWS, grad.shape[1])

    def swap(side):
        return send(full.at[side, :, 1 - c], from_core.at[side], 48 + side, "core", 1 - c)

    def chip_sum(side, copy):
        copy.wait_recv()
        for plane in range(16):
            first, second = (plane % 4, plane // 4) if side == 2 else (plane // 4, plane % 4)
            added(chip.at[side, first, second], full.at[side, plane, c], from_core.at[side, plane])

    def first_sum(side, axis):
        return Reduce(
            plan, 6 * side, axis, lambda i: chip.at[side, i], bufs[side], half_rows
        ).start()

    def second_sum(side, axis, reduce):
        line[side] = reduce.total().astype(bf16)
        return Reduce(
            plan, 18 + 6 * side, axis, lambda i: line.at[side, i], bufs[3 + side], half_lanes
        ).start()

    for block in range(3):
        cols = slice(512 * block, 512 * (block + 1))
        grad = dot(attended_ref[...], branch_ref[:, cols], ((0,), (0,))).astype(bf16)
        full[0, :, :, :, cols] = spread(grad)
    swaps = [swap(0)]
    outs = Reduce(plan, 36, "seq", lambda i: out_sum_ref.at[i], bufs[6], half_rows).start()

    def turn_back(kv):
        pair = Q_OWN + 2 * HD * kv
        for head in range(PER_KV * kv, PER_KV * (kv + 1)):
            grad = dot(branch_ref[...], exit_ref[head_of(head), :], ((1,), (1,))).astype(bf16)
            attended = attended_ref[:, head_of(head)].astype(f32)
            delta = jnp.sum(grad.astype(f32) * attended, axis=1, keepdims=True)
            for block in range(GROUP // BLOCK):
                bias = block_bias(lengths_ref, block)
                keys = BLOCK * (block + 1)
                rows = slice(BLOCK * block, keys)
                key = qkv_ref[:keys, pair : pair + HD]
                value = qkv_ref[:keys, pair + HD : pair + 2 * HD]
                query, grad_rows = qkv_ref[rows, head_of(head)], grad[rows]
                scores = dot(query, key, ((1,), (1,))) * HD**-0.5 + bias
                probs = jnp.exp(scores - lse_ref[rows, head : head + 1])
                prob_grad = dot(grad_rows, value, ((1,), (1,)))
                score_grad = probs * (prob_grad - delta[rows]) * HD**-0.5
                score_grad = score_grad.astype(bf16)
                turned[rows, head_of(head)] = dot(score_grad, key, ((1,), (0,)))
                key_grad = dot(score_grad, query, ((0,), (0,)))
                value_grad = dot(probs.astype(bf16), grad_rows, ((0,), (0,)))
                if head == PER_KV * kv and block == GROUP // BLOCK - 1:
                    turned[:, pair : pair + HD] = key_grad
                    turned[:, pair + HD : pair + 2 * HD] = value_grad
                    turned[:BLOCK, pair : pair + HD] += held[0]
                    turned[:BLOCK, pair + HD : pair + 2 * HD] += held[1]
                elif head == PER_KV * kv:
                    held = (key_grad, value_grad)
                else:
                    turned[:keys, pair : pair + HD] += key_grad
                    turned[:keys, pair + HD : pair + 2 * HD] += value_grad

    turn_back(0)
    chip_sum(0, swaps[0])
    first_0 = first_sum(0, "x")
    outs.relay()
    handed = [copy for e in range(3) for copy in to_owner(e, sums_ref.at[e])]
    expert_sums[0].relay()
    expert_sums[1].start()
    turn_back(1)
    first_0.relay()
    expert_sums[0].turn()
    grads = turned[...]
    cosine, sine = rope_tables(lengths_ref, trig_ref)
    grads = grads * cosine + swap_halves(grads, 1.0, -1.0) * sine
    mixed_grad[...] = grads.astype(bf16)
    part[...] = (
        dot(mixed_grad[...], entry_ref[...], ((1,), (1,))).astype(bf16).reshape(part.shape)
    )
    rows = Reduce(plan, 42, "seq", lambda i: part.at[i], bufs[7], half_rows).start()

    def entry_rows(block):
        rows_of = slice(QOWN * block, QOWN * (block + 1))
        grad = dot(normed_ref[:, rows_of], mixed_grad[...], ((0,), (0,))).astype(bf16)
        return spread(grad)

    full[1, :, :, :, :640] = entry_rows(0)
    full[1, :, :, :, 640:1280] = entry_rows(1)
    third = entry_rows(2)
    full[1, :, :, :, 1280:] = third[..., :256]
    swaps.append(swap(1))
    rows.relay()
    second_0 = second_sum(0, "y", first_0)
    expert_sums[0].relay_again()
    full[2, :, :, :, :384] = third[..., 256:]
    full[2, :, :, :, 384:1024] = entry_rows(3)
    chip_sum(1, swaps[1])
    first_1 = first_sum(1, "x")
    back, gain_one = norm_back(in_ref[...].astype(f32), gain_ref[...], rows.total())
    input_ref[...] = grad_ref[...] + back
    row_of = lax.broadcasted_iota(jnp.int32, (128, D), 0)
    gains = jnp.where(row_of == EXPERTS, gain_one, 0.0)
    gains = jnp.where(row_of == EXPERTS + 1, gain_two_ref[...], gains)
    shared = router_grad_ref[...] + gains.T
    for block in range(4):
        shared_rows = shared[QOWN * block : QOWN * (block + 1), :].astype(bf16)
        full[2, :, :, :, 1024 + 128 * block : 1152 + 128 * block] = spread(shared_rows)
    swaps.append(swap(2))
    second_0.relay()
    expert_sums[1].relay()
    block_ref[...] = middle_ref[...] + outs.total()
    chip_sum(2, swaps[2])
    first_2 = first_sum(2, "y")
    expert_sums[0].finish(last_sums.at[0])
    handed += to_owner(3, last_sums.at[0])
    first_1.relay()
    first_2.relay()
    exit_out[...] = second_0.total()
    expert_sums[1].turn()
    second_1 = second_sum(1, "y", first_1)
    second_2 = second_sum(2, "x", first_2)
    second_1.relay()
    second_2.relay()
    expert_sums[1].relay_again()
    final[0] = second_1.total()
    final[1] = second_2.total()
    give[0, :, :MIX_OWN] = final[0, :, :640]
    give[1, :, :MIX_OWN] = final[0, :, 640:1280]
    give[2, :, :256] = final[0, :, 1280:]
    give[2, :, 256:MIX_OWN] = final[1, :, :384]
    give[3, :, :MIX_OWN] = final[1, :, 384:1024]
    for block in range(4):
        give[block, :, MIX_OWN:] = final[1, :, 1024 + 128 * block : 1152 + 128 * block]
    home = [
        send(give.at[peer], got_z.at[k], 51 + k, "seq", peer)
        for k, peer in enumerate((right, far, left))
    ]
    entry_out[z] = give[z]
    expert_sums[1].finish(last_sums.at[1])
    handed += to_owner(4, last_sums.at[1])
    for k, source in enumerate((left, far, right)):
        home[k].wait_recv()
        entry_out[source] = got_z[k]
    for copy in swaps + home:
        copy.wait_send()
    for copy in handed:
        copy.wait()
    for plane_sum in expert_sums:
        plane_sum.drain()
    for reduce in (rows, outs, first_0, first_1, first_2, second_0, second_1, second_2):
        reduce.drain()


def closing(*operands):
    row_bufs = reduce_scratch((TOK_DEV, D), (HALF, D))
    chip_bufs = reduce_scratch((4, PAD_ROWS, D), (2, PAD_ROWS, D))
    line_bufs = reduce_scratch((PAD_ROWS, D), (PAD_ROWS, D // 2))
    tile = (PAD_ROWS, D)
    return pl.pallas_call(
        closing_kernel,
        out_shape=[
            jax.ShapeDtypeStruct((TOK_DEV, D), f32),
            jax.ShapeDtypeStruct((TOK_DEV, D), f32),
            jax.ShapeDtypeStruct((4, PAD_ROWS, WIDE), f32),
            jax.ShapeDtypeStruct((PAD_ROWS, D), f32),
            jax.ShapeDtypeStruct((2 * LOCAL_E, 48, 1024), bf16),
            jax.ShapeDtypeStruct((2 * LOCAL_E, 16, D), bf16),
        ],
        in_specs=[VMEM] * 2
        + [pl.BlockSpec(memory_space=pltpu.SMEM)]
        + [VMEM] * (len(operands) - 3),
        out_specs=[VMEM] * 6,
        scratch_shapes=[
            pltpu.VMEM((2, 144, 1024), bf16),
            pltpu.VMEM((GROUP, MIX_OWN), f32),
            pltpu.VMEM((GROUP, MIX_OWN), bf16),
            pltpu.VMEM((N_SEQ, TOK_DEV, D), bf16),
            pltpu.VMEM((3, 16, 2) + tile, bf16),
            pltpu.VMEM((3, 16) + tile, bf16),
            pltpu.VMEM((3, 4, 4) + tile, bf16),
            pltpu.VMEM((3, 4) + tile, bf16),
            pltpu.VMEM((2,) + tile, f32),
            pltpu.VMEM((4, PAD_ROWS, WIDE), f32),
            pltpu.VMEM((3, PAD_ROWS, WIDE), f32),
        ]
        + chip_bufs * 3
        + line_bufs * 3
        + row_bufs * 2
        + plane_scratch() * 2
        + sems(117),
        compiler_params=remote_params(5),
    )(*operands)


def weights_of(w_ref):
    expand = w_ref[:, 0, :96, :].reshape(D, 2 * FF)
    left = w_ref[:, 0, 96:128, :].reshape(FF, 1024)
    right = jnp.concatenate([w_ref[:, 0, 128:144, :512], w_ref[:, 0, 128:144, 512:]], axis=1)
    return expand, left, right.reshape(FF, 512)

def grads_kernel(
    rows_ref, cot_ref, gate_ref, w_ref, hidden_ref, up_ref, out_ref, later_ref, line_ref,
    own, *rest
):
    bufs, (send_sem, recv_sem) = [rest[6 * i : 6 * i + 6] for i in range(2)], rest[12:]
    e = pl.program_id(0)
    plan = planner(send_sem, recv_sem)
    low, high = pl.ds(0, 512), pl.ds(512, 512)
    low_x = Reduce(plan, 0, "x", lambda i: own.at[i, :, :, low], bufs[0], half_rows)
    high_y = Reduce(plan, 6, "y", lambda i: own.at[:, i, :, high], bufs[1], half_rows)

    @pl.when(e == 0)
    def _():
        greet(near("x") + near("y"))

    expand, left, right = weights_of(w_ref)
    grad_rows = (gate_ref[0] * cot_ref[0].astype(f32)).astype(bf16)
    rows = rows_ref[0]
    gate_pre = dot(rows, expand[:, :FF], ((1,), (0,)))
    up_part = dot(rows, expand[:, FF:], ((1,), (0,)))
    sig = jax.nn.sigmoid(gate_pre)
    hidden = (gate_pre * sig * up_part).astype(bf16)
    hidden_ref[0] = hidden

    @pl.when(e == 2)
    def _():
        low_x.relay()
        high_y.relay()

    hidden_grad = dot(grad_rows[:, :1024], left, ((1,), (1,))) + dot(
        grad_rows[:, 1024:], right, ((1,), (1,))
    )
    up_ref[0, :, :FF] = (hidden_grad * up_part * sig * (1.0 + gate_pre * (1.0 - sig))).astype(bf16)
    up_ref[0, :, FF:] = (hidden_grad * gate_pre * sig).astype(bf16)

    def write(shrink_at, end_at, expand_at):
        grad_left = dot(hidden, grad_rows[:, :1024], ((0,), (0,))).astype(bf16)
        grad_right = dot(hidden, grad_rows[:, 1024:], ((0,), (0,))).astype(bf16)
        grad_right = grad_right.reshape(4, 4, 32, 512)
        shrink_at(grad_left.reshape(4, 4, 32, 1024))
        end_at(grad_right[:, :, :16], grad_right[:, :, 16:])
        up_grad = up_ref[0]
        for j in range(4):
            part = dot(rows[:, 384 * j : 384 * (j + 1)], up_grad, ((0,), (0,))).astype(bf16)
            expand_at(j, part.reshape(4, 96, 1024))

    @pl.when(e == 0)
    def _():
        def shrink_at(value):
            own[:, :, 96:128, :] = value

        def end_at(first, second):
            own[:, :, 128:144, :512] = first
            own[:, :, 128:144, 512:] = second

        def expand_at(j, value):
            own[j, :, :96, :] = value

        write(shrink_at, end_at, expand_at)
        low_x.start()
        high_y.start()

    def write_out(out_ref):
        def shrink_at(value):
            out_ref[:, :, 0, 96:128, :] = value

        def end_at(first, second):
            out_ref[:, :, 0, 128:144, :512] = first
            out_ref[:, :, 0, 128:144, 512:] = second

        def expand_at(j, value):
            out_ref[j, :, 0, :96, :] = value

        write(shrink_at, end_at, expand_at)

    @pl.when((e == 1) | (e == 2))
    def _():
        write_out(out_ref)

    @pl.when(e >= 3)
    def _():
        write_out(later_ref)

    @pl.when(e == LOCAL_E - 1)
    def _():
        line_ref[0] = low_x.total().astype(bf16)
        line_ref[1] = high_y.total().astype(bf16)
        low_x.drain()
        high_y.drain()


def expert_grads(rows, cot_rows, row_gates, weights):
    one = lambda e: (e, 0, 0)
    wide = lambda e: (0, e, 0, 0)
    out = lambda e: (0, 0, jnp.clip(e - 1, 0, 1), 0, 0)
    later = lambda e: (0, 0, jnp.maximum(e - 3, 0), 0, 0)
    return pl.pallas_call(
        grads_kernel,
        grid=(LOCAL_E,),
        in_specs=[
            pl.BlockSpec((1, SLOTS, D), one),
            pl.BlockSpec((1, SLOTS, D), one),
            pl.BlockSpec((1, SLOTS, 1), one),
            pl.BlockSpec((16, 1, 144, 1024), wide),
        ],
        out_specs=[
            pl.BlockSpec((1, SLOTS, FF), one),
            pl.BlockSpec((1, SLOTS, 2 * FF), one),
            pl.BlockSpec((4, 4, 1, 144, 1024), out),
            pl.BlockSpec((4, 4, 1, 144, 1024), later),
            pl.BlockSpec((2, 4, 144, 512), lambda e: (0, 0, 0, 0)),
        ],
        out_shape=[
            jax.ShapeDtypeStruct((LOCAL_E, SLOTS, FF), bf16),
            jax.ShapeDtypeStruct((LOCAL_E, SLOTS, 2 * FF), bf16),
            jax.ShapeDtypeStruct((4, 4, 2, 144, 1024), bf16),
            jax.ShapeDtypeStruct((4, 4, 2, 144, 1024), bf16),
            jax.ShapeDtypeStruct((2, 4, 144, 512), bf16),
        ],
        scratch_shapes=[pltpu.VMEM((4, 4, 144, 1024), bf16)]
        + reduce_scratch((4, 144, 512), (2, 144, 512)) * 2
        + sems(12),
        compiler_params=remote_params(7),
        cost_estimate=pl.CostEstimate(
            flops=12 * LOCAL_E * SLOTS * D * FF, bytes_accessed=60 << 20, transcendentals=0
        ),
    )(rows, cot_rows, row_gates, weights)


def token_trig():
    frequency = rope_base ** (-np.arange(HD // 2, dtype=np.float64) * 2.0 / HD)
    phase = np.arange(GROUP, dtype=np.float64)[:, None] * np.tile(frequency, 4)[None, :]
    return np.stack([np.cos(phase), np.sin(phase)]).astype(np.float32)


def adamw_step(weight, gradient, mean_old, square_old, rate, decay):
    drift = beta_first * mean_old + (1.0 - beta_first) * gradient
    spread = beta_second * square_old + (1.0 - beta_second) * gradient * gradient
    mean_hat = drift / (1.0 - beta_first**STEP)
    square_hat = spread / (1.0 - beta_second**STEP)
    master = weight - rate * (mean_hat / (jnp.sqrt(square_hat) + adam_eps) + decay * weight)
    return (drift, spread, master)


def on_device(
    activations,
    cotangent,
    seq_lengths,
    deal_order,
    routes,
    entry_weight,
    entry_mean,
    entry_square,
    exit_weight,
    exit_mean,
    exit_square,
    router_weight,
    router_mean,
    router_square,
    expand_weight,
    expand_mean,
    expand_square,
    shrink_weight,
    shrink_mean,
    shrink_square,
    norm_gains,
    gains_mean,
    gains_square,
):
    angles = (seq_lengths, token_trig())
    (
        weights, entry_own, shared, exit_own, gains, normed, qkv, attended, lse, middle,
        normed_two, rows, cot_rows, row_gates, rank, my_gates,
    ) = forward(
        activations[0],
        cotangent[0],
        activations[0],
        routes[0].T,
        deal_order,
        *angles,
        entry_weight,
        exit_weight,
        router_weight,
        norm_gains,
        expand_weight,
        shrink_weight,
    )
    weights = weights.reshape(16, LOCAL_E, 144, 1024)
    hidden, up_grad, second_grads, last_grads, line = expert_grads(
        rows, cot_rows, row_gates, weights
    )
    middle_grad, branch_grad, logit_grad, gain_two_grad, out_sum, sums = turn(
        rank,
        up_grad,
        hidden,
        row_gates,
        cot_rows,
        weights,
        line,
        second_grads,
        middle,
        cotangent[0],
        my_gates,
        shared,
        gains[1:2],
    )
    branch_grad = branch_grad.reshape(GROUP, D)
    router_grad = dot(normed_two, logit_grad, ((0,), (0,)))

    input_rows, block_rows, entry_got, exit_got, expand_sum, shrink_sum = closing(
        qkv,
        lse,
        *angles,
        exit_own,
        entry_own,
        activations[0],
        middle_grad,
        gains[0:1],
        normed,
        attended,
        branch_grad,
        router_grad,
        gain_two_grad,
        out_sum,
        middle,
        last_grads,
        sums,
    )

    input_grad, block_output = input_rows.astype(bf16), block_rows.astype(bf16)

    entry_got = entry_got[:, :ROWS]
    entry_sum = jnp.concatenate(
        [
            entry_got[:, :, :Q_OWN].transpose(1, 0, 2).reshape(ROWS, QH * HD),
            entry_got[:, :, Q_OWN:MIX_OWN].transpose(1, 0, 2).reshape(ROWS, 2 * KVH * HD),
        ],
        axis=1,
    )
    shared_sum = jnp.sum(entry_got[:, :, MIX_OWN:], axis=0)
    router_sum = shared_sum[:, :EXPERTS]
    gains_sum = shared_sum[:, EXPERTS : EXPERTS + 2].T
    exit_sum = exit_got[:ROWS]

    expand_sum, shrink_sum = expand_sum.astype(f32), shrink_sum.astype(f32)
    entry_new = adamw_step(entry_weight, entry_sum, entry_mean, entry_square, 0.02, weight_decay)
    exit_new = adamw_step(exit_weight, exit_sum, exit_mean, exit_square, 0.15, weight_decay)
    router_new = adamw_step(
        router_weight, router_sum, router_mean, router_square, 0.01, weight_decay
    )
    expand_new = adamw_step(
        expand_weight, expand_sum, expand_mean, expand_square, 0.02, weight_decay
    )
    shrink_new = adamw_step(
        shrink_weight, shrink_sum, shrink_mean, shrink_square, 0.12, weight_decay
    )
    gains_new = adamw_step(norm_gains, gains_sum, gains_mean, gains_square, 0.5, 0.0)
    return (
        block_output[None],
        input_grad[None],
        *entry_new,
        *exit_new,
        *router_new,
        *expand_new,
        *shrink_new,
        *gains_new,
    )


def solution(mesh):
    fine = Mesh(mesh.devices.reshape(4, 4, 4, 2), ("seq", "x", "y", "core"))
    rows = P(FSDP, "seq", None)
    lists = P(FSDP, None)
    owned = P(("seq",) + FSDP, None)
    experts = P("seq", FSDP, None)
    gains = P(None, ("seq",) + FSDP)
    return jax.shard_map(
        on_device,
        mesh=fine,
        in_specs=(rows, rows, lists, lists, rows)
        + (owned,) * 9
        + (experts,) * 6
        + (gains,) * 3,
        out_specs=(rows, rows) + (owned,) * 9 + (experts,) * 6 + (gains,) * 3,
        check_vma=False,
    )
```

```python
import jax
import jax.numpy as jnp
import numpy as np
from jax import lax
from jax.experimental import pallas as pl
from jax.experimental.pallas import tpu as pltpu
from jax.sharding import Mesh, PartitionSpec as P

D = 1536
QH = 24
KVH = 8
HD = 64
FF = 512
EXPERTS = 40
TOP = 8
STEP = 10
CAP = 29

N_SEQ = 4
TOK_DEV = 128
GROUP = 512
PAIR_TOK = 2 * GROUP
LOCAL_E = EXPERTS // (2 * N_SEQ)
SLOTS = 256
Q_OWN = QH * HD // N_SEQ
KV_OWN = 2 * KVH * HD // N_SEQ
MIX_OWN = Q_OWN + KV_OWN
HEADS_OWN = QH // N_SEQ
KV_HEADS_OWN = KVH // N_SEQ
PER_KV = QH // KVH
ROWS = 12

norm_eps = 1e-06
rope_base = 10000.0
beta_first = 0.9
beta_second = 0.95
adam_eps = 1e-08
weight_decay = 0.1

FSDP = ("x", "y", "core")
PLANE = ("x", "y")
f32 = jnp.float32
bf16 = jnp.bfloat16


BIG = 60 * 1024 * 1024
HALF = TOK_DEV // 2
QOWN = Q_OWN
MESH = pl.DeviceIdType.MESH
ANY = pl.BlockSpec(memory_space=pl.ANY)
VMEM = pl.BlockSpec(memory_space=pltpu.VMEM)


def dot(a, b, dims):
    return lax.dot_general(a, b, (dims, ((), ())), preferred_element_type=f32)


def greet(peers):
    barrier = pltpu.get_barrier_semaphore()
    for axis, peer in peers:
        pl.semaphore_signal(barrier, inc=1, device_id={axis: peer}, device_id_type=MESH)
    pl.semaphore_wait(barrier, len(peers))


def planner(send_sem, recv_sem):
    def plan(src, dst, index, axis, peer):
        return pltpu.make_async_remote_copy(
            src_ref=src,
            dst_ref=dst,
            send_sem=send_sem.at[index],
            recv_sem=recv_sem.at[index],
            device_id={axis: peer},
            device_id_type=MESH,
        )

    return plan


def sender(send_sem, recv_sem):
    plan = planner(send_sem, recv_sem)

    def send(*args):
        copy = plan(*args)
        copy.start()
        return copy

    return send


def sems(count):
    return [pltpu.SemaphoreType.DMA((count,)), pltpu.SemaphoreType.DMA((count,))]


def ring(me):
    right, left = lax.rem(me + 1, 4), lax.rem(me + 3, 4)
    return right, left, lax.rem(me + 2, 4)


def near(axis):
    right, left, _ = ring(lax.axis_index(axis))
    return [(axis, right), (axis, left)]


def sibling():
    return ("core", 1 - lax.axis_index("core"))


def half_rows(ref, half):
    size = ref.shape[0] // 2
    return ref.at[pl.ds(half * size, size)]


def half_lanes(ref, half):
    size = ref.shape[-1] // 2
    return ref.at[(slice(None),) * (len(ref.shape) - 1) + (pl.ds(half * size, size),)]


class Gather:
    def __init__(self, plan, base, axis, mine, slot, cut):
        me = lax.axis_index(axis)
        right, left, self.far = ring(me)
        self.right, self.left = right, left
        here, from_left, from_right = slot(me), cut(slot(left), 0), cut(slot(right), 1)
        self.first = [
            plan(cut(mine, 0), cut(here, 0), base, axis, right),
            plan(cut(mine, 1), cut(here, 1), base + 1, axis, left),
            plan(cut(mine, 1), cut(here, 1), base + 2, axis, right),
            plan(cut(mine, 0), cut(here, 0), base + 3, axis, left),
        ]
        self.later = [
            plan(from_left, from_left, base + 4, axis, right),
            plan(from_right, from_right, base + 5, axis, left),
        ]

    def start(self):
        for copy in self.first:
            copy.start()
        return self

    def relay(self):
        for got, on in zip(self.first, self.later):
            got.wait_recv()
            on.start()

    def wait_left(self):
        self.first[2].wait_recv()

    def wait_right(self):
        self.first[3].wait_recv()

    def wait_far(self):
        for copy in self.later:
            copy.wait_recv()

    def finish(self):
        self.wait_left()
        self.wait_right()
        self.wait_far()

    def drain(self):
        for copy in self.first + self.later:
            copy.wait_send()


def hand_over(send, base, mine, out, gather):
    me, core = lax.axis_index("seq"), lax.axis_index("core")
    other = 1 - core
    copies = [send(mine, out.at[core, me], base, "core", other)]
    gather.relay()
    gather.wait_left()
    block = out.at[core, gather.left]
    copies.append(send(block, block, base + 1, "core", other))
    gather.wait_right()
    block = out.at[core, gather.right]
    copies.append(send(block, block, base + 2, "core", other))
    gather.wait_far()
    block = out.at[core, gather.far]
    copies.append(send(block, block, base + 3, "core", other))
    return copies


def reduce_scratch(block, half):
    return [pltpu.VMEM(half, bf16)] * 4 + [pltpu.VMEM(block, bf16)] * 2


def added(target, first, second):
    target[...] = (first[...].astype(f32) + second[...].astype(f32)).astype(bf16)


class Reduce:
    def __init__(self, plan, base, axis, block, bufs, cut):
        me = lax.axis_index(axis)
        right, left, far = ring(me)
        from_left, from_right, to_right, to_left, got_left, got_right = bufs
        far, on_right, on_left = block(far), block(right), block(left)
        self.mine, self.got = block(me), (got_left, got_right)
        self.hops = (
            (to_right, cut(on_right, 0), from_left),
            (to_left, cut(on_left, 1), from_right),
        )
        self.far = [
            plan(cut(far, 0), from_left, base, axis, right),
            plan(cut(far, 1), from_right, base + 1, axis, left),
        ]
        self.near = [
            plan(cut(on_right, 1), cut(got_left, 1), base + 2, axis, right),
            plan(cut(on_left, 0), cut(got_right, 0), base + 3, axis, left),
        ]
        self.later = [
            plan(to_right, cut(got_left, 0), base + 4, axis, right),
            plan(to_left, cut(got_right, 1), base + 5, axis, left),
        ]

    def start_far(self):
        for copy in self.far:
            copy.start()

    def start_near(self):
        for copy in self.near:
            copy.start()

    def start(self):
        self.start_far()
        self.start_near()
        return self

    def relay(self):
        for got, hop, on in zip(self.far, self.hops, self.later):
            got.wait_recv()
            added(*hop)
            on.start()

    def total(self):
        for copy in self.near + self.later:
            copy.wait_recv()
        total = self.mine[...].astype(f32)
        for part in self.got:
            total += part[...].astype(f32)
        return total

    def drain(self):
        for copy in self.far + self.near + self.later:
            copy.wait_send()


def remote_params(call_id, vmem=BIG):
    return pltpu.CompilerParams(
        collective_id=call_id, has_side_effects=True, vmem_limit_bytes=vmem
    )


def unit_scale(vector):
    return lax.rsqrt(jnp.mean(vector * vector, axis=-1, keepdims=True) + norm_eps)


def norm_back(vector, gain, grad):
    scale = unit_scale(vector)
    unit = vector * scale
    pulled = grad * gain
    back = scale * (pulled - unit * jnp.mean(pulled * unit, axis=-1, keepdims=True))
    return back, jnp.sum(unit * grad, axis=0, keepdims=True)


MAIN_E = LOCAL_E - 1


def row_pick(shape, padded_axis):
    padded = lax.broadcasted_iota(jnp.int32, shape, padded_axis)
    plain = lax.broadcasted_iota(jnp.int32, shape, 1 - padded_axis)
    row = lax.rem(padded, 16)
    return ((plain == lax.div(padded, 16) * 12 + row) & (row < 12)).astype(bf16)


def swap_halves(rows, lower, upper):
    lane = lax.broadcasted_iota(jnp.int32, rows.shape, 1)
    ahead = pltpu.roll(rows, rows.shape[1] - HD // 2, 1)
    behind = pltpu.roll(rows, HD // 2, 1)
    return jnp.where(lax.rem(lane, HD) < HD // 2, lower * ahead, upper * behind)


BLOCK = 256


def sequence_of(lengths_ref, token):
    first_end = lengths_ref[0, 0]
    second_end = first_end + lengths_ref[0, 1]
    return (token >= first_end).astype(jnp.int32) + (token >= second_end).astype(jnp.int32)


def block_bias(lengths_ref, block):
    keys = BLOCK * (block + 1)
    row = lax.broadcasted_iota(jnp.int32, (BLOCK, keys), 0) + BLOCK * block
    column = lax.broadcasted_iota(jnp.int32, (BLOCK, keys), 1)
    same = sequence_of(lengths_ref, row) == sequence_of(lengths_ref, column)
    return jnp.where(same & (column <= row), 0.0, -1e30)


def rope_tables(lengths_ref, trig_ref):
    seq = sequence_of(lengths_ref, lax.broadcasted_iota(jnp.int32, (GROUP, 128), 0))
    second = lengths_ref[0, 0]
    third = second + lengths_ref[0, 1]

    def of_start(table):
        later = jnp.where(
            seq == 1, trig_ref[table, pl.ds(second, 1)], trig_ref[table, pl.ds(third, 1)]
        )
        return jnp.where(seq == 0, trig_ref[table, 0:1], later)

    start_cos, start_sin = of_start(0), of_start(1)
    cosine = trig_ref[0] * start_cos + trig_ref[1] * start_sin
    sine = trig_ref[1] * start_cos - trig_ref[0] * start_sin
    is_key = lax.broadcasted_iota(jnp.int32, (GROUP, 128), 1) < HD
    pair_cos, pair_sin = jnp.where(is_key, cosine, 1.0), jnp.where(is_key, sine, 0.0)
    return (
        jnp.concatenate([cosine] * 3 + [pair_cos] * 2, axis=1),
        jnp.concatenate([sine] * 3 + [pair_sin] * 2, axis=1),
    )


def head_of(index):
    return slice(HD * index, HD * (index + 1))


def lane_pick(first, rows):
    row = lax.broadcasted_iota(jnp.int32, (rows, 128), 0)
    lane = lax.broadcasted_iota(jnp.int32, (rows, 128), 1)
    return (lane == row + first).astype(bf16)


def forward_kernel(
    in_hbm, cot_hbm, in_ref, route_ref, order_ref, lengths_ref, trig_ref,
    entry_ref, exit_ref, router_ref, gain_ref, expand_ref, shrink_ref,
    weights_out, entry_hbm, exit_hbm, normed_hbm, rows_hbm, cot_rows_hbm,
    shared_out, gains_out, qkv_ref, attended_ref,
    lse_ref, middle_ref, mine, row_gate_out, rank_out, my_gate_out,
    entry_out, exit_out, normed_ref, rows_out, cot_rows_out,
    stage, stage_end, packed, shared, columns, hold, full,
    in_all, cot_all, hit_all, hit_pair, tokens, part, gates, *rest
):
    bufs, (send_sem, recv_sem, copy_sem) = rest[:6], rest[6:]
    z, x, y, c = (lax.axis_index(a) for a in ("seq", "x", "y", "core"))
    right, left, far = ring(z)
    other = 1 - c
    greet(near("seq") + [("seq", far)] + near("x") + near("y") + [sibling()])
    send, plan = sender(send_sem, recv_sem), planner(send_sem, recv_sem)

    for e in range(LOCAL_E):
        theirs = other * LOCAL_E + e
        stage[e, :48] = expand_ref[theirs].astype(bf16)
        stage[e, 48:] = shrink_ref[theirs, :, :1024].astype(bf16)
        stage_end[e] = shrink_ref[theirs, :, 1024:].astype(bf16)
    of_core = pl.ds(pl.multiple_of(c * 48, 16), 48)
    lefts = pl.ds(pl.multiple_of(96 + c * 16, 16), 16)
    ends = pl.ds(pl.multiple_of(c * 512, 512), 512)
    to_core = [
        send(stage.at[:, pl.ds(0, 48)], packed.at[:, of_core], 51, "core", other),
        send(stage.at[:, pl.ds(48, 16)], packed.at[:, lefts], 52, "core", other),
        send(stage_end, packed.at[:, pl.ds(128, 16), ends], 53, "core", other),
    ]
    for e in range(LOCAL_E):
        own_e = c * LOCAL_E + e
        packed[e, of_core, :] = expand_ref[own_e].astype(bf16)
        packed[e, lefts, :] = shrink_ref[own_e, :, :1024].astype(bf16)
        packed[e, pl.ds(128, 16), ends] = shrink_ref[own_e, :, 1024:].astype(bf16)
    rows = Gather(plan, 9, "seq", in_hbm, lambda i: in_all.at[i], half_rows).start()
    expert = lax.broadcasted_iota(jnp.int32, (128, TOK_DEV), 0)
    hit = route_ref[0:1] == expert
    for k in range(1, TOP):
        hit = hit | (route_ref[k : k + 1] == expert)
    hit_all[z] = hit.astype(bf16)
    hits = Gather(plan, 3, "seq", hit_all.at[z], lambda i: hit_all.at[i], half_rows).start()

    lane = lax.broadcasted_iota(jnp.int32, (ROWS, 128), 1)
    square = lax.broadcasted_iota(jnp.int32, (ROWS, ROWS), 0)
    square = square == lax.broadcasted_iota(jnp.int32, (ROWS, ROWS), 1)
    shared[...] = jnp.zeros_like(shared)
    shared[:, :EXPERTS] = router_ref[...]
    block_of = shared[...]
    for k in range(2):
        column = jnp.sum(jnp.where(square, gain_ref[k : k + 1], 0.0), axis=1, keepdims=True)
        block_of = jnp.where(lane == EXPERTS + k, column, block_of)
    empty = jnp.zeros((PAD_ROWS - ROWS, WIDE), f32)
    for block in range(4):
        cols = jnp.concatenate(
            [
                entry_ref[:, Q_OWN * block : Q_OWN * (block + 1)],
                entry_ref[:, QH * HD + KV_OWN * block : QH * HD + KV_OWN * (block + 1)],
                block_of,
            ],
            axis=1,
        )
        columns[block] = jnp.concatenate([cols, empty], axis=0).astype(bf16)
    to_seq = [
        send(columns.at[peer], hold.at[z], k, "seq", peer)
        for k, peer in enumerate((right, far, left))
    ]
    for block in range(2):
        cols = exit_ref[:, WIDE * block : WIDE * (block + 1)]
        hold[4 + block] = jnp.concatenate([cols, empty], axis=0).astype(bf16)
    hold[z] = columns[z]
    local = [
        pltpu.make_async_copy(in_hbm, in_all.at[z], copy_sem.at[0]),
        pltpu.make_async_copy(cot_hbm, cot_all.at[c, z], copy_sem.at[1]),
    ]
    for copy in local:
        copy.start()

    for copy in to_seq:
        copy.wait_recv()
    for block in range(6):
        full[block, x, y, c] = hold[block]
    low, high = pl.ds(0, 3), pl.ds(3, 3)
    low_x = Gather(plan, 15, "x", hold.at[low], lambda i: full.at[low, i, y, c], half_lanes)
    low_x.start()
    high_y = Gather(plan, 21, "y", hold.at[high], lambda i: full.at[high, x, i, c], half_lanes)
    high_y.start()
    for copy in to_core:
        copy.wait_recv()
    own_weights = pltpu.make_async_copy(packed, weights_out.at[x, y], copy_sem.at[2])
    own_weights.start()
    start, end = pl.ds(0, 512), pl.ds(512, 512)
    expert_x = Gather(
        plan,
        54,
        "x",
        packed.at[:, :, start],
        lambda i: weights_out.at[i, y, :, :, start],
        half_lanes,
    ).start()
    expert_y = Gather(
        plan,
        60,
        "y",
        packed.at[:, :, end],
        lambda i: weights_out.at[x, i, :, :, end],
        half_lanes,
    ).start()

    def cut_low(ref, half):
        return ref.at[:, pl.ds(2 * half, 2)]

    hits.relay()
    low_x.relay()
    high_y.relay()
    rows.relay()
    cots = Gather(plan, 27, "seq", cot_hbm, lambda i: cot_all.at[c, i], half_rows).start()
    low_x.finish()
    low_y = Gather(
        plan, 33, "y", full.at[low, :, y, c], lambda i: full.at[low, :, i, c], cut_low
    ).start()
    high_y.finish()
    high_x = Gather(
        plan, 39, "x", full.at[high, x, :, c], lambda i: full.at[high, i, :, c], cut_low
    ).start()
    expert_x.relay()
    expert_y.relay()

    hits.finish()
    token = lax.broadcasted_iota(jnp.int32, (GROUP, GROUP), 0)
    back_hot = (order_ref[...] == token).astype(bf16)
    natural = jnp.zeros((GROUP, 128), f32)
    for block in range(N_SEQ):
        slots = back_hot[:, TOK_DEV * block : TOK_DEV * (block + 1)]
        natural += dot(slots, hit_all[block], ((1,), (1,)))
    hit_pair[c] = natural.astype(bf16)
    hit_swap = send(hit_pair.at[c], hit_pair.at[c], 66, "core", other)
    low_y.relay()
    high_x.relay()
    hit_swap.wait_recv()
    hit_both = hit_pair[...].reshape(PAIR_TOK, 128)
    first = (z * 2 + c) * LOCAL_E
    lower = lax.broadcasted_iota(jnp.int32, (PAIR_TOK, PAIR_TOK), 0)
    lower = (lower >= lax.broadcasted_iota(jnp.int32, (PAIR_TOK, PAIR_TOK), 1)).astype(bf16)
    rank = dot(lower, hit_both, ((1,), (0,))) - 1.0
    rank = jnp.where(hit_both.astype(f32) > 0.0, rank, -1.0).astype(bf16)
    mine_of = lane_pick(first, 8)
    rank_out[...] = dot(rank, mine_of, ((1,), (1,))).astype(jnp.int32)
    rank_rows = dot(mine_of, rank, ((1,), (1,))).astype(jnp.int32)

    low_y.finish()
    half = full.at[low, :, :, c]
    last = [send(half, half, 49, "core", other)]
    high_x.finish()
    half = full.at[high, :, :, c]
    last.append(send(half, half, 50, "core", other))
    own_weights.wait()
    expert_x.finish()
    expert_low = Gather(
        plan,
        67,
        "y",
        weights_out.at[:, y, :, :, start],
        lambda i: weights_out.at[:, i, :, :, start],
        half_rows,
    ).start()
    expert_y.finish()
    expert_high = Gather(
        plan,
        73,
        "x",
        weights_out.at[x, :, :, :, end],
        lambda i: weights_out.at[i, :, :, :, end],
        half_rows,
    ).start()
    cosine, sine = rope_tables(lengths_ref, trig_ref)
    rows.finish()
    local[0].wait()
    for copy in last:
        copy.wait_recv()
    pick = row_pick((QOWN, 512), 1)
    for block in range(4):
        got = dot(pick, full[block].reshape(512, WIDE), ((1,), (0,))).astype(bf16)
        entry_out[QOWN * block : QOWN * (block + 1), :] = got[:, :MIX_OWN]
        shared_out[QOWN * block : QOWN * (block + 1), :] = got[:, MIX_OWN:]
    for block in range(2):
        got = dot(pick, full[4 + block].reshape(512, WIDE), ((1,), (0,))).astype(bf16)
        exit_out[:, WIDE * block : WIDE * (block + 1)] = got
    gains = dot(lane_pick(EXPERTS, 8), shared_out[...], ((1,), (1,)))
    gains_out[...] = gains
    for block in range(N_SEQ):
        at = slice(TOK_DEV * block, TOK_DEV * (block + 1))
        vector = in_all[block].astype(f32)
        normed_ref[at, :] = (vector * unit_scale(vector) * gains[0:1]).astype(bf16)
    results = [(entry_out, entry_hbm), (exit_out, exit_hbm), (normed_ref, normed_hbm)]
    results = [
        pltpu.make_async_copy(source, target, copy_sem.at[3 + k])
        for k, (source, target) in enumerate(results)
    ]
    for copy in results:
        copy.start()
    mixed = dot(normed_ref[...], entry_out[...], ((1,), (0,)))
    mixed = mixed * cosine + swap_halves(mixed, -1.0, 1.0) * sine
    qkv_ref[...] = mixed.astype(bf16)
    for block in range(GROUP // BLOCK):
        bias = block_bias(lengths_ref, block)
        keys = BLOCK * (block + 1)
        at = slice(BLOCK * block, keys)
        for head in range(HEADS_OWN):
            pair = Q_OWN + 2 * HD * (head // PER_KV)
            key = qkv_ref[:keys, pair : pair + HD]
            value = qkv_ref[:keys, pair + HD : pair + 2 * HD]
            scores = dot(qkv_ref[at, head_of(head)], key, ((1,), (1,))) * HD**-0.5 + bias
            peak = jnp.max(scores, axis=1, keepdims=True)
            expo = jnp.exp(scores - peak)
            total = jnp.sum(expo, axis=1, keepdims=True)
            probs = (expo / total).astype(bf16)
            attended_ref[at, head_of(head)] = dot(probs, value, ((1,), (0,))).astype(bf16)
            lse_ref[at, head : head + 1] = peak + jnp.log(total)
    part[...] = dot(attended_ref[...], exit_out[...], ((1,), (0,))).astype(bf16).reshape(part.shape)
    reduce = Reduce(plan, 79, "seq", lambda i: part.at[i], bufs, half_rows).start()
    pairs = hand_over(send, 45, cot_hbm, cot_all, cots)
    reduce.relay()
    middle = in_ref[...].astype(f32) + reduce.total()
    middle_ref[...] = middle
    mine[...] = (middle * unit_scale(middle) * gains[1:2]).astype(bf16)
    gather = Gather(plan, 85, "seq", mine, lambda i: tokens.at[c, i], half_rows).start()
    tokens[c, z] = mine[...]
    pairs += hand_over(send, 91, mine, tokens, gather)
    for copy in pairs:
        copy.wait()
    local[1].wait()

    logits = dot(tokens[...].reshape(PAIR_TOK, D), shared_out[...], ((1,), (0,)))
    masked = jnp.where(hit_both.astype(f32) > 0.0, logits, -jnp.inf)
    gate_expo = jnp.exp(masked - jnp.max(masked, axis=1, keepdims=True))
    gates[...] = gate_expo / jnp.sum(gate_expo, axis=1, keepdims=True)
    my_gate_out[...] = gates[pl.ds(pl.multiple_of(c * GROUP + z * TOK_DEV, TOK_DEV), TOK_DEV), :]
    rest_of = gates[...]
    gate_rows = jnp.zeros((8, PAIR_TOK), f32)
    for _ in range(3):
        piece = rest_of.astype(bf16)
        gate_rows += dot(mine_of, piece, ((1,), (1,)))
        rest_of -= piece.astype(f32)
    slot = lax.broadcasted_iota(jnp.int32, (SLOTS, PAIR_TOK), 0)
    for e in range(LOCAL_E):
        if e == 3:
            expert_low.relay()
            expert_high.relay()
        match = rank_rows[e : e + 1] == slot
        row_gate_out[e] = jnp.sum(
            jnp.where(match, gate_rows[e : e + 1], 0.0), axis=1, keepdims=True
        )
        match = match.astype(bf16)
        for half in range(2):
            lanes = slice(768 * half, 768 * (half + 1))
            table = tokens[:, :, :, lanes].reshape(PAIR_TOK, 768)
            rows_out[e, :, lanes] = dot(match, table, ((1,), (0,))).astype(bf16)
            table = cot_all[:, :, :, lanes].reshape(PAIR_TOK, 768)
            cot_rows_out[e, :, lanes] = dot(match, table, ((1,), (0,))).astype(bf16)
        for k, (source, target) in enumerate(((rows_out, rows_hbm), (cot_rows_out, cot_rows_hbm))):
            copy = pltpu.make_async_copy(
                source.at[e], target.at[e], copy_sem.at[6 + 2 * e + k]
            )
            copy.start()
            results.append(copy)
    expert_low.finish()
    expert_high.finish()
    for copy in to_seq + to_core + last + [hit_swap]:
        copy.wait_send()
    for copy in results:
        copy.wait()
    for transfer in (hits, rows, cots, low_x, high_y, low_y, high_x, reduce, gather):
        transfer.drain()
    for transfer in (expert_x, expert_y, expert_low, expert_high):
        transfer.drain()


def forward(*operands):
    scalar = pl.BlockSpec(memory_space=pltpu.SMEM)
    block = (PAD_ROWS, WIDE)
    group = (N_SEQ, TOK_DEV, D)
    return pl.pallas_call(
        forward_kernel,
        out_shape=[
            jax.ShapeDtypeStruct((4, 4, LOCAL_E, 144, 1024), bf16),
            jax.ShapeDtypeStruct((D, MIX_OWN), bf16),
            jax.ShapeDtypeStruct((QOWN, D), bf16),
            jax.ShapeDtypeStruct((GROUP, D), bf16),
            jax.ShapeDtypeStruct((LOCAL_E, SLOTS, D), bf16),
            jax.ShapeDtypeStruct((LOCAL_E, SLOTS, D), bf16),
            jax.ShapeDtypeStruct((D, 128), bf16),
            jax.ShapeDtypeStruct((8, D), f32),
            jax.ShapeDtypeStruct((GROUP, MIX_OWN), bf16),
            jax.ShapeDtypeStruct((GROUP, Q_OWN), bf16),
            jax.ShapeDtypeStruct((GROUP, HEADS_OWN), f32),
            jax.ShapeDtypeStruct((TOK_DEV, D), f32),
            jax.ShapeDtypeStruct((TOK_DEV, D), bf16),
            jax.ShapeDtypeStruct((LOCAL_E, SLOTS, 1), f32),
            jax.ShapeDtypeStruct((PAIR_TOK, 8), jnp.int32),
            jax.ShapeDtypeStruct((TOK_DEV, 128), f32),
        ],
        in_specs=[ANY] * 2 + [VMEM] * 3 + [scalar] + [VMEM] * 7,
        out_specs=[ANY] * 6 + [VMEM] * 10,
        scratch_shapes=[
            pltpu.VMEM((D, MIX_OWN), bf16),
            pltpu.VMEM((QOWN, D), bf16),
            pltpu.VMEM((GROUP, D), bf16),
            pltpu.VMEM((LOCAL_E, SLOTS, D), bf16),
            pltpu.VMEM((LOCAL_E, SLOTS, D), bf16),
            pltpu.VMEM((LOCAL_E, 64, 1024), bf16),
            pltpu.VMEM((LOCAL_E, 16, 512), bf16),
            pltpu.VMEM((LOCAL_E, 144, 1024), bf16),
            pltpu.VMEM((ROWS, 128), f32),
            pltpu.VMEM((4,) + block, bf16),
            pltpu.VMEM((6,) + block, bf16),
            pltpu.VMEM((6, 4, 4, 2) + block, bf16),
            pltpu.VMEM(group, bf16),
            pltpu.VMEM((2,) + group, bf16),
            pltpu.VMEM((N_SEQ, TOK_DEV, 128), bf16),
            pltpu.VMEM((2, GROUP, 128), bf16),
            pltpu.VMEM((2,) + group, bf16),
            pltpu.VMEM(group, bf16),
            pltpu.VMEM((PAIR_TOK, 128), f32),
        ]
        + reduce_scratch((TOK_DEV, D), (HALF, D))
        + sems(95)
        + [pltpu.SemaphoreType.DMA((16,))],
        compiler_params=remote_params(2),
    )(*operands)


def turn_kernel(
    rank_ref, up_ref, hidden_ref, gate_ref, cot_rows_ref, w_ref,
    line, middle_ref, cot_ref, my_gate_ref, router_ref, gain_ref,
    grad_ref, branch_ref, logit_ref, gain_grad_ref, out_sum_ref, extra_sum_ref,
    back_s, out_s, other_back, from_core, part, other_out, out_core, mine, *rest
):
    bufs, (send_sem, recv_sem, copy_sem) = [rest[6 * i : 6 * i + 6] for i in range(3)], rest[18:]
    e = pl.program_id(0)
    me, core = lax.axis_index("seq"), lax.axis_index("core")
    send, plan = sender(send_sem, recv_sem), planner(send_sem, recv_sem)
    low_y = Reduce(plan, 17, "y", lambda i: line.at[0, i], bufs[1], half_lanes)
    high_x = Reduce(plan, 23, "x", lambda i: line.at[1, i], bufs[2], half_lanes)

    @pl.when(e == 0)
    def _():
        greet(near("seq") + near("x") + near("y") + [sibling()])
        low_y.start()
        high_x.start()

    @pl.when(e == 2)
    def _():
        low_y.relay()
        high_x.relay()

    @pl.when(e < LOCAL_E)
    def _():
        expand, left, right = weights_of(w_ref)
        at = pl.ds(pl.multiple_of(e * SLOTS, SLOTS), SLOTS)
        back_s[at, :D] = dot(up_ref[0], expand, ((1,), (1,))).astype(bf16)
        hidden = hidden_ref[0]
        expert_out = jnp.concatenate(
            [dot(hidden, left, ((1,), (0,))), dot(hidden, right, ((1,), (0,)))], axis=1
        )
        expert_out = expert_out.astype(bf16).astype(f32)
        gate_grad = jnp.sum(expert_out * cot_rows_ref[0].astype(f32), axis=1, keepdims=True)
        lane = lax.broadcasted_iota(jnp.int32, (SLOTS, 128), 1)
        column = (me * 2 + core) * LOCAL_E + e
        back_s[at, D:] = jnp.where(lane == column, gate_grad, 0.0).astype(bf16)
        out_s[at, :] = (gate_ref[0] * expert_out).astype(bf16)

    @pl.when(e == LOCAL_E)
    def _():
        other = 1 - core
        right, left, far = ring(me)
        slot = lax.broadcasted_iota(jnp.int32, (GROUP, SLOTS), 1)

        def picks(group):
            at = pl.ds(pl.multiple_of(group * GROUP, GROUP), GROUP)
            ranks = rank_ref[at, :]
            return jnp.concatenate(
                [(ranks[:, k : k + 1] == slot).astype(bf16) for k in range(LOCAL_E)], axis=1
            )

        theirs, ours = picks(other), picks(core)
        order = (far, right, left, me)
        other_back[...] = (
            dot(theirs, back_s[...], ((1,), (0,))).astype(bf16).reshape(other_back.shape)
        )
        swaps = [
            send(other_back.at[block], from_core.at[block], 12 + i, "core", other)
            for i, block in enumerate(order)
        ]
        part[...] = dot(ours, back_s[...], ((1,), (0,))).astype(bf16).reshape(part.shape)
        reduce = Reduce(plan, 0, "seq", lambda i: part.at[i], bufs[0], half_rows)
        for i, block in enumerate(order):
            swaps[i].wait_recv()
            added(part.at[block], part.at[block], from_core.at[block])
            if i == 0:
                reduce.start_far()
            if i == 2:
                reduce.start_near()
        other_out[...] = (
            dot(theirs, out_s[...], ((1,), (0,))).astype(bf16).reshape(other_out.shape)
        )
        out_swap = send(other_out, out_core, 16, "core", other)
        reduce.relay()
        out_sum_ref[...] = (
            dot(ours, out_s[...], ((1,), (0,))).astype(bf16).reshape(out_sum_ref.shape)
        )
        total = reduce.total()
        gates, gate_grad = my_gate_ref[...], total[:, D:]
        mean_term = jnp.sum(gates * gate_grad, axis=1, keepdims=True)
        logit_grad = (gates * (gate_grad - mean_term)).astype(bf16)
        logit_ref[...] = logit_grad
        normed_grad = total[:, :D] + dot(logit_grad, router_ref[...], ((1,), (1,)))
        back, gain_grad = norm_back(middle_ref[...], gain_ref[...], normed_grad)
        gain_grad_ref[...] = gain_grad
        middle_grad = cot_ref[...].astype(f32) + back
        grad_ref[...] = middle_grad
        mine[...] = middle_grad.astype(bf16)
        gather = Gather(plan, 6, "seq", mine, lambda i: branch_ref.at[i], half_rows).start()
        local = pltpu.make_async_copy(mine, branch_ref.at[me], copy_sem)
        local.start()
        out_swap.wait_recv()
        added(out_sum_ref, out_sum_ref, out_core)
        gather.relay()
        extra_sum_ref[:, :512] = low_y.total().astype(bf16)
        extra_sum_ref[:, 512:] = high_x.total().astype(bf16)
        gather.finish()
        for transfer in (gather, reduce, low_y, high_x):
            transfer.drain()
        for copy in swaps + [out_swap]:
            copy.wait_send()
        local.wait()


BACK_WIDTH = D + 128


def turn(*operands):
    one = lambda e: (jnp.minimum(e, LOCAL_E - 1), 0, 0)
    wide = lambda e: (0, jnp.minimum(e, LOCAL_E - 1), 0, 0)
    cubes = lambda e: (0, 0, 0, 0)
    whole = lambda e: (0, 0)
    blocks = lambda e: (0, 0, 0)
    row_block = pl.BlockSpec((TOK_DEV, D), whole)
    lane_block = pl.BlockSpec((TOK_DEV, 128), whole)
    gain_block = pl.BlockSpec((1, D), whole)
    group = pltpu.VMEM((N_SEQ, TOK_DEV, BACK_WIDTH), bf16)
    group_out = pltpu.VMEM((N_SEQ, TOK_DEV, D), bf16)
    return pl.pallas_call(
        turn_kernel,
        grid=(LOCAL_E + 1,),
        in_specs=[
            pl.BlockSpec((PAIR_TOK, 8), whole),
            pl.BlockSpec((1, SLOTS, 2 * FF), one),
            pl.BlockSpec((1, SLOTS, FF), one),
            pl.BlockSpec((1, SLOTS, 1), one),
            pl.BlockSpec((1, SLOTS, D), one),
            pl.BlockSpec((16, 1, 144, 1024), wide),
            pl.BlockSpec((2, 4, 144, 512), cubes),
            row_block,
            row_block,
            lane_block,
            pl.BlockSpec((D, 128), whole),
            gain_block,
        ],
        out_specs=[
            row_block,
            ANY,
            lane_block,
            gain_block,
            pl.BlockSpec((N_SEQ, TOK_DEV, D), blocks),
            pl.BlockSpec((144, 1024), whole),
        ],
        out_shape=[
            jax.ShapeDtypeStruct((TOK_DEV, D), f32),
            jax.ShapeDtypeStruct((N_SEQ, TOK_DEV, D), bf16),
            jax.ShapeDtypeStruct((TOK_DEV, 128), bf16),
            jax.ShapeDtypeStruct((1, D), f32),
            jax.ShapeDtypeStruct((N_SEQ, TOK_DEV, D), bf16),
            jax.ShapeDtypeStruct((144, 1024), bf16),
        ],
        scratch_shapes=[
            pltpu.VMEM((LOCAL_E * SLOTS, BACK_WIDTH), bf16),
            pltpu.VMEM((LOCAL_E * SLOTS, D), bf16),
            group,
            group,
            group,
            group_out,
            group_out,
            pltpu.VMEM((TOK_DEV, D), bf16),
        ]
        + reduce_scratch((TOK_DEV, BACK_WIDTH), (HALF, BACK_WIDTH))
        + reduce_scratch((144, 512), (144, 256)) * 2
        + sems(29)
        + [pltpu.SemaphoreType.DMA],
        compiler_params=remote_params(4),
        cost_estimate=pl.CostEstimate(
            flops=6 * LOCAL_E * SLOTS * D * FF + 4 * LOCAL_E * SLOTS * PAIR_TOK * D,
            bytes_accessed=40 << 20,
            transcendentals=0,
        ),
    )(*operands)


PAD_ROWS = 16
WIDE = 768
def owner_order(y_first):
    target = lax.broadcasted_iota(jnp.int32, (QOWN, QOWN), 0)
    source = lax.broadcasted_iota(jnp.int32, (QOWN, QOWN), 1)
    core = lax.div(target, 192)
    first = lax.div(lax.rem(target, 192), 48)
    second = lax.div(lax.rem(target, 48), ROWS)
    x, y = (second, first) if y_first else (first, second)
    owner = x * 8 + y * 2 + core
    return (source == owner * ROWS + lax.rem(target, ROWS)).astype(bf16)


def closing_kernel(
    qkv_ref, lse_ref, lengths_ref, trig_ref, exit_ref, entry_ref,
    in_ref, grad_ref, gain_ref, normed_ref, attended_ref, branch_ref,
    router_grad_ref, gain_two_ref, out_sum_ref, middle_ref,
    input_ref, block_ref, entry_out, exit_out,
    turned, mixed_grad, part, full, from_core, chip, line, final, give, got_z, *rest
):
    bufs, (send_sem, recv_sem) = [rest[6 * i : 6 * i + 6] for i in range(8)], rest[48:]
    z, x, y, c = (lax.axis_index(a) for a in ("seq", "x", "y", "core"))
    right, left, far = ring(z)
    greet(near("seq") + [("seq", far)] + near("x") + near("y") + [sibling()])
    send, plan = sender(send_sem, recv_sem), planner(send_sem, recv_sem)
    picks = (owner_order(False), owner_order(True))
    widen = row_pick((64, 48), 0)

    def spread(side, grad):
        return dot(picks[side == 2], grad, ((1,), (0,))).astype(bf16).reshape(2, 4, 48, -1)

    def swap(side):
        return send(full.at[side, 1 - c], from_core.at[side], 48 + side, "core", 1 - c)

    def chip_sum(side, copy):
        copy.wait_recv()
        added(chip.at[side], full.at[side, c], from_core.at[side])

    def first_sum(side, axis):
        return Reduce(
            plan, 6 * side, axis, lambda i: chip.at[side, i], bufs[side], half_lanes
        ).start()

    def second_sum(side, axis, reduce):
        total = dot(widen, reduce.total().astype(bf16), ((1,), (0,))).astype(bf16)
        line[side] = total.reshape(4, PAD_ROWS, D)
        return Reduce(
            plan, 18 + 6 * side, axis, lambda i: line.at[side, i], bufs[3 + side], half_lanes
        ).start()

    for block in range(3):
        cols = slice(512 * block, 512 * (block + 1))
        grad = dot(attended_ref[...], branch_ref[:, cols], ((0,), (0,))).astype(bf16)
        full[0, :, :, :, cols] = spread(0, grad)
    swaps = [swap(0)]
    outs = Reduce(plan, 36, "seq", lambda i: out_sum_ref.at[i], bufs[6], half_rows).start()

    def turn_back(kv):
        pair = Q_OWN + 2 * HD * kv
        for head in range(PER_KV * kv, PER_KV * (kv + 1)):
            grad = dot(branch_ref[...], exit_ref[head_of(head), :], ((1,), (1,))).astype(bf16)
            attended = attended_ref[:, head_of(head)].astype(f32)
            delta = jnp.sum(grad.astype(f32) * attended, axis=1, keepdims=True)
            for block in range(GROUP // BLOCK):
                bias = block_bias(lengths_ref, block)
                keys = BLOCK * (block + 1)
                rows = slice(BLOCK * block, keys)
                key = qkv_ref[:keys, pair : pair + HD]
                value = qkv_ref[:keys, pair + HD : pair + 2 * HD]
                query, grad_rows = qkv_ref[rows, head_of(head)], grad[rows]
                scores = dot(query, key, ((1,), (1,))) * HD**-0.5 + bias
                probs = jnp.exp(scores - lse_ref[rows, head : head + 1])
                prob_grad = dot(grad_rows, value, ((1,), (1,)))
                score_grad = probs * (prob_grad - delta[rows]) * HD**-0.5
                score_grad = score_grad.astype(bf16)
                turned[rows, head_of(head)] = dot(score_grad, key, ((1,), (0,)))
                key_grad = dot(score_grad, query, ((0,), (0,)))
                value_grad = dot(probs.astype(bf16), grad_rows, ((0,), (0,)))
                if head == PER_KV * kv and block == GROUP // BLOCK - 1:
                    turned[:, pair : pair + HD] = key_grad
                    turned[:, pair + HD : pair + 2 * HD] = value_grad
                    turned[:BLOCK, pair : pair + HD] += held[0]
                    turned[:BLOCK, pair + HD : pair + 2 * HD] += held[1]
                elif head == PER_KV * kv:
                    held = (key_grad, value_grad)
                else:
                    turned[:keys, pair : pair + HD] += key_grad
                    turned[:keys, pair + HD : pair + 2 * HD] += value_grad

    turn_back(0)
    chip_sum(0, swaps[0])
    first_0 = first_sum(0, "x")
    outs.relay()
    turn_back(1)
    first_0.relay()
    grads = turned[...]
    cosine, sine = rope_tables(lengths_ref, trig_ref)
    grads = grads * cosine + swap_halves(grads, 1.0, -1.0) * sine
    mixed_grad[...] = grads.astype(bf16)
    part[...] = (
        dot(mixed_grad[...], entry_ref[...], ((1,), (1,))).astype(bf16).reshape(part.shape)
    )
    rows = Reduce(plan, 42, "seq", lambda i: part.at[i], bufs[7], half_rows).start()

    def entry_rows(block):
        rows_of = slice(QOWN * block, QOWN * (block + 1))
        return dot(normed_ref[:, rows_of], mixed_grad[...], ((0,), (0,))).astype(bf16)

    full[1, :, :, :, :640] = spread(1, entry_rows(0))
    full[1, :, :, :, 640:1280] = spread(1, entry_rows(1))
    third = entry_rows(2)
    full[1, :, :, :, 1280:] = spread(1, third[:, :256])
    swaps.append(swap(1))
    rows.relay()
    second_0 = second_sum(0, "y", first_0)
    full[2, :, :, :, :384] = spread(2, third[:, 256:])
    full[2, :, :, :, 384:1024] = spread(2, entry_rows(3))
    chip_sum(1, swaps[1])
    first_1 = first_sum(1, "x")
    back, gain_one = norm_back(in_ref[...].astype(f32), gain_ref[...], rows.total())
    input_ref[...] = grad_ref[...] + back
    row_of = lax.broadcasted_iota(jnp.int32, (128, D), 0)
    gains = jnp.where(row_of == EXPERTS, gain_one, 0.0)
    gains = jnp.where(row_of == EXPERTS + 1, gain_two_ref[...], gains)
    shared = router_grad_ref[...] + gains.T
    for block in range(4):
        shared_rows = shared[QOWN * block : QOWN * (block + 1), :].astype(bf16)
        full[2, :, :, :, 1024 + 128 * block : 1152 + 128 * block] = spread(2, shared_rows)
    swaps.append(swap(2))
    second_0.relay()
    block_ref[...] = middle_ref[...] + outs.total()
    chip_sum(2, swaps[2])
    first_2 = first_sum(2, "y")
    first_1.relay()
    first_2.relay()
    exit_out[...] = second_0.total()
    second_1 = second_sum(1, "y", first_1)
    second_2 = second_sum(2, "x", first_2)
    second_1.relay()
    second_2.relay()
    final[0] = second_1.total()
    final[1] = second_2.total()
    give[0, :, :MIX_OWN] = final[0, :, :640]
    give[1, :, :MIX_OWN] = final[0, :, 640:1280]
    give[2, :, :256] = final[0, :, 1280:]
    give[2, :, 256:MIX_OWN] = final[1, :, :384]
    give[3, :, :MIX_OWN] = final[1, :, 384:1024]
    for block in range(4):
        give[block, :, MIX_OWN:] = final[1, :, 1024 + 128 * block : 1152 + 128 * block]
    home = [
        send(give.at[peer], got_z.at[k], 51 + k, "seq", peer)
        for k, peer in enumerate((right, far, left))
    ]
    entry_out[z] = give[z]
    for k, source in enumerate((left, far, right)):
        home[k].wait_recv()
        entry_out[source] = got_z[k]
    for copy in swaps + home:
        copy.wait_send()
    for reduce in (rows, outs, first_0, first_1, first_2, second_0, second_1, second_2):
        reduce.drain()


def closing(*operands):
    row_bufs = reduce_scratch((TOK_DEV, D), (HALF, D))
    chip_bufs = reduce_scratch((48, D), (48, D // 2))
    line_bufs = reduce_scratch((PAD_ROWS, D), (PAD_ROWS, D // 2))
    tile = (PAD_ROWS, D)
    return pl.pallas_call(
        closing_kernel,
        out_shape=[
            jax.ShapeDtypeStruct((TOK_DEV, D), f32),
            jax.ShapeDtypeStruct((TOK_DEV, D), f32),
            jax.ShapeDtypeStruct((4, PAD_ROWS, WIDE), f32),
            jax.ShapeDtypeStruct((PAD_ROWS, D), f32),
        ],
        in_specs=[VMEM] * 2
        + [pl.BlockSpec(memory_space=pltpu.SMEM)]
        + [VMEM] * (len(operands) - 3),
        out_specs=[VMEM] * 4,
        scratch_shapes=[
            pltpu.VMEM((GROUP, MIX_OWN), f32),
            pltpu.VMEM((GROUP, MIX_OWN), bf16),
            pltpu.VMEM((N_SEQ, TOK_DEV, D), bf16),
            pltpu.VMEM((3, 2, 4, 48, D), bf16),
            pltpu.VMEM((3, 4, 48, D), bf16),
            pltpu.VMEM((3, 4, 48, D), bf16),
            pltpu.VMEM((3, 4) + tile, bf16),
            pltpu.VMEM((2,) + tile, f32),
            pltpu.VMEM((4, PAD_ROWS, WIDE), f32),
            pltpu.VMEM((3, PAD_ROWS, WIDE), f32),
        ]
        + chip_bufs * 3
        + line_bufs * 3
        + row_bufs * 2
        + sems(54),
        compiler_params=remote_params(5),
    )(*operands)


def owner_kernel(sum_ref, extra_ref, expand_ref, shrink_ref, send_sem, recv_sem):
    core = lax.axis_index("core")
    greet([sibling()])
    send = sender(send_sem, recv_sem)
    most, single = pl.ds(core * LOCAL_E + 1, MAIN_E), core * LOCAL_E

    def parts(owner):
        return (
            pl.ds(pl.multiple_of(owner * 48, 16), 48),
            pl.ds(pl.multiple_of(96 + owner * 16, 16), 16),
            pl.ds(pl.multiple_of(owner * 512, 512), 512),
        )

    rows, left, ends = parts(1 - core)
    low, start, end = pl.ds(128, 16), pl.ds(0, 1024), pl.ds(1024, 512)
    pieces = [
        (sum_ref.at[:, rows], expand_ref.at[most]),
        (sum_ref.at[:, left], shrink_ref.at[most, :, start]),
        (sum_ref.at[:, low, ends], shrink_ref.at[most, :, end]),
        (extra_ref.at[rows], expand_ref.at[single]),
        (extra_ref.at[left], shrink_ref.at[single, :, start]),
        (extra_ref.at[low, ends], shrink_ref.at[single, :, end]),
    ]
    copies = [
        send(source, target, k, "core", 1 - core) for k, (source, target) in enumerate(pieces)
    ]
    rows, left, ends = parts(core)
    for e in range(LOCAL_E):
        source = extra_ref if e == 0 else sum_ref.at[e - 1]
        expert = core * LOCAL_E + e
        expand_ref[expert] = source[rows, :]
        shrink_ref[expert, :, :1024] = source[left, :]
        shrink_ref[expert, :, 1024:] = source[low, ends]
    for copy in copies:
        copy.wait()


def to_owners(summed, extra):
    return pl.pallas_call(
        owner_kernel,
        out_shape=[
            jax.ShapeDtypeStruct((2 * LOCAL_E, 48, 1024), bf16),
            jax.ShapeDtypeStruct((2 * LOCAL_E, 16, D), bf16),
        ],
        in_specs=[VMEM] * 2,
        out_specs=[VMEM] * 2,
        scratch_shapes=sems(6),
        compiler_params=remote_params(6, 8 * 1024 * 1024),
    )(summed, extra)


def weights_of(w_ref):
    expand = w_ref[:, 0, :96, :].reshape(D, 2 * FF)
    left = w_ref[:, 0, 96:128, :].reshape(FF, 1024)
    right = jnp.concatenate([w_ref[:, 0, 128:144, :512], w_ref[:, 0, 128:144, 512:]], axis=1)
    return expand, left, right.reshape(FF, 512)

def grads_kernel(
    rows_ref, cot_ref, gate_ref, w_ref, hidden_ref, up_ref, out_ref, line_ref, own, *rest
):
    bufs, (send_sem, recv_sem) = [rest[6 * i : 6 * i + 6] for i in range(2)], rest[12:]
    e = pl.program_id(0)
    plan = planner(send_sem, recv_sem)
    low, high = pl.ds(0, 512), pl.ds(512, 512)
    low_x = Reduce(plan, 0, "x", lambda i: own.at[i, :, :, low], bufs[0], half_rows)
    high_y = Reduce(plan, 6, "y", lambda i: own.at[:, i, :, high], bufs[1], half_rows)

    @pl.when(e == 0)
    def _():
        greet(near("x") + near("y"))

    expand, left, right = weights_of(w_ref)
    grad_rows = (gate_ref[0] * cot_ref[0].astype(f32)).astype(bf16)
    rows = rows_ref[0]
    gate_pre = dot(rows, expand[:, :FF], ((1,), (0,)))
    up_part = dot(rows, expand[:, FF:], ((1,), (0,)))
    sig = jax.nn.sigmoid(gate_pre)
    hidden = (gate_pre * sig * up_part).astype(bf16)
    hidden_ref[0] = hidden

    @pl.when(e == 2)
    def _():
        low_x.relay()
        high_y.relay()

    hidden_grad = dot(grad_rows[:, :1024], left, ((1,), (1,))) + dot(
        grad_rows[:, 1024:], right, ((1,), (1,))
    )
    up_ref[0, :, :FF] = (hidden_grad * up_part * sig * (1.0 + gate_pre * (1.0 - sig))).astype(bf16)
    up_ref[0, :, FF:] = (hidden_grad * gate_pre * sig).astype(bf16)

    def write(shrink_at, end_at, expand_at):
        grad_left = dot(hidden, grad_rows[:, :1024], ((0,), (0,))).astype(bf16)
        grad_right = dot(hidden, grad_rows[:, 1024:], ((0,), (0,))).astype(bf16)
        grad_right = grad_right.reshape(4, 4, 32, 512)
        shrink_at(grad_left.reshape(4, 4, 32, 1024))
        end_at(grad_right[:, :, :16], grad_right[:, :, 16:])
        up_grad = up_ref[0]
        for j in range(4):
            part = dot(rows[:, 384 * j : 384 * (j + 1)], up_grad, ((0,), (0,))).astype(bf16)
            expand_at(j, part.reshape(4, 96, 1024))

    @pl.when(e == 0)
    def _():
        def shrink_at(value):
            own[:, :, 96:128, :] = value

        def end_at(first, second):
            own[:, :, 128:144, :512] = first
            own[:, :, 128:144, 512:] = second

        def expand_at(j, value):
            own[j, :, :96, :] = value

        write(shrink_at, end_at, expand_at)
        low_x.start()
        high_y.start()

    @pl.when(e > 0)
    def _():
        def shrink_at(value):
            out_ref[:, :, 0, 96:128, :] = value

        def end_at(first, second):
            out_ref[:, :, 0, 128:144, :512] = first
            out_ref[:, :, 0, 128:144, 512:] = second

        def expand_at(j, value):
            out_ref[j, :, 0, :96, :] = value

        write(shrink_at, end_at, expand_at)

    @pl.when(e == LOCAL_E - 1)
    def _():
        line_ref[0] = low_x.total().astype(bf16)
        line_ref[1] = high_y.total().astype(bf16)
        low_x.drain()
        high_y.drain()


def expert_grads(rows, cot_rows, row_gates, weights):
    one = lambda e: (e, 0, 0)
    wide = lambda e: (0, e, 0, 0)
    out = lambda e: (0, 0, jnp.maximum(e - 1, 0), 0, 0)
    return pl.pallas_call(
        grads_kernel,
        grid=(LOCAL_E,),
        in_specs=[
            pl.BlockSpec((1, SLOTS, D), one),
            pl.BlockSpec((1, SLOTS, D), one),
            pl.BlockSpec((1, SLOTS, 1), one),
            pl.BlockSpec((16, 1, 144, 1024), wide),
        ],
        out_specs=[
            pl.BlockSpec((1, SLOTS, FF), one),
            pl.BlockSpec((1, SLOTS, 2 * FF), one),
            pl.BlockSpec((4, 4, 1, 144, 1024), out),
            pl.BlockSpec((2, 4, 144, 512), lambda e: (0, 0, 0, 0)),
        ],
        out_shape=[
            jax.ShapeDtypeStruct((LOCAL_E, SLOTS, FF), bf16),
            jax.ShapeDtypeStruct((LOCAL_E, SLOTS, 2 * FF), bf16),
            jax.ShapeDtypeStruct((4, 4, MAIN_E, 144, 1024), bf16),
            jax.ShapeDtypeStruct((2, 4, 144, 512), bf16),
        ],
        scratch_shapes=[pltpu.VMEM((4, 4, 144, 1024), bf16)]
        + reduce_scratch((4, 144, 512), (2, 144, 512)) * 2
        + sems(12),
        compiler_params=remote_params(7),
        cost_estimate=pl.CostEstimate(
            flops=12 * LOCAL_E * SLOTS * D * FF, bytes_accessed=60 << 20, transcendentals=0
        ),
    )(rows, cot_rows, row_gates, weights)


def token_trig():
    frequency = rope_base ** (-np.arange(HD // 2, dtype=np.float64) * 2.0 / HD)
    phase = np.arange(GROUP, dtype=np.float64)[:, None] * np.tile(frequency, 4)[None, :]
    return np.stack([np.cos(phase), np.sin(phase)]).astype(np.float32)


def adamw_step(weight, gradient, mean_old, square_old, rate, decay):
    drift = beta_first * mean_old + (1.0 - beta_first) * gradient
    spread = beta_second * square_old + (1.0 - beta_second) * gradient * gradient
    mean_hat = drift / (1.0 - beta_first**STEP)
    square_hat = spread / (1.0 - beta_second**STEP)
    master = weight - rate * (mean_hat / (jnp.sqrt(square_hat) + adam_eps) + decay * weight)
    return (drift, spread, master)


def on_device(
    activations,
    cotangent,
    seq_lengths,
    deal_order,
    routes,
    entry_weight,
    entry_mean,
    entry_square,
    exit_weight,
    exit_mean,
    exit_square,
    router_weight,
    router_mean,
    router_square,
    expand_weight,
    expand_mean,
    expand_square,
    shrink_weight,
    shrink_mean,
    shrink_square,
    norm_gains,
    gains_mean,
    gains_square,
):
    angles = (seq_lengths, token_trig())
    (
        weights, entry_own, exit_own, normed, rows, cot_rows, shared, gains, qkv, attended, lse,
        middle, normed_two, row_gates, rank, my_gates,
    ) = forward(
        activations[0],
        cotangent[0],
        activations[0],
        routes[0].T,
        deal_order,
        *angles,
        entry_weight,
        exit_weight,
        router_weight,
        norm_gains,
        expand_weight,
        shrink_weight,
    )
    weights = weights.reshape(16, LOCAL_E, 144, 1024)
    hidden, up_grad, expert_grad, line = expert_grads(rows, cot_rows, row_gates, weights)
    expert_grad = expert_grad.reshape(16, MAIN_E, 144, 1024)
    expert_sum = lax.psum_scatter(expert_grad, PLANE, scatter_dimension=0, tiled=False)
    middle_grad, branch_grad, logit_grad, gain_two_grad, out_sum, extra_sum = turn(
        rank,
        up_grad,
        hidden,
        row_gates,
        cot_rows,
        weights,
        line,
        middle,
        cotangent[0],
        my_gates,
        shared,
        gains[1:2],
    )
    branch_grad = branch_grad.reshape(GROUP, D)
    router_grad = dot(normed_two, logit_grad, ((0,), (0,)))

    input_rows, block_rows, entry_got, exit_got = closing(
        qkv,
        lse,
        *angles,
        exit_own,
        entry_own,
        activations[0],
        middle_grad,
        gains[0:1],
        normed,
        attended,
        branch_grad,
        router_grad,
        gain_two_grad,
        out_sum,
        middle,
    )

    input_grad, block_output = input_rows.astype(bf16), block_rows.astype(bf16)

    entry_got = entry_got[:, :ROWS]
    entry_sum = jnp.concatenate(
        [
            entry_got[:, :, :Q_OWN].transpose(1, 0, 2).reshape(ROWS, QH * HD),
            entry_got[:, :, Q_OWN:MIX_OWN].transpose(1, 0, 2).reshape(ROWS, 2 * KVH * HD),
        ],
        axis=1,
    )
    shared_sum = jnp.sum(entry_got[:, :, MIX_OWN:], axis=0)
    router_sum = shared_sum[:, :EXPERTS]
    gains_sum = shared_sum[:, EXPERTS : EXPERTS + 2].T
    exit_sum = exit_got[:ROWS]

    expand_sum, shrink_sum = to_owners(expert_sum, extra_sum)
    expand_sum, shrink_sum = expand_sum.astype(f32), shrink_sum.astype(f32)
    entry_new = adamw_step(entry_weight, entry_sum, entry_mean, entry_square, 0.02, weight_decay)
    exit_new = adamw_step(exit_weight, exit_sum, exit_mean, exit_square, 0.15, weight_decay)
    router_new = adamw_step(
        router_weight, router_sum, router_mean, router_square, 0.01, weight_decay
    )
    expand_new = adamw_step(
        expand_weight, expand_sum, expand_mean, expand_square, 0.02, weight_decay
    )
    shrink_new = adamw_step(
        shrink_weight, shrink_sum, shrink_mean, shrink_square, 0.12, weight_decay
    )
    gains_new = adamw_step(norm_gains, gains_sum, gains_mean, gains_square, 0.5, 0.0)
    return (
        block_output[None],
        input_grad[None],
        *entry_new,
        *exit_new,
        *router_new,
        *expand_new,
        *shrink_new,
        *gains_new,
    )


def solution(mesh):
    fine = Mesh(mesh.devices.reshape(4, 4, 4, 2), ("seq", "x", "y", "core"))
    rows = P(FSDP, "seq", None)
    lists = P(FSDP, None)
    owned = P(("seq",) + FSDP, None)
    experts = P("seq", FSDP, None)
    gains = P(None, ("seq",) + FSDP)
    return jax.shard_map(
        on_device,
        mesh=fine,
        in_specs=(rows, rows, lists, lists, rows)
        + (owned,) * 9
        + (experts,) * 6
        + (gains,) * 3,
        out_specs=(rows, rows) + (owned,) * 9 + (experts,) * 6 + (gains,) * 3,
        check_vma=False,
    )
```

```python
import jax
import jax.numpy as jnp
import numpy as np
from jax import lax
from jax.experimental import pallas as pl
from jax.experimental.pallas import tpu as pltpu
from jax.sharding import Mesh, PartitionSpec as P

D = 1536
QH = 24
KVH = 8
HD = 64
FF = 512
EXPERTS = 40
TOP = 8
STEP = 10
CAP = 29

N_SEQ = 4
TOK_DEV = 128
GROUP = 512
PAIR_TOK = 2 * GROUP
LOCAL_E = EXPERTS // (2 * N_SEQ)
SLOTS = 256
Q_OWN = QH * HD // N_SEQ
KV_OWN = 2 * KVH * HD // N_SEQ
MIX_OWN = Q_OWN + KV_OWN
HEADS_OWN = QH // N_SEQ
KV_HEADS_OWN = KVH // N_SEQ
PER_KV = QH // KVH
ROWS = 12

norm_eps = 1e-06
rope_base = 10000.0
beta_first = 0.9
beta_second = 0.95
adam_eps = 1e-08
weight_decay = 0.1

FSDP = ("x", "y", "core")
PLANE = ("x", "y")
f32 = jnp.float32
bf16 = jnp.bfloat16


BIG = 60 * 1024 * 1024
HALF = TOK_DEV // 2
QOWN = Q_OWN
MESH = pl.DeviceIdType.MESH
ANY = pl.BlockSpec(memory_space=pl.ANY)
VMEM = pl.BlockSpec(memory_space=pltpu.VMEM)


def dot(a, b, dims):
    return lax.dot_general(a, b, (dims, ((), ())), preferred_element_type=f32)


def greet(peers):
    barrier = pltpu.get_barrier_semaphore()
    for axis, peer in peers:
        pl.semaphore_signal(barrier, inc=1, device_id={axis: peer}, device_id_type=MESH)
    pl.semaphore_wait(barrier, len(peers))


def planner(send_sem, recv_sem):
    def plan(src, dst, index, axis, peer):
        return pltpu.make_async_remote_copy(
            src_ref=src,
            dst_ref=dst,
            send_sem=send_sem.at[index],
            recv_sem=recv_sem.at[index],
            device_id={axis: peer},
            device_id_type=MESH,
        )

    return plan


def sender(send_sem, recv_sem):
    plan = planner(send_sem, recv_sem)

    def send(*args):
        copy = plan(*args)
        copy.start()
        return copy

    return send


def sems(count):
    return [pltpu.SemaphoreType.DMA((count,)), pltpu.SemaphoreType.DMA((count,))]


def ring(me):
    right, left = lax.rem(me + 1, 4), lax.rem(me + 3, 4)
    return right, left, lax.rem(me + 2, 4)


def near(axis):
    right, left, _ = ring(lax.axis_index(axis))
    return [(axis, right), (axis, left)]


def sibling():
    return ("core", 1 - lax.axis_index("core"))


def half_rows(ref, half):
    size = ref.shape[0] // 2
    return ref.at[pl.ds(half * size, size)]


def half_lanes(ref, half):
    size = ref.shape[-1] // 2
    return ref.at[(slice(None),) * (len(ref.shape) - 1) + (pl.ds(half * size, size),)]


class Gather:
    def __init__(self, plan, base, axis, mine, slot, cut):
        me = lax.axis_index(axis)
        right, left, self.far = ring(me)
        self.right, self.left = right, left
        here, from_left, from_right = slot(me), cut(slot(left), 0), cut(slot(right), 1)
        self.first = [
            plan(cut(mine, 0), cut(here, 0), base, axis, right),
            plan(cut(mine, 1), cut(here, 1), base + 1, axis, left),
            plan(cut(mine, 1), cut(here, 1), base + 2, axis, right),
            plan(cut(mine, 0), cut(here, 0), base + 3, axis, left),
        ]
        self.later = [
            plan(from_left, from_left, base + 4, axis, right),
            plan(from_right, from_right, base + 5, axis, left),
        ]

    def start(self):
        for copy in self.first:
            copy.start()
        return self

    def relay(self):
        for got, on in zip(self.first, self.later):
            got.wait_recv()
            on.start()

    def wait_left(self):
        self.first[2].wait_recv()

    def wait_right(self):
        self.first[3].wait_recv()

    def wait_far(self):
        for copy in self.later:
            copy.wait_recv()

    def finish(self):
        self.wait_left()
        self.wait_right()
        self.wait_far()

    def drain(self):
        for copy in self.first + self.later:
            copy.wait_send()


def hand_over(send, base, mine, out, gather):
    me, core = lax.axis_index("seq"), lax.axis_index("core")
    other = 1 - core
    copies = [send(mine, out.at[core, me], base, "core", other)]
    gather.relay()
    gather.wait_left()
    block = out.at[core, gather.left]
    copies.append(send(block, block, base + 1, "core", other))
    gather.wait_right()
    block = out.at[core, gather.right]
    copies.append(send(block, block, base + 2, "core", other))
    gather.wait_far()
    block = out.at[core, gather.far]
    copies.append(send(block, block, base + 3, "core", other))
    return copies


def reduce_scratch(block, half):
    return [pltpu.VMEM(half, bf16)] * 4 + [pltpu.VMEM(block, bf16)] * 2


def added(target, first, second):
    target[...] = (first[...].astype(f32) + second[...].astype(f32)).astype(bf16)


class Reduce:
    def __init__(self, plan, base, axis, block, bufs, cut):
        me = lax.axis_index(axis)
        right, left, far = ring(me)
        from_left, from_right, to_right, to_left, got_left, got_right = bufs
        far, on_right, on_left = block(far), block(right), block(left)
        self.mine, self.got = block(me), (got_left, got_right)
        self.hops = (
            (to_right, cut(on_right, 0), from_left),
            (to_left, cut(on_left, 1), from_right),
        )
        self.far = [
            plan(cut(far, 0), from_left, base, axis, right),
            plan(cut(far, 1), from_right, base + 1, axis, left),
        ]
        self.near = [
            plan(cut(on_right, 1), cut(got_left, 1), base + 2, axis, right),
            plan(cut(on_left, 0), cut(got_right, 0), base + 3, axis, left),
        ]
        self.later = [
            plan(to_right, cut(got_left, 0), base + 4, axis, right),
            plan(to_left, cut(got_right, 1), base + 5, axis, left),
        ]

    def start_far(self):
        for copy in self.far:
            copy.start()

    def start_near(self):
        for copy in self.near:
            copy.start()

    def start(self):
        self.start_far()
        self.start_near()
        return self

    def relay(self):
        for got, hop, on in zip(self.far, self.hops, self.later):
            got.wait_recv()
            added(*hop)
            on.start()

    def total(self):
        for copy in self.near + self.later:
            copy.wait_recv()
        total = self.mine[...].astype(f32)
        for part in self.got:
            total += part[...].astype(f32)
        return total

    def drain(self):
        for copy in self.far + self.near + self.later:
            copy.wait_send()


def remote_params(call_id, vmem=BIG):
    return pltpu.CompilerParams(
        collective_id=call_id, has_side_effects=True, vmem_limit_bytes=vmem
    )


def unit_scale(vector):
    return lax.rsqrt(jnp.mean(vector * vector, axis=-1, keepdims=True) + norm_eps)


def norm_back(vector, gain, grad):
    scale = unit_scale(vector)
    unit = vector * scale
    pulled = grad * gain
    back = scale * (pulled - unit * jnp.mean(pulled * unit, axis=-1, keepdims=True))
    return back, jnp.sum(unit * grad, axis=0, keepdims=True)


MAIN_E = LOCAL_E - 1


def row_pick(shape, padded_axis):
    padded = lax.broadcasted_iota(jnp.int32, shape, padded_axis)
    plain = lax.broadcasted_iota(jnp.int32, shape, 1 - padded_axis)
    row = lax.rem(padded, 16)
    return ((plain == lax.div(padded, 16) * 12 + row) & (row < 12)).astype(bf16)


def swap_halves(rows, lower, upper):
    lane = lax.broadcasted_iota(jnp.int32, rows.shape, 1)
    ahead = pltpu.roll(rows, rows.shape[1] - HD // 2, 1)
    behind = pltpu.roll(rows, HD // 2, 1)
    return jnp.where(lax.rem(lane, HD) < HD // 2, lower * ahead, upper * behind)


BLOCK = 256


def sequence_of(lengths_ref, token):
    first_end = lengths_ref[0, 0]
    second_end = first_end + lengths_ref[0, 1]
    return (token >= first_end).astype(jnp.int32) + (token >= second_end).astype(jnp.int32)


def block_bias(lengths_ref, block):
    keys = BLOCK * (block + 1)
    row = lax.broadcasted_iota(jnp.int32, (BLOCK, keys), 0) + BLOCK * block
    column = lax.broadcasted_iota(jnp.int32, (BLOCK, keys), 1)
    same = sequence_of(lengths_ref, row) == sequence_of(lengths_ref, column)
    return jnp.where(same & (column <= row), 0.0, -1e30)


def rope_tables(lengths_ref, trig_ref):
    seq = sequence_of(lengths_ref, lax.broadcasted_iota(jnp.int32, (GROUP, 128), 0))
    second = lengths_ref[0, 0]
    third = second + lengths_ref[0, 1]

    def of_start(table):
        later = jnp.where(
            seq == 1, trig_ref[table, pl.ds(second, 1)], trig_ref[table, pl.ds(third, 1)]
        )
        return jnp.where(seq == 0, trig_ref[table, 0:1], later)

    start_cos, start_sin = of_start(0), of_start(1)
    cosine = trig_ref[0] * start_cos + trig_ref[1] * start_sin
    sine = trig_ref[1] * start_cos - trig_ref[0] * start_sin
    is_key = lax.broadcasted_iota(jnp.int32, (GROUP, 128), 1) < HD
    pair_cos, pair_sin = jnp.where(is_key, cosine, 1.0), jnp.where(is_key, sine, 0.0)
    return (
        jnp.concatenate([cosine] * 3 + [pair_cos] * 2, axis=1),
        jnp.concatenate([sine] * 3 + [pair_sin] * 2, axis=1),
    )


def head_of(index):
    return slice(HD * index, HD * (index + 1))


def lane_pick(first, rows):
    row = lax.broadcasted_iota(jnp.int32, (rows, 128), 0)
    lane = lax.broadcasted_iota(jnp.int32, (rows, 128), 1)
    return (lane == row + first).astype(bf16)


def forward_kernel(
    in_hbm, cot_hbm, in_ref, route_ref, order_ref, lengths_ref, trig_ref,
    entry_ref, exit_ref, router_ref, gain_ref, expand_ref, shrink_ref,
    weights_out, entry_hbm, exit_hbm, normed_hbm, rows_hbm, cot_rows_hbm, own_hbm,
    hidden_out, up_out, shared_out, gains_out, qkv_ref, attended_ref,
    lse_ref, middle_ref, mine, row_gate_out, rank_out, my_gate_out,
    entry_out, exit_out, normed_ref, rows_out, cot_rows_out, first_weights, own_grads,
    stage, stage_end, packed, shared, columns, hold, full,
    in_all, cot_all, hit_all, hit_pair, tokens, part, gates, *rest
):
    bufs, (send_sem, recv_sem, copy_sem) = rest[:6], rest[6:]
    z, x, y, c = (lax.axis_index(a) for a in ("seq", "x", "y", "core"))
    right, left, far = ring(z)
    other = 1 - c
    greet(near("seq") + [("seq", far)] + near("x") + near("y") + [sibling()])
    send, plan = sender(send_sem, recv_sem), planner(send_sem, recv_sem)

    for e in range(LOCAL_E):
        theirs = other * LOCAL_E + e
        stage[e, :48] = expand_ref[theirs].astype(bf16)
        stage[e, 48:] = shrink_ref[theirs, :, :1024].astype(bf16)
        stage_end[e] = shrink_ref[theirs, :, 1024:].astype(bf16)
    of_core = pl.ds(pl.multiple_of(c * 48, 16), 48)
    lefts = pl.ds(pl.multiple_of(96 + c * 16, 16), 16)
    ends = pl.ds(pl.multiple_of(c * 512, 512), 512)
    to_core = [
        send(stage.at[:, pl.ds(0, 48)], packed.at[:, of_core], 51, "core", other),
        send(stage.at[:, pl.ds(48, 16)], packed.at[:, lefts], 52, "core", other),
        send(stage_end, packed.at[:, pl.ds(128, 16), ends], 53, "core", other),
    ]
    for e in range(LOCAL_E):
        own_e = c * LOCAL_E + e
        packed[e, of_core, :] = expand_ref[own_e].astype(bf16)
        packed[e, lefts, :] = shrink_ref[own_e, :, :1024].astype(bf16)
        packed[e, pl.ds(128, 16), ends] = shrink_ref[own_e, :, 1024:].astype(bf16)
    rows = Gather(plan, 9, "seq", in_hbm, lambda i: in_all.at[i], half_rows).start()
    expert = lax.broadcasted_iota(jnp.int32, (128, TOK_DEV), 0)
    hit = route_ref[0:1] == expert
    for k in range(1, TOP):
        hit = hit | (route_ref[k : k + 1] == expert)
    hit_all[z] = hit.astype(bf16)
    hits = Gather(plan, 3, "seq", hit_all.at[z], lambda i: hit_all.at[i], half_rows).start()

    lane = lax.broadcasted_iota(jnp.int32, (ROWS, 128), 1)
    square = lax.broadcasted_iota(jnp.int32, (ROWS, ROWS), 0)
    square = square == lax.broadcasted_iota(jnp.int32, (ROWS, ROWS), 1)
    shared[...] = jnp.zeros_like(shared)
    shared[:, :EXPERTS] = router_ref[...]
    block_of = shared[...]
    for k in range(2):
        column = jnp.sum(jnp.where(square, gain_ref[k : k + 1], 0.0), axis=1, keepdims=True)
        block_of = jnp.where(lane == EXPERTS + k, column, block_of)
    empty = jnp.zeros((PAD_ROWS - ROWS, WIDE), f32)
    for block in range(4):
        cols = jnp.concatenate(
            [
                entry_ref[:, Q_OWN * block : Q_OWN * (block + 1)],
                entry_ref[:, QH * HD + KV_OWN * block : QH * HD + KV_OWN * (block + 1)],
                block_of,
            ],
            axis=1,
        )
        columns[block] = jnp.concatenate([cols, empty], axis=0).astype(bf16)
    to_seq = [
        send(columns.at[peer], hold.at[z], k, "seq", peer)
        for k, peer in enumerate((right, far, left))
    ]
    for block in range(2):
        cols = exit_ref[:, WIDE * block : WIDE * (block + 1)]
        hold[4 + block] = jnp.concatenate([cols, empty], axis=0).astype(bf16)
    hold[z] = columns[z]
    local = [
        pltpu.make_async_copy(in_hbm, in_all.at[z], copy_sem.at[0]),
        pltpu.make_async_copy(cot_hbm, cot_all.at[c, z], copy_sem.at[1]),
    ]
    for copy in local:
        copy.start()

    for copy in to_seq:
        copy.wait_recv()
    for block in range(6):
        full[block, x, y, c] = hold[block]
    low, high = pl.ds(0, 3), pl.ds(3, 3)
    low_x = Gather(plan, 15, "x", hold.at[low], lambda i: full.at[low, i, y, c], half_lanes)
    low_x.start()
    high_y = Gather(plan, 21, "y", hold.at[high], lambda i: full.at[high, x, i, c], half_lanes)
    high_y.start()
    for copy in to_core:
        copy.wait_recv()
    own_weights = pltpu.make_async_copy(packed, weights_out.at[x, y], copy_sem.at[2])
    own_weights.start()
    start, end = pl.ds(0, 512), pl.ds(512, 512)
    rings = []
    for k, group in enumerate((pl.ds(0, 1), pl.ds(1, MAIN_E))):
        base = (54, 95)[k]
        first_phase = (
            Gather(
                plan,
                base,
                "x",
                packed.at[group, :, start],
                lambda i, group=group: weights_out.at[i, y, group, :, start],
                half_lanes,
            ),
            Gather(
                plan,
                base + 6,
                "y",
                packed.at[group, :, end],
                lambda i, group=group: weights_out.at[x, i, group, :, end],
                half_lanes,
            ),
        )
        base = (67, 107)[k]
        second_phase = (
            Gather(
                plan,
                base,
                "y",
                weights_out.at[:, y, group, :, start],
                lambda i, group=group: weights_out.at[:, i, group, :, start],
                half_rows,
            ),
            Gather(
                plan,
                base + 6,
                "x",
                weights_out.at[x, :, group, :, end],
                lambda i, group=group: weights_out.at[i, :, group, :, end],
                half_rows,
            ),
        )
        rings.append((first_phase, second_phase))

    def start_ring(group, phase):
        for gather in rings[group][phase]:
            gather.start()

    def relay_ring(group, phase):
        for gather in rings[group][phase]:
            gather.relay()

    def turn_ring(group):
        for before, after in zip(*rings[group]):
            before.finish()
            after.start()

    start_ring(0, 0)

    def cut_low(ref, half):
        return ref.at[:, pl.ds(2 * half, 2)]

    hits.relay()
    low_x.relay()
    high_y.relay()
    relay_ring(0, 0)
    start_ring(1, 0)
    rows.relay()
    cots = Gather(plan, 27, "seq", cot_hbm, lambda i: cot_all.at[c, i], half_rows).start()
    low_x.finish()
    low_y = Gather(
        plan, 33, "y", full.at[low, :, y, c], lambda i: full.at[low, :, i, c], cut_low
    ).start()
    high_y.finish()
    high_x = Gather(
        plan, 39, "x", full.at[high, x, :, c], lambda i: full.at[high, i, :, c], cut_low
    ).start()
    own_weights.wait()
    turn_ring(0)

    hits.finish()
    token = lax.broadcasted_iota(jnp.int32, (GROUP, GROUP), 0)
    back_hot = (order_ref[...] == token).astype(bf16)
    natural = jnp.zeros((GROUP, 128), f32)
    for block in range(N_SEQ):
        slots = back_hot[:, TOK_DEV * block : TOK_DEV * (block + 1)]
        natural += dot(slots, hit_all[block], ((1,), (1,)))
    hit_pair[c] = natural.astype(bf16)
    hit_swap = send(hit_pair.at[c], hit_pair.at[c], 66, "core", other)
    low_y.relay()
    high_x.relay()
    relay_ring(1, 0)
    hit_swap.wait_recv()
    hit_both = hit_pair[...].reshape(PAIR_TOK, 128)
    first = (z * 2 + c) * LOCAL_E
    lower = lax.broadcasted_iota(jnp.int32, (PAIR_TOK, PAIR_TOK), 0)
    lower = (lower >= lax.broadcasted_iota(jnp.int32, (PAIR_TOK, PAIR_TOK), 1)).astype(bf16)
    rank = dot(lower, hit_both, ((1,), (0,))) - 1.0
    rank = jnp.where(hit_both.astype(f32) > 0.0, rank, -1.0).astype(bf16)
    mine_of = lane_pick(first, 8)
    rank_out[...] = dot(rank, mine_of, ((1,), (1,))).astype(jnp.int32)
    rank_rows = dot(mine_of, rank, ((1,), (1,))).astype(jnp.int32)

    low_y.finish()
    half = full.at[low, :, :, c]
    last = [send(half, half, 49, "core", other)]
    high_x.finish()
    half = full.at[high, :, :, c]
    last.append(send(half, half, 50, "core", other))
    relay_ring(0, 1)
    turn_ring(1)
    cosine, sine = rope_tables(lengths_ref, trig_ref)
    rows.finish()
    local[0].wait()
    for copy in last:
        copy.wait_recv()
    pick = row_pick((QOWN, 512), 1)
    for block in range(4):
        got = dot(pick, full[block].reshape(512, WIDE), ((1,), (0,))).astype(bf16)
        entry_out[QOWN * block : QOWN * (block + 1), :] = got[:, :MIX_OWN]
        shared_out[QOWN * block : QOWN * (block + 1), :] = got[:, MIX_OWN:]
    for block in range(2):
        got = dot(pick, full[4 + block].reshape(512, WIDE), ((1,), (0,))).astype(bf16)
        exit_out[:, WIDE * block : WIDE * (block + 1)] = got
    gains = dot(lane_pick(EXPERTS, 8), shared_out[...], ((1,), (1,)))
    gains_out[...] = gains
    for block in range(N_SEQ):
        at = slice(TOK_DEV * block, TOK_DEV * (block + 1))
        vector = in_all[block].astype(f32)
        normed_ref[at, :] = (vector * unit_scale(vector) * gains[0:1]).astype(bf16)
    results = [(entry_out, entry_hbm), (exit_out, exit_hbm), (normed_ref, normed_hbm)]
    results = [
        pltpu.make_async_copy(source, target, copy_sem.at[3 + k])
        for k, (source, target) in enumerate(results)
    ]
    for copy in results:
        copy.start()
    mixed = dot(normed_ref[...], entry_out[...], ((1,), (0,)))
    mixed = mixed * cosine + swap_halves(mixed, -1.0, 1.0) * sine
    qkv_ref[...] = mixed.astype(bf16)
    for block in range(GROUP // BLOCK):
        bias = block_bias(lengths_ref, block)
        keys = BLOCK * (block + 1)
        at = slice(BLOCK * block, keys)
        for head in range(HEADS_OWN):
            pair = Q_OWN + 2 * HD * (head // PER_KV)
            key = qkv_ref[:keys, pair : pair + HD]
            value = qkv_ref[:keys, pair + HD : pair + 2 * HD]
            scores = dot(qkv_ref[at, head_of(head)], key, ((1,), (1,))) * HD**-0.5 + bias
            peak = jnp.max(scores, axis=1, keepdims=True)
            expo = jnp.exp(scores - peak)
            total = jnp.sum(expo, axis=1, keepdims=True)
            probs = (expo / total).astype(bf16)
            attended_ref[at, head_of(head)] = dot(probs, value, ((1,), (0,))).astype(bf16)
            lse_ref[at, head : head + 1] = peak + jnp.log(total)
    part[...] = dot(attended_ref[...], exit_out[...], ((1,), (0,))).astype(bf16).reshape(part.shape)
    reduce = Reduce(plan, 79, "seq", lambda i: part.at[i], bufs, half_rows).start()
    pairs = hand_over(send, 45, cot_hbm, cot_all, cots)
    reduce.relay()
    middle = in_ref[...].astype(f32) + reduce.total()
    middle_ref[...] = middle
    mine[...] = (middle * unit_scale(middle) * gains[1:2]).astype(bf16)
    gather = Gather(plan, 85, "seq", mine, lambda i: tokens.at[c, i], half_rows).start()
    tokens[c, z] = mine[...]
    pairs += hand_over(send, 91, mine, tokens, gather)
    for copy in pairs:
        copy.wait()
    local[1].wait()

    for transfer in rings[0][1]:
        transfer.finish()
    fetch = pltpu.make_async_copy(weights_out.at[:, :, 0], first_weights, copy_sem.at[16])
    fetch.start()

    logits = dot(tokens[...].reshape(PAIR_TOK, D), shared_out[...], ((1,), (0,)))
    masked = jnp.where(hit_both.astype(f32) > 0.0, logits, -jnp.inf)
    gate_expo = jnp.exp(masked - jnp.max(masked, axis=1, keepdims=True))
    gates[...] = gate_expo / jnp.sum(gate_expo, axis=1, keepdims=True)
    my_gate_out[...] = gates[pl.ds(pl.multiple_of(c * GROUP + z * TOK_DEV, TOK_DEV), TOK_DEV), :]
    rest_of = gates[...]
    gate_rows = jnp.zeros((8, PAIR_TOK), f32)
    for _ in range(3):
        piece = rest_of.astype(bf16)
        gate_rows += dot(mine_of, piece, ((1,), (1,)))
        rest_of -= piece.astype(f32)
    slot = lax.broadcasted_iota(jnp.int32, (SLOTS, PAIR_TOK), 0)
    for e in range(LOCAL_E):
        if e == 3:
            relay_ring(1, 1)
        match = rank_rows[e : e + 1] == slot
        row_gate_out[e] = jnp.sum(
            jnp.where(match, gate_rows[e : e + 1], 0.0), axis=1, keepdims=True
        )
        match = match.astype(bf16)
        for half in range(2):
            lanes = slice(768 * half, 768 * (half + 1))
            table = tokens[:, :, :, lanes].reshape(PAIR_TOK, 768)
            rows_out[e, :, lanes] = dot(match, table, ((1,), (0,))).astype(bf16)
            table = cot_all[:, :, :, lanes].reshape(PAIR_TOK, 768)
            cot_rows_out[e, :, lanes] = dot(match, table, ((1,), (0,))).astype(bf16)
        for k, (source, target) in enumerate(((rows_out, rows_hbm), (cot_rows_out, cot_rows_hbm))):
            copy = pltpu.make_async_copy(
                source.at[e], target.at[e], copy_sem.at[6 + 2 * e + k]
            )
            copy.start()
            results.append(copy)

    fetch.wait()

    def own_shrink(value):
        own_grads[:, :, 96:128, :] = value

    def own_end(first, second):
        own_grads[:, :, 128:144, :512] = first
        own_grads[:, :, 128:144, 512:] = second

    def own_expand(j, value):
        own_grads[j, :, :96, :] = value

    expert_pass(
        rows_out[0],
        cot_rows_out[0],
        row_gate_out[0],
        weights_of(first_weights[...].reshape(16, 1, 144, 1024)),
        hidden_out,
        up_out,
        (own_shrink, own_end, own_expand),
    )
    copy = pltpu.make_async_copy(own_grads, own_hbm, copy_sem.at[17])
    copy.start()
    results.append(copy)
    for transfer in rings[1][1]:
        transfer.finish()
    for copy in to_seq + to_core + last + [hit_swap]:
        copy.wait_send()
    for copy in results:
        copy.wait()
    for transfer in (hits, rows, cots, low_x, high_y, low_y, high_x, reduce, gather):
        transfer.drain()
    for transfer in rings[0][0] + rings[0][1] + rings[1][0] + rings[1][1]:
        transfer.drain()


def forward(*operands):
    scalar = pl.BlockSpec(memory_space=pltpu.SMEM)
    block = (PAD_ROWS, WIDE)
    group = (N_SEQ, TOK_DEV, D)
    return pl.pallas_call(
        forward_kernel,
        out_shape=[
            jax.ShapeDtypeStruct((4, 4, LOCAL_E, 144, 1024), bf16),
            jax.ShapeDtypeStruct((D, MIX_OWN), bf16),
            jax.ShapeDtypeStruct((QOWN, D), bf16),
            jax.ShapeDtypeStruct((GROUP, D), bf16),
            jax.ShapeDtypeStruct((LOCAL_E, SLOTS, D), bf16),
            jax.ShapeDtypeStruct((LOCAL_E, SLOTS, D), bf16),
            jax.ShapeDtypeStruct((4, 4, 144, 1024), bf16),
            jax.ShapeDtypeStruct((SLOTS, FF), bf16),
            jax.ShapeDtypeStruct((SLOTS, 2 * FF), bf16),
            jax.ShapeDtypeStruct((D, 128), bf16),
            jax.ShapeDtypeStruct((8, D), f32),
            jax.ShapeDtypeStruct((GROUP, MIX_OWN), bf16),
            jax.ShapeDtypeStruct((GROUP, Q_OWN), bf16),
            jax.ShapeDtypeStruct((GROUP, HEADS_OWN), f32),
            jax.ShapeDtypeStruct((TOK_DEV, D), f32),
            jax.ShapeDtypeStruct((TOK_DEV, D), bf16),
            jax.ShapeDtypeStruct((LOCAL_E, SLOTS, 1), f32),
            jax.ShapeDtypeStruct((PAIR_TOK, 8), jnp.int32),
            jax.ShapeDtypeStruct((TOK_DEV, 128), f32),
        ],
        in_specs=[ANY] * 2 + [VMEM] * 3 + [scalar] + [VMEM] * 7,
        out_specs=[ANY] * 7 + [VMEM] * 12,
        scratch_shapes=[
            pltpu.VMEM((D, MIX_OWN), bf16),
            pltpu.VMEM((QOWN, D), bf16),
            pltpu.VMEM((GROUP, D), bf16),
            pltpu.VMEM((LOCAL_E, SLOTS, D), bf16),
            pltpu.VMEM((LOCAL_E, SLOTS, D), bf16),
            pltpu.VMEM((4, 4, 144, 1024), bf16),
            pltpu.VMEM((4, 4, 144, 1024), bf16),
            pltpu.VMEM((LOCAL_E, 64, 1024), bf16),
            pltpu.VMEM((LOCAL_E, 16, 512), bf16),
            pltpu.VMEM((LOCAL_E, 144, 1024), bf16),
            pltpu.VMEM((ROWS, 128), f32),
            pltpu.VMEM((4,) + block, bf16),
            pltpu.VMEM((6,) + block, bf16),
            pltpu.VMEM((6, 4, 4, 2) + block, bf16),
            pltpu.VMEM(group, bf16),
            pltpu.VMEM((2,) + group, bf16),
            pltpu.VMEM((N_SEQ, TOK_DEV, 128), bf16),
            pltpu.VMEM((2, GROUP, 128), bf16),
            pltpu.VMEM((2,) + group, bf16),
            pltpu.VMEM(group, bf16),
            pltpu.VMEM((PAIR_TOK, 128), f32),
        ]
        + reduce_scratch((TOK_DEV, D), (HALF, D))
        + sems(119)
        + [pltpu.SemaphoreType.DMA((18,))],
        compiler_params=remote_params(2),
    )(*operands)


def turn_kernel(
    rank_ref, up_ref, hidden_ref, gate_ref, cot_rows_ref, w_ref,
    line, first_up_ref, first_hidden_ref, middle_ref, cot_ref, my_gate_ref, router_ref, gain_ref,
    grad_ref, branch_ref, logit_ref, gain_grad_ref, out_sum_ref, extra_sum_ref,
    back_s, out_s, other_back, from_core, part, other_out, out_core, mine, *rest
):
    bufs, (send_sem, recv_sem, copy_sem) = [rest[6 * i : 6 * i + 6] for i in range(3)], rest[18:]
    e = pl.program_id(0)
    me, core = lax.axis_index("seq"), lax.axis_index("core")
    send, plan = sender(send_sem, recv_sem), planner(send_sem, recv_sem)
    low_y = Reduce(plan, 17, "y", lambda i: line.at[0, i], bufs[1], half_lanes)
    high_x = Reduce(plan, 23, "x", lambda i: line.at[1, i], bufs[2], half_lanes)

    @pl.when(e == 0)
    def _():
        greet(near("seq") + near("x") + near("y") + [sibling()])
        low_y.start()
        high_x.start()

    @pl.when(e == 2)
    def _():
        low_y.relay()
        high_x.relay()

    @pl.when(e < LOCAL_E)
    def _():
        expand, left, right = weights_of(w_ref)
        at = pl.ds(pl.multiple_of(e * SLOTS, SLOTS), SLOTS)
        up_grad = jnp.where(e == 0, first_up_ref[...], up_ref[0])
        back_s[at, :D] = dot(up_grad, expand, ((1,), (1,))).astype(bf16)
        hidden = jnp.where(e == 0, first_hidden_ref[...], hidden_ref[0])
        expert_out = jnp.concatenate(
            [dot(hidden, left, ((1,), (0,))), dot(hidden, right, ((1,), (0,)))], axis=1
        )
        expert_out = expert_out.astype(bf16).astype(f32)
        gate_grad = jnp.sum(expert_out * cot_rows_ref[0].astype(f32), axis=1, keepdims=True)
        lane = lax.broadcasted_iota(jnp.int32, (SLOTS, 128), 1)
        column = (me * 2 + core) * LOCAL_E + e
        back_s[at, D:] = jnp.where(lane == column, gate_grad, 0.0).astype(bf16)
        out_s[at, :] = (gate_ref[0] * expert_out).astype(bf16)

    @pl.when(e == LOCAL_E)
    def _():
        other = 1 - core
        right, left, far = ring(me)
        slot = lax.broadcasted_iota(jnp.int32, (GROUP, SLOTS), 1)

        def picks(group):
            at = pl.ds(pl.multiple_of(group * GROUP, GROUP), GROUP)
            ranks = rank_ref[at, :]
            return jnp.concatenate(
                [(ranks[:, k : k + 1] == slot).astype(bf16) for k in range(LOCAL_E)], axis=1
            )

        theirs, ours = picks(other), picks(core)
        order = (far, right, left, me)
        other_back[...] = (
            dot(theirs, back_s[...], ((1,), (0,))).astype(bf16).reshape(other_back.shape)
        )
        swaps = [
            send(other_back.at[block], from_core.at[block], 12 + i, "core", other)
            for i, block in enumerate(order)
        ]
        part[...] = dot(ours, back_s[...], ((1,), (0,))).astype(bf16).reshape(part.shape)
        reduce = Reduce(plan, 0, "seq", lambda i: part.at[i], bufs[0], half_rows)
        for i, block in enumerate(order):
            swaps[i].wait_recv()
            added(part.at[block], part.at[block], from_core.at[block])
            if i == 0:
                reduce.start_far()
            if i == 2:
                reduce.start_near()
        other_out[...] = (
            dot(theirs, out_s[...], ((1,), (0,))).astype(bf16).reshape(other_out.shape)
        )
        out_swap = send(other_out, out_core, 16, "core", other)
        reduce.relay()
        out_sum_ref[...] = (
            dot(ours, out_s[...], ((1,), (0,))).astype(bf16).reshape(out_sum_ref.shape)
        )
        total = reduce.total()
        gates, gate_grad = my_gate_ref[...], total[:, D:]
        mean_term = jnp.sum(gates * gate_grad, axis=1, keepdims=True)
        logit_grad = (gates * (gate_grad - mean_term)).astype(bf16)
        logit_ref[...] = logit_grad
        normed_grad = total[:, :D] + dot(logit_grad, router_ref[...], ((1,), (1,)))
        back, gain_grad = norm_back(middle_ref[...], gain_ref[...], normed_grad)
        gain_grad_ref[...] = gain_grad
        middle_grad = cot_ref[...].astype(f32) + back
        grad_ref[...] = middle_grad
        mine[...] = middle_grad.astype(bf16)
        gather = Gather(plan, 6, "seq", mine, lambda i: branch_ref.at[i], half_rows).start()
        local = pltpu.make_async_copy(mine, branch_ref.at[me], copy_sem)
        local.start()
        out_swap.wait_recv()
        added(out_sum_ref, out_sum_ref, out_core)
        gather.relay()
        extra_sum_ref[:, :512] = low_y.total().astype(bf16)
        extra_sum_ref[:, 512:] = high_x.total().astype(bf16)
        gather.finish()
        for transfer in (gather, reduce, low_y, high_x):
            transfer.drain()
        for copy in swaps + [out_swap]:
            copy.wait_send()
        local.wait()


BACK_WIDTH = D + 128


def turn(*operands):
    one = lambda e: (jnp.minimum(e, LOCAL_E - 1), 0, 0)
    other = lambda e: (jnp.clip(e - 1, 0, MAIN_E - 1), 0, 0)
    wide = lambda e: (0, jnp.minimum(e, LOCAL_E - 1), 0, 0)
    cubes = lambda e: (0, 0, 0, 0)
    whole = lambda e: (0, 0)
    blocks = lambda e: (0, 0, 0)
    row_block = pl.BlockSpec((TOK_DEV, D), whole)
    lane_block = pl.BlockSpec((TOK_DEV, 128), whole)
    gain_block = pl.BlockSpec((1, D), whole)
    group = pltpu.VMEM((N_SEQ, TOK_DEV, BACK_WIDTH), bf16)
    group_out = pltpu.VMEM((N_SEQ, TOK_DEV, D), bf16)
    return pl.pallas_call(
        turn_kernel,
        grid=(LOCAL_E + 1,),
        in_specs=[
            pl.BlockSpec((PAIR_TOK, 8), whole),
            pl.BlockSpec((1, SLOTS, 2 * FF), other),
            pl.BlockSpec((1, SLOTS, FF), other),
            pl.BlockSpec((1, SLOTS, 1), one),
            pl.BlockSpec((1, SLOTS, D), one),
            pl.BlockSpec((16, 1, 144, 1024), wide),
            pl.BlockSpec((2, 4, 144, 512), cubes),
            pl.BlockSpec((SLOTS, 2 * FF), whole),
            pl.BlockSpec((SLOTS, FF), whole),
            row_block,
            row_block,
            lane_block,
            pl.BlockSpec((D, 128), whole),
            gain_block,
        ],
        out_specs=[
            row_block,
            ANY,
            lane_block,
            gain_block,
            pl.BlockSpec((N_SEQ, TOK_DEV, D), blocks),
            pl.BlockSpec((144, 1024), whole),
        ],
        out_shape=[
            jax.ShapeDtypeStruct((TOK_DEV, D), f32),
            jax.ShapeDtypeStruct((N_SEQ, TOK_DEV, D), bf16),
            jax.ShapeDtypeStruct((TOK_DEV, 128), bf16),
            jax.ShapeDtypeStruct((1, D), f32),
            jax.ShapeDtypeStruct((N_SEQ, TOK_DEV, D), bf16),
            jax.ShapeDtypeStruct((144, 1024), bf16),
        ],
        scratch_shapes=[
            pltpu.VMEM((LOCAL_E * SLOTS, BACK_WIDTH), bf16),
            pltpu.VMEM((LOCAL_E * SLOTS, D), bf16),
            group,
            group,
            group,
            group_out,
            group_out,
            pltpu.VMEM((TOK_DEV, D), bf16),
        ]
        + reduce_scratch((TOK_DEV, BACK_WIDTH), (HALF, BACK_WIDTH))
        + reduce_scratch((144, 512), (144, 256)) * 2
        + sems(29)
        + [pltpu.SemaphoreType.DMA],
        compiler_params=remote_params(4),
        cost_estimate=pl.CostEstimate(
            flops=6 * LOCAL_E * SLOTS * D * FF + 4 * LOCAL_E * SLOTS * PAIR_TOK * D,
            bytes_accessed=40 << 20,
            transcendentals=0,
        ),
    )(*operands)


PAD_ROWS = 16
WIDE = 768
def owner_order(y_first):
    target = lax.broadcasted_iota(jnp.int32, (QOWN, QOWN), 0)
    source = lax.broadcasted_iota(jnp.int32, (QOWN, QOWN), 1)
    core = lax.div(target, 192)
    first = lax.div(lax.rem(target, 192), 48)
    second = lax.div(lax.rem(target, 48), ROWS)
    x, y = (second, first) if y_first else (first, second)
    owner = x * 8 + y * 2 + core
    return (source == owner * ROWS + lax.rem(target, ROWS)).astype(bf16)


def closing_kernel(
    qkv_ref, lse_ref, lengths_ref, trig_ref, exit_ref, entry_ref,
    in_ref, grad_ref, gain_ref, normed_ref, attended_ref, branch_ref,
    router_grad_ref, gain_two_ref, out_sum_ref, middle_ref,
    input_ref, block_ref, entry_out, exit_out,
    turned, mixed_grad, part, full, from_core, chip, line, final, give, got_z, *rest
):
    bufs, (send_sem, recv_sem) = [rest[6 * i : 6 * i + 6] for i in range(8)], rest[48:]
    z, x, y, c = (lax.axis_index(a) for a in ("seq", "x", "y", "core"))
    right, left, far = ring(z)
    greet(near("seq") + [("seq", far)] + near("x") + near("y") + [sibling()])
    send, plan = sender(send_sem, recv_sem), planner(send_sem, recv_sem)
    picks = (owner_order(False), owner_order(True))
    widen = row_pick((64, 48), 0)

    def spread(side, grad):
        return dot(picks[side == 2], grad, ((1,), (0,))).astype(bf16).reshape(2, 4, 48, -1)

    def swap(side):
        return send(full.at[side, 1 - c], from_core.at[side], 48 + side, "core", 1 - c)

    def chip_sum(side, copy):
        copy.wait_recv()
        added(chip.at[side], full.at[side, c], from_core.at[side])

    def first_sum(side, axis):
        return Reduce(
            plan, 6 * side, axis, lambda i: chip.at[side, i], bufs[side], half_lanes
        ).start()

    def second_sum(side, axis, reduce):
        total = dot(widen, reduce.total().astype(bf16), ((1,), (0,))).astype(bf16)
        line[side] = total.reshape(4, PAD_ROWS, D)
        return Reduce(
            plan, 18 + 6 * side, axis, lambda i: line.at[side, i], bufs[3 + side], half_lanes
        ).start()

    for block in range(3):
        cols = slice(512 * block, 512 * (block + 1))
        grad = dot(attended_ref[...], branch_ref[:, cols], ((0,), (0,))).astype(bf16)
        full[0, :, :, :, cols] = spread(0, grad)
    swaps = [swap(0)]
    outs = Reduce(plan, 36, "seq", lambda i: out_sum_ref.at[i], bufs[6], half_rows).start()

    def turn_back(kv):
        pair = Q_OWN + 2 * HD * kv
        for head in range(PER_KV * kv, PER_KV * (kv + 1)):
            grad = dot(branch_ref[...], exit_ref[head_of(head), :], ((1,), (1,))).astype(bf16)
            attended = attended_ref[:, head_of(head)].astype(f32)
            delta = jnp.sum(grad.astype(f32) * attended, axis=1, keepdims=True)
            for block in range(GROUP // BLOCK):
                bias = block_bias(lengths_ref, block)
                keys = BLOCK * (block + 1)
                rows = slice(BLOCK * block, keys)
                key = qkv_ref[:keys, pair : pair + HD]
                value = qkv_ref[:keys, pair + HD : pair + 2 * HD]
                query, grad_rows = qkv_ref[rows, head_of(head)], grad[rows]
                scores = dot(query, key, ((1,), (1,))) * HD**-0.5 + bias
                probs = jnp.exp(scores - lse_ref[rows, head : head + 1])
                prob_grad = dot(grad_rows, value, ((1,), (1,)))
                score_grad = probs * (prob_grad - delta[rows]) * HD**-0.5
                score_grad = score_grad.astype(bf16)
                turned[rows, head_of(head)] = dot(score_grad, key, ((1,), (0,)))
                key_grad = dot(score_grad, query, ((0,), (0,)))
                value_grad = dot(probs.astype(bf16), grad_rows, ((0,), (0,)))
                if head == PER_KV * kv and block == GROUP // BLOCK - 1:
                    turned[:, pair : pair + HD] = key_grad
                    turned[:, pair + HD : pair + 2 * HD] = value_grad
                    turned[:BLOCK, pair : pair + HD] += held[0]
                    turned[:BLOCK, pair + HD : pair + 2 * HD] += held[1]
                elif head == PER_KV * kv:
                    held = (key_grad, value_grad)
                else:
                    turned[:keys, pair : pair + HD] += key_grad
                    turned[:keys, pair + HD : pair + 2 * HD] += value_grad

    turn_back(0)
    chip_sum(0, swaps[0])
    first_0 = first_sum(0, "x")
    outs.relay()
    turn_back(1)
    first_0.relay()
    grads = turned[...]
    cosine, sine = rope_tables(lengths_ref, trig_ref)
    grads = grads * cosine + swap_halves(grads, 1.0, -1.0) * sine
    mixed_grad[...] = grads.astype(bf16)
    part[...] = (
        dot(mixed_grad[...], entry_ref[...], ((1,), (1,))).astype(bf16).reshape(part.shape)
    )
    rows = Reduce(plan, 42, "seq", lambda i: part.at[i], bufs[7], half_rows).start()

    def entry_rows(block):
        rows_of = slice(QOWN * block, QOWN * (block + 1))
        return dot(normed_ref[:, rows_of], mixed_grad[...], ((0,), (0,))).astype(bf16)

    full[1, :, :, :, :640] = spread(1, entry_rows(0))
    full[1, :, :, :, 640:1280] = spread(1, entry_rows(1))
    third = entry_rows(2)
    full[1, :, :, :, 1280:] = spread(1, third[:, :256])
    swaps.append(swap(1))
    rows.relay()
    second_0 = second_sum(0, "y", first_0)
    full[2, :, :, :, :384] = spread(2, third[:, 256:])
    full[2, :, :, :, 384:1024] = spread(2, entry_rows(3))
    chip_sum(1, swaps[1])
    first_1 = first_sum(1, "x")
    back, gain_one = norm_back(in_ref[...].astype(f32), gain_ref[...], rows.total())
    input_ref[...] = grad_ref[...] + back
    row_of = lax.broadcasted_iota(jnp.int32, (128, D), 0)
    gains = jnp.where(row_of == EXPERTS, gain_one, 0.0)
    gains = jnp.where(row_of == EXPERTS + 1, gain_two_ref[...], gains)
    shared = router_grad_ref[...] + gains.T
    for block in range(4):
        shared_rows = shared[QOWN * block : QOWN * (block + 1), :].astype(bf16)
        full[2, :, :, :, 1024 + 128 * block : 1152 + 128 * block] = spread(2, shared_rows)
    swaps.append(swap(2))
    second_0.relay()
    block_ref[...] = middle_ref[...] + outs.total()
    chip_sum(2, swaps[2])
    first_2 = first_sum(2, "y")
    first_1.relay()
    first_2.relay()
    exit_out[...] = second_0.total()
    second_1 = second_sum(1, "y", first_1)
    second_2 = second_sum(2, "x", first_2)
    second_1.relay()
    second_2.relay()
    final[0] = second_1.total()
    final[1] = second_2.total()
    give[0, :, :MIX_OWN] = final[0, :, :640]
    give[1, :, :MIX_OWN] = final[0, :, 640:1280]
    give[2, :, :256] = final[0, :, 1280:]
    give[2, :, 256:MIX_OWN] = final[1, :, :384]
    give[3, :, :MIX_OWN] = final[1, :, 384:1024]
    for block in range(4):
        give[block, :, MIX_OWN:] = final[1, :, 1024 + 128 * block : 1152 + 128 * block]
    home = [
        send(give.at[peer], got_z.at[k], 51 + k, "seq", peer)
        for k, peer in enumerate((right, far, left))
    ]
    entry_out[z] = give[z]
    for k, source in enumerate((left, far, right)):
        home[k].wait_recv()
        entry_out[source] = got_z[k]
    for copy in swaps + home:
        copy.wait_send()
    for reduce in (rows, outs, first_0, first_1, first_2, second_0, second_1, second_2):
        reduce.drain()


def closing(*operands):
    row_bufs = reduce_scratch((TOK_DEV, D), (HALF, D))
    chip_bufs = reduce_scratch((48, D), (48, D // 2))
    line_bufs = reduce_scratch((PAD_ROWS, D), (PAD_ROWS, D // 2))
    tile = (PAD_ROWS, D)
    return pl.pallas_call(
        closing_kernel,
        out_shape=[
            jax.ShapeDtypeStruct((TOK_DEV, D), f32),
            jax.ShapeDtypeStruct((TOK_DEV, D), f32),
            jax.ShapeDtypeStruct((4, PAD_ROWS, WIDE), f32),
            jax.ShapeDtypeStruct((PAD_ROWS, D), f32),
        ],
        in_specs=[VMEM] * 2
        + [pl.BlockSpec(memory_space=pltpu.SMEM)]
        + [VMEM] * (len(operands) - 3),
        out_specs=[VMEM] * 4,
        scratch_shapes=[
            pltpu.VMEM((GROUP, MIX_OWN), f32),
            pltpu.VMEM((GROUP, MIX_OWN), bf16),
            pltpu.VMEM((N_SEQ, TOK_DEV, D), bf16),
            pltpu.VMEM((3, 2, 4, 48, D), bf16),
            pltpu.VMEM((3, 4, 48, D), bf16),
            pltpu.VMEM((3, 4, 48, D), bf16),
            pltpu.VMEM((3, 4) + tile, bf16),
            pltpu.VMEM((2,) + tile, f32),
            pltpu.VMEM((4, PAD_ROWS, WIDE), f32),
            pltpu.VMEM((3, PAD_ROWS, WIDE), f32),
        ]
        + chip_bufs * 3
        + line_bufs * 3
        + row_bufs * 2
        + sems(54),
        compiler_params=remote_params(5),
    )(*operands)


def owner_kernel(sum_ref, extra_ref, expand_ref, shrink_ref, send_sem, recv_sem):
    core = lax.axis_index("core")
    greet([sibling()])
    send = sender(send_sem, recv_sem)
    most, single = pl.ds(core * LOCAL_E + 1, MAIN_E), core * LOCAL_E

    def parts(owner):
        return (
            pl.ds(pl.multiple_of(owner * 48, 16), 48),
            pl.ds(pl.multiple_of(96 + owner * 16, 16), 16),
            pl.ds(pl.multiple_of(owner * 512, 512), 512),
        )

    rows, left, ends = parts(1 - core)
    low, start, end = pl.ds(128, 16), pl.ds(0, 1024), pl.ds(1024, 512)
    pieces = [
        (sum_ref.at[:, rows], expand_ref.at[most]),
        (sum_ref.at[:, left], shrink_ref.at[most, :, start]),
        (sum_ref.at[:, low, ends], shrink_ref.at[most, :, end]),
        (extra_ref.at[rows], expand_ref.at[single]),
        (extra_ref.at[left], shrink_ref.at[single, :, start]),
        (extra_ref.at[low, ends], shrink_ref.at[single, :, end]),
    ]
    copies = [
        send(source, target, k, "core", 1 - core) for k, (source, target) in enumerate(pieces)
    ]
    rows, left, ends = parts(core)
    for e in range(LOCAL_E):
        source = extra_ref if e == 0 else sum_ref.at[e - 1]
        expert = core * LOCAL_E + e
        expand_ref[expert] = source[rows, :]
        shrink_ref[expert, :, :1024] = source[left, :]
        shrink_ref[expert, :, 1024:] = source[low, ends]
    for copy in copies:
        copy.wait()


def to_owners(summed, extra):
    return pl.pallas_call(
        owner_kernel,
        out_shape=[
            jax.ShapeDtypeStruct((2 * LOCAL_E, 48, 1024), bf16),
            jax.ShapeDtypeStruct((2 * LOCAL_E, 16, D), bf16),
        ],
        in_specs=[VMEM] * 2,
        out_specs=[VMEM] * 2,
        scratch_shapes=sems(6),
        compiler_params=remote_params(6, 8 * 1024 * 1024),
    )(summed, extra)


def weights_of(w_ref):
    expand = w_ref[:, 0, :96, :].reshape(D, 2 * FF)
    left = w_ref[:, 0, 96:128, :].reshape(FF, 1024)
    right = jnp.concatenate([w_ref[:, 0, 128:144, :512], w_ref[:, 0, 128:144, 512:]], axis=1)
    return expand, left, right.reshape(FF, 512)


def expert_pass(rows, cot_rows, row_gates, weights, hidden_ref, up_ref, stores, midway=None):
    expand, left, right = weights
    shrink_at, end_at, expand_at = stores
    grad_rows = (row_gates * cot_rows.astype(f32)).astype(bf16)
    gate_pre = dot(rows, expand[:, :FF], ((1,), (0,)))
    up_part = dot(rows, expand[:, FF:], ((1,), (0,)))
    sig = jax.nn.sigmoid(gate_pre)
    hidden = (gate_pre * sig * up_part).astype(bf16)
    hidden_ref[...] = hidden
    if midway is not None:
        midway()
    hidden_grad = dot(grad_rows[:, :1024], left, ((1,), (1,))) + dot(
        grad_rows[:, 1024:], right, ((1,), (1,))
    )
    up_ref[:, :FF] = (hidden_grad * up_part * sig * (1.0 + gate_pre * (1.0 - sig))).astype(bf16)
    up_ref[:, FF:] = (hidden_grad * gate_pre * sig).astype(bf16)
    grad_left = dot(hidden, grad_rows[:, :1024], ((0,), (0,))).astype(bf16)
    grad_right = dot(hidden, grad_rows[:, 1024:], ((0,), (0,))).astype(bf16)
    grad_right = grad_right.reshape(4, 4, 32, 512)
    shrink_at(grad_left.reshape(4, 4, 32, 1024))
    end_at(grad_right[:, :, :16], grad_right[:, :, 16:])
    up_grad = up_ref[...]
    for j in range(4):
        part = dot(rows[:, 384 * j : 384 * (j + 1)], up_grad, ((0,), (0,))).astype(bf16)
        expand_at(j, part.reshape(4, 96, 1024))


def grads_kernel(
    rows_ref, cot_ref, gate_ref, w_ref, own, hidden_ref, up_ref, out_ref, line_ref, *rest
):
    bufs, (send_sem, recv_sem) = [rest[6 * i : 6 * i + 6] for i in range(2)], rest[12:]
    e = pl.program_id(0)
    plan = planner(send_sem, recv_sem)
    low, high = pl.ds(0, 512), pl.ds(512, 512)
    low_x = Reduce(plan, 0, "x", lambda i: own.at[i, :, :, low], bufs[0], half_rows)
    high_y = Reduce(plan, 6, "y", lambda i: own.at[:, i, :, high], bufs[1], half_rows)

    @pl.when(e == 0)
    def _():
        greet(near("x") + near("y"))
        low_x.start()
        high_y.start()

    def midway():
        @pl.when(e == 2)
        def _():
            low_x.relay()
            high_y.relay()

    def shrink_at(value):
        out_ref[:, :, 0, 96:128, :] = value

    def end_at(first, second):
        out_ref[:, :, 0, 128:144, :512] = first
        out_ref[:, :, 0, 128:144, 512:] = second

    def expand_at(j, value):
        out_ref[j, :, 0, :96, :] = value

    expert_pass(
        rows_ref[0],
        cot_ref[0],
        gate_ref[0],
        weights_of(w_ref),
        hidden_ref.at[0],
        up_ref.at[0],
        (shrink_at, end_at, expand_at),
        midway,
    )

    @pl.when(e == MAIN_E - 1)
    def _():
        line_ref[0] = low_x.total().astype(bf16)
        line_ref[1] = high_y.total().astype(bf16)
        low_x.drain()
        high_y.drain()


def expert_grads(rows, cot_rows, row_gates, weights, own):
    one = lambda e: (e, 0, 0)
    next_one = lambda e: (e + 1, 0, 0)
    cubes = lambda e: (0, 0, 0, 0)
    return pl.pallas_call(
        grads_kernel,
        grid=(MAIN_E,),
        in_specs=[
            pl.BlockSpec((1, SLOTS, D), next_one),
            pl.BlockSpec((1, SLOTS, D), next_one),
            pl.BlockSpec((1, SLOTS, 1), next_one),
            pl.BlockSpec((16, 1, 144, 1024), lambda e: (0, e + 1, 0, 0)),
            pl.BlockSpec((4, 4, 144, 1024), cubes, pipeline_mode=pl.Buffered(1)),
        ],
        out_specs=[
            pl.BlockSpec((1, SLOTS, FF), one),
            pl.BlockSpec((1, SLOTS, 2 * FF), one),
            pl.BlockSpec((4, 4, 1, 144, 1024), lambda e: (0, 0, e, 0, 0)),
            pl.BlockSpec((2, 4, 144, 512), cubes),
        ],
        out_shape=[
            jax.ShapeDtypeStruct((MAIN_E, SLOTS, FF), bf16),
            jax.ShapeDtypeStruct((MAIN_E, SLOTS, 2 * FF), bf16),
            jax.ShapeDtypeStruct((4, 4, MAIN_E, 144, 1024), bf16),
            jax.ShapeDtypeStruct((2, 4, 144, 512), bf16),
        ],
        scratch_shapes=reduce_scratch((4, 144, 512), (2, 144, 512)) * 2 + sems(12),
        compiler_params=remote_params(7),
        cost_estimate=pl.CostEstimate(
            flops=12 * MAIN_E * SLOTS * D * FF, bytes_accessed=60 << 20, transcendentals=0
        ),
    )(rows, cot_rows, row_gates, weights, own)


def token_trig():
    frequency = rope_base ** (-np.arange(HD // 2, dtype=np.float64) * 2.0 / HD)
    phase = np.arange(GROUP, dtype=np.float64)[:, None] * np.tile(frequency, 4)[None, :]
    return np.stack([np.cos(phase), np.sin(phase)]).astype(np.float32)


def adamw_step(weight, gradient, mean_old, square_old, rate, decay):
    drift = beta_first * mean_old + (1.0 - beta_first) * gradient
    spread = beta_second * square_old + (1.0 - beta_second) * gradient * gradient
    mean_hat = drift / (1.0 - beta_first**STEP)
    square_hat = spread / (1.0 - beta_second**STEP)
    master = weight - rate * (mean_hat / (jnp.sqrt(square_hat) + adam_eps) + decay * weight)
    return (drift, spread, master)


def on_device(
    activations,
    cotangent,
    seq_lengths,
    deal_order,
    routes,
    entry_weight,
    entry_mean,
    entry_square,
    exit_weight,
    exit_mean,
    exit_square,
    router_weight,
    router_mean,
    router_square,
    expand_weight,
    expand_mean,
    expand_square,
    shrink_weight,
    shrink_mean,
    shrink_square,
    norm_gains,
    gains_mean,
    gains_square,
):
    angles = (seq_lengths, token_trig())
    (
        weights, entry_own, exit_own, normed, rows, cot_rows, own_grads, first_hidden, first_up,
        shared, gains, qkv, attended, lse, middle, normed_two, row_gates, rank, my_gates,
    ) = forward(
        activations[0],
        cotangent[0],
        activations[0],
        routes[0].T,
        deal_order,
        *angles,
        entry_weight,
        exit_weight,
        router_weight,
        norm_gains,
        expand_weight,
        shrink_weight,
    )
    weights = weights.reshape(16, LOCAL_E, 144, 1024)
    hidden, up_grad, expert_grad, line = expert_grads(
        rows, cot_rows, row_gates, weights, own_grads
    )
    expert_grad = expert_grad.reshape(16, MAIN_E, 144, 1024)
    expert_sum = lax.psum_scatter(expert_grad, PLANE, scatter_dimension=0, tiled=False)
    middle_grad, branch_grad, logit_grad, gain_two_grad, out_sum, extra_sum = turn(
        rank,
        up_grad,
        hidden,
        row_gates,
        cot_rows,
        weights,
        line,
        first_up,
        first_hidden,
        middle,
        cotangent[0],
        my_gates,
        shared,
        gains[1:2],
    )
    branch_grad = branch_grad.reshape(GROUP, D)
    router_grad = dot(normed_two, logit_grad, ((0,), (0,)))

    input_rows, block_rows, entry_got, exit_got = closing(
        qkv,
        lse,
        *angles,
        exit_own,
        entry_own,
        activations[0],
        middle_grad,
        gains[0:1],
        normed,
        attended,
        branch_grad,
        router_grad,
        gain_two_grad,
        out_sum,
        middle,
    )

    input_grad, block_output = input_rows.astype(bf16), block_rows.astype(bf16)

    entry_got = entry_got[:, :ROWS]
    entry_sum = jnp.concatenate(
        [
            entry_got[:, :, :Q_OWN].transpose(1, 0, 2).reshape(ROWS, QH * HD),
            entry_got[:, :, Q_OWN:MIX_OWN].transpose(1, 0, 2).reshape(ROWS, 2 * KVH * HD),
        ],
        axis=1,
    )
    shared_sum = jnp.sum(entry_got[:, :, MIX_OWN:], axis=0)
    router_sum = shared_sum[:, :EXPERTS]
    gains_sum = shared_sum[:, EXPERTS : EXPERTS + 2].T
    exit_sum = exit_got[:ROWS]

    expand_sum, shrink_sum = to_owners(expert_sum, extra_sum)
    expand_sum, shrink_sum = expand_sum.astype(f32), shrink_sum.astype(f32)
    entry_new = adamw_step(entry_weight, entry_sum, entry_mean, entry_square, 0.02, weight_decay)
    exit_new = adamw_step(exit_weight, exit_sum, exit_mean, exit_square, 0.15, weight_decay)
    router_new = adamw_step(
        router_weight, router_sum, router_mean, router_square, 0.01, weight_decay
    )
    expand_new = adamw_step(
        expand_weight, expand_sum, expand_mean, expand_square, 0.02, weight_decay
    )
    shrink_new = adamw_step(
        shrink_weight, shrink_sum, shrink_mean, shrink_square, 0.12, weight_decay
    )
    gains_new = adamw_step(norm_gains, gains_sum, gains_mean, gains_square, 0.5, 0.0)
    return (
        block_output[None],
        input_grad[None],
        *entry_new,
        *exit_new,
        *router_new,
        *expand_new,
        *shrink_new,
        *gains_new,
    )


def solution(mesh):
    fine = Mesh(mesh.devices.reshape(4, 4, 4, 2), ("seq", "x", "y", "core"))
    rows = P(FSDP, "seq", None)
    lists = P(FSDP, None)
    owned = P(("seq",) + FSDP, None)
    experts = P("seq", FSDP, None)
    gains = P(None, ("seq",) + FSDP)
    return jax.shard_map(
        on_device,
        mesh=fine,
        in_specs=(rows, rows, lists, lists, rows)
        + (owned,) * 9
        + (experts,) * 6
        + (gains,) * 3,
        out_specs=(rows, rows) + (owned,) * 9 + (experts,) * 6 + (gains,) * 3,
        check_vma=False,
    )
```

```python
import jax
import jax.numpy as jnp
import numpy as np
from jax import lax
from jax.experimental import pallas as pl
from jax.experimental.pallas import tpu as pltpu
from jax.sharding import Mesh, PartitionSpec as P

D = 1536
QH = 24
KVH = 8
HD = 64
FF = 512
EXPERTS = 40
TOP = 8
STEP = 10
CAP = 29

N_SEQ = 4
TOK_DEV = 128
GROUP = 512
PAIR_TOK = 2 * GROUP
LOCAL_E = EXPERTS // (2 * N_SEQ)
SLOTS = 256
Q_OWN = QH * HD // N_SEQ
KV_OWN = 2 * KVH * HD // N_SEQ
MIX_OWN = Q_OWN + KV_OWN
HEADS_OWN = QH // N_SEQ
KV_HEADS_OWN = KVH // N_SEQ
PER_KV = QH // KVH
ROWS = 12

norm_eps = 1e-06
rope_base = 10000.0
beta_first = 0.9
beta_second = 0.95
adam_eps = 1e-08
weight_decay = 0.1

FSDP = ("x", "y", "core")
PLANE = ("x", "y")
f32 = jnp.float32
bf16 = jnp.bfloat16


BIG = 60 * 1024 * 1024
HALF = TOK_DEV // 2
QOWN = Q_OWN
MESH = pl.DeviceIdType.MESH
ANY = pl.BlockSpec(memory_space=pl.ANY)
VMEM = pl.BlockSpec(memory_space=pltpu.VMEM)


def dot(a, b, dims):
    return lax.dot_general(a, b, (dims, ((), ())), preferred_element_type=f32)


def greet(peers):
    barrier = pltpu.get_barrier_semaphore()
    for axis, peer in peers:
        pl.semaphore_signal(barrier, inc=1, device_id={axis: peer}, device_id_type=MESH)
    pl.semaphore_wait(barrier, len(peers))


def planner(send_sem, recv_sem):
    def plan(src, dst, index, axis, peer):
        return pltpu.make_async_remote_copy(
            src_ref=src,
            dst_ref=dst,
            send_sem=send_sem.at[index],
            recv_sem=recv_sem.at[index],
            device_id={axis: peer},
            device_id_type=MESH,
        )

    return plan


def sender(send_sem, recv_sem):
    plan = planner(send_sem, recv_sem)

    def send(*args):
        copy = plan(*args)
        copy.start()
        return copy

    return send


def sems(count):
    return [pltpu.SemaphoreType.DMA((count,)), pltpu.SemaphoreType.DMA((count,))]


def ring(me):
    right, left = lax.rem(me + 1, 4), lax.rem(me + 3, 4)
    return right, left, lax.rem(me + 2, 4)


def near(axis):
    right, left, _ = ring(lax.axis_index(axis))
    return [(axis, right), (axis, left)]


def sibling():
    return ("core", 1 - lax.axis_index("core"))


def half_rows(ref, half):
    size = ref.shape[0] // 2
    return ref.at[pl.ds(half * size, size)]


def half_lanes(ref, half):
    size = ref.shape[-1] // 2
    return ref.at[(slice(None),) * (len(ref.shape) - 1) + (pl.ds(half * size, size),)]


class Gather:
    def __init__(self, plan, base, axis, mine, slot, cut):
        me = lax.axis_index(axis)
        right, left, self.far = ring(me)
        self.right, self.left = right, left
        here, from_left, from_right = slot(me), cut(slot(left), 0), cut(slot(right), 1)
        self.first = [
            plan(cut(mine, 0), cut(here, 0), base, axis, right),
            plan(cut(mine, 1), cut(here, 1), base + 1, axis, left),
            plan(cut(mine, 1), cut(here, 1), base + 2, axis, right),
            plan(cut(mine, 0), cut(here, 0), base + 3, axis, left),
        ]
        self.later = [
            plan(from_left, from_left, base + 4, axis, right),
            plan(from_right, from_right, base + 5, axis, left),
        ]

    def start(self):
        for copy in self.first:
            copy.start()
        return self

    def relay(self):
        for got, on in zip(self.first, self.later):
            got.wait_recv()
            on.start()

    def wait_left(self):
        self.first[2].wait_recv()

    def wait_right(self):
        self.first[3].wait_recv()

    def wait_far(self):
        for copy in self.later:
            copy.wait_recv()

    def finish(self):
        self.wait_left()
        self.wait_right()
        self.wait_far()

    def drain(self):
        for copy in self.first + self.later:
            copy.wait_send()


def hand_over(send, base, mine, out, gather):
    me, core = lax.axis_index("seq"), lax.axis_index("core")
    other = 1 - core
    copies = [send(mine, out.at[core, me], base, "core", other)]
    gather.relay()
    gather.wait_left()
    block = out.at[core, gather.left]
    copies.append(send(block, block, base + 1, "core", other))
    gather.wait_right()
    block = out.at[core, gather.right]
    copies.append(send(block, block, base + 2, "core", other))
    gather.wait_far()
    block = out.at[core, gather.far]
    copies.append(send(block, block, base + 3, "core", other))
    return copies


def reduce_scratch(block, half):
    return [pltpu.VMEM(half, bf16)] * 4 + [pltpu.VMEM(block, bf16)] * 2


def added(target, first, second):
    target[...] = (first[...].astype(f32) + second[...].astype(f32)).astype(bf16)


class Reduce:
    def __init__(self, plan, base, axis, block, bufs, cut):
        me = lax.axis_index(axis)
        right, left, far = ring(me)
        from_left, from_right, to_right, to_left, got_left, got_right = bufs
        far, on_right, on_left = block(far), block(right), block(left)
        self.mine, self.got = block(me), (got_left, got_right)
        self.hops = (
            (to_right, cut(on_right, 0), from_left),
            (to_left, cut(on_left, 1), from_right),
        )
        self.far = [
            plan(cut(far, 0), from_left, base, axis, right),
            plan(cut(far, 1), from_right, base + 1, axis, left),
        ]
        self.near = [
            plan(cut(on_right, 1), cut(got_left, 1), base + 2, axis, right),
            plan(cut(on_left, 0), cut(got_right, 0), base + 3, axis, left),
        ]
        self.later = [
            plan(to_right, cut(got_left, 0), base + 4, axis, right),
            plan(to_left, cut(got_right, 1), base + 5, axis, left),
        ]

    def start_far(self):
        for copy in self.far:
            copy.start()

    def start_near(self):
        for copy in self.near:
            copy.start()

    def start(self):
        self.start_far()
        self.start_near()
        return self

    def relay(self):
        for got, hop, on in zip(self.far, self.hops, self.later):
            got.wait_recv()
            added(*hop)
            on.start()

    def total(self):
        for copy in self.near + self.later:
            copy.wait_recv()
        total = self.mine[...].astype(f32)
        for part in self.got:
            total += part[...].astype(f32)
        return total

    def drain(self):
        for copy in self.far + self.near + self.later:
            copy.wait_send()


def remote_params(call_id, vmem=BIG):
    return pltpu.CompilerParams(
        collective_id=call_id, has_side_effects=True, vmem_limit_bytes=vmem
    )


def unit_scale(vector):
    return lax.rsqrt(jnp.mean(vector * vector, axis=-1, keepdims=True) + norm_eps)


def norm_back(vector, gain, grad):
    scale = unit_scale(vector)
    unit = vector * scale
    pulled = grad * gain
    back = scale * (pulled - unit * jnp.mean(pulled * unit, axis=-1, keepdims=True))
    return back, jnp.sum(unit * grad, axis=0, keepdims=True)


MAIN_E = LOCAL_E - 1


def row_pick(shape, padded_axis):
    padded = lax.broadcasted_iota(jnp.int32, shape, padded_axis)
    plain = lax.broadcasted_iota(jnp.int32, shape, 1 - padded_axis)
    row = lax.rem(padded, 16)
    return ((plain == lax.div(padded, 16) * 12 + row) & (row < 12)).astype(bf16)


def swap_halves(rows, lower, upper):
    lane = lax.broadcasted_iota(jnp.int32, rows.shape, 1)
    ahead = pltpu.roll(rows, rows.shape[1] - HD // 2, 1)
    behind = pltpu.roll(rows, HD // 2, 1)
    return jnp.where(lax.rem(lane, HD) < HD // 2, lower * ahead, upper * behind)


BLOCK = 256


def sequence_of(lengths_ref, token):
    first_end = lengths_ref[0, 0]
    second_end = first_end + lengths_ref[0, 1]
    return (token >= first_end).astype(jnp.int32) + (token >= second_end).astype(jnp.int32)


def block_bias(lengths_ref, block):
    keys = BLOCK * (block + 1)
    row = lax.broadcasted_iota(jnp.int32, (BLOCK, keys), 0) + BLOCK * block
    column = lax.broadcasted_iota(jnp.int32, (BLOCK, keys), 1)
    same = sequence_of(lengths_ref, row) == sequence_of(lengths_ref, column)
    return jnp.where(same & (column <= row), 0.0, -1e30)


def rope_tables(lengths_ref, trig_ref):
    seq = sequence_of(lengths_ref, lax.broadcasted_iota(jnp.int32, (GROUP, 128), 0))
    second = lengths_ref[0, 0]
    third = second + lengths_ref[0, 1]

    def of_start(table):
        later = jnp.where(
            seq == 1, trig_ref[table, pl.ds(second, 1)], trig_ref[table, pl.ds(third, 1)]
        )
        return jnp.where(seq == 0, trig_ref[table, 0:1], later)

    start_cos, start_sin = of_start(0), of_start(1)
    cosine = trig_ref[0] * start_cos + trig_ref[1] * start_sin
    sine = trig_ref[1] * start_cos - trig_ref[0] * start_sin
    is_key = lax.broadcasted_iota(jnp.int32, (GROUP, 128), 1) < HD
    pair_cos, pair_sin = jnp.where(is_key, cosine, 1.0), jnp.where(is_key, sine, 0.0)
    return (
        jnp.concatenate([cosine] * 3 + [pair_cos] * 2, axis=1),
        jnp.concatenate([sine] * 3 + [pair_sin] * 2, axis=1),
    )


def head_of(index):
    return slice(HD * index, HD * (index + 1))


def lane_pick(first, rows):
    row = lax.broadcasted_iota(jnp.int32, (rows, 128), 0)
    lane = lax.broadcasted_iota(jnp.int32, (rows, 128), 1)
    return (lane == row + first).astype(bf16)


def forward_kernel(
    in_hbm, cot_hbm, in_ref, route_ref, order_ref, lengths_ref, trig_ref,
    entry_ref, exit_ref, router_ref, gain_ref, expand_ref, shrink_ref,
    weights_out, entry_hbm, exit_hbm, normed_hbm, rows_hbm, cot_rows_hbm,
    shared_out, gains_out, qkv_ref, attended_ref,
    lse_ref, middle_ref, mine, row_gate_out, rank_out, my_gate_out,
    entry_out, exit_out, normed_ref, rows_out, cot_rows_out,
    stage, stage_end, packed, shared, columns, hold, full, lines,
    in_all, cot_all, hit_all, hit_pair, tokens, part, gates, *rest
):
    bufs, (send_sem, recv_sem, copy_sem) = rest[:6], rest[6:]
    z, x, y, c = (lax.axis_index(a) for a in ("seq", "x", "y", "core"))
    right, left, far = ring(z)
    other = 1 - c
    greet(near("seq") + [("seq", far)] + near("x") + near("y") + [sibling()])
    send, plan = sender(send_sem, recv_sem), planner(send_sem, recv_sem)

    for e in range(LOCAL_E):
        theirs = other * LOCAL_E + e
        stage[e, :48] = expand_ref[theirs].astype(bf16)
        stage[e, 48:] = shrink_ref[theirs, :, :1024].astype(bf16)
        stage_end[e] = shrink_ref[theirs, :, 1024:].astype(bf16)
    of_core = pl.ds(pl.multiple_of(c * 48, 16), 48)
    lefts = pl.ds(pl.multiple_of(96 + c * 16, 16), 16)
    ends = pl.ds(pl.multiple_of(c * 512, 512), 512)
    to_core = [
        send(stage.at[:, pl.ds(0, 48)], packed.at[:, of_core], 51, "core", other),
        send(stage.at[:, pl.ds(48, 16)], packed.at[:, lefts], 52, "core", other),
        send(stage_end, packed.at[:, pl.ds(128, 16), ends], 53, "core", other),
    ]
    for e in range(LOCAL_E):
        own_e = c * LOCAL_E + e
        packed[e, of_core, :] = expand_ref[own_e].astype(bf16)
        packed[e, lefts, :] = shrink_ref[own_e, :, :1024].astype(bf16)
        packed[e, pl.ds(128, 16), ends] = shrink_ref[own_e, :, 1024:].astype(bf16)
    rows = Gather(plan, 9, "seq", in_hbm, lambda i: in_all.at[i], half_rows).start()
    expert = lax.broadcasted_iota(jnp.int32, (128, TOK_DEV), 0)
    hit = route_ref[0:1] == expert
    for k in range(1, TOP):
        hit = hit | (route_ref[k : k + 1] == expert)
    hit_all[z] = hit.astype(bf16)
    hits = Gather(plan, 3, "seq", hit_all.at[z], lambda i: hit_all.at[i], half_rows).start()

    lane = lax.broadcasted_iota(jnp.int32, (ROWS, 128), 1)
    square = lax.broadcasted_iota(jnp.int32, (ROWS, ROWS), 0)
    square = square == lax.broadcasted_iota(jnp.int32, (ROWS, ROWS), 1)
    shared[...] = jnp.zeros_like(shared)
    shared[:, :EXPERTS] = router_ref[...]
    block_of = shared[...]
    for k in range(2):
        column = jnp.sum(jnp.where(square, gain_ref[k : k + 1], 0.0), axis=1, keepdims=True)
        block_of = jnp.where(lane == EXPERTS + k, column, block_of)
    empty = jnp.zeros((PAD_ROWS - ROWS, WIDE), f32)
    for block in range(4):
        cols = jnp.concatenate(
            [
                entry_ref[:, Q_OWN * block : Q_OWN * (block + 1)],
                entry_ref[:, QH * HD + KV_OWN * block : QH * HD + KV_OWN * (block + 1)],
                block_of,
            ],
            axis=1,
        )
        columns[block] = jnp.concatenate([cols, empty], axis=0).astype(bf16)
    to_seq = [
        send(columns.at[peer], hold.at[z], k, "seq", peer)
        for k, peer in enumerate((right, far, left))
    ]
    for block in range(2):
        cols = exit_ref[:, WIDE * block : WIDE * (block + 1)]
        hold[4 + block] = jnp.concatenate([cols, empty], axis=0).astype(bf16)
    hold[z] = columns[z]
    local = [
        pltpu.make_async_copy(in_hbm, in_all.at[z], copy_sem.at[0]),
        pltpu.make_async_copy(cot_hbm, cot_all.at[c, z], copy_sem.at[1]),
    ]
    for copy in local:
        copy.start()

    for copy in to_seq:
        copy.wait_recv()
    for block in range(6):
        full[block, x if block < 3 else y] = hold[block]
    low, high = pl.ds(0, 3), pl.ds(3, 3)
    low_x = Gather(plan, 15, "x", hold.at[low], lambda i: full.at[low, i], half_lanes)
    low_x.start()
    high_y = Gather(plan, 21, "y", hold.at[high], lambda i: full.at[high, i], half_lanes)
    high_y.start()
    for copy in to_core:
        copy.wait_recv()
    own_weights = pltpu.make_async_copy(packed, weights_out.at[x, y], copy_sem.at[2])
    own_weights.start()
    start, end = pl.ds(0, 512), pl.ds(512, 512)
    expert_x = Gather(
        plan,
        54,
        "x",
        packed.at[:, :, start],
        lambda i: weights_out.at[i, y, :, :, start],
        half_lanes,
    ).start()
    expert_y = Gather(
        plan,
        60,
        "y",
        packed.at[:, :, end],
        lambda i: weights_out.at[x, i, :, :, end],
        half_lanes,
    ).start()

    narrow = row_pick((48, 64), 1)

    def compact(blocks, place):
        for block in blocks:
            got = dot(narrow, full[block].reshape(64, WIDE), ((1,), (0,)))
            lines[c, block, place] = got.astype(bf16)

    hits.relay()
    low_x.relay()
    high_y.relay()
    rows.relay()
    cots = Gather(plan, 27, "seq", cot_hbm, lambda i: cot_all.at[c, i], half_rows).start()
    low_x.finish()
    compact(range(3), y)
    low_y = Gather(
        plan, 33, "y", lines.at[c, low, y], lambda i: lines.at[c, low, i], half_lanes
    ).start()
    high_y.finish()
    compact(range(3, 6), x)
    high_x = Gather(
        plan, 39, "x", lines.at[c, high, x], lambda i: lines.at[c, high, i], half_lanes
    ).start()
    expert_x.relay()
    expert_y.relay()

    hits.finish()
    token = lax.broadcasted_iota(jnp.int32, (GROUP, GROUP), 0)
    back_hot = (order_ref[...] == token).astype(bf16)
    natural = jnp.zeros((GROUP, 128), f32)
    for block in range(N_SEQ):
        slots = back_hot[:, TOK_DEV * block : TOK_DEV * (block + 1)]
        natural += dot(slots, hit_all[block], ((1,), (1,)))
    hit_pair[c] = natural.astype(bf16)
    hit_swap = send(hit_pair.at[c], hit_pair.at[c], 66, "core", other)
    low_y.relay()
    high_x.relay()
    hit_swap.wait_recv()
    hit_both = hit_pair[...].reshape(PAIR_TOK, 128)
    first = (z * 2 + c) * LOCAL_E
    lower = lax.broadcasted_iota(jnp.int32, (PAIR_TOK, PAIR_TOK), 0)
    lower = (lower >= lax.broadcasted_iota(jnp.int32, (PAIR_TOK, PAIR_TOK), 1)).astype(bf16)
    rank = dot(lower, hit_both, ((1,), (0,))) - 1.0
    rank = jnp.where(hit_both.astype(f32) > 0.0, rank, -1.0).astype(bf16)
    mine_of = lane_pick(first, 8)
    rank_out[...] = dot(rank, mine_of, ((1,), (1,))).astype(jnp.int32)
    rank_rows = dot(mine_of, rank, ((1,), (1,))).astype(jnp.int32)

    low_y.finish()
    half = lines.at[c, low]
    last = [send(half, half, 49, "core", other)]
    high_x.finish()
    half = lines.at[c, high]
    last.append(send(half, half, 50, "core", other))
    own_weights.wait()
    expert_x.finish()
    expert_low = Gather(
        plan,
        67,
        "y",
        weights_out.at[:, y, :, :, start],
        lambda i: weights_out.at[:, i, :, :, start],
        half_rows,
    ).start()
    expert_y.finish()
    expert_high = Gather(
        plan,
        73,
        "x",
        weights_out.at[x, :, :, :, end],
        lambda i: weights_out.at[i, :, :, :, end],
        half_rows,
    ).start()
    cosine, sine = rope_tables(lengths_ref, trig_ref)
    rows.finish()
    local[0].wait()
    for copy in last:
        copy.wait_recv()
    orders = (owner_order(True), owner_order(False))

    def whole(block):
        rows_in = lines[:, block].reshape(QOWN, WIDE)
        return dot(orders[block >= 3], rows_in, ((0,), (0,))).astype(bf16)

    for block in range(4):
        got = whole(block)
        entry_out[QOWN * block : QOWN * (block + 1), :] = got[:, :MIX_OWN]
        shared_out[QOWN * block : QOWN * (block + 1), :] = got[:, MIX_OWN:]
    for block in range(2):
        got = whole(4 + block)
        exit_out[:, WIDE * block : WIDE * (block + 1)] = got
    gains = dot(lane_pick(EXPERTS, 8), shared_out[...], ((1,), (1,)))
    gains_out[...] = gains
    for block in range(N_SEQ):
        at = slice(TOK_DEV * block, TOK_DEV * (block + 1))
        vector = in_all[block].astype(f32)
        normed_ref[at, :] = (vector * unit_scale(vector) * gains[0:1]).astype(bf16)
    results = [(entry_out, entry_hbm), (exit_out, exit_hbm), (normed_ref, normed_hbm)]
    results = [
        pltpu.make_async_copy(source, target, copy_sem.at[3 + k])
        for k, (source, target) in enumerate(results)
    ]
    for copy in results:
        copy.start()
    mixed = dot(normed_ref[...], entry_out[...], ((1,), (0,)))
    mixed = mixed * cosine + swap_halves(mixed, -1.0, 1.0) * sine
    qkv_ref[...] = mixed.astype(bf16)
    for block in range(GROUP // BLOCK):
        bias = block_bias(lengths_ref, block)
        keys = BLOCK * (block + 1)
        at = slice(BLOCK * block, keys)
        for head in range(HEADS_OWN):
            pair = Q_OWN + 2 * HD * (head // PER_KV)
            key = qkv_ref[:keys, pair : pair + HD]
            value = qkv_ref[:keys, pair + HD : pair + 2 * HD]
            scores = dot(qkv_ref[at, head_of(head)], key, ((1,), (1,))) * HD**-0.5 + bias
            peak = jnp.max(scores, axis=1, keepdims=True)
            expo = jnp.exp(scores - peak)
            total = jnp.sum(expo, axis=1, keepdims=True)
            probs = (expo / total).astype(bf16)
            attended_ref[at, head_of(head)] = dot(probs, value, ((1,), (0,))).astype(bf16)
            lse_ref[at, head : head + 1] = peak + jnp.log(total)
    part[...] = dot(attended_ref[...], exit_out[...], ((1,), (0,))).astype(bf16).reshape(part.shape)
    reduce = Reduce(plan, 79, "seq", lambda i: part.at[i], bufs, half_rows).start()
    pairs = hand_over(send, 45, cot_hbm, cot_all, cots)
    reduce.relay()
    middle = in_ref[...].astype(f32) + reduce.total()
    middle_ref[...] = middle
    mine[...] = (middle * unit_scale(middle) * gains[1:2]).astype(bf16)
    gather = Gather(plan, 85, "seq", mine, lambda i: tokens.at[c, i], half_rows).start()
    tokens[c, z] = mine[...]
    pairs += hand_over(send, 91, mine, tokens, gather)
    for copy in pairs:
        copy.wait()
    local[1].wait()

    logits = dot(tokens[...].reshape(PAIR_TOK, D), shared_out[...], ((1,), (0,)))
    masked = jnp.where(hit_both.astype(f32) > 0.0, logits, -jnp.inf)
    gate_expo = jnp.exp(masked - jnp.max(masked, axis=1, keepdims=True))
    gates[...] = gate_expo / jnp.sum(gate_expo, axis=1, keepdims=True)
    my_gate_out[...] = gates[pl.ds(pl.multiple_of(c * GROUP + z * TOK_DEV, TOK_DEV), TOK_DEV), :]
    rest_of = gates[...]
    gate_rows = jnp.zeros((8, PAIR_TOK), f32)
    for _ in range(3):
        piece = rest_of.astype(bf16)
        gate_rows += dot(mine_of, piece, ((1,), (1,)))
        rest_of -= piece.astype(f32)
    slot = lax.broadcasted_iota(jnp.int32, (SLOTS, PAIR_TOK), 0)
    for e in range(LOCAL_E):
        if e == 3:
            expert_low.relay()
            expert_high.relay()
        match = rank_rows[e : e + 1] == slot
        row_gate_out[e] = jnp.sum(
            jnp.where(match, gate_rows[e : e + 1], 0.0), axis=1, keepdims=True
        )
        match = match.astype(bf16)
        for half in range(2):
            lanes = slice(768 * half, 768 * (half + 1))
            table = tokens[:, :, :, lanes].reshape(PAIR_TOK, 768)
            rows_out[e, :, lanes] = dot(match, table, ((1,), (0,))).astype(bf16)
            table = cot_all[:, :, :, lanes].reshape(PAIR_TOK, 768)
            cot_rows_out[e, :, lanes] = dot(match, table, ((1,), (0,))).astype(bf16)
        for k, (source, target) in enumerate(((rows_out, rows_hbm), (cot_rows_out, cot_rows_hbm))):
            copy = pltpu.make_async_copy(
                source.at[e], target.at[e], copy_sem.at[6 + 2 * e + k]
            )
            copy.start()
            results.append(copy)
    expert_low.finish()
    expert_high.finish()
    for copy in to_seq + to_core + last + [hit_swap]:
        copy.wait_send()
    for copy in results:
        copy.wait()
    for transfer in (hits, rows, cots, low_x, high_y, low_y, high_x, reduce, gather):
        transfer.drain()
    for transfer in (expert_x, expert_y, expert_low, expert_high):
        transfer.drain()


def forward(*operands):
    scalar = pl.BlockSpec(memory_space=pltpu.SMEM)
    block = (PAD_ROWS, WIDE)
    group = (N_SEQ, TOK_DEV, D)
    return pl.pallas_call(
        forward_kernel,
        out_shape=[
            jax.ShapeDtypeStruct((4, 4, LOCAL_E, 144, 1024), bf16),
            jax.ShapeDtypeStruct((D, MIX_OWN), bf16),
            jax.ShapeDtypeStruct((QOWN, D), bf16),
            jax.ShapeDtypeStruct((GROUP, D), bf16),
            jax.ShapeDtypeStruct((LOCAL_E, SLOTS, D), bf16),
            jax.ShapeDtypeStruct((LOCAL_E, SLOTS, D), bf16),
            jax.ShapeDtypeStruct((D, 128), bf16),
            jax.ShapeDtypeStruct((8, D), f32),
            jax.ShapeDtypeStruct((GROUP, MIX_OWN), bf16),
            jax.ShapeDtypeStruct((GROUP, Q_OWN), bf16),
            jax.ShapeDtypeStruct((GROUP, HEADS_OWN), f32),
            jax.ShapeDtypeStruct((TOK_DEV, D), f32),
            jax.ShapeDtypeStruct((TOK_DEV, D), bf16),
            jax.ShapeDtypeStruct((LOCAL_E, SLOTS, 1), f32),
            jax.ShapeDtypeStruct((PAIR_TOK, 8), jnp.int32),
            jax.ShapeDtypeStruct((TOK_DEV, 128), f32),
        ],
        in_specs=[ANY] * 2 + [VMEM] * 3 + [scalar] + [VMEM] * 7,
        out_specs=[ANY] * 6 + [VMEM] * 10,
        scratch_shapes=[
            pltpu.VMEM((D, MIX_OWN), bf16),
            pltpu.VMEM((QOWN, D), bf16),
            pltpu.VMEM((GROUP, D), bf16),
            pltpu.VMEM((LOCAL_E, SLOTS, D), bf16),
            pltpu.VMEM((LOCAL_E, SLOTS, D), bf16),
            pltpu.VMEM((LOCAL_E, 64, 1024), bf16),
            pltpu.VMEM((LOCAL_E, 16, 512), bf16),
            pltpu.VMEM((LOCAL_E, 144, 1024), bf16),
            pltpu.VMEM((ROWS, 128), f32),
            pltpu.VMEM((4,) + block, bf16),
            pltpu.VMEM((6,) + block, bf16),
            pltpu.VMEM((6, 4) + block, bf16),
            pltpu.VMEM((2, 6, 4, 48, WIDE), bf16),
            pltpu.VMEM(group, bf16),
            pltpu.VMEM((2,) + group, bf16),
            pltpu.VMEM((N_SEQ, TOK_DEV, 128), bf16),
            pltpu.VMEM((2, GROUP, 128), bf16),
            pltpu.VMEM((2,) + group, bf16),
            pltpu.VMEM(group, bf16),
            pltpu.VMEM((PAIR_TOK, 128), f32),
        ]
        + reduce_scratch((TOK_DEV, D), (HALF, D))
        + sems(95)
        + [pltpu.SemaphoreType.DMA((16,))],
        compiler_params=remote_params(2),
    )(*operands)


def turn_kernel(
    rank_ref, up_ref, hidden_ref, gate_ref, cot_rows_ref, w_ref,
    line, middle_ref, cot_ref, my_gate_ref, router_ref, gain_ref,
    grad_ref, branch_ref, logit_ref, gain_grad_ref, out_sum_ref, extra_sum_ref,
    back_s, out_s, other_back, from_core, part, other_out, out_core, mine, *rest
):
    bufs, (send_sem, recv_sem, copy_sem) = [rest[6 * i : 6 * i + 6] for i in range(3)], rest[18:]
    e = pl.program_id(0)
    me, core = lax.axis_index("seq"), lax.axis_index("core")
    send, plan = sender(send_sem, recv_sem), planner(send_sem, recv_sem)
    low_y = Reduce(plan, 17, "y", lambda i: line.at[0, i], bufs[1], half_lanes)
    high_x = Reduce(plan, 23, "x", lambda i: line.at[1, i], bufs[2], half_lanes)

    @pl.when(e == 0)
    def _():
        greet(near("seq") + near("x") + near("y") + [sibling()])
        low_y.start()
        high_x.start()

    @pl.when(e == 2)
    def _():
        low_y.relay()
        high_x.relay()

    @pl.when(e < LOCAL_E)
    def _():
        expand, left, right = weights_of(w_ref)
        at = pl.ds(pl.multiple_of(e * SLOTS, SLOTS), SLOTS)
        back_s[at, :D] = dot(up_ref[0], expand, ((1,), (1,))).astype(bf16)
        hidden = hidden_ref[0]
        expert_out = jnp.concatenate(
            [dot(hidden, left, ((1,), (0,))), dot(hidden, right, ((1,), (0,)))], axis=1
        )
        expert_out = expert_out.astype(bf16).astype(f32)
        gate_grad = jnp.sum(expert_out * cot_rows_ref[0].astype(f32), axis=1, keepdims=True)
        lane = lax.broadcasted_iota(jnp.int32, (SLOTS, 128), 1)
        column = (me * 2 + core) * LOCAL_E + e
        back_s[at, D:] = jnp.where(lane == column, gate_grad, 0.0).astype(bf16)
        out_s[at, :] = (gate_ref[0] * expert_out).astype(bf16)

    @pl.when(e == LOCAL_E)
    def _():
        other = 1 - core
        right, left, far = ring(me)
        slot = lax.broadcasted_iota(jnp.int32, (GROUP, SLOTS), 1)

        def picks(group):
            at = pl.ds(pl.multiple_of(group * GROUP, GROUP), GROUP)
            ranks = rank_ref[at, :]
            return jnp.concatenate(
                [(ranks[:, k : k + 1] == slot).astype(bf16) for k in range(LOCAL_E)], axis=1
            )

        theirs, ours = picks(other), picks(core)
        order = (far, right, left, me)
        other_back[...] = (
            dot(theirs, back_s[...], ((1,), (0,))).astype(bf16).reshape(other_back.shape)
        )
        swaps = [
            send(other_back.at[block], from_core.at[block], 12 + i, "core", other)
            for i, block in enumerate(order)
        ]
        part[...] = dot(ours, back_s[...], ((1,), (0,))).astype(bf16).reshape(part.shape)
        reduce = Reduce(plan, 0, "seq", lambda i: part.at[i], bufs[0], half_rows)
        for i, block in enumerate(order):
            swaps[i].wait_recv()
            added(part.at[block], part.at[block], from_core.at[block])
            if i == 0:
                reduce.start_far()
            if i == 2:
                reduce.start_near()
        other_out[...] = (
            dot(theirs, out_s[...], ((1,), (0,))).astype(bf16).reshape(other_out.shape)
        )
        out_swap = send(other_out, out_core, 16, "core", other)
        reduce.relay()
        out_sum_ref[...] = (
            dot(ours, out_s[...], ((1,), (0,))).astype(bf16).reshape(out_sum_ref.shape)
        )
        total = reduce.total()
        gates, gate_grad = my_gate_ref[...], total[:, D:]
        mean_term = jnp.sum(gates * gate_grad, axis=1, keepdims=True)
        logit_grad = (gates * (gate_grad - mean_term)).astype(bf16)
        logit_ref[...] = logit_grad
        normed_grad = total[:, :D] + dot(logit_grad, router_ref[...], ((1,), (1,)))
        back, gain_grad = norm_back(middle_ref[...], gain_ref[...], normed_grad)
        gain_grad_ref[...] = gain_grad
        middle_grad = cot_ref[...].astype(f32) + back
        grad_ref[...] = middle_grad
        mine[...] = middle_grad.astype(bf16)
        gather = Gather(plan, 6, "seq", mine, lambda i: branch_ref.at[i], half_rows).start()
        local = pltpu.make_async_copy(mine, branch_ref.at[me], copy_sem)
        local.start()
        out_swap.wait_recv()
        added(out_sum_ref, out_sum_ref, out_core)
        gather.relay()
        extra_sum_ref[:, :512] = low_y.total().astype(bf16)
        extra_sum_ref[:, 512:] = high_x.total().astype(bf16)
        gather.finish()
        for transfer in (gather, reduce, low_y, high_x):
            transfer.drain()
        for copy in swaps + [out_swap]:
            copy.wait_send()
        local.wait()


BACK_WIDTH = D + 128


def turn(*operands):
    one = lambda e: (jnp.minimum(e, LOCAL_E - 1), 0, 0)
    wide = lambda e: (0, jnp.minimum(e, LOCAL_E - 1), 0, 0)
    cubes = lambda e: (0, 0, 0, 0)
    whole = lambda e: (0, 0)
    blocks = lambda e: (0, 0, 0)
    row_block = pl.BlockSpec((TOK_DEV, D), whole)
    lane_block = pl.BlockSpec((TOK_DEV, 128), whole)
    gain_block = pl.BlockSpec((1, D), whole)
    group = pltpu.VMEM((N_SEQ, TOK_DEV, BACK_WIDTH), bf16)
    group_out = pltpu.VMEM((N_SEQ, TOK_DEV, D), bf16)
    return pl.pallas_call(
        turn_kernel,
        grid=(LOCAL_E + 1,),
        in_specs=[
            pl.BlockSpec((PAIR_TOK, 8), whole),
            pl.BlockSpec((1, SLOTS, 2 * FF), one),
            pl.BlockSpec((1, SLOTS, FF), one),
            pl.BlockSpec((1, SLOTS, 1), one),
            pl.BlockSpec((1, SLOTS, D), one),
            pl.BlockSpec((16, 1, 144, 1024), wide),
            pl.BlockSpec((2, 4, 144, 512), cubes),
            row_block,
            row_block,
            lane_block,
            pl.BlockSpec((D, 128), whole),
            gain_block,
        ],
        out_specs=[
            row_block,
            ANY,
            lane_block,
            gain_block,
            pl.BlockSpec((N_SEQ, TOK_DEV, D), blocks),
            pl.BlockSpec((144, 1024), whole),
        ],
        out_shape=[
            jax.ShapeDtypeStruct((TOK_DEV, D), f32),
            jax.ShapeDtypeStruct((N_SEQ, TOK_DEV, D), bf16),
            jax.ShapeDtypeStruct((TOK_DEV, 128), bf16),
            jax.ShapeDtypeStruct((1, D), f32),
            jax.ShapeDtypeStruct((N_SEQ, TOK_DEV, D), bf16),
            jax.ShapeDtypeStruct((144, 1024), bf16),
        ],
        scratch_shapes=[
            pltpu.VMEM((LOCAL_E * SLOTS, BACK_WIDTH), bf16),
            pltpu.VMEM((LOCAL_E * SLOTS, D), bf16),
            group,
            group,
            group,
            group_out,
            group_out,
            pltpu.VMEM((TOK_DEV, D), bf16),
        ]
        + reduce_scratch((TOK_DEV, BACK_WIDTH), (HALF, BACK_WIDTH))
        + reduce_scratch((144, 512), (144, 256)) * 2
        + sems(29)
        + [pltpu.SemaphoreType.DMA],
        compiler_params=remote_params(4),
        cost_estimate=pl.CostEstimate(
            flops=6 * LOCAL_E * SLOTS * D * FF + 4 * LOCAL_E * SLOTS * PAIR_TOK * D,
            bytes_accessed=40 << 20,
            transcendentals=0,
        ),
    )(*operands)


PAD_ROWS = 16
WIDE = 768
def owner_order(y_first):
    target = lax.broadcasted_iota(jnp.int32, (QOWN, QOWN), 0)
    source = lax.broadcasted_iota(jnp.int32, (QOWN, QOWN), 1)
    core = lax.div(target, 192)
    first = lax.div(lax.rem(target, 192), 48)
    second = lax.div(lax.rem(target, 48), ROWS)
    x, y = (second, first) if y_first else (first, second)
    owner = x * 8 + y * 2 + core
    return (source == owner * ROWS + lax.rem(target, ROWS)).astype(bf16)


def closing_kernel(
    qkv_ref, lse_ref, lengths_ref, trig_ref, exit_ref, entry_ref,
    in_ref, grad_ref, gain_ref, normed_ref, attended_ref, branch_ref,
    router_grad_ref, gain_two_ref, out_sum_ref, middle_ref,
    input_ref, block_ref, entry_out, exit_out,
    turned, mixed_grad, part, full, from_core, chip, line, final, give, got_z, *rest
):
    bufs, (send_sem, recv_sem) = [rest[6 * i : 6 * i + 6] for i in range(8)], rest[48:]
    z, x, y, c = (lax.axis_index(a) for a in ("seq", "x", "y", "core"))
    right, left, far = ring(z)
    greet(near("seq") + [("seq", far)] + near("x") + near("y") + [sibling()])
    send, plan = sender(send_sem, recv_sem), planner(send_sem, recv_sem)
    picks = (owner_order(False), owner_order(True))
    widen = row_pick((64, 48), 0)

    def spread(side, grad):
        return dot(picks[side == 2], grad, ((1,), (0,))).astype(bf16).reshape(2, 4, 48, -1)

    def swap(side):
        return send(full.at[side, 1 - c], from_core.at[side], 48 + side, "core", 1 - c)

    def chip_sum(side, copy):
        copy.wait_recv()
        added(chip.at[side], full.at[side, c], from_core.at[side])

    def first_sum(side, axis):
        return Reduce(
            plan, 6 * side, axis, lambda i: chip.at[side, i], bufs[side], half_lanes
        ).start()

    def second_sum(side, axis, reduce):
        total = dot(widen, reduce.total().astype(bf16), ((1,), (0,))).astype(bf16)
        line[side] = total.reshape(4, PAD_ROWS, D)
        return Reduce(
            plan, 18 + 6 * side, axis, lambda i: line.at[side, i], bufs[3 + side], half_lanes
        ).start()

    for block in range(3):
        cols = slice(512 * block, 512 * (block + 1))
        grad = dot(attended_ref[...], branch_ref[:, cols], ((0,), (0,))).astype(bf16)
        full[0, :, :, :, cols] = spread(0, grad)
    swaps = [swap(0)]
    outs = Reduce(plan, 36, "seq", lambda i: out_sum_ref.at[i], bufs[6], half_rows).start()

    def turn_back(kv):
        pair = Q_OWN + 2 * HD * kv
        for head in range(PER_KV * kv, PER_KV * (kv + 1)):
            grad = dot(branch_ref[...], exit_ref[head_of(head), :], ((1,), (1,))).astype(bf16)
            attended = attended_ref[:, head_of(head)].astype(f32)
            delta = jnp.sum(grad.astype(f32) * attended, axis=1, keepdims=True)
            for block in range(GROUP // BLOCK):
                bias = block_bias(lengths_ref, block)
                keys = BLOCK * (block + 1)
                rows = slice(BLOCK * block, keys)
                key = qkv_ref[:keys, pair : pair + HD]
                value = qkv_ref[:keys, pair + HD : pair + 2 * HD]
                query, grad_rows = qkv_ref[rows, head_of(head)], grad[rows]
                scores = dot(query, key, ((1,), (1,))) * HD**-0.5 + bias
                probs = jnp.exp(scores - lse_ref[rows, head : head + 1])
                prob_grad = dot(grad_rows, value, ((1,), (1,)))
                score_grad = probs * (prob_grad - delta[rows]) * HD**-0.5
                score_grad = score_grad.astype(bf16)
                turned[rows, head_of(head)] = dot(score_grad, key, ((1,), (0,)))
                key_grad = dot(score_grad, query, ((0,), (0,)))
                value_grad = dot(probs.astype(bf16), grad_rows, ((0,), (0,)))
                if head == PER_KV * kv and block == GROUP // BLOCK - 1:
                    turned[:, pair : pair + HD] = key_grad
                    turned[:, pair + HD : pair + 2 * HD] = value_grad
                    turned[:BLOCK, pair : pair + HD] += held[0]
                    turned[:BLOCK, pair + HD : pair + 2 * HD] += held[1]
                elif head == PER_KV * kv:
                    held = (key_grad, value_grad)
                else:
                    turned[:keys, pair : pair + HD] += key_grad
                    turned[:keys, pair + HD : pair + 2 * HD] += value_grad

    turn_back(0)
    chip_sum(0, swaps[0])
    first_0 = first_sum(0, "x")
    outs.relay()
    turn_back(1)
    first_0.relay()
    grads = turned[...]
    cosine, sine = rope_tables(lengths_ref, trig_ref)
    grads = grads * cosine + swap_halves(grads, 1.0, -1.0) * sine
    mixed_grad[...] = grads.astype(bf16)
    part[...] = (
        dot(mixed_grad[...], entry_ref[...], ((1,), (1,))).astype(bf16).reshape(part.shape)
    )
    rows = Reduce(plan, 42, "seq", lambda i: part.at[i], bufs[7], half_rows).start()

    def entry_rows(block):
        rows_of = slice(QOWN * block, QOWN * (block + 1))
        return dot(normed_ref[:, rows_of], mixed_grad[...], ((0,), (0,))).astype(bf16)

    full[1, :, :, :, :640] = spread(1, entry_rows(0))
    full[1, :, :, :, 640:1280] = spread(1, entry_rows(1))
    third = entry_rows(2)
    full[1, :, :, :, 1280:] = spread(1, third[:, :256])
    swaps.append(swap(1))
    rows.relay()
    second_0 = second_sum(0, "y", first_0)
    full[2, :, :, :, :384] = spread(2, third[:, 256:])
    full[2, :, :, :, 384:1024] = spread(2, entry_rows(3))
    chip_sum(1, swaps[1])
    first_1 = first_sum(1, "x")
    back, gain_one = norm_back(in_ref[...].astype(f32), gain_ref[...], rows.total())
    input_ref[...] = grad_ref[...] + back
    row_of = lax.broadcasted_iota(jnp.int32, (128, D), 0)
    gains = jnp.where(row_of == EXPERTS, gain_one, 0.0)
    gains = jnp.where(row_of == EXPERTS + 1, gain_two_ref[...], gains)
    shared = router_grad_ref[...] + gains.T
    for block in range(4):
        shared_rows = shared[QOWN * block : QOWN * (block + 1), :].astype(bf16)
        full[2, :, :, :, 1024 + 128 * block : 1152 + 128 * block] = spread(2, shared_rows)
    swaps.append(swap(2))
    second_0.relay()
    block_ref[...] = middle_ref[...] + outs.total()
    chip_sum(2, swaps[2])
    first_2 = first_sum(2, "y")
    first_1.relay()
    first_2.relay()
    exit_out[...] = second_0.total()
    second_1 = second_sum(1, "y", first_1)
    second_2 = second_sum(2, "x", first_2)
    second_1.relay()
    second_2.relay()
    final[0] = second_1.total()
    final[1] = second_2.total()
    give[0, :, :MIX_OWN] = final[0, :, :640]
    give[1, :, :MIX_OWN] = final[0, :, 640:1280]
    give[2, :, :256] = final[0, :, 1280:]
    give[2, :, 256:MIX_OWN] = final[1, :, :384]
    give[3, :, :MIX_OWN] = final[1, :, 384:1024]
    for block in range(4):
        give[block, :, MIX_OWN:] = final[1, :, 1024 + 128 * block : 1152 + 128 * block]
    home = [
        send(give.at[peer], got_z.at[k], 51 + k, "seq", peer)
        for k, peer in enumerate((right, far, left))
    ]
    entry_out[z] = give[z]
    for k, source in enumerate((left, far, right)):
        home[k].wait_recv()
        entry_out[source] = got_z[k]
    for copy in swaps + home:
        copy.wait_send()
    for reduce in (rows, outs, first_0, first_1, first_2, second_0, second_1, second_2):
        reduce.drain()


def closing(*operands):
    row_bufs = reduce_scratch((TOK_DEV, D), (HALF, D))
    chip_bufs = reduce_scratch((48, D), (48, D // 2))
    line_bufs = reduce_scratch((PAD_ROWS, D), (PAD_ROWS, D // 2))
    tile = (PAD_ROWS, D)
    return pl.pallas_call(
        closing_kernel,
        out_shape=[
            jax.ShapeDtypeStruct((TOK_DEV, D), f32),
            jax.ShapeDtypeStruct((TOK_DEV, D), f32),
            jax.ShapeDtypeStruct((4, PAD_ROWS, WIDE), f32),
            jax.ShapeDtypeStruct((PAD_ROWS, D), f32),
        ],
        in_specs=[VMEM] * 2
        + [pl.BlockSpec(memory_space=pltpu.SMEM)]
        + [VMEM] * (len(operands) - 3),
        out_specs=[VMEM] * 4,
        scratch_shapes=[
            pltpu.VMEM((GROUP, MIX_OWN), f32),
            pltpu.VMEM((GROUP, MIX_OWN), bf16),
            pltpu.VMEM((N_SEQ, TOK_DEV, D), bf16),
            pltpu.VMEM((3, 2, 4, 48, D), bf16),
            pltpu.VMEM((3, 4, 48, D), bf16),
            pltpu.VMEM((3, 4, 48, D), bf16),
            pltpu.VMEM((3, 4) + tile, bf16),
            pltpu.VMEM((2,) + tile, f32),
            pltpu.VMEM((4, PAD_ROWS, WIDE), f32),
            pltpu.VMEM((3, PAD_ROWS, WIDE), f32),
        ]
        + chip_bufs * 3
        + line_bufs * 3
        + row_bufs * 2
        + sems(54),
        compiler_params=remote_params(5),
    )(*operands)


def owner_kernel(sum_ref, extra_ref, expand_ref, shrink_ref, send_sem, recv_sem):
    core = lax.axis_index("core")
    greet([sibling()])
    send = sender(send_sem, recv_sem)
    most, single = pl.ds(core * LOCAL_E + 1, MAIN_E), core * LOCAL_E

    def parts(owner):
        return (
            pl.ds(pl.multiple_of(owner * 48, 16), 48),
            pl.ds(pl.multiple_of(96 + owner * 16, 16), 16),
            pl.ds(pl.multiple_of(owner * 512, 512), 512),
        )

    rows, left, ends = parts(1 - core)
    low, start, end = pl.ds(128, 16), pl.ds(0, 1024), pl.ds(1024, 512)
    pieces = [
        (sum_ref.at[:, rows], expand_ref.at[most]),
        (sum_ref.at[:, left], shrink_ref.at[most, :, start]),
        (sum_ref.at[:, low, ends], shrink_ref.at[most, :, end]),
        (extra_ref.at[rows], expand_ref.at[single]),
        (extra_ref.at[left], shrink_ref.at[single, :, start]),
        (extra_ref.at[low, ends], shrink_ref.at[single, :, end]),
    ]
    copies = [
        send(source, target, k, "core", 1 - core) for k, (source, target) in enumerate(pieces)
    ]
    rows, left, ends = parts(core)
    for e in range(LOCAL_E):
        source = extra_ref if e == 0 else sum_ref.at[e - 1]
        expert = core * LOCAL_E + e
        expand_ref[expert] = source[rows, :]
        shrink_ref[expert, :, :1024] = source[left, :]
        shrink_ref[expert, :, 1024:] = source[low, ends]
    for copy in copies:
        copy.wait()


def to_owners(summed, extra):
    return pl.pallas_call(
        owner_kernel,
        out_shape=[
            jax.ShapeDtypeStruct((2 * LOCAL_E, 48, 1024), bf16),
            jax.ShapeDtypeStruct((2 * LOCAL_E, 16, D), bf16),
        ],
        in_specs=[VMEM] * 2,
        out_specs=[VMEM] * 2,
        scratch_shapes=sems(6),
        compiler_params=remote_params(6, 8 * 1024 * 1024),
    )(summed, extra)


def weights_of(w_ref):
    expand = w_ref[:, 0, :96, :].reshape(D, 2 * FF)
    left = w_ref[:, 0, 96:128, :].reshape(FF, 1024)
    right = jnp.concatenate([w_ref[:, 0, 128:144, :512], w_ref[:, 0, 128:144, 512:]], axis=1)
    return expand, left, right.reshape(FF, 512)

def grads_kernel(
    rows_ref, cot_ref, gate_ref, w_ref, hidden_ref, up_ref, out_ref, line_ref, own, *rest
):
    bufs, (send_sem, recv_sem) = [rest[6 * i : 6 * i + 6] for i in range(2)], rest[12:]
    e = pl.program_id(0)
    plan = planner(send_sem, recv_sem)
    low, high = pl.ds(0, 512), pl.ds(512, 512)
    low_x = Reduce(plan, 0, "x", lambda i: own.at[i, :, :, low], bufs[0], half_rows)
    high_y = Reduce(plan, 6, "y", lambda i: own.at[:, i, :, high], bufs[1], half_rows)

    @pl.when(e == 0)
    def _():
        greet(near("x") + near("y"))

    expand, left, right = weights_of(w_ref)
    grad_rows = (gate_ref[0] * cot_ref[0].astype(f32)).astype(bf16)
    rows = rows_ref[0]
    gate_pre = dot(rows, expand[:, :FF], ((1,), (0,)))
    up_part = dot(rows, expand[:, FF:], ((1,), (0,)))
    sig = jax.nn.sigmoid(gate_pre)
    hidden = (gate_pre * sig * up_part).astype(bf16)
    hidden_ref[0] = hidden

    @pl.when(e == 2)
    def _():
        low_x.relay()
        high_y.relay()

    hidden_grad = dot(grad_rows[:, :1024], left, ((1,), (1,))) + dot(
        grad_rows[:, 1024:], right, ((1,), (1,))
    )
    up_ref[0, :, :FF] = (hidden_grad * up_part * sig * (1.0 + gate_pre * (1.0 - sig))).astype(bf16)
    up_ref[0, :, FF:] = (hidden_grad * gate_pre * sig).astype(bf16)

    def write(shrink_at, end_at, expand_at):
        grad_left = dot(hidden, grad_rows[:, :1024], ((0,), (0,))).astype(bf16)
        grad_right = dot(hidden, grad_rows[:, 1024:], ((0,), (0,))).astype(bf16)
        grad_right = grad_right.reshape(4, 4, 32, 512)
        shrink_at(grad_left.reshape(4, 4, 32, 1024))
        end_at(grad_right[:, :, :16], grad_right[:, :, 16:])
        up_grad = up_ref[0]
        for j in range(4):
            part = dot(rows[:, 384 * j : 384 * (j + 1)], up_grad, ((0,), (0,))).astype(bf16)
            expand_at(j, part.reshape(4, 96, 1024))

    @pl.when(e == 0)
    def _():
        def shrink_at(value):
            own[:, :, 96:128, :] = value

        def end_at(first, second):
            own[:, :, 128:144, :512] = first
            own[:, :, 128:144, 512:] = second

        def expand_at(j, value):
            own[j, :, :96, :] = value

        write(shrink_at, end_at, expand_at)
        low_x.start()
        high_y.start()

    @pl.when(e > 0)
    def _():
        def shrink_at(value):
            out_ref[:, :, 0, 96:128, :] = value

        def end_at(first, second):
            out_ref[:, :, 0, 128:144, :512] = first
            out_ref[:, :, 0, 128:144, 512:] = second

        def expand_at(j, value):
            out_ref[j, :, 0, :96, :] = value

        write(shrink_at, end_at, expand_at)

    @pl.when(e == LOCAL_E - 1)
    def _():
        line_ref[0] = low_x.total().astype(bf16)
        line_ref[1] = high_y.total().astype(bf16)
        low_x.drain()
        high_y.drain()


def expert_grads(rows, cot_rows, row_gates, weights):
    one = lambda e: (e, 0, 0)
    wide = lambda e: (0, e, 0, 0)
    out = lambda e: (0, 0, jnp.maximum(e - 1, 0), 0, 0)
    return pl.pallas_call(
        grads_kernel,
        grid=(LOCAL_E,),
        in_specs=[
            pl.BlockSpec((1, SLOTS, D), one),
            pl.BlockSpec((1, SLOTS, D), one),
            pl.BlockSpec((1, SLOTS, 1), one),
            pl.BlockSpec((16, 1, 144, 1024), wide),
        ],
        out_specs=[
            pl.BlockSpec((1, SLOTS, FF), one),
            pl.BlockSpec((1, SLOTS, 2 * FF), one),
            pl.BlockSpec((4, 4, 1, 144, 1024), out),
            pl.BlockSpec((2, 4, 144, 512), lambda e: (0, 0, 0, 0)),
        ],
        out_shape=[
            jax.ShapeDtypeStruct((LOCAL_E, SLOTS, FF), bf16),
            jax.ShapeDtypeStruct((LOCAL_E, SLOTS, 2 * FF), bf16),
            jax.ShapeDtypeStruct((4, 4, MAIN_E, 144, 1024), bf16),
            jax.ShapeDtypeStruct((2, 4, 144, 512), bf16),
        ],
        scratch_shapes=[pltpu.VMEM((4, 4, 144, 1024), bf16)]
        + reduce_scratch((4, 144, 512), (2, 144, 512)) * 2
        + sems(12),
        compiler_params=remote_params(7),
        cost_estimate=pl.CostEstimate(
            flops=12 * LOCAL_E * SLOTS * D * FF, bytes_accessed=60 << 20, transcendentals=0
        ),
    )(rows, cot_rows, row_gates, weights)


def token_trig():
    frequency = rope_base ** (-np.arange(HD // 2, dtype=np.float64) * 2.0 / HD)
    phase = np.arange(GROUP, dtype=np.float64)[:, None] * np.tile(frequency, 4)[None, :]
    return np.stack([np.cos(phase), np.sin(phase)]).astype(np.float32)


def adamw_step(weight, gradient, mean_old, square_old, rate, decay):
    drift = beta_first * mean_old + (1.0 - beta_first) * gradient
    spread = beta_second * square_old + (1.0 - beta_second) * gradient * gradient
    mean_hat = drift / (1.0 - beta_first**STEP)
    square_hat = spread / (1.0 - beta_second**STEP)
    master = weight - rate * (mean_hat / (jnp.sqrt(square_hat) + adam_eps) + decay * weight)
    return (drift, spread, master)


def on_device(
    activations,
    cotangent,
    seq_lengths,
    deal_order,
    routes,
    entry_weight,
    entry_mean,
    entry_square,
    exit_weight,
    exit_mean,
    exit_square,
    router_weight,
    router_mean,
    router_square,
    expand_weight,
    expand_mean,
    expand_square,
    shrink_weight,
    shrink_mean,
    shrink_square,
    norm_gains,
    gains_mean,
    gains_square,
):
    angles = (seq_lengths, token_trig())
    (
        weights, entry_own, exit_own, normed, rows, cot_rows, shared, gains, qkv, attended, lse,
        middle, normed_two, row_gates, rank, my_gates,
    ) = forward(
        activations[0],
        cotangent[0],
        activations[0],
        routes[0].T,
        deal_order,
        *angles,
        entry_weight,
        exit_weight,
        router_weight,
        norm_gains,
        expand_weight,
        shrink_weight,
    )
    weights = weights.reshape(16, LOCAL_E, 144, 1024)
    hidden, up_grad, expert_grad, line = expert_grads(rows, cot_rows, row_gates, weights)
    expert_grad = expert_grad.reshape(16, MAIN_E, 144, 1024)
    expert_sum = lax.psum_scatter(expert_grad, PLANE, scatter_dimension=0, tiled=False)
    middle_grad, branch_grad, logit_grad, gain_two_grad, out_sum, extra_sum = turn(
        rank,
        up_grad,
        hidden,
        row_gates,
        cot_rows,
        weights,
        line,
        middle,
        cotangent[0],
        my_gates,
        shared,
        gains[1:2],
    )
    branch_grad = branch_grad.reshape(GROUP, D)
    router_grad = dot(normed_two, logit_grad, ((0,), (0,)))

    input_rows, block_rows, entry_got, exit_got = closing(
        qkv,
        lse,
        *angles,
        exit_own,
        entry_own,
        activations[0],
        middle_grad,
        gains[0:1],
        normed,
        attended,
        branch_grad,
        router_grad,
        gain_two_grad,
        out_sum,
        middle,
    )

    input_grad, block_output = input_rows.astype(bf16), block_rows.astype(bf16)

    entry_got = entry_got[:, :ROWS]
    entry_sum = jnp.concatenate(
        [
            entry_got[:, :, :Q_OWN].transpose(1, 0, 2).reshape(ROWS, QH * HD),
            entry_got[:, :, Q_OWN:MIX_OWN].transpose(1, 0, 2).reshape(ROWS, 2 * KVH * HD),
        ],
        axis=1,
    )
    shared_sum = jnp.sum(entry_got[:, :, MIX_OWN:], axis=0)
    router_sum = shared_sum[:, :EXPERTS]
    gains_sum = shared_sum[:, EXPERTS : EXPERTS + 2].T
    exit_sum = exit_got[:ROWS]

    expand_sum, shrink_sum = to_owners(expert_sum, extra_sum)
    expand_sum, shrink_sum = expand_sum.astype(f32), shrink_sum.astype(f32)
    entry_new = adamw_step(entry_weight, entry_sum, entry_mean, entry_square, 0.02, weight_decay)
    exit_new = adamw_step(exit_weight, exit_sum, exit_mean, exit_square, 0.15, weight_decay)
    router_new = adamw_step(
        router_weight, router_sum, router_mean, router_square, 0.01, weight_decay
    )
    expand_new = adamw_step(
        expand_weight, expand_sum, expand_mean, expand_square, 0.02, weight_decay
    )
    shrink_new = adamw_step(
        shrink_weight, shrink_sum, shrink_mean, shrink_square, 0.12, weight_decay
    )
    gains_new = adamw_step(norm_gains, gains_sum, gains_mean, gains_square, 0.5, 0.0)
    return (
        block_output[None],
        input_grad[None],
        *entry_new,
        *exit_new,
        *router_new,
        *expand_new,
        *shrink_new,
        *gains_new,
    )


def solution(mesh):
    fine = Mesh(mesh.devices.reshape(4, 4, 4, 2), ("seq", "x", "y", "core"))
    rows = P(FSDP, "seq", None)
    lists = P(FSDP, None)
    owned = P(("seq",) + FSDP, None)
    experts = P("seq", FSDP, None)
    gains = P(None, ("seq",) + FSDP)
    return jax.shard_map(
        on_device,
        mesh=fine,
        in_specs=(rows, rows, lists, lists, rows)
        + (owned,) * 9
        + (experts,) * 6
        + (gains,) * 3,
        out_specs=(rows, rows) + (owned,) * 9 + (experts,) * 6 + (gains,) * 3,
        check_vma=False,
    )
```
